32 devices in a mesh: img: 4 (over y, core), rows: 2 (over x), scale: 4 (over z).
Axes of the slice: x: 2, y: 2, z: 4, core: 2. Of those that a mesh axis runs over, the one named last changes fastest.
Arguments:
- block_input: bfloat16 [4, 16, 64, 768], P('img', ('rows', 'scale')), may hold values from -6 to 6
- pre_gain: bfloat16 [768], replicated, may hold values from 0.5 to 1.5
- pre_shift: bfloat16 [768], replicated, may hold values from -0.625 to 0.625
- qkv_weight: bfloat16 [768, 2304], replicated, may hold values from -0.21875 to 0.21875
- qv_bias: bfloat16 [1536], replicated, may hold values from -0.125 to 0.125
- rel_rows: bfloat16 [31, 64], replicated, may hold values from -0.875 to 0.875
- rel_cols: bfloat16 [127, 64], replicated, may hold values from -0.875 to 0.875
- proj_weight: bfloat16 [768, 768], replicated, may hold values from -2.5 to 2.5
- proj_bias: bfloat16 [768], replicated, may hold values from -0.625 to 0.625
- mid_gain: bfloat16 [768], replicated, may hold values from 0.5 to 1.5
- mid_shift: bfloat16 [768], replicated, may hold values from -0.625 to 0.625
- fc1_weight: bfloat16 [768, 3072], replicated, may hold values from -0.21875 to 0.21875
- fc1_bias: bfloat16 [3072], replicated, may hold values from -0.625 to 0.625
- fc2_weight: bfloat16 [3072, 768], replicated, may hold values from -0.109375 to 0.109375
- fc2_bias: bfloat16 [768], replicated, may hold values from -0.625 to 0.625
- deconv_first: bfloat16 [768, 1536], replicated, may hold values from -0.21875 to 0.21875
- first_bias: bfloat16 [384], replicated, may hold values from -0.625 to 0.625
- upnorm_gain: bfloat16 [384], replicated, may hold values from 0.5 to 1.5
- upnorm_shift: bfloat16 [384], replicated, may hold values from -0.625 to 0.625
- deconv_second: bfloat16 [768, 384], replicated, may hold values from -0.3125 to 0.3125
- second_bias: bfloat16 [192], replicated, may hold values from -0.625 to 0.625
- deconv_eight: bfloat16 [768, 1536], replicated, may hold values from -0.21875 to 0.21875
- eight_bias: bfloat16 [384], replicated, may hold values from -0.625 to 0.625
- lateral_four: bfloat16 [256, 192], replicated, may hold values from -0.4375 to 0.4375
- lateral_eight: bfloat16 [256, 384], replicated, may hold values from -0.3125 to 0.3125
- lateral_sixteen: bfloat16 [256, 768], replicated, may hold values from -0.21875 to 0.21875
- lateral_thirty: bfloat16 [256, 768], replicated, may hold values from -0.21875 to 0.21875
- lateral_gain: bfloat16 [4, 256], replicated, may hold values from 0.5 to 1.5
- lateral_shift: bfloat16 [4, 256], replicated, may hold values from -0.625 to 0.625
- smooth_weight: bfloat16 [4, 2304, 256], replicated, may hold values from -0.125 to 0.125
- output_gain: bfloat16 [4, 256], replicated, may hold values from 0.5 to 1.5
- grad_four: bfloat16 [4, 64, 256, 256], P('img', 'rows'), may hold values from -6 to 6
- grad_eight: bfloat16 [4, 32, 128, 256], P('img', 'rows'), may hold values from -6 to 6
- grad_sixteen: bfloat16 [4, 16, 64, 256], P('img', 'rows'), may hold values from -6 to 6
- grad_thirty: bfloat16 [4, 8, 32, 256], P('img', 'rows'), may hold values from -6 to 6
- anchor_four: int32 [4, 64, 256], P('img', 'rows'), may hold values 0 or 1
- anchor_eight: int32 [4, 32, 128], P('img', 'rows'), may hold values 0 or 1
- anchor_sixteen: int32 [4, 16, 64], P('img', 'rows'), may hold values 0 or 1
- anchor_thirty: int32 [4, 8, 32], P('img', 'rows'), may hold values 0 or 1
- roi_mask: int32 [4, 16, 64], P('img', 'rows'), may hold values 0 or 1
Outputs:
- block_output: bfloat16 [4, 16, 64, 768], P('img', ('rows', 'scale'))
- input_grad: float32 [4, 16, 64, 768], P('img', ('rows', 'scale'))
- pre_gain_grad: float32 [768], replicated
- pre_shift_grad: float32 [768], replicated
- qkv_weight_grad: float32 [1769472], P(('img', 'rows', 'scale'))
- qv_bias_grad: float32 [1536], replicated
- rel_rows_grad: float32 [31, 64], replicated
- rel_cols_grad: float32 [127, 64], replicated
- proj_weight_grad: float32 [589824], P(('img', 'rows', 'scale'))
- proj_bias_grad: float32 [768], replicated
- mid_gain_grad: float32 [768], replicated
- mid_shift_grad: float32 [768], replicated
- fc1_weight_grad: float32 [2359296], P(('img', 'rows', 'scale'))
- fc1_bias_grad: float32 [3072], replicated
- fc2_weight_grad: float32 [2359296], P(('img', 'rows', 'scale'))
- fc2_bias_grad: float32 [768], replicated
- deconv_first_grad: float32 [1179648], P(('img', 'rows', 'scale'))
- first_bias_grad: float32 [384], replicated
- upnorm_gain_grad: float32 [384], replicated
- upnorm_shift_grad: float32 [384], replicated
- deconv_second_grad: float32 [294912], P(('img', 'rows', 'scale'))
- second_bias_grad: float32 [192], replicated
- deconv_eight_grad: float32 [1179648], P(('img', 'rows', 'scale'))
- eight_bias_grad: float32 [384], replicated
- lateral_four_grad: float32 [49152], P(('img', 'rows', 'scale'))
- lateral_eight_grad: float32 [98304], P(('img', 'rows', 'scale'))
- lateral_sixteen_grad: float32 [196608], P(('img', 'rows', 'scale'))
- lateral_thirty_grad: float32 [196608], P(('img', 'rows', 'scale'))
- lateral_gain_grad: float32 [4, 256], replicated
- lateral_shift_grad: float32 [4, 256], replicated
- smooth_weight_grad: float32 [2359296], P(('img', 'rows', 'scale'))
- output_gain_grad: float32 [4, 256], replicated
The draws below stay inside these ranges and needn't reach their ends.
All inputs are finite; a program needn't handle non-finite values. No bound on the sum of `anchor_four` or of `anchor_eight` or of `anchor_sixteen` or of `anchor_thirty` or of `roi_mask` on one device may be relied on, other than what follows from the above.
Results may differ from the reference program's by a relative error of at most 0.024.
Values may be sent and summed in bfloat16 or wider, within the bound.
A program may use at most 320 MiB of HBM per device.

```python
import jax
import jax.numpy as jnp
from jax import lax

D = 768
HEADS = 12
HDIM = 64
FF = 3072
OUT = 256
C8 = 384
C4 = 192
W = 64
H = 16
IMAGES = 4


def plant(drawn, rng, least, largest):
    extent = drawn.shape
    place = [jax.random.randint(jax.random.fold_in(rng, axis), (), 0, extent[axis]) for axis in range(len(extent))]
    drawn = drawn.at[tuple(place)].set(least)
    longest = extent.index(max(extent))
    place[longest] = (place[longest] + 1) % extent[longest]
    return drawn.at[tuple(place)].set(largest)


def steps_of(own_key, extent, split, low, top_value):
    def one(dim, shards_of):
        steps = jax.random.uniform(jax.random.fold_in(jax.random.fold_in(own_key, 6), dim), (shards_of,), jnp.float32, low / len(split), top_value / len(split))
        return jnp.repeat(jnp.exp(steps), extent[dim] // shards_of).reshape((-1,) + (1,) * (len(extent) - dim - 1))

    gain = one(*split[0])
    for cut in split[1:]:
        gain = gain * one(*cut)
    return gain


def bell_draw(key, shape, deviation, bound, pieces=(), kind=jnp.bfloat16):
    loudness = steps_of(key, shape, pieces, -0.22, 0.18) if pieces else 1.0
    values = jax.random.normal(key, shape, jnp.float32) * deviation * loudness
    return jnp.minimum(jnp.maximum(values, -bound), bound).astype(kind)


def setup_inputs(seed: int = 0) -> dict:
    arg_keys = jax.random.split(jax.random.key(seed), 41)
    block_input = bell_draw(arg_keys[0], (IMAGES, H, W, D), 1.0, 6.0, ((0, 4), (1, 8)))
    pre_gain = jnp.clip(1.0 + 0.1 * jax.random.normal(arg_keys[1], (D,), jnp.float32), 0.5, 1.5).astype(jnp.bfloat16)
    pre_shift = bell_draw(arg_keys[2], (D,), 0.1, 0.625)
    qkv_weight = bell_draw(arg_keys[3], (D, 3 * D), D ** -0.5, 0.21875)
    qv_bias = bell_draw(arg_keys[4], (2 * D,), 0.02, 0.125)
    rel_rows = bell_draw(arg_keys[5], (2 * H - 1, HDIM), 0.15, 0.875)
    rel_cols = bell_draw(arg_keys[6], (2 * W - 1, HDIM), 0.15, 0.875)
    proj_weight = bell_draw(arg_keys[7], (D, D), (max(2, D // 128)) ** -0.5, 2.5)
    proj_bias = bell_draw(arg_keys[8], (D,), 0.1, 0.625)
    mid_gain = jnp.clip(1.0 + 0.1 * jax.random.normal(arg_keys[9], (D,), jnp.float32), 0.5, 1.5).astype(jnp.bfloat16)
    mid_shift = bell_draw(arg_keys[10], (D,), 0.1, 0.625)
    fc1_weight = bell_draw(arg_keys[11], (D, FF), D ** -0.5, 0.21875)
    fc1_bias = bell_draw(arg_keys[12], (FF,), 0.1, 0.625)
    fc2_weight = bell_draw(arg_keys[13], (FF, D), FF ** -0.5, 0.109375)
    fc2_bias = bell_draw(arg_keys[14], (D,), 0.1, 0.625)
    deconv_first = bell_draw(arg_keys[15], (D, 4 * C8), D ** -0.5, 0.21875)
    first_bias = bell_draw(arg_keys[16], (C8,), 0.1, 0.625)
    upnorm_gain = jnp.clip(1.0 + 0.1 * jax.random.normal(arg_keys[17], (C8,), jnp.float32), 0.5, 1.5).astype(jnp.bfloat16)
    upnorm_shift = bell_draw(arg_keys[18], (C8,), 0.1, 0.625)
    deconv_second = bell_draw(arg_keys[19], (4 * C4, C8), C8 ** -0.5, 0.3125)
    second_bias = bell_draw(arg_keys[20], (C4,), 0.1, 0.625)
    deconv_eight = bell_draw(arg_keys[21], (D, 4 * C8), D ** -0.5, 0.21875)
    eight_bias = bell_draw(arg_keys[22], (C8,), 0.1, 0.625)
    lateral_four = bell_draw(arg_keys[23], (OUT, C4), C4 ** -0.5, 0.4375)
    lateral_eight = bell_draw(arg_keys[24], (OUT, C8), C8 ** -0.5, 0.3125)
    lateral_sixteen = bell_draw(arg_keys[25], (OUT, D), D ** -0.5, 0.21875)
    lateral_thirty = bell_draw(arg_keys[26], (OUT, D), D ** -0.5, 0.21875)
    lateral_gain = jnp.clip(1.0 + 0.1 * jax.random.normal(arg_keys[27], (4, OUT), jnp.float32), 0.5, 1.5).astype(jnp.bfloat16)
    lateral_shift = bell_draw(arg_keys[28], (4, OUT), 0.1, 0.625)
    smooth_weight = bell_draw(arg_keys[29], (4, 9 * OUT, OUT), (9 * OUT) ** -0.5, 0.125)
    output_gain = jnp.clip(1.0 + 0.1 * jax.random.normal(arg_keys[30], (4, OUT), jnp.float32), 0.5, 1.5).astype(jnp.bfloat16)
    grad_four = bell_draw(arg_keys[31], (IMAGES, 4 * H, 4 * W, OUT), 1.0, 6.0, ((0, 4), (1, 2)))
    grad_eight = bell_draw(arg_keys[32], (IMAGES, 2 * H, 2 * W, OUT), 1.0, 6.0, ((0, 4), (1, 2)))
    grad_sixteen = bell_draw(arg_keys[33], (IMAGES, H, W, OUT), 1.0, 6.0, ((0, 4), (1, 2)))
    grad_thirty = bell_draw(arg_keys[34], (IMAGES, H // 2, W // 2, OUT), 1.0, 6.0, ((0, 4), (1, 2)))
    anchor_four = plant((jax.random.randint(arg_keys[35], (IMAGES, 4 * H, 4 * W), 0, 3) < 1).astype(jnp.int32), jax.random.fold_in(arg_keys[35], 1), 0, 1)
    anchor_eight = plant((jax.random.randint(arg_keys[36], (IMAGES, 2 * H, 2 * W), 0, 3) < 1).astype(jnp.int32), jax.random.fold_in(arg_keys[36], 1), 0, 1)
    anchor_sixteen = plant((jax.random.randint(arg_keys[37], (IMAGES, H, W), 0, 3) < 1).astype(jnp.int32), jax.random.fold_in(arg_keys[37], 1), 0, 1)
    anchor_thirty = plant((jax.random.randint(arg_keys[38], (IMAGES, H // 2, W // 2), 0, 3) < 1).astype(jnp.int32), jax.random.fold_in(arg_keys[38], 1), 0, 1)
    roi_mask = plant((jax.random.randint(arg_keys[39], (IMAGES, H, W), 0, 4) < 1).astype(jnp.int32), jax.random.fold_in(arg_keys[39], 1), 0, 1)
    return dict(block_input=block_input, pre_gain=pre_gain, pre_shift=pre_shift, qkv_weight=qkv_weight, qv_bias=qv_bias, rel_rows=rel_rows, rel_cols=rel_cols, proj_weight=proj_weight, proj_bias=proj_bias, mid_gain=mid_gain, mid_shift=mid_shift, fc1_weight=fc1_weight, fc1_bias=fc1_bias, fc2_weight=fc2_weight, fc2_bias=fc2_bias, deconv_first=deconv_first, first_bias=first_bias, upnorm_gain=upnorm_gain, upnorm_shift=upnorm_shift, deconv_second=deconv_second, second_bias=second_bias, deconv_eight=deconv_eight, eight_bias=eight_bias, lateral_four=lateral_four, lateral_eight=lateral_eight, lateral_sixteen=lateral_sixteen, lateral_thirty=lateral_thirty, lateral_gain=lateral_gain, lateral_shift=lateral_shift, smooth_weight=smooth_weight, output_gain=output_gain, grad_four=grad_four, grad_eight=grad_eight, grad_sixteen=grad_sixteen, grad_thirty=grad_thirty, anchor_four=anchor_four, anchor_eight=anchor_eight, anchor_sixteen=anchor_sixteen, anchor_thirty=anchor_thirty, roi_mask=roi_mask)


@jax.custom_vjp
def low(v):
    return lax.optimization_barrier(v.astype(jnp.bfloat16)).astype(jnp.float32)

@jax.custom_vjp
def low_back(v):
    return v

def low_keep(v):
    return (low(v), None)

def low_pass(kept, grad):
    return (grad,)

def back_keep(v):
    return (v, None)

def back_low(kept, grad):
    return (low(grad),)
low.defvjp(low_keep, low_pass)
low_back.defvjp(back_keep, back_low)
highest = lax.Precision.HIGHEST
norm_eps = 1e-06

def layer_norm(values, gain_vec, shift_vec):
    centre = values - lax.optimization_barrier(jnp.mean(values, axis=-1, keepdims=True))
    spread = lax.optimization_barrier(jnp.mean(centre * centre, axis=-1, keepdims=True))
    return centre * lax.rsqrt(spread + norm_eps) * gain_vec + shift_vec

def apply_right(values, weight):
    return jnp.einsum('...c,cn->...n', values, weight, precision=highest)

def apply_left(values, weight):
    return jnp.einsum('...c,nc->...n', values, weight, precision=highest)

def unfold_taps(values):
    images, row_count, col_count, tap_count = values.shape
    channels = tap_count // 4
    values = values.reshape(images, row_count, col_count, 2, 2, channels).transpose(0, 1, 3, 2, 4, 5)
    return values.reshape(images, 2 * row_count, 2 * col_count, channels)

def smooth_conv(values, weight):
    channels = values.shape[-1]
    row_count, col_count = (values.shape[1], values.shape[2])
    padded = jnp.pad(values, ((0, 0), (1, 1), (1, 1), (0, 0)))
    summed = jnp.zeros(values.shape[:3] + (weight.shape[1],), jnp.float32)
    for offset_tap in range(9):
        row_step, col_step = (offset_tap // 3, offset_tap % 3)
        window = padded[:, row_step:row_step + row_count, col_step:col_step + col_count]
        summed = summed + apply_right(window, weight[offset_tap * channels:(offset_tap + 1) * channels])
    return summed

def offset_table(table_in, q_count, k_count, length):
    offsets = jnp.arange(q_count, dtype=jnp.int32)[:, None] - jnp.arange(k_count, dtype=jnp.int32)[None, :] + length - 1
    onehot = (offsets[:, :, None] == jnp.arange(2 * length - 1, dtype=jnp.int32)[None, None, :]).astype(jnp.float32)
    return jnp.einsum('ijr,rc->ijc', onehot, table_in, precision=highest)

def head_attend(row_table, col_table, element):
    queries, keys_all, values = element
    height, col_count, head_size = queries.shape
    plain_part = jnp.einsum('xyc,abc->xyab', queries, keys_all, precision=highest) * head_size ** (-0.5)
    by_row = jnp.einsum('xyc,xac->xya', queries, row_table, precision=highest)
    by_col = jnp.einsum('xyc,ybc->xyb', queries, col_table, precision=highest)
    scores = plain_part + by_row[:, :, :, None] + by_col[:, :, None, :]
    scores = low_back(scores.reshape(height * col_count, height * col_count))
    weights = low(jax.nn.softmax(scores, axis=-1))
    return jnp.einsum('qk,kc->qc', weights, values.reshape(height * col_count, head_size), precision=highest)

def image_forward(params, element):
    pre_gain, pre_shift, qkv_weight, qv_bias, rel_rows, rel_cols, proj_weight, proj_bias, mid_gain, mid_shift, fc1_weight, fc1_bias, fc2_weight, fc2_bias, deconv_first, first_bias, upnorm_gain, upnorm_shift, deconv_second, second_bias, deconv_eight, eight_bias, lateral_four, lateral_eight, lateral_sixteen, lateral_thirty, lateral_gain, lateral_shift, smooth_weight, output_gain = params
    block_in, weight_four, weight_eight, weight_sixteen, weight_thirty = element
    block_in = block_in[None]
    height, col_count = (block_in.shape[1], block_in.shape[2])
    normed = low(layer_norm(block_in, pre_gain, pre_shift))
    mixed_all = apply_right(normed, qkv_weight)
    queries = low(low_back(mixed_all[..., :D] + qv_bias[:D]))
    keys_all = low(low_back(mixed_all[..., D:2 * D]))
    values = low(low_back(mixed_all[..., 2 * D:] + qv_bias[D:]))

    def split_heads(tensor):
        return tensor.reshape(height, col_count, HEADS, HDIM).transpose(2, 0, 1, 3)
    row_table = offset_table(rel_rows, height, height, height)
    col_table = offset_table(rel_cols, col_count, col_count, col_count)

    def attend_one(element_in):
        return head_attend(row_table, col_table, element_in)
    attended = lax.map(jax.checkpoint(attend_one), (split_heads(queries), split_heads(keys_all), split_heads(values)))
    attended = attended.transpose(1, 0, 2).reshape(1, height, col_count, D)
    attended = low(low_back(attended))
    branch = low_back(apply_right(attended, proj_weight) + proj_bias)
    middle = block_in + branch
    hidden = low_back(apply_right(low(layer_norm(middle, mid_gain, mid_shift)), fc1_weight) + fc1_bias)
    hidden = low(jax.nn.gelu(hidden, approximate=False))
    result = low(low_back(middle + low_back(apply_right(hidden, fc2_weight) + fc2_bias)))

    def finish(source, lateral, scale_level):
        reduced = low_back(apply_left(source, lateral))
        lateral_out = low(layer_norm(reduced, lateral_gain[scale_level], lateral_shift[scale_level]))
        smoothed = low_back(smooth_conv(lateral_out, smooth_weight[scale_level]))
        return layer_norm(smoothed, output_gain[scale_level], 0.0)
    first_map = low_back(unfold_taps(apply_right(result, deconv_first)) + first_bias)
    first_map = low(jax.nn.gelu(layer_norm(first_map, upnorm_gain, upnorm_shift), approximate=False))
    second = low(low_back(unfold_taps(apply_left(first_map, deconv_second)) + second_bias))
    level_four = finish(second, lateral_four, 0)
    eight_map = low(low_back(unfold_taps(apply_right(result, deconv_eight)) + eight_bias))
    level_eight = finish(eight_map, lateral_eight, 1)
    level_sixteen = finish(result, lateral_sixteen, 2)
    pooled = low(lax.optimization_barrier(jnp.mean(result.reshape(1, height // 2, 2, col_count // 2, 2, D), axis=(2, 4))))
    level_thirty = finish(pooled, lateral_thirty, 3)
    loss_sum = jnp.sum(weight_four[None] * level_four) + jnp.sum(weight_eight[None] * level_eight) + jnp.sum(weight_sixteen[None] * level_sixteen) + jnp.sum(weight_thirty[None] * level_thirty)
    return (result[0], loss_sum)

def reference(block_input, pre_gain, pre_shift, qkv_weight, qv_bias, rel_rows, rel_cols, proj_weight, proj_bias, mid_gain, mid_shift, fc1_weight, fc1_bias, fc2_weight, fc2_bias, deconv_first, first_bias, upnorm_gain, upnorm_shift, deconv_second, second_bias, deconv_eight, eight_bias, lateral_four, lateral_eight, lateral_sixteen, lateral_thirty, lateral_gain, lateral_shift, smooth_weight, output_gain, grad_four, grad_eight, grad_sixteen, grad_thirty, anchor_four, anchor_eight, anchor_sixteen, anchor_thirty, roi_mask):
    params = tuple((tensor.astype(jnp.float32) for tensor in (pre_gain, pre_shift, qkv_weight, qv_bias, rel_rows, rel_cols, proj_weight, proj_bias, mid_gain, mid_shift, fc1_weight, fc1_bias, fc2_weight, fc2_bias, deconv_first, first_bias, upnorm_gain, upnorm_shift, deconv_second, second_bias, deconv_eight, eight_bias, lateral_four, lateral_eight, lateral_sixteen, lateral_thirty, lateral_gain, lateral_shift, smooth_weight, output_gain)))
    roi_four = jnp.repeat(jnp.repeat(roi_mask, 4, axis=1), 4, axis=2)
    roi_eight = jnp.repeat(jnp.repeat(roi_mask, 2, axis=1), 2, axis=2)
    roi_thirty = roi_mask[:, ::2, ::2]
    weighted = ((anchor_four + roi_four).astype(jnp.float32)[..., None] * grad_four.astype(jnp.float32), (anchor_eight + roi_eight).astype(jnp.float32)[..., None] * grad_eight.astype(jnp.float32), (anchor_sixteen + roi_mask).astype(jnp.float32)[..., None] * grad_sixteen.astype(jnp.float32), (anchor_thirty + roi_thirty).astype(jnp.float32)[..., None] * grad_thirty.astype(jnp.float32))

    def whole_batch(param_set, block_in):

        def one_image(element):
            return image_forward(param_set, element)
        outputs, losses = lax.map(jax.checkpoint(one_image), (block_in,) + weighted)
        return (outputs, jnp.sum(losses))
    (outputs, loss_sum), pullback = jax.vjp(whole_batch, params, block_input.astype(jnp.float32))
    param_grads, input_grad = pullback((jnp.zeros_like(outputs), jnp.ones_like(loss_sum)))
    pre_gain_grad, pre_shift_grad, qkv_weight_grad, qv_bias_grad, rel_rows_grad, rel_cols_grad, proj_weight_grad, proj_bias_grad, mid_gain_grad, mid_shift_grad, fc1_weight_grad, fc1_bias_grad, fc2_weight_grad, fc2_bias_grad, deconv_first_grad, first_bias_grad, upnorm_gain_grad, upnorm_shift_grad, deconv_second_grad, second_bias_grad, deconv_eight_grad, eight_bias_grad, lateral_four_grad, lateral_eight_grad, lateral_sixteen_grad, lateral_thirty_grad, lateral_gain_grad, lateral_shift_grad, smooth_weight_grad, output_gain_grad = param_grads
    return (outputs.astype(jnp.bfloat16), input_grad, pre_gain_grad, pre_shift_grad, qkv_weight_grad.reshape(-1), qv_bias_grad, rel_rows_grad, rel_cols_grad, proj_weight_grad.reshape(-1), proj_bias_grad, mid_gain_grad, mid_shift_grad, fc1_weight_grad.reshape(-1), fc1_bias_grad, fc2_weight_grad.reshape(-1), fc2_bias_grad, deconv_first_grad.reshape(-1), first_bias_grad, upnorm_gain_grad, upnorm_shift_grad, deconv_second_grad.reshape(-1), second_bias_grad, deconv_eight_grad.reshape(-1), eight_bias_grad, lateral_four_grad.reshape(-1), lateral_eight_grad.reshape(-1), lateral_sixteen_grad.reshape(-1), lateral_thirty_grad.reshape(-1), lateral_gain_grad, lateral_shift_grad, smooth_weight_grad.reshape(-1), output_gain_grad)
```

```python
from functools import partial

import jax
import jax.numpy as jnp
from jax import lax
from jax.experimental import pallas as pl
from jax.experimental.pallas import tpu as pltpu
from jax.sharding import PartitionSpec as P

highest = lax.Precision.HIGHEST
norm_eps = 1e-06
wide_type = jnp.float32
narrow_type = jnp.bfloat16

MESH_ID = pl.DeviceIdType.MESH
lanes = 128


def axis_bits(size):
    bits = []
    step = 1
    while step < size:
        bits.append(step)
        step *= 2
    return bits


def bit_partner(axis, step):
    here = lax.axis_index(axis)
    bit = lax.rem(lax.div(here, step), 2)
    return {axis: here + step - 2 * step * bit}, bit


def reduce_kernel(orders, dims, stages, refs):
    count = len(orders)
    sources = refs[:count]
    small_in = refs[count]
    outs = refs[count + 1 : 2 * count + 1]
    small_out = refs[2 * count + 1]
    scratch = refs[2 * count + 2 :]
    held = scratch[:count]
    landed = [scratch[count + t * stages : count + (t + 1) * stages] for t in range(count)]
    rest = scratch[count + count * stages :]
    small_held, small_landed = rest[0], rest[1]
    send_sem, recv_sem, local_sem, small_send, small_recv = rest[2:]
    partners = [bit_partner(axis, step) for axis, step in dims]
    barrier = pltpu.get_barrier_semaphore()
    for partner, _ in partners:
        pl.semaphore_signal(barrier, inc=1, device_id=partner, device_id_type=MESH_ID)
    pl.semaphore_wait(barrier, len(dims))

    def picked(taken, current, keep):
        index = []
        for dim in range(len(dims)):
            bit = partners[dim][1]
            if dim in taken:
                index.append(bit)
            elif dim == current:
                index.append(bit if keep else 1 - bit)
            else:
                index.append(slice(None))
        return index

    def held_index(index):
        core = core_dim(dims)
        return tuple(index[:core] + index[core + 1 :])

    def copy(t, stage):
        current = orders[t][stage]
        taken = set(orders[t][:stage])
        index = picked(taken, current, False)
        if stage == 0:
            source = sources[t].at[tuple(index)]
        else:
            source = held[t].at[held_index(index)]
        return pltpu.make_async_remote_copy(
            src_ref=source,
            dst_ref=landed[t][stage],
            send_sem=send_sem.at[t, stage],
            recv_sem=recv_sem.at[t, stage],
            device_id=partners[current][0],
            device_id_type=MESH_ID,
        )

    def local_copy(t):
        index = picked(set(), orders[t][0], True)
        return pltpu.make_async_copy(sources[t].at[tuple(index)], held[t], local_sem.at[t])

    def add(t, stage):
        current = orders[t][stage]
        taken = set(orders[t][:stage])
        index = held_index(picked(taken, current, True))
        target = held[t].at[index]
        arrived = landed[t][stage]
        lead = arrived.shape[:-2]
        rows = arrived.shape[-2]
        total = 1
        for size in lead:
            total *= size
        def body(step, carry):
            place = []
            rem_step = step
            for size in reversed(lead):
                place.append(lax.rem(rem_step, size))
                rem_step = lax.div(rem_step, size)
            place = tuple(reversed(place))
            target[place] = target[place] + arrived[place]
            return carry

        if lead:
            lax.fori_loop(0, total, body, 0)
        else:
            target[...] = target[...] + arrived[...]

    def small_copy(stage):
        return pltpu.make_async_remote_copy(
            src_ref=small_held,
            dst_ref=small_landed.at[stage],
            send_sem=small_send.at[stage],
            recv_sem=small_recv.at[stage],
            device_id=partners[orders[0][stage]][0],
            device_id_type=MESH_ID,
        )

    small_held[...] = small_in[...]
    small_copy(0).start()
    for t in range(count):
        copy(t, 0).start()
        local_copy(t).start()
    for stage in range(stages):
        for t in range(count):
            copy(t, stage).wait_recv()
            if stage == 0:
                local_copy(t).wait()
            add(t, stage)
            if stage + 1 < stages:
                copy(t, stage + 1).start()
            else:
                index = held_index(picked(set(orders[t]), -1, True))
                outs[t][...] = held[t][index].astype(jnp.float32)
        small_copy(stage).wait()
        small_held[...] = small_held[...] + small_landed[stage]
        if stage + 1 < stages:
            small_copy(stage + 1).start()
    small_out[...] = small_held[...]
    for t in range(count):
        for stage in range(stages):
            copy(t, stage).wait_send()


def core_dim(dims):
    return [i for i, (axis, step) in enumerate(dims) if axis == "img" and step == 1][0]


def reduce_all(pieces, small, call_id):
    sizes = {axis: lax.axis_size(axis) for axis in ("img", "rows", "scale")}
    dims = []
    for axis in ("img", "rows", "scale"):
        for step in reversed(axis_bits(sizes[axis])):
            dims.append((axis, step))
    core = core_dim(dims)
    plane = [i for i, (axis, step) in enumerate(dims) if axis == "img" and i != core]
    across = [i for i, (axis, step) in enumerate(dims) if axis == "rows"]
    along = list(reversed([i for i, (axis, step) in enumerate(dims) if axis == "scale"]))
    first_order = [core] + across + plane + along
    second_order = [core] + plane + across + along
    count, stages = len(pieces), len(dims)
    orders = [first_order if t % 2 == 0 else second_order for t in range(count)]
    shapes = [piece.shape[1:] for piece in pieces]
    shaped = [piece.reshape((2,) * stages + piece.shape[1:]) for piece in pieces]
    scratch = [pltpu.VMEM((2,) * (stages - 1) + shape, jnp.bfloat16) for shape in shapes]
    for t in range(count):
        for stage in range(stages):
            scratch.append(pltpu.VMEM((2,) * (stages - 1 - stage) + shapes[t], jnp.bfloat16))
    scratch += [
        pltpu.VMEM(small.shape, jnp.float32),
        pltpu.VMEM((stages,) + small.shape, jnp.float32),
        pltpu.SemaphoreType.DMA((count, stages)),
        pltpu.SemaphoreType.DMA((count, stages)),
        pltpu.SemaphoreType.DMA((count,)),
        pltpu.SemaphoreType.DMA((stages,)),
        pltpu.SemaphoreType.DMA((stages,)),
    ]

    def body(*refs):
        reduce_kernel(orders, dims, stages, refs)

    vmem = pl.BlockSpec(memory_space=pltpu.VMEM)
    got = pl.pallas_call(
        body,
        out_shape=[jax.ShapeDtypeStruct(shape, jnp.float32) for shape in shapes]
        + [jax.ShapeDtypeStruct(small.shape, jnp.float32)],
        in_specs=[pl.BlockSpec(memory_space=pl.ANY)] * count + [vmem],
        out_specs=[vmem] * (count + 1),
        scratch_shapes=scratch,
        compiler_params=pltpu.CompilerParams(
            collective_id=call_id, has_side_effects=True, vmem_limit_bytes=62 << 20
        ),
        name="reduce_grads",
    )(*shaped, small)
    return got[:-1], got[-1]


def pack_small(parts):
    flat = jnp.concatenate([part.reshape(-1) for part in parts])
    unit = 8 * lanes
    total = -(-flat.shape[0] // unit) * unit
    return jnp.pad(flat, (0, total - flat.shape[0])).reshape(-1, lanes)


def unpack_small(packed, parts):
    flat = packed.reshape(-1)
    out, at = [], 0
    for part in parts:
        out.append(flat[at : at + part.size].reshape(part.shape))
        at += part.size
    return out


def chunk_piece(parts):
    stacked = jnp.concatenate(parts, axis=1) if len(parts) > 1 else parts[0]
    rows = stacked.shape[1]
    extra = -rows % 16
    if extra:
        stacked = jnp.pad(stacked, ((0, 0), (0, extra), (0, 0)))
    return stacked


def reduce_weights(groups, small_parts, call_id):
    devices = lax.axis_size(("img", "rows", "scale"))
    pieces, plans = [], []
    for group in groups:
        cut, plan = [], []
        for grad in group:
            rows, columns = grad.shape
            own = rows // devices
            chunk = grad.astype(narrow_type).reshape(devices, own, columns)
            folds = 1
            while (own * folds) % 16 and columns % (2 * folds * lanes) == 0:
                folds *= 2
            width = columns // folds
            if folds > 1:
                cut += [chunk[:, :, f * width : (f + 1) * width] for f in range(folds)]
            else:
                cut.append(chunk)
            plan.append((own, columns, folds))
        pieces.append(chunk_piece(cut))
        plans.append(plan)
    sums, small = reduce_all(pieces, pack_small(small_parts), call_id)
    out = []
    for plan, summed in zip(plans, sums):
        at, got = 0, []
        for own, columns, folds in plan:
            parts = []
            for f in range(folds):
                parts.append(summed[at : at + own])
                at += own
            whole = jnp.concatenate(parts, axis=1) if folds > 1 else parts[0]
            got.append(whole.reshape(-1))
        out.append(got)
    return out, unpack_small(small, small_parts)


def with_edges(value):
    axes = ("rows", "scale")
    size, length = (lax.axis_size(axes), value.shape[1])
    up = [(i, i + 1) for i in range(size - 1)]
    down = [(j, i) for i, j in up]
    before = lax.ppermute(value[:, length - 1 :], axes, up)
    after = lax.ppermute(value[:, :1], axes, down)
    return jnp.concatenate([before, value, after], axis=1)


def as_sent(value):
    return jax.tree.map(lambda a: a.astype(jnp.bfloat16) if a.dtype == jnp.float32 else a, value)


def layer_norm(values, gain_vec, shift_vec):
    centre = values - jnp.mean(values, axis=-1, keepdims=True)
    spread = jnp.mean(centre * centre, axis=-1, keepdims=True)
    return centre * lax.rsqrt(spread + norm_eps) * gain_vec + shift_vec


def scaled_norm(values, gain_vec):
    centre = values - jnp.mean(values, axis=-1, keepdims=True)
    spread = jnp.mean(centre * centre, axis=-1, keepdims=True)
    return centre * lax.rsqrt(spread + norm_eps) * gain_vec


def apply_right(values, weight):
    return jnp.einsum("...c,cn->...n", values, weight, preferred_element_type=wide_type)


def apply_left(values, weight):
    return jnp.einsum("...c,nc->...n", values, weight, preferred_element_type=wide_type)


def outer_sum(left_side, right_side):
    return jnp.einsum("...a,...b->ab", left_side, right_side, preferred_element_type=wide_type)


def position_sum(values):
    return jnp.sum(values, axis=(0, 1, 2), dtype=wide_type)


def unfold_taps(values):
    images, row_count, col_count, tap_count = values.shape
    channels = tap_count // 4
    values = values.reshape(images, row_count, col_count, 2, 2, channels).transpose(
        0, 1, 3, 2, 4, 5
    )
    return values.reshape(images, 2 * row_count, 2 * col_count, channels)


def fold_taps(values):
    images, row_count, col_count, channels = values.shape
    values = values.reshape(images, row_count // 2, 2, col_count // 2, 2, channels).transpose(
        0, 1, 3, 2, 4, 5
    )
    return values.reshape(images, row_count // 2, col_count // 2, 4 * channels)


def offset_hot(q_start, q_count, k_count, length):
    offsets = (
        (q_start + jnp.arange(q_count, dtype=jnp.int32))[:, None]
        - jnp.arange(k_count, dtype=jnp.int32)[None, :]
        + length
        - 1
    )
    return (
        offsets[:, :, None] == jnp.arange(2 * length - 1, dtype=jnp.int32)[None, None, :]
    ).astype(wide_type)


def offset_rows(onehot, table_in):
    return jnp.einsum("ijr,rc->ijc", onehot, table_in, precision=highest)


def per_head(values, head_count, head_size):
    return values.reshape(values.shape[:-1] + (head_count, head_size))


def attention_scores(query_img, key_img, row_table, col_table):
    q_rows, col_count, head_count, head_size = query_img.shape
    k_rows = key_img.shape[0]
    plain_part = jnp.einsum(
        "xyhc,abhc->hxyab", query_img, key_img, preferred_element_type=wide_type
    ) * head_size ** (-0.5)
    query_wide = query_img.astype(wide_type)
    by_row = jnp.einsum("xyhc,xac->hxya", query_wide, row_table, precision=highest)
    by_col = jnp.einsum("xyhc,ybc->hxyb", query_wide, col_table, precision=highest)
    summed = plain_part + by_row[:, :, :, :, None] + by_col[:, :, :, None, :]
    return summed.reshape(head_count, q_rows * col_count, k_rows * col_count)


def score_back(score_grad, query_img, key_flat, row_table, col_table):
    q_rows, col_count, head_count, head_size = query_img.shape
    k_rows = row_table.shape[1]
    blocks = score_grad.reshape(head_count, q_rows, col_count, k_rows, col_count)
    by_row = jnp.sum(blocks, axis=4, dtype=wide_type)
    by_col = jnp.sum(blocks, axis=3, dtype=wide_type)
    plain_part = jnp.einsum(
        "hqk,khc->qhc", score_grad, key_flat, preferred_element_type=wide_type
    ) * head_size ** (-0.5)
    plain_part = plain_part.reshape(query_img.shape)
    query_wide = query_img.astype(wide_type)
    rel_part = jnp.einsum("hxya,xac->xyhc", by_row, row_table, precision=highest) + jnp.einsum(
        "hxyb,ybc->xyhc", by_col, col_table, precision=highest
    )
    row_part = jnp.einsum("hxya,xyhc->xac", by_row, query_wide, precision=highest)
    col_part = jnp.einsum("hxyb,xyhc->ybc", by_col, query_wide, precision=highest)
    return (plain_part + rel_part, row_part, col_part)


def smooth_forward(values, weight):
    padded = with_edges(values)
    channels = values.shape[-1]
    kernel = weight.reshape(3, 3, channels, weight.shape[1])
    summed = lax.conv_general_dilated(
        padded,
        kernel,
        (1, 1),
        ((0, 0), (1, 1)),
        dimension_numbers=("NHWC", "HWIO", "NHWC"),
        preferred_element_type=wide_type,
    )
    return (summed, padded)


def smooth_backward(padded, upstream, weight):
    channels, outputs = padded.shape[3], upstream.shape[3]
    beside_all = with_edges(upstream)
    kernel = weight.reshape(3, 3, channels, outputs)[::-1, ::-1]
    input_grad = lax.conv_general_dilated(
        beside_all,
        kernel,
        (1, 1),
        ((0, 0), (1, 1)),
        dimension_numbers=("NHWC", "HWOI", "NHWC"),
        preferred_element_type=wide_type,
    )
    weight_grad = lax.conv_general_dilated(
        padded,
        upstream,
        (1, 1),
        ((0, 0), (1, 1)),
        dimension_numbers=("CHWN", "IHWO", "HWNC"),
        preferred_element_type=wide_type,
    )
    return (input_grad, weight_grad.reshape(9 * channels, outputs))


def finish_level(source, lateral, gain_vec, shift_vec, smooth, out_gain, loss_weight):
    reduced = apply_left(source, lateral)
    normed, norm_pull = jax.vjp(
        layer_norm, reduced, gain_vec.astype(wide_type), shift_vec.astype(wide_type)
    )
    normed_low = normed.astype(narrow_type)
    smoothed, padded = smooth_forward(normed_low, smooth)
    level_out, out_pull = jax.vjp(scaled_norm, smoothed, out_gain.astype(wide_type))
    smoothed_grad, out_gain_grad = out_pull(loss_weight)
    smoothed_low = smoothed_grad.astype(narrow_type)
    normed_grad, smooth_grad = smooth_backward(padded, smoothed_low, smooth)
    reduced_grad, gain_grad, shift_grad = norm_pull(normed_grad)
    reduced_low = reduced_grad.astype(narrow_type)
    lateral_grad = outer_sum(reduced_low, source)
    source_grad = apply_right(reduced_low, lateral)
    return (source_grad, lateral_grad, gain_grad, shift_grad, smooth_grad, out_gain_grad)


def squash(pre_values, gain_vec, shift_vec):
    return jax.nn.gelu(layer_norm(pre_values, gain_vec, shift_vec), approximate=False)


def pyramid_level(scale_level, strip, loss_weight, pyramid):
    (
        deconv_first,
        first_bias,
        upnorm_gain,
        upnorm_shift,
        deconv_second,
        second_bias,
        deconv_eight,
        eight_bias,
        lateral_four,
        lateral_eight,
        lateral_sixteen,
        lateral_thirty,
        lateral_gain,
        lateral_shift,
        smooth_weight,
        output_gain,
    ) = pyramid
    grads = [jnp.zeros(tensor.shape, wide_type) for tensor in pyramid]
    laterals = (lateral_four, lateral_eight, lateral_sixteen, lateral_thirty)
    if scale_level == 0:
        first_map = unfold_taps(apply_right(strip, deconv_first)) + first_bias.astype(wide_type)
        active, squash_pull = jax.vjp(
            squash, first_map, upnorm_gain.astype(wide_type), upnorm_shift.astype(wide_type)
        )
        active_low = active.astype(narrow_type)
        source = (
            unfold_taps(apply_left(active_low, deconv_second)) + second_bias.astype(wide_type)
        ).astype(narrow_type)
    elif scale_level == 1:
        source = (
            unfold_taps(apply_right(strip, deconv_eight)) + eight_bias.astype(wide_type)
        ).astype(narrow_type)
    elif scale_level == 2:
        source = strip
    else:
        images, row_count, col_count, channels = strip.shape
        pooled = jnp.mean(
            strip.astype(wide_type).reshape(images, row_count // 2, 2, col_count // 2, 2, channels),
            axis=(2, 4),
        )
        source = pooled.astype(narrow_type)
    source_grad, lateral_grad, gain_grad, shift_grad, smooth_grad, out_gain_grad = finish_level(
        source,
        laterals[scale_level],
        lateral_gain[scale_level],
        lateral_shift[scale_level],
        smooth_weight[scale_level],
        output_gain[scale_level],
        loss_weight,
    )
    grads[8 + scale_level] = lateral_grad
    grads[12] = grads[12].at[scale_level].set(gain_grad)
    grads[13] = grads[13].at[scale_level].set(shift_grad)
    grads[14] = grads[14].at[scale_level].set(smooth_grad)
    grads[15] = grads[15].at[scale_level].set(out_gain_grad)
    if scale_level == 0:
        second_low = source_grad.astype(narrow_type)
        folded = fold_taps(second_low)
        grads[5] = position_sum(second_low)
        grads[4] = outer_sum(folded, active_low)
        active_grad = apply_right(folded, deconv_second)
        first_grad, grads[2], grads[3] = squash_pull(active_grad)
        first_low = first_grad.astype(narrow_type)
        folded = fold_taps(first_low)
        grads[1] = position_sum(first_low)
        grads[0] = outer_sum(strip, folded)
        strip_grad = apply_left(folded, deconv_first)
    elif scale_level == 1:
        eight_low = source_grad.astype(narrow_type)
        folded = fold_taps(eight_low)
        grads[7] = position_sum(eight_low)
        grads[6] = outer_sum(strip, folded)
        strip_grad = apply_left(folded, deconv_eight)
    elif scale_level == 2:
        strip_grad = source_grad
    else:
        images, row_count, col_count, channels = strip.shape
        spread_out = jnp.broadcast_to(
            source_grad[:, :, None, :, None, :] * 0.25,
            (images, row_count // 2, 2, col_count // 2, 2, channels),
        )
        strip_grad = spread_out.reshape(images, row_count, col_count, channels)
    return (strip_grad, tuple(grads))


def own_rows(values, count):
    return lax.dynamic_slice_in_dim(values, lax.axis_index("scale") * count, count, axis=1)


def level_weight(scale_level, strip_rows, cotans, anchors, roi_mask):
    region = own_rows(roi_mask, strip_rows)
    if scale_level < 3:
        factor = (4, 2, 1)[scale_level]
        region = jnp.repeat(jnp.repeat(region, factor, axis=1), factor, axis=2)
        count = factor * strip_rows
    else:
        region = region[:, ::2, ::2]
        count = strip_rows // 2
    anchor = own_rows(anchors[scale_level], count)
    cotangent = own_rows(cotans[scale_level], count)
    return (anchor + region).astype(wide_type)[..., None] * cotangent.astype(wide_type)


def on_device(
    block_input,
    pre_gain,
    pre_shift,
    qkv_weight,
    qv_bias,
    rel_rows,
    rel_cols,
    proj_weight,
    proj_bias,
    mid_gain,
    mid_shift,
    fc1_weight,
    fc1_bias,
    fc2_weight,
    fc2_bias,
    deconv_first,
    first_bias,
    upnorm_gain,
    upnorm_shift,
    deconv_second,
    second_bias,
    deconv_eight,
    eight_bias,
    lateral_four,
    lateral_eight,
    lateral_sixteen,
    lateral_thirty,
    lateral_gain,
    lateral_shift,
    smooth_weight,
    output_gain,
    grad_four,
    grad_eight,
    grad_sixteen,
    grad_thirty,
    anchor_four,
    anchor_eight,
    anchor_sixteen,
    anchor_thirty,
    roi_mask,
):
    images, strip_rows, col_count, model_width = block_input.shape
    head_size = rel_rows.shape[1]
    head_count = model_width // head_size
    scale_factor = head_size ** (-0.5)
    height = strip_rows * lax.axis_size(("rows", "scale"))
    first_row = lax.axis_index(("rows", "scale")) * strip_rows
    pyramid = (
        deconv_first,
        first_bias,
        upnorm_gain,
        upnorm_shift,
        deconv_second,
        second_bias,
        deconv_eight,
        eight_bias,
        lateral_four,
        lateral_eight,
        lateral_sixteen,
        lateral_thirty,
        lateral_gain,
        lateral_shift,
        smooth_weight,
        output_gain,
    )
    cotans = (grad_four, grad_eight, grad_sixteen, grad_thirty)
    anchors = (anchor_four, anchor_eight, anchor_sixteen, anchor_thirty)
    inputs_wide = block_input.astype(wide_type)
    normed, pre_pull = jax.vjp(
        layer_norm, inputs_wide, pre_gain.astype(wide_type), pre_shift.astype(wide_type)
    )
    normed_low = normed.astype(narrow_type)
    mixed_all = apply_right(normed_low, qkv_weight)
    bias_wide = qv_bias.astype(wide_type)
    queries = (mixed_all[..., :model_width] + bias_wide[:model_width]).astype(narrow_type)
    keys_own = mixed_all[..., model_width : 2 * model_width].astype(narrow_type)
    values_own = (mixed_all[..., 2 * model_width :] + bias_wide[model_width:]).astype(narrow_type)
    keys_all, values_all = (
        lax.all_gather(keys_own, ("rows", "scale"), axis=1, tiled=True),
        lax.all_gather(values_own, ("rows", "scale"), axis=1, tiled=True),
    )
    row_wide = rel_rows.astype(wide_type)
    col_wide = rel_cols.astype(wide_type)
    row_hot = offset_hot(first_row, strip_rows, height, height)
    col_hot = offset_hot(0, col_count, col_count, col_count)
    row_table = offset_rows(row_hot, row_wide)
    col_table = offset_rows(col_hot, col_wide)
    query_heads = per_head(queries, head_count, head_size)
    key_heads = per_head(keys_all, head_count, head_size)
    value_heads = per_head(values_all, head_count, head_size)

    def attend_image(element):
        query_img, key_img, value_img = element
        scores = attention_scores(query_img, key_img, row_table, col_table)
        row_peak = jnp.max(scores, axis=-1, keepdims=True)
        exponent = jnp.exp(scores - row_peak)
        summed = jnp.sum(exponent, axis=-1, keepdims=True)
        weights = (exponent / summed).astype(narrow_type)
        mixed_out = jnp.einsum(
            "hqk,khc->qhc",
            weights,
            value_img.reshape(-1, head_count, head_size),
            preferred_element_type=wide_type,
        )
        return (mixed_out, (row_peak + jnp.log(summed))[..., 0])

    attended, log_norm = lax.map(attend_image, (query_heads, key_heads, value_heads))
    attended_low = attended.reshape(images, strip_rows, col_count, model_width).astype(narrow_type)
    branch = apply_right(attended_low, proj_weight) + proj_bias.astype(wide_type)
    middle = inputs_wide + branch
    normed_mid, mid_pull = jax.vjp(
        layer_norm, middle, mid_gain.astype(wide_type), mid_shift.astype(wide_type)
    )
    normed_mid_low = normed_mid.astype(narrow_type)
    hidden_pre = apply_right(normed_mid_low, fc1_weight) + fc1_bias.astype(wide_type)
    hidden_act, act_pull = jax.vjp(partial(jax.nn.gelu, approximate=False), hidden_pre)
    hidden_low = hidden_act.astype(narrow_type)
    result = middle + (apply_right(hidden_low, fc2_weight) + fc2_bias.astype(wide_type))
    result_low = result.astype(narrow_type)
    strip_grad = 0.0
    pyramid_grads = [jnp.zeros(tensor.shape, wide_type) for tensor in pyramid]
    for scale_level in range(4):
        weight = level_weight(scale_level, strip_rows, cotans, anchors, roi_mask)
        level_strip, level_grads = pyramid_level(scale_level, result_low, weight, pyramid)
        strip_grad = strip_grad + level_strip
        pyramid_grads = [held + grad for held, grad in zip(pyramid_grads, level_grads)]
    result_grad = strip_grad.astype(narrow_type)
    fc2_bias_grad = position_sum(result_grad)
    (pre_act_grad,) = act_pull(apply_left(result_grad, fc2_weight))
    pre_low = pre_act_grad.astype(narrow_type)
    fc1_bias_grad = position_sum(pre_low)
    mid_grad, mid_gain_grad, mid_shift_grad = mid_pull(apply_left(pre_low, fc1_weight))
    middle_grad = result_grad.astype(wide_type) + mid_grad
    branch_low = middle_grad.astype(narrow_type)
    proj_bias_grad = position_sum(branch_low)
    attended_grad = apply_left(branch_low, proj_weight).astype(narrow_type)
    grad_heads = per_head(attended_grad, head_count, head_size)

    def query_pass(with_keys, element):
        query_img, grad_img, lse_img, key_img, value_img = element
        scores = attention_scores(query_img, key_img, row_table, col_table)
        weights = jnp.exp(scores - lse_img[..., None])
        grad_flat = grad_img.reshape(-1, head_count, head_size)
        key_flat = key_img.reshape(-1, head_count, head_size)
        prob_grad = jnp.einsum(
            "qhc,khc->hqk",
            grad_flat,
            value_img.reshape(-1, head_count, head_size),
            preferred_element_type=wide_type,
        )
        spread_sum = jnp.sum(weights * prob_grad, axis=-1)
        score_grad = (weights * (prob_grad - spread_sum[..., None])).astype(narrow_type)
        query_grad, row_part, col_part = score_back(
            score_grad, query_img, key_flat, row_table, col_table
        )
        query_flat = query_img.reshape(-1, head_count, head_size)
        key_grad = (
            jnp.einsum("hqk,qhc->khc", score_grad, query_flat, preferred_element_type=wide_type)
            * scale_factor
        )
        value_grad = jnp.einsum(
            "hqk,qhc->khc", weights.astype(narrow_type), grad_flat, preferred_element_type=wide_type
        )
        return (query_grad, row_part, col_part, spread_sum, key_grad, value_grad)

    query_grad, row_part, col_part, spread_sums, key_grad, value_grad = lax.map(
        partial(query_pass, True), (query_heads, grad_heads, log_norm, key_heads, value_heads)
    )
    full_shape = (images, height, col_count, model_width)
    key_part, value_part = (
        lax.psum_scatter(
            key_grad.reshape(full_shape).astype(jnp.bfloat16),
            ("rows", "scale"),
            scatter_dimension=1,
            tiled=True,
        ).astype(jnp.float32),
        lax.psum_scatter(
            value_grad.reshape(full_shape).astype(jnp.bfloat16),
            ("rows", "scale"),
            scatter_dimension=1,
            tiled=True,
        ).astype(jnp.float32),
    )
    rel_rows_grad = jnp.einsum("ijr,ijc->rc", row_hot, jnp.sum(row_part, axis=0), precision=highest)
    rel_cols_grad = jnp.einsum("ijr,ijc->rc", col_hot, jnp.sum(col_part, axis=0), precision=highest)
    query_low = query_grad.reshape(images, strip_rows, col_count, model_width).astype(narrow_type)
    key_low = key_part.astype(narrow_type)
    value_low = value_part.astype(narrow_type)
    joined_low = jnp.concatenate((query_low, key_low, value_low), axis=-1)
    qv_bias_grad = jnp.concatenate((position_sum(query_low), position_sum(value_low)))
    pre_in_grad, pre_gain_grad, pre_shift_grad = pre_pull(apply_left(joined_low, qkv_weight))
    input_grad = middle_grad + pre_in_grad
    smooth_grad = pyramid_grads[14].reshape(-1, pyramid_grads[14].shape[-1])
    groups = [
        [smooth_grad],
        [pyramid_grads[0], pyramid_grads[6]],
        [outer_sum(normed_mid_low, pre_low)],
        [outer_sum(hidden_low, result_grad)],
        [outer_sum(normed_low, joined_low)],
        [
            outer_sum(attended_low, branch_low),
            pyramid_grads[4],
            pyramid_grads[10],
            pyramid_grads[11],
            pyramid_grads[9],
        ],
        [pyramid_grads[8]],
    ]
    group_sums, small_sums = reduce_weights(
        groups,
        (
            pre_gain_grad,
            pre_shift_grad,
            qv_bias_grad,
            rel_rows_grad,
            rel_cols_grad,
            proj_bias_grad,
            mid_gain_grad,
            mid_shift_grad,
            fc1_bias_grad,
            fc2_bias_grad,
            pyramid_grads[1],
            pyramid_grads[2],
            pyramid_grads[3],
            pyramid_grads[5],
            pyramid_grads[7],
            pyramid_grads[12],
            pyramid_grads[13],
            pyramid_grads[15],
        ),
        0,
    )
    block_sums = (group_sums[4][0], group_sums[5][0], group_sums[2][0], group_sums[3][0])
    level_sums = (
        group_sums[1][0],
        group_sums[5][1],
        group_sums[1][1],
        group_sums[6][0],
        group_sums[5][4],
        group_sums[5][2],
        group_sums[5][3],
        group_sums[0][0],
    )
    return (
        result_low,
        input_grad,
        small_sums[0],
        small_sums[1],
        block_sums[0],
        small_sums[2],
        small_sums[3],
        small_sums[4],
        block_sums[1],
        small_sums[5],
        small_sums[6],
        small_sums[7],
        block_sums[2],
        small_sums[8],
        block_sums[3],
        small_sums[9],
        level_sums[0],
        small_sums[10],
        small_sums[11],
        small_sums[12],
        level_sums[1],
        small_sums[13],
        level_sums[2],
        small_sums[14],
        level_sums[3],
        level_sums[4],
        level_sums[5],
        level_sums[6],
        small_sums[15],
        small_sums[16],
        level_sums[7],
        small_sums[17],
    )


def solution(mesh):
    in_specs = (
        P("img", ("rows", "scale"), None, None),
        P(),
        P(),
        P(),
        P(),
        P(),
        P(),
        P(),
        P(),
        P(),
        P(),
        P(),
        P(),
        P(),
        P(),
        P(),
        P(),
        P(),
        P(),
        P(),
        P(),
        P(),
        P(),
        P(),
        P(),
        P(),
        P(),
        P(),
        P(),
        P(),
        P(),
        P("img", "rows", None, None),
        P("img", "rows", None, None),
        P("img", "rows", None, None),
        P("img", "rows", None, None),
        P("img", "rows", None),
        P("img", "rows", None),
        P("img", "rows", None),
        P("img", "rows", None),
        P("img", "rows", None),
    )
    out_specs = (
        P("img", ("rows", "scale"), None, None),
        P("img", ("rows", "scale"), None, None),
        P(),
        P(),
        P(("img", "rows", "scale")),
        P(),
        P(),
        P(),
        P(("img", "rows", "scale")),
        P(),
        P(),
        P(),
        P(("img", "rows", "scale")),
        P(),
        P(("img", "rows", "scale")),
        P(),
        P(("img", "rows", "scale")),
        P(),
        P(),
        P(),
        P(("img", "rows", "scale")),
        P(),
        P(("img", "rows", "scale")),
        P(),
        P(("img", "rows", "scale")),
        P(("img", "rows", "scale")),
        P(("img", "rows", "scale")),
        P(("img", "rows", "scale")),
        P(),
        P(),
        P(("img", "rows", "scale")),
        P(),
    )
    return jax.shard_map(
        on_device, mesh=mesh, in_specs=in_specs, out_specs=out_specs, check_vma=False
    )
```

```python
from functools import partial

import jax
import jax.numpy as jnp
from jax import lax
from jax.experimental import pallas as pl
from jax.experimental.pallas import tpu as pltpu
from jax.sharding import PartitionSpec as P

norm_eps = 1e-06
wide_type = jnp.float32
narrow_type = jnp.bfloat16

MESH_ID = pl.DeviceIdType.MESH
lanes = 128


def axis_bits(size):
    bits = []
    step = 1
    while step < size:
        bits.append(step)
        step *= 2
    return bits


def bit_partner(axis, step):
    here = lax.axis_index(axis)
    bit = lax.rem(lax.div(here, step), 2)
    return {axis: here + step - 2 * step * bit}, bit


def halving_dims():
    dims = []
    for axis in ("img", "rows", "scale"):
        for step in reversed(axis_bits(lax.axis_size(axis))):
            dims.append((axis, step))
    return dims


class ReducePlan:
    def __init__(self, shapes, pieces, near=()):
        self.dims = halving_dims()
        self.stages = len(self.dims)
        self.core = self.dims.index(("img", 1))
        plane = [i for i, d in enumerate(self.dims) if d[0] == "img" and i != self.core]
        across = [i for i, d in enumerate(self.dims) if d[0] == "rows"]
        along = [i for i, d in enumerate(self.dims) if d[0] == "scale"][::-1]
        orders = ([self.core] + across + plane + along, [self.core] + plane + across + along)
        self.shapes = shapes
        self.near = near
        self.pieces = []
        for t, (source, begin, size) in enumerate(pieces):
            self.pieces.append((source, begin, size, shapes[source][2], orders[t % 2]))
        self.staging = sorted({piece[2:4] for piece in self.pieces if piece[0] not in near})

    def scratch(self):
        out = []
        for _, _, rows, columns, _ in self.pieces:
            out.append(pltpu.VMEM((2,) * (self.stages - 1) + (rows, columns), narrow_type))
        for _, _, rows, columns, _ in self.pieces:
            for stage in range(1, self.stages):
                lead = (2,) * (self.stages - 1 - stage)
                out.append(pltpu.VMEM(lead + (rows, columns), narrow_type))
        for shape in self.staging:
            out.append(pltpu.VMEM((2,) * (self.stages - 1) + shape, narrow_type))
        count = len(self.pieces)
        out += [pltpu.SemaphoreType.DMA((count, self.stages))] * 2
        out += [pltpu.SemaphoreType.DMA((count,))]
        return out

    def waves(self):
        return (len(self.pieces) + 1) // 2 + self.stages

    def shaped(self, arrays):
        return [array.reshape((2,) * self.stages + array.shape[1:]) for array in arrays]

    def sums(self):
        return [jax.ShapeDtypeStruct(shape[1:], wide_type) for shape in self.shapes]


class Reducer:
    def __init__(self, plan, sources, outs, scratch):
        self.plan, self.sources, self.outs = plan, sources, outs
        count, stages = len(plan.pieces), plan.stages
        scratch = list(scratch)
        self.held = scratch[:count]
        rest = scratch[count:]
        self.landed = [rest[t * (stages - 1) : (t + 1) * (stages - 1)] for t in range(count)]
        rest = rest[count * (stages - 1) :]
        self.staging = dict(zip(plan.staging, rest[: len(plan.staging)]))
        self.send_sem, self.recv_sem, self.local_sem = rest[len(plan.staging) :]
        self.partners = [bit_partner(axis, step) for axis, step in plan.dims]
        users = {shape: [] for shape in plan.staging}
        self.following = {}
        for t, piece in enumerate(plan.pieces):
            if piece[0] in plan.near:
                continue
            used = users[piece[2:4]]
            if used:
                self.following[used[-1]] = t
            used.append(t)
        self.first_local = [used[0] for used in users.values()]

    def greet(self, barrier):
        for partner, _ in self.partners:
            pl.semaphore_signal(barrier, inc=1, device_id=partner, device_id_type=MESH_ID)
        return len(self.partners)

    def index(self, taken, current, keep):
        out = []
        for dim in range(self.plan.stages):
            bit = self.partners[dim][1]
            if dim in taken:
                out.append(bit)
            elif dim == current:
                out.append(bit if keep else 1 - bit)
            else:
                out.append(slice(None))
        return tuple(out)

    def held_index(self, index):
        return index[: self.plan.core] + index[self.plan.core + 1 :]

    def copy(self, t, stage):
        source, begin, rows, _, order = self.plan.pieces[t]
        index = self.index(set(order[:stage]), order[stage], False)
        if stage == 0:
            view = self.sources[source].at[index + (pl.ds(begin, rows),)]
            target = self.held[t]
        else:
            view = self.held[t].at[self.held_index(index)]
            target = self.landed[t][stage - 1]
        return pltpu.make_async_remote_copy(
            src_ref=view,
            dst_ref=target,
            send_sem=self.send_sem.at[t, stage],
            recv_sem=self.recv_sem.at[t, stage],
            device_id=self.partners[order[stage]][0],
            device_id_type=MESH_ID,
        )

    def local(self, t):
        source, begin, rows, columns, order = self.plan.pieces[t]
        index = self.index(set(), order[0], True)
        return pltpu.make_async_copy(
            self.sources[source].at[index + (pl.ds(begin, rows),)],
            self.staging[(rows, columns)],
            self.local_sem.at[t],
        )

    def add(self, t, target, arrived, begin=0):
        lead, rows = target.shape[:-2], target.shape[-2]
        arrived = arrived.at[(slice(None),) * len(lead) + (pl.ds(begin, rows),)]
        total = 1
        for size in lead:
            total *= size

        def body(step, carry):
            place, left = [], step
            for size in reversed(lead):
                place.append(lax.rem(left, size))
                left = lax.div(left, size)
            place = tuple(reversed(place))
            target[place] = target[place] + arrived[place]
            return carry

        if lead:
            lax.fori_loop(0, total, body, 0)
        else:
            target[...] = target[...] + arrived[...]

    def start(self):
        for t in range(len(self.plan.pieces)):
            if self.plan.pieces[t][0] not in self.plan.near:
                self.copy(t, 0).start()
        for t in self.first_local:
            self.local(t).start()

    def start_near(self):
        for t in range(len(self.plan.pieces)):
            if self.plan.pieces[t][0] in self.plan.near:
                self.copy(t, 0).start()

    def event(self, t, stage):
        source, begin, rows, columns, order = self.plan.pieces[t]
        self.copy(t, stage).wait_recv()
        if stage == 0 and source in self.plan.near:
            own = self.sources[source].at[self.index(set(), order[0], True)]
            self.add(t, self.held[t], own, begin)
        elif stage == 0:
            self.local(t).wait()
            self.add(t, self.held[t], self.staging[(rows, columns)])
            if t in self.following:
                self.local(self.following[t]).start()
        else:
            index = self.index(set(order[:stage]), order[stage], True)
            kept = self.held[t].at[self.held_index(index)]
            self.add(t, kept, self.landed[t][stage - 1])
        if stage + 1 < self.plan.stages:
            self.copy(t, stage + 1).start()
        else:
            index = self.held_index(self.index(set(order), -1, True))
            self.emit(source, begin, self.held[t][index].astype(wide_type))

    def emit(self, source, begin, value):
        out = self.outs[source]
        if not isinstance(out, list):
            out[begin : begin + value.shape[0], :] = value
            return
        for first, count, tile, tiles, ref in out:
            low, high = max(first, begin), min(first + count, begin + value.shape[0])
            if low < high:
                part = value[low - begin : high - begin]
                if tiles == 0:
                    ref[low - first : high - first, :] = part
                for c in range(min(tiles, part.shape[1] // lanes)):
                    here = part[:, c * lanes : (c + 1) * lanes]
                    at = (low - first) * tiles + tile + c
                    ref[pl.ds(at, high - low, stride=tiles), :] = here

    def wave(self, number):
        for stage in range(self.plan.stages):
            pair = number - stage - (1 if stage else 0)
            for t in (2 * pair, 2 * pair + 1):
                if 0 <= t < len(self.plan.pieces):
                    self.event(t, stage)

    def finish(self):
        for t in range(len(self.plan.pieces)):
            for stage in range(self.plan.stages):
                self.copy(t, stage).wait_send()


class StripGather:
    def __init__(self, owns, wholes, send_sem, recv_sem):
        self.owns, self.wholes = owns, wholes
        self.send_sem, self.recv_sem = send_sem, recv_sem
        self.deep, self.wide = lax.axis_size("scale"), lax.axis_size("rows")
        self.here, self.line = lax.axis_index("scale"), lax.axis_index("rows")

    @staticmethod
    def slots():
        deep, wide = lax.axis_size("scale"), lax.axis_size("rows")
        return 2 * (deep - 1) + (wide - 1) * (2 * deep - 1)

    def greet(self, barrier):
        waits = self.wide - 1
        for k in range(1, self.wide):
            device = {"rows": lax.rem(self.line + k, self.wide)}
            pl.semaphore_signal(barrier, inc=1, device_id=device, device_id_type=MESH_ID)

        @pl.when(self.here > 0)
        def _():
            device = {"scale": self.here - 1}
            pl.semaphore_signal(barrier, inc=1, device_id=device, device_id_type=MESH_ID)

        @pl.when(self.here < self.deep - 1)
        def _():
            device = {"scale": self.here + 1}
            pl.semaphore_signal(barrier, inc=1, device_id=device, device_id_type=MESH_ID)

        more = jnp.where(self.here > 0, 1, 0) + jnp.where(self.here < self.deep - 1, 1, 0)
        return waits + more

    def copies(self, block, slot, device):
        out = []
        for i, whole in enumerate(self.wholes):
            view = whole.at[self.line * self.deep + block]
            out.append(
                pltpu.make_async_remote_copy(
                    src_ref=view,
                    dst_ref=view,
                    send_sem=self.send_sem.at[slot, i],
                    recv_sem=self.recv_sem.at[slot, i],
                    device_id=device,
                    device_id_type=MESH_ID,
                )
            )
        return out

    def along(self, step, right):
        if right:
            block, device = self.here - step, {"scale": jnp.minimum(self.here + 1, self.deep - 1)}
            sent = (block >= 0) & (self.here < self.deep - 1)
            got = self.here - 1 - step >= 0
            return block, step, device, sent, got
        block, device = self.here + step, {"scale": jnp.maximum(self.here - 1, 0)}
        sent = (block < self.deep) & (self.here > 0)
        got = self.here + 1 + step < self.deep
        return block, self.deep - 1 + step, device, sent, got

    def across(self, block, kind, action):
        base = 2 * (self.deep - 1)
        for k in range(1, self.wide):
            slot = base + (k - 1) * (2 * self.deep - 1) + kind
            device = {"rows": lax.rem(self.line + k, self.wide)}
            for copy in self.copies(block, slot, device):
                action(copy)

    def start(self):
        for own, whole in zip(self.owns, self.wholes):
            whole[self.line * self.deep + self.here] = own[...]
        for right in (True, False):
            block, slot, device, sent, _ = self.along(0, right)

            @pl.when(sent)
            def _():
                for copy in self.copies(block, slot, device):
                    copy.start()

        self.across(self.here, 0, lambda copy: copy.start())

    def step(self, number):
        for right in (True, False):
            _, slot, device, _, got = self.along(number, right)
            block = self.here - 1 - number if right else self.here + 1 + number

            @pl.when(got)
            def _():
                for copy in self.copies(block, slot, device):
                    copy.wait_recv()
                kind = 1 + 2 * number + (0 if right else 1)
                self.across(block, kind, lambda copy: copy.start())

            if number + 1 < self.deep - 1:
                later, slot, device, sent, _ = self.along(number + 1, right)

                @pl.when(sent)
                def _():
                    for copy in self.copies(later, slot, device):
                        copy.start()

    def finish(self):
        self.across(self.here, 0, lambda copy: copy.wait())
        for number in range(self.deep - 1):
            for right in (True, False):
                _, _, _, _, got = self.along(number, right)
                block = self.here - 1 - number if right else self.here + 1 + number
                kind = 1 + 2 * number + (0 if right else 1)

                @pl.when(got)
                def _():
                    self.across(block, kind, lambda copy: copy.wait())

                sent_block, slot, device, sent, _ = self.along(number, right)

                @pl.when(sent)
                def _():
                    for copy in self.copies(sent_block, slot, device):
                        copy.wait_send()


def fold_chunks(grads, width):
    devices = lax.axis_size(("img", "rows", "scale"))
    cut, plan = [], []
    for grad in grads:
        rows, columns = grad.shape
        own = rows // devices
        chunk = grad.astype(narrow_type).reshape(devices, own, columns)
        folds = max(columns // width, 1)
        if columns < width:
            chunk = jnp.pad(chunk, ((0, 0), (0, 0), (0, width - columns)))
        cut += [chunk[:, :, f * width : (f + 1) * width] for f in range(folds)]
        plan.append((own, columns, folds))
    stacked = jnp.concatenate(cut, axis=1) if len(cut) > 1 else cut[0]
    extra = -stacked.shape[1] % 16
    if extra:
        stacked = jnp.pad(stacked, ((0, 0), (0, extra), (0, 0)))
    return stacked, plan


def unfold_chunks(summed, plan):
    at, out = 0, []
    for own, columns, folds in plan:
        parts = []
        for _ in range(folds):
            parts.append(summed[at : at + own, : min(columns, summed.shape[1])])
            at += own
        whole = jnp.concatenate(parts, axis=1) if folds > 1 else parts[0]
        out.append(whole.reshape(-1))
    return out


def last_reduce_kernel(plan, count, refs):
    sources, small_in = refs[:count], refs[count]
    outs, small_out = refs[count + 1 : 2 * count + 1], refs[2 * count + 1]
    scratch = refs[2 * count + 2 :]
    small_held, small_landed, small_send, small_recv = scratch[:4]
    reducer = Reducer(plan, sources, outs, scratch[4:])
    barrier = pltpu.get_barrier_semaphore()
    pl.semaphore_wait(barrier, reducer.greet(barrier))

    def small_copy(stage):
        return pltpu.make_async_remote_copy(
            src_ref=small_held,
            dst_ref=small_landed.at[stage],
            send_sem=small_send.at[stage],
            recv_sem=small_recv.at[stage],
            device_id=reducer.partners[plan.pieces[0][4][stage]][0],
            device_id_type=MESH_ID,
        )

    small_held[...] = small_in[...]
    reducer.start()
    small_copy(0).start()
    for number in range(plan.waves()):
        reducer.wave(number)
        if number < plan.stages:
            small_copy(number).wait()
            small_held[...] = small_held[...] + small_landed[number]
            if number + 1 < plan.stages:
                small_copy(number + 1).start()
    small_out[...] = small_held[...]
    reducer.finish()


def cut_rows(shapes):
    out = []
    for source, (_, rows, _) in enumerate(shapes):
        first = -(-rows // 32) * 16
        out.append((source, 0, first))
        if first < rows:
            out.append((source, first, rows - first))
    return out


def last_reduce(arrays, small, call_id):
    shapes = [array.shape for array in arrays]
    plan = ReducePlan(shapes, cut_rows(shapes))
    count = len(arrays)

    def body(*refs):
        last_reduce_kernel(plan, count, refs)

    vmem = pl.BlockSpec(memory_space=pltpu.VMEM)
    got = pl.pallas_call(
        body,
        out_shape=plan.sums() + [jax.ShapeDtypeStruct(small.shape, wide_type)],
        in_specs=[pl.BlockSpec(memory_space=pl.ANY)] * count + [vmem],
        out_specs=[vmem] * (count + 1),
        scratch_shapes=[
            pltpu.VMEM(small.shape, wide_type),
            pltpu.VMEM((plan.stages,) + small.shape, wide_type),
            pltpu.SemaphoreType.DMA((plan.stages,)),
            pltpu.SemaphoreType.DMA((plan.stages,)),
        ]
        + plan.scratch(),
        compiler_params=pltpu.CompilerParams(
            collective_id=call_id, has_side_effects=True, vmem_limit_bytes=60 << 20
        ),
        name="last_reduce",
    )(*plan.shaped(arrays), small)
    return got[:count], got[count]


def pack_small(parts):
    flat = jnp.concatenate([part.reshape(-1) for part in parts])
    unit = 8 * lanes
    total = -(-flat.shape[0] // unit) * unit
    return jnp.pad(flat, (0, total - flat.shape[0])).reshape(-1, lanes)


def unpack_small(packed, parts):
    flat = packed.reshape(-1)
    out, at = [], 0
    for part in parts:
        out.append(flat[at : at + part.size].reshape(part.shape))
        at += part.size
    return out


def gather_kernel(own, whole, send_sem, recv_sem):
    gather = StripGather([own], [whole], send_sem, recv_sem)
    barrier = pltpu.get_barrier_semaphore()
    pl.semaphore_wait(barrier, gather.greet(barrier))
    gather.start()
    for number in range(gather.deep - 1):
        gather.step(number)
    gather.finish()


def gather_strips(own, call_id):
    strips = lax.axis_size(("rows", "scale"))
    slots = StripGather.slots()
    return pl.pallas_call(
        gather_kernel,
        out_shape=jax.ShapeDtypeStruct((strips,) + own.shape, own.dtype),
        in_specs=[pl.BlockSpec(memory_space=pltpu.VMEM)],
        out_specs=pl.BlockSpec(memory_space=pltpu.VMEM),
        scratch_shapes=[
            pltpu.SemaphoreType.DMA((slots, 1)),
            pltpu.SemaphoreType.DMA((slots, 1)),
        ],
        compiler_params=pltpu.CompilerParams(collective_id=call_id, has_side_effects=True),
        name="gather_strips",
    )(own)


def dot_nn(left, right):
    return lax.dot_general(left, right, (((1,), (0,)), ((), ())), preferred_element_type=wide_type)


def dot_nt(left, right):
    return lax.dot_general(left, right, (((1,), (1,)), ((), ())), preferred_element_type=wide_type)


def dot_tn(left, right):
    return lax.dot_general(left, right, (((0,), (0,)), ((), ())), preferred_element_type=wide_type)


def norm_parts(values):
    centre = values - jnp.mean(values, axis=-1, keepdims=True)
    inverse = lax.rsqrt(jnp.mean(centre * centre, axis=-1, keepdims=True) + norm_eps)
    return centre * inverse, inverse


def norm_back(hat, inverse, hat_grad):
    inner = jnp.mean(hat_grad * hat, axis=-1, keepdims=True)
    return inverse * (hat_grad - jnp.mean(hat_grad, axis=-1, keepdims=True) - hat * inner)


def normal_cdf(values):
    return 0.5 + 0.5 * lax.erf(values * (0.5**0.5))


def gelu_slope(values):
    density = jnp.exp(-0.5 * values * values) * (0.5 / jnp.pi) ** 0.5
    return normal_cdf(values) + values * density


def lane_ids(shape):
    return lax.broadcasted_iota(jnp.int32, shape, len(shape) - 1)


def column_sum(values):
    return jnp.sum(values, axis=0, keepdims=True)


def half_mask(half, head_size, value):
    lane = lane_ids((1, 2 * head_size))
    inside = (lane >= half * head_size) & (lane < (half + 1) * head_size)
    return jnp.where(inside, value, 0.0).astype(narrow_type)


def split_lanes(values, used):
    lane = lane_ids(values.shape)
    twice = jnp.where(lane < used, values, pltpu.roll(values, used, 1))
    near = twice.astype(narrow_type).astype(wide_type)
    both = jnp.where(lane < used, near, twice - near)
    return jnp.where(lane < 2 * used, both, 0.0).astype(narrow_type)


def place_cols(tab, width):
    by_col = pltpu.roll(tab, lanes - (width - 1), 1, stride=1, stride_axis=0)
    return split_lanes(by_col, width)


def place_rows(tab, row, height):
    by_row = pltpu.roll(tab, lax.rem(lanes - (height - 1) + row, lanes), 1)
    return split_lanes(by_row, height)


def both_halves(values, head_size, scale):
    masked = [values * half_mask(half, head_size, scale) for half in range(2)]
    return jnp.concatenate(masked, axis=0)


def own_extra(tab, strip_rows, width, height):
    out = []
    for half in range(2):
        for i in range(strip_rows):
            piece = tab[i * width : (i + 1) * width, 2 * half * lanes : 2 * (half + 1) * lanes]
            row = strip_index() * strip_rows + i
            cols = place_cols(piece[:, :lanes], width)
            out.append(jnp.concatenate([cols, place_rows(piece[:, lanes:], row, height)], axis=1))
    return jnp.concatenate(out, axis=0)


def strip_index():
    return lax.axis_index("rows") * lax.axis_size("scale") + lax.axis_index("scale")


def block_forward_kernel(
    height,
    width,
    x_all,
    vec,
    qkv_weight,
    tables,
    hot,
    proj_hbm,
    fc1_hbm,
    fc2_hbm,
    q_all,
    k_all,
    v_all,
    attended,
    attended_wide,
    log_norm,
    middle,
    normed_mid,
    hidden_pre,
    hidden,
    result,
    proj,
    fc1,
    fc2,
    sems,
):
    model = x_all.shape[2]
    tokens = middle.shape[0]
    strip_rows = tokens // width
    head_size = lanes // 2
    copies = [
        pltpu.make_async_copy(source, target, sems.at[i])
        for i, (source, target) in enumerate(((proj_hbm, proj), (fc1_hbm, fc1), (fc2_hbm, fc2)))
    ]
    for copy in copies:
        copy.start()
    start = pl.multiple_of(strip_index() * tokens, tokens)

    def mix(step, carry):
        at = pl.ds(pl.multiple_of(step * tokens, tokens), tokens)
        hat, _ = norm_parts(x_all[step].astype(wide_type))
        normed = (hat * vec[0:1, :] + vec[1:2, :]).astype(narrow_type)
        mixed = dot_nn(normed, qkv_weight[...])
        q_all[at, :] = (mixed[:, :model] + vec[2:3, :]).astype(narrow_type)
        k_all[at, :] = mixed[:, model : 2 * model].astype(narrow_type)
        v_all[at, :] = (mixed[:, 2 * model :] + vec[3:4, :]).astype(narrow_type)
        return carry

    lax.fori_loop(0, x_all.shape[0], mix, 0)
    log_norm[...] = jnp.zeros_like(log_norm)
    lane = lane_ids((tokens, lanes))

    def pair_step(pair, carry):
        cols = pl.ds(pl.multiple_of(pair * lanes, lanes), lanes)
        queries = q_all[pl.ds(start, tokens), cols]
        values = v_all[:, cols]
        keys = jnp.concatenate([k_all[:, cols], hot[...]], axis=1)
        extra = own_extra(dot_nn(queries, tables[...]), strip_rows, width, height)
        masked = both_halves(queries, head_size, head_size**-0.5)
        scores = dot_nt(jnp.concatenate([masked, extra], axis=1), keys)
        peak = jnp.max(scores, axis=-1, keepdims=True)
        raised = jnp.exp(scores - peak)
        total = jnp.sum(raised, axis=-1, keepdims=True)
        probs = (raised * (1.0 / total)).astype(narrow_type)
        out = dot_nn(probs, values)
        mixed = (out[:tokens], out[tokens:])
        norm = peak + jnp.log(total)
        kept = jnp.where(lane == 2 * pair, norm[:tokens], log_norm[...])
        log_norm[...] = jnp.where(lane == 2 * pair + 1, norm[tokens:], kept)
        joined = jnp.where(lane < head_size, mixed[0], mixed[1])
        attended_wide[:, cols] = joined
        attended[:, cols] = joined.astype(narrow_type)
        return carry

    lax.fori_loop(0, model // lanes, pair_step, 0)
    copies[0].wait()
    inputs = x_all[strip_index()].astype(wide_type)
    centre = inputs + (dot_nn(attended[...], proj[...]) + vec[4:5, :])
    middle[...] = centre
    hat, _ = norm_parts(centre)
    normed_low = (hat * vec[5:6, :] + vec[6:7, :]).astype(narrow_type)
    normed_mid[...] = normed_low
    copies[1].wait()
    copies[2].wait()
    result_wide = centre + vec[7:8, :]
    for j in range(fc1.shape[1] // model):
        cols = slice(j * model, (j + 1) * model)
        pre = dot_nn(normed_mid[...], fc1[:, cols]) + vec[8 + j : 9 + j, :]
        hidden_pre[:, cols] = pre
        low = (pre * normal_cdf(pre)).astype(narrow_type)
        hidden[:, cols] = low
        result_wide = result_wide + dot_nn(low, fc2[cols, :])
    result[...] = result_wide.astype(narrow_type)


def vmem_specs(count):
    return [pl.BlockSpec(memory_space=pltpu.VMEM)] * count


def any_specs(count):
    return [pl.BlockSpec(memory_space=pl.ANY)] * count


def block_forward(height, width, tokens, x_all, vec, qkv_weight, tables, hot, proj, fc1, fc2):
    model = x_all.shape[2]
    total = x_all.shape[0] * tokens
    ff = fc1.shape[1]

    def shape(rows, cols, kind):
        return jax.ShapeDtypeStruct((rows, cols), kind)

    outs = [
        shape(total, model, narrow_type),
        shape(total, model, narrow_type),
        shape(total, model, narrow_type),
        shape(tokens, model, narrow_type),
        shape(tokens, model, wide_type),
        shape(tokens, lanes, wide_type),
        shape(tokens, model, wide_type),
        shape(tokens, model, narrow_type),
        shape(tokens, ff, wide_type),
        shape(tokens, ff, narrow_type),
        shape(tokens, model, narrow_type),
    ]
    return pl.pallas_call(
        partial(block_forward_kernel, height, width),
        out_shape=outs,
        in_specs=vmem_specs(5) + any_specs(3),
        out_specs=vmem_specs(len(outs)),
        scratch_shapes=[
            pltpu.VMEM(proj.shape, narrow_type),
            pltpu.VMEM(fc1.shape, narrow_type),
            pltpu.VMEM(fc2.shape, narrow_type),
            pltpu.SemaphoreType.DMA((3,)),
        ],
        compiler_params=pltpu.CompilerParams(vmem_limit_bytes=60 << 20),
        name="block_forward",
    )(x_all, vec, qkv_weight, tables, hot, proj, fc1, fc2)


def fold_store(target, number, parts, value):
    devices = target.shape[0]
    own = value.shape[0] // devices
    parts[number] = value.reshape(devices, own, value.shape[1])
    if number % 2:
        both = jnp.concatenate([parts.pop(number - 1), parts.pop(number)], axis=1)
        begin = (number - 1) * own
        target[:, begin : begin + 2 * own, :] = both.astype(narrow_type)


def block_backward_kernel(
    result_grad,
    hidden_pre,
    hidden,
    normed_mid,
    middle,
    attended,
    attended_wide,
    log_norm,
    vec,
    proj,
    fc1,
    fc2,
    middle_grad,
    attended_grad,
    stats,
    stat_rows,
    sums,
    fc1_sum,
    proj_grad,
    fc1_grad,
    fc2_grad,
):
    model = middle.shape[1]
    ff = hidden.shape[1]
    grad_low = result_grad[...]
    grad_wide = grad_low.astype(wide_type)
    back = jnp.zeros(middle.shape, wide_type)
    normed_turned = normed_mid[...].T
    parts = {}
    for j in range(ff // model):
        cols = slice(j * model, (j + 1) * model)
        pre = hidden_pre[:, cols]
        pre_grad = dot_nt(grad_low, fc2[cols, :]) * gelu_slope(pre)
        pre_low = pre_grad.astype(narrow_type)
        fc1_sum[:, cols] = column_sum(pre_low.astype(wide_type))
        back = back + dot_nt(pre_low, fc1[:, cols])
        part = dot_nn(normed_turned, pre_low)
        if len(fc1_grad.shape) == 2:
            fc1_grad[:, cols] = part.astype(narrow_type)
        else:
            fold_store(fc1_grad, j, parts, part)
        fc2_grad[cols, :] = dot_nn(hidden[:, cols].T, grad_low).astype(narrow_type)
    hat, inverse = norm_parts(middle[...])
    gain_grad = column_sum(back * hat)
    shift_grad = column_sum(back)
    centre_grad = grad_wide + norm_back(hat, inverse, back * vec[5:6, :])
    middle_grad[...] = centre_grad
    branch_low = centre_grad.astype(narrow_type)
    sums[0:1, :] = column_sum(branch_low.astype(wide_type))
    sums[1:2, :] = gain_grad
    sums[2:3, :] = shift_grad
    sums[3:4, :] = column_sum(grad_wide)
    sums[4:8, :] = jnp.zeros((4, model), wide_type)
    proj_grad[...] = dot_nn(attended[...].T, branch_low).astype(narrow_type)
    out_grad = dot_nt(branch_low, proj[...]).astype(narrow_type)
    attended_grad[...] = out_grad
    product = out_grad.astype(wide_type) * attended_wide[...]
    near = product.astype(narrow_type)
    rest = (product - near.astype(wide_type)).astype(narrow_type)
    head_size = lanes // 2
    channel = lax.broadcasted_iota(jnp.int32, (model, lanes), 0)
    head = lax.broadcasted_iota(jnp.int32, (model, lanes), 1)
    member = (lax.div(channel, head_size) == head - 16).astype(wide_type).astype(narrow_type)
    delta = dot_nn(near, member) + dot_nn(rest, member)
    both = jnp.where(lane_ids(delta.shape) < 16, log_norm[...], delta)
    stats[...] = both
    stat_rows[...] = both.T[:32, :]


def block_backward(result_grad, kept, log_norm, vec, proj, fc1, fc2, devices):
    hidden_pre, hidden, normed_mid, middle, attended, attended_wide = kept
    tokens, model = middle.shape
    ff = fc1.shape[1]

    def shape(rows, cols, kind):
        return jax.ShapeDtypeStruct((rows, cols), kind)

    outs = [
        shape(tokens, model, wide_type),
        shape(tokens, model, narrow_type),
        shape(tokens, lanes, wide_type),
        shape(32, tokens, wide_type),
        shape(8, model, wide_type),
        shape(1, ff, wide_type),
        shape(model, model, narrow_type),
        shape(model, ff, narrow_type),
        shape(ff, model, narrow_type),
    ]
    if devices:
        outs[7] = jax.ShapeDtypeStruct((devices, model // devices * (ff // model), model), narrow_type)
    return pl.pallas_call(
        block_backward_kernel,
        out_shape=outs,
        in_specs=vmem_specs(12),
        out_specs=vmem_specs(len(outs)),
        compiler_params=pltpu.CompilerParams(vmem_limit_bytes=60 << 20),
        name="block_backward",
    )(
        result_grad,
        hidden_pre,
        hidden,
        normed_mid,
        middle,
        attended,
        attended_wide,
        log_norm,
        vec,
        proj,
        fc1,
        fc2,
    )


def attention_backward_kernel(height, width, plan, shares, refs):
    (
        x_own,
        q_all,
        k_all,
        v_all,
        grad_own,
        own_stats,
        stat_own,
        middle_grad,
        vec,
        tables,
        rel_all,
        hot,
        hot_turned,
        qkv_weight,
    ) = refs[:14]
    refs = refs[14:]
    if plan is None:
        input_grad, sums, rel_sum, weight_grad = refs[:4]
        scratch = refs[4:]
    else:
        block_sums, fc1_sum, level_sums, gain_sums = refs[:4]
        count = len(plan.shapes) - 1
        sources = refs[4 : 4 + count]
        input_grad, small_out, rel_out = refs[4 + count : 7 + count]
        flat = refs[7 + count : 7 + count + len(shares)]
        scratch = refs[7 + count + len(shares) :]
        sums, rel_sum, small_landed, rel_landed, small_send, small_recv, weight_grad = scratch[:7]
        scratch = scratch[7:]
        outs = [[] for _ in plan.shapes]
        for ref, (source, places) in zip(flat, shares):
            for place in places:
                outs[source].append(place + (ref,))
        for source, out in enumerate(outs):
            if len(out) == 1 and out[0][3] == 0:
                outs[source] = out[0][4]
    joined, wide_tab, cols_extra, rows_extra, grad_all, stat_all, stat_rows, rel_grad = scratch[:8]
    gather = StripGather([grad_own, stat_own], [grad_all, stat_all], scratch[8], scratch[9])
    total, model = q_all.shape
    tokens = x_own.shape[0]
    strip_rows = tokens // width
    head_size = lanes // 2
    scale = head_size**-0.5
    strip = strip_index()
    strips = grad_all.shape[0]
    own = pl.ds(pl.multiple_of(strip * tokens, tokens), tokens)
    pairs = model // lanes
    barrier = pltpu.get_barrier_semaphore()
    greeted = gather.greet(barrier)
    if plan is not None:
        reducer = Reducer(plan, (*sources, weight_grad), outs, scratch[10:])
        greeted = greeted + reducer.greet(barrier)
    pl.semaphore_wait(barrier, greeted)
    gather.start()
    if plan is not None:
        reducer.start()

    def wave(number):
        if plan is not None:
            reducer.wave(number)

    rel_grad[...] = jnp.zeros_like(rel_grad)
    lane = lane_ids((tokens, lanes))

    def own_queries(pair, carry):
        cols = pl.ds(pl.multiple_of(pair * lanes, lanes), lanes)
        queries = q_all[own, cols]
        keys = k_all[:, cols]
        extra = own_extra(dot_nn(queries, tables[...]), strip_rows, width, height)
        masked = both_halves(queries, head_size, scale)
        keys_hot = jnp.concatenate([keys, hot[...]], axis=1)
        scores = dot_nt(jnp.concatenate([masked, extra], axis=1), keys_hot)
        norms, means = [], []
        for half in range(2):
            head = 2 * pair + half
            stats = own_stats[...]
            norms.append(jnp.sum(jnp.where(lane == head, stats, 0.0), axis=-1, keepdims=True))
            means.append(jnp.sum(jnp.where(lane == 16 + head, stats, 0.0), axis=-1, keepdims=True))
        probs = jnp.exp(scores - jnp.concatenate(norms, axis=0))
        prob_grad = dot_nt(both_halves(grad_own[:, cols], head_size, 1.0), v_all[:, cols])
        score_grad = probs * (prob_grad - jnp.concatenate(means, axis=0))
        keys_turned = jnp.concatenate([keys, hot_turned[...]], axis=1)
        back = dot_nn(score_grad.astype(narrow_type), keys_turned)
        offsets = []
        for half in range(2):
            parts = []
            for i in range(strip_rows):
                at = half * tokens + i * width
                piece = back[at : at + width]
                by_col = pltpu.roll(piece[:, lanes : 2 * lanes], 0, 1, stride=1, stride_axis=0)
                by_row = pltpu.roll(piece[:, 2 * lanes :], strip * strip_rows + i, 1)
                parts.append(jnp.concatenate([by_col, by_row], axis=1))
            offsets.append(jnp.concatenate(parts, axis=0))
        off = jnp.concatenate(offsets, axis=1).astype(narrow_type)
        plain = jnp.where(lane < head_size, back[:tokens, :lanes], back[tokens:, :lanes])
        query_grad = plain * scale + dot_nn(off, rel_all[...])
        joined[:, cols] = query_grad.astype(narrow_type)
        rel_grad[...] += dot_tn(off, queries)
        return carry

    def own_keys(pair, carry):
        at = pl.multiple_of(pair * lanes, lanes)
        cols = pl.ds(at, lanes)
        all_queries = q_all[:, cols]
        wide_tab[...] = dot_nn(all_queries, tables[...])

        def widen(row, inner):
            rows = pl.ds(pl.multiple_of(row * width, width), width)
            for half in range(2):
                begin = 2 * half * lanes
                cols_extra[half, rows, :] = place_cols(wide_tab[rows, begin : begin + lanes], width)
                piece = wide_tab[rows, begin + lanes : begin + 2 * lanes]
                rows_extra[half, rows, :] = place_rows(piece, row, height)
            return inner

        lax.fori_loop(0, height, widen, 0)
        all_grads = grad_all[:, :, cols].reshape(total, lanes)
        hot_own = hot[own, :]
        blank = jnp.zeros((tokens, lanes), narrow_type)
        hot_col, hot_row = hot_own[:, :lanes], hot_own[:, lanes:]
        keys = both_halves(k_all[own, cols], head_size, scale)
        left = jnp.concatenate(
            [
                jnp.concatenate([hot_col, blank, hot_row, blank], axis=1),
                jnp.concatenate([blank, hot_col, blank, hot_row], axis=1),
            ],
            axis=0,
        )
        right = jnp.concatenate(
            [all_queries, cols_extra[0], cols_extra[1], rows_extra[0], rows_extra[1]], axis=1
        )
        scores = dot_nt(jnp.concatenate([keys, left], axis=1), right)
        prob_grad = dot_nt(both_halves(v_all[own, cols], head_size, 1.0), all_grads)
        probs, score_grads = [], []
        for half in range(2):
            head = 2 * pair + half
            here = slice(half * tokens, (half + 1) * tokens)
            prob = jnp.exp(scores[here] - stat_rows[pl.ds(head, 1), :])
            probs.append(prob.astype(narrow_type))
            score_grad = prob * (prob_grad[here] - stat_rows[pl.ds(16 + head, 1), :])
            score_grads.append(score_grad.astype(narrow_type))
        key_both = dot_nn(jnp.concatenate(score_grads, axis=0), all_queries)
        value_both = dot_nn(jnp.concatenate(probs, axis=0), all_grads)
        key_grad = jnp.where(lane < head_size, key_both[:tokens], key_both[tokens:]) * scale
        value_grad = jnp.where(lane < head_size, value_both[:tokens], value_both[tokens:])
        joined[:, pl.ds(pl.multiple_of(model + at, lanes), lanes)] = key_grad.astype(narrow_type)
        joined[:, pl.ds(pl.multiple_of(2 * model + at, lanes), lanes)] = value_grad.astype(
            narrow_type
        )
        return carry

    wave(0)
    wave(1)
    done = 0
    steps = gather.deep - 1
    for number in range(steps):
        upto = pairs * (number + 1) // steps
        lax.fori_loop(done, upto, own_queries, 0)
        done = upto
        gather.step(number)
        if number == 1:
            wave(2)
    gather.finish()
    for block in range(strips):
        stat_rows[:, block * tokens : (block + 1) * tokens] = stat_all[block]
    done = 0
    for number in range(3):
        upto = pairs * (number + 1) // 3
        lax.fori_loop(done, upto, own_keys, 0)
        done = upto
        if number == 0:
            wave(3)
        if number == 2:
            wave(4)
    hat, inverse = norm_parts(x_own[...].astype(wide_type))
    normed_turned = (hat * vec[0:1, :] + vec[1:2, :]).astype(narrow_type).T
    back = jnp.zeros((tokens, model), wide_type)
    parts = {}
    for j in range(3):
        cols = slice(j * model, (j + 1) * model)
        part = joined[:, cols]
        sums[j : j + 1, :] = column_sum(part.astype(wide_type))
        back = back + dot_nt(part, qkv_weight[:, cols])
        if plan is None:
            weight_grad[:, cols] = dot_nn(normed_turned, part).astype(narrow_type)
    sums[3:4, :] = column_sum(back * hat)
    sums[4:5, :] = column_sum(back)
    sums[5:8, :] = jnp.zeros((3, model), wide_type)
    input_grad[...] = middle_grad[...] + norm_back(hat, inverse, back * vec[0:1, :])
    turned = pltpu.roll(rel_grad[2 * lanes :, :], head_size, 1)
    both = rel_grad[: 2 * lanes, :] + turned
    low = lane_ids((lanes, lanes)) < head_size
    rel_sum[...] = jnp.where(low, both[:lanes], pltpu.roll(both[lanes:], head_size, 1))
    if plan is None:
        return
    fold = weight_grad.shape[-1]
    for f in range(3 * model // fold):
        value = dot_nn(normed_turned, joined[:, f * fold : (f + 1) * fold])
        devices = 2**plan.stages
        own_count = model // devices
        parts[f] = value.reshape((2,) * plan.stages + (own_count, fold))
        if f % 2:
            pair = jnp.concatenate([parts.pop(f - 1), parts.pop(f)], axis=plan.stages)
            begin = (f - 1) * own_count
            lead = (slice(None),) * plan.stages
            weight_grad[lead + (slice(begin, begin + 2 * own_count),)] = pair.astype(narrow_type)
    reducer.start_near()
    sums[8:16, :] = block_sums[...]
    for j in range(fc1_sum.shape[1] // model):
        sums[16 + j : 17 + j, :] = fc1_sum[:, j * model : (j + 1) * model]
    sums[20:36, :] = level_sums[...]
    sums[36:44, :] = jnp.zeros((8, model), wide_type)
    sums[36:44, : gain_sums.shape[1]] = gain_sums[...]
    sums[44:48, :] = jnp.zeros((4, model), wide_type)

    def small_copies(stage):
        out = []
        for i, (own_ref, landed) in enumerate(((sums, small_landed), (rel_sum, rel_landed))):
            out.append(
                pltpu.make_async_remote_copy(
                    src_ref=own_ref,
                    dst_ref=landed.at[stage],
                    send_sem=small_send.at[stage, i],
                    recv_sem=small_recv.at[stage, i],
                    device_id=reducer.partners[plan.pieces[0][4][stage]][0],
                    device_id_type=MESH_ID,
                )
            )
        return out

    for copy in small_copies(0):
        copy.start()
    stage = 0
    first = 5
    last = plan.waves()
    for number in range(first, max(last, first + plan.stages)):
        if number < last:
            reducer.wave(number)
        if stage < plan.stages:
            for copy in small_copies(stage):
                copy.wait()
            sums[...] = sums[...] + small_landed[stage]
            rel_sum[...] = rel_sum[...] + rel_landed[stage]
            stage += 1
            if stage < plan.stages:
                for copy in small_copies(stage):
                    copy.start()
    small_out[...] = sums[...]
    rel_out[...] = rel_sum[...]
    reducer.finish()


def attention_backward(height, width, operands, small, arrays, plan, shares, call_id):
    tokens, model = operands[0].shape
    total = operands[1].shape[0]
    strips = total // tokens
    slots = StripGather.slots()

    def shape(rows, cols, kind):
        return jax.ShapeDtypeStruct((rows, cols), kind)

    outs = [shape(tokens, model, wide_type)]
    scratch = []
    extra = []
    if plan is None:
        outs += [
            shape(8, model, wide_type),
            shape(lanes, lanes, wide_type),
            shape(model, 3 * model, narrow_type),
        ]
    else:
        rows = 48
        outs += [shape(rows, model, wide_type), shape(lanes, lanes, wide_type)]
        outs += [flat for flat, _ in shares]
        shares = [share for _, share in shares]
        stages = plan.stages
        scratch += [
            pltpu.VMEM((rows, model), wide_type),
            pltpu.VMEM((lanes, lanes), wide_type),
            pltpu.VMEM((stages, rows, model), wide_type),
            pltpu.VMEM((stages, lanes, lanes), wide_type),
            pltpu.SemaphoreType.DMA((stages, 2)),
            pltpu.SemaphoreType.DMA((stages, 2)),
            pltpu.VMEM((2,) * stages + plan.shapes[-1][1:], narrow_type),
        ]
        extra = plan.scratch()
    scratch += [
        pltpu.VMEM((tokens, 3 * model), narrow_type),
        pltpu.VMEM((total, 4 * lanes), wide_type),
        pltpu.VMEM((2, total, lanes), narrow_type),
        pltpu.VMEM((2, total, lanes), narrow_type),
        pltpu.VMEM((strips, tokens, model), narrow_type),
        pltpu.VMEM((strips, 32, tokens), wide_type),
        pltpu.VMEM((32, total), wide_type),
        pltpu.VMEM((4 * lanes, lanes), wide_type),
        pltpu.SemaphoreType.DMA((slots, 2)),
        pltpu.SemaphoreType.DMA((slots, 2)),
    ]

    def body(*refs):
        attention_backward_kernel(height, width, plan, shares, refs)

    given = operands + (small if plan is not None else ())
    far = plan.shaped(arrays) if plan is not None else []
    return pl.pallas_call(
        body,
        out_shape=outs,
        in_specs=vmem_specs(len(given)) + any_specs(len(far)),
        out_specs=vmem_specs(len(outs)),
        scratch_shapes=scratch + extra,
        compiler_params=pltpu.CompilerParams(
            collective_id=call_id, has_side_effects=True, vmem_limit_bytes=62 << 20
        ),
        name="attention_backward",
    )(*given, *far)


class Levels:
    def __init__(self, strip_rows, width):
        self.rows = (4 * strip_rows, 2 * strip_rows, strip_rows, strip_rows // 2)
        self.cols = (4 * width, 2 * width, width, width // 2)
        self.at, self.edge_at, self.wide_at = [], [], []
        total = edge = wide = 0
        for rows, cols in zip(self.rows, self.cols):
            self.at.append(total)
            self.edge_at.append(edge)
            self.wide_at.append(wide)
            total += rows * cols
            edge += cols
            wide += (rows + 2) * cols
        self.total, self.edge, self.wide = total, edge, wide


def put_strided(target, at, count, stride, value):
    for part in range(target.shape[0]):
        target[part, pl.ds(at, count, stride=stride), :] = value[:, part * lanes : (part + 1) * lanes]


def get_strided(source, at, count, stride):
    parts = [source[part, pl.ds(at, count, stride=stride), :] for part in range(source.shape[0])]
    return jnp.concatenate(parts, axis=1)


def join_parts(source, begin, end):
    return jnp.concatenate([source[part, begin:end, :] for part in range(source.shape[0])], axis=1)


def store_edges(levels, level, source, offset, top, bottom):
    rows, cols = levels.rows[level], levels.cols[level]
    at = levels.edge_at[level]
    top[at : at + cols, :] = source[offset : offset + cols, :]
    last = offset + (rows - 1) * cols
    bottom[at : at + cols, :] = source[last : last + cols, :]


def level_source_kernel(
    levels,
    strip_rows,
    width,
    base,
    y,
    vec,
    first,
    second,
    eight,
    lat_four,
    lat_eight,
    lat_sixteen,
    lat_thirty,
    lateral,
    top,
    bottom,
    first_map,
    active,
    source_zero,
    source_one,
    pooled,
    reduced,
    spread_zero,
    spread_one,
    wide_y,
):
    tokens, model = y.shape
    out = lat_sixteen.shape[0]
    mid = first.shape[1] // 4
    values = y[...]

    def finish(level, value, at):
        reduced[at : at + value.shape[0], :] = value
        hat, _ = norm_parts(value)
        gain = vec[base + 5 + level : base + 6 + level, :out]
        shift = vec[base + 9 + level : base + 10 + level, :out]
        return hat * gain + shift

    for tap in range(4):
        a, b = tap // 2, tap % 2
        cols = slice(tap * mid, (tap + 1) * mid)
        rows = slice(tap * tokens, (tap + 1) * tokens)
        mapped = dot_nn(values, first[:, cols]) + vec[base : base + 1, :mid]
        first_map[:, cols] = mapped
        hat, _ = norm_parts(mapped)
        normed = hat * vec[base + 1 : base + 2, :mid] + vec[base + 2 : base + 3, :mid]
        act = (normed * normal_cdf(normed)).astype(narrow_type)
        active[rows, :] = act
        source = (dot_nt(act, second[...]) + vec[base + 3 : base + 4, :]).astype(narrow_type)
        source_zero[rows, :] = source
        half = source.shape[1] // 2
        for pair in range(2):
            both = dot_nt(source[:, pair * half : (pair + 1) * half], lat_four[...])
            for side in range(2):
                place = (4 * tap + 2 * pair + side) * tokens
                value = finish(0, both[:, side * out : (side + 1) * out], place)
                for i in range(strip_rows):
                    at = (4 * i + 2 * a + pair) * levels.cols[0] + 2 * b + side
                    put_strided(spread_zero, at, width, 4, value[i * width : (i + 1) * width])
        mapped = dot_nn(values, eight[:, cols]) + vec[base + 4 : base + 5, :mid]
        source = mapped.astype(narrow_type)
        source_one[rows, :] = source
        value = finish(1, dot_nt(source, lat_eight[...]), levels.at[1] + tap * tokens)
        for i in range(strip_rows):
            at = (2 * i + a) * levels.cols[1] + b
            put_strided(spread_one, at, width, 2, value[i * width : (i + 1) * width])
    for target, begin, end in ((spread_zero, 0, levels.at[1]), (spread_one, *levels.at[1:3])):
        joined = join_parts(target, 0, end - begin)
        lateral[begin:end, :] = joined.astype(narrow_type)
    value = finish(2, dot_nt(values, lat_sixteen[...]), levels.at[2])
    lateral[levels.at[2] : levels.at[3], :] = value.astype(narrow_type)
    for part in range(model // lanes):
        wide_y[part] = values[:, part * lanes : (part + 1) * lanes].astype(wide_type)
    quarter = width // 2
    for i in range(strip_rows // 2):
        summed = 0.0
        for a in range(2):
            for b in range(2):
                at = (2 * i + a) * width + b
                summed = summed + get_strided(wide_y, at, quarter, 2)
        pooled[i * quarter : (i + 1) * quarter, :] = (summed * 0.25).astype(narrow_type)
    value = finish(3, dot_nt(pooled[...], lat_thirty[...]), levels.at[3])
    lateral[levels.at[3] : levels.total, :] = value.astype(narrow_type)
    for level in range(4):
        store_edges(levels, level, lateral, levels.at[level], top, bottom)


def level_sources(levels, strip_rows, width, base, y, vec, first, second, eight, laterals):
    tokens, model = y.shape
    out = laterals[2].shape[0]

    def shape(rows, cols, kind):
        return jax.ShapeDtypeStruct((rows, cols), kind)

    mid = first.shape[1] // 4
    outs = [
        shape(levels.total, out, narrow_type),
        shape(levels.edge, out, narrow_type),
        shape(levels.edge, out, narrow_type),
        shape(tokens, 4 * mid, wide_type),
        shape(4 * tokens, mid, narrow_type),
        shape(4 * tokens, second.shape[0], narrow_type),
        shape(4 * tokens, mid, narrow_type),
        shape(tokens // 4, model, narrow_type),
        shape(levels.total, out, wide_type),
    ]
    return pl.pallas_call(
        partial(level_source_kernel, levels, strip_rows, width, base),
        out_shape=outs,
        in_specs=vmem_specs(9),
        out_specs=vmem_specs(len(outs)),
        scratch_shapes=[
            pltpu.VMEM((out // lanes, levels.at[1], lanes), wide_type),
            pltpu.VMEM((out // lanes, levels.at[2] - levels.at[1], lanes), wide_type),
            pltpu.VMEM((model // lanes, tokens, lanes), wide_type),
        ],
        compiler_params=pltpu.CompilerParams(vmem_limit_bytes=60 << 20),
        name="level_sources",
    )(y, vec, first, second, eight, *laterals)


def edge_kernel(top, bottom, above, below, send_sem, recv_sem):
    strip = strip_index()
    scale = lax.axis_size("scale")
    count = lax.axis_size("rows") * scale
    above[...] = jnp.zeros_like(above)
    below[...] = jnp.zeros_like(below)

    def place(index):
        return {"rows": lax.div(index, scale), "scale": lax.rem(index, scale)}

    has_up = strip > 0
    has_down = strip < count - 1
    barrier = pltpu.get_barrier_semaphore()
    up, down = place(jnp.maximum(strip - 1, 0)), place(jnp.minimum(strip + 1, count - 1))

    @pl.when(has_up)
    def _():
        pl.semaphore_signal(barrier, inc=1, device_id=up, device_id_type=MESH_ID)

    @pl.when(has_down)
    def _():
        pl.semaphore_signal(barrier, inc=1, device_id=down, device_id_type=MESH_ID)

    pl.semaphore_wait(barrier, jnp.where(has_up, 1, 0) + jnp.where(has_down, 1, 0))

    def send(source, target, i, device):
        return pltpu.make_async_remote_copy(
            src_ref=source,
            dst_ref=target,
            send_sem=send_sem.at[i],
            recv_sem=recv_sem.at[i],
            device_id=device,
            device_id_type=MESH_ID,
        )

    @pl.when(has_down)
    def _():
        send(bottom, above, 0, down).start()

    @pl.when(has_up)
    def _():
        send(top, below, 1, up).start()

    @pl.when(has_down)
    def _():
        send(bottom, above, 0, down).wait_send()
        send(top, below, 1, up).wait_recv()

    @pl.when(has_up)
    def _():
        send(top, below, 1, up).wait_send()
        send(bottom, above, 0, down).wait_recv()


def exchange_edges(top, bottom, call_id):
    shape = jax.ShapeDtypeStruct(top.shape, top.dtype)
    return pl.pallas_call(
        edge_kernel,
        out_shape=[shape, shape],
        in_specs=vmem_specs(2),
        out_specs=vmem_specs(2),
        scratch_shapes=[pltpu.SemaphoreType.DMA((2,)), pltpu.SemaphoreType.DMA((2,))],
        compiler_params=pltpu.CompilerParams(collective_id=call_id, has_side_effects=True),
        name="exchange_edges",
    )(top, bottom)


def widen_slab(levels, level, source, above, below, padded, slab, offset):
    rows, cols = levels.rows[level], levels.cols[level]
    at, edge = levels.at[level], levels.edge_at[level]
    channels = source.shape[1]
    size = rows * cols
    padded[8 : 8 + cols, :] = above[edge : edge + cols, :].astype(wide_type)
    padded[8 + cols : 8 + cols + size, :] = source[at : at + size, :].astype(wide_type)
    padded[8 + cols + size : 8 + 2 * cols + size, :] = below[edge : edge + cols, :].astype(wide_type)
    wide = size + 2 * cols
    block = min(256, wide)
    while wide % block:
        block //= 2

    def step(i, carry):
        begin = pl.multiple_of(i * block, block)
        got = padded[pl.ds(begin, block + 16), :]
        col = lax.rem(begin + lax.broadcasted_iota(jnp.int32, (block, channels), 0), cols)
        left = jnp.where(col > 0, got[7 : 7 + block], 0.0)
        right = jnp.where(col < cols - 1, got[9 : 9 + block], 0.0)
        joined = jnp.concatenate([left, got[8 : 8 + block], right], axis=1)
        slab[pl.ds(pl.multiple_of(offset + begin, block), block), :] = joined.astype(narrow_type)
        return carry

    lax.fori_loop(0, wide // block, step, 0)


def smooth_kernel(
    levels,
    base,
    lateral,
    above,
    below,
    weight,
    smooth,
    vec,
    grads,
    top,
    bottom,
    slabs,
    gain_sums,
    padded,
):
    channels = lateral.shape[1]
    gain_sums[...] = jnp.zeros_like(gain_sums)
    for level in range(4):
        rows, cols = levels.rows[level], levels.cols[level]
        offset = levels.wide_at[level]
        widen_slab(levels, level, lateral, above, below, padded, slabs, offset)
        size = rows * cols
        block = min(256, size)
        gain = vec[base + 13 + level : base + 14 + level, :channels]

        def step(i, carry):
            begin = pl.multiple_of(i * block, block)
            total = None
            for a in range(3):
                window = slabs[pl.ds(pl.multiple_of(offset + a * cols + begin, 32), block), :]
                part = dot_nn(
                    window, smooth[level, 3 * a * channels : 3 * (a + 1) * channels, :]
                )
                total = part if total is None else total + part
            hat, inverse = norm_parts(total)
            here = pl.ds(pl.multiple_of(levels.at[level] + begin, 32), block)
            upstream = weight[here, :].astype(wide_type)
            gain_sums[level : level + 1, :] += column_sum(upstream * hat)
            grads[here, :] = norm_back(hat, inverse, upstream * gain).astype(narrow_type)
            return carry

        lax.fori_loop(0, size // block, step, 0)
        store_edges(levels, level, grads, levels.at[level], top, bottom)


def smooth_levels(levels, base, lateral, above, below, weight, smooth, vec):
    channels = lateral.shape[1]
    biggest = (levels.rows[0] + 2) * levels.cols[0]
    outs = [
        jax.ShapeDtypeStruct(lateral.shape, narrow_type),
        jax.ShapeDtypeStruct(above.shape, narrow_type),
        jax.ShapeDtypeStruct(above.shape, narrow_type),
        jax.ShapeDtypeStruct((levels.wide, 3 * channels), narrow_type),
        jax.ShapeDtypeStruct((8, channels), wide_type),
    ]
    return pl.pallas_call(
        partial(smooth_kernel, levels, base),
        out_shape=outs,
        in_specs=vmem_specs(6),
        out_specs=vmem_specs(len(outs)),
        scratch_shapes=[pltpu.VMEM((biggest + 16, channels), wide_type)],
        compiler_params=pltpu.CompilerParams(vmem_limit_bytes=60 << 20),
        name="smooth_levels",
    )(lateral, above, below, weight, smooth, vec)


def level_back_kernel(
    levels,
    strip_rows,
    width,
    base,
    grads,
    above,
    below,
    slabs,
    reduced,
    first_map,
    active,
    source_zero,
    source_one,
    pooled,
    y,
    vec,
    smooth,
    first,
    second,
    eight,
    lat_four,
    lat_eight,
    lat_sixteen,
    lat_thirty,
    y_grad,
    sums,
    smooth_grad,
    first_grad,
    second_grad,
    eight_grad,
    lat_four_grad,
    lat_eight_grad,
    lat_sixteen_grad,
    lat_thirty_grad,
    padded,
    slab,
    spread,
    second_sum,
    four_sum,
    eight_sum,
    total_grad,
    pool_grad,
):
    tokens, model = y.shape
    channels = grads.shape[1]
    mid = first.shape[1] // 4
    sums[...] = jnp.zeros_like(sums)

    def smooth_back(level):
        rows, cols = levels.rows[level], levels.cols[level]
        size = rows * cols
        widen_slab(levels, level, grads, above, below, padded, slab, 0)
        block = min(256, size)

        def step(i, carry):
            begin = pl.multiple_of(i * block, block)
            total = None
            for a in range(3):
                for b in range(3):
                    window = slab[
                        pl.ds(pl.multiple_of((2 - a) * cols + begin, 32), block),
                        (2 - b) * channels : (3 - b) * channels,
                    ]
                    tap = (3 * a + b) * channels
                    part = dot_nt(window, smooth[level, tap : tap + channels, :])
                    total = part if total is None else total + part
            for part in range(channels // lanes):
                spread[part, pl.ds(begin, block), :] = total[:, part * lanes : (part + 1) * lanes]
            return carry

        lax.fori_loop(0, size // block, step, 0)
        turned = grads[levels.at[level] : levels.at[level] + size, :].T
        for a in range(3):
            begin = levels.wide_at[level] + a * cols
            for b in range(3):
                part = dot_nn(turned, slabs[begin : begin + size, b * channels : (b + 1) * channels])
                at = (level * 9 + 3 * a + b) * channels
                smooth_grad[at : at + channels, :] = part.T.astype(narrow_type)

    def reduced_back(level, upstream, at):
        hat, inverse = norm_parts(reduced[at : at + upstream.shape[0], :])
        gain = vec[base + 5 + level : base + 6 + level, :channels]
        sums[5 + level : 6 + level, :channels] += column_sum(upstream * hat)
        sums[9 + level : 10 + level, :channels] += column_sum(upstream)
        return norm_back(hat, inverse, upstream * gain).astype(narrow_type)

    def keep_tap(target, tap, parts, value):
        if len(target.shape) == 2:
            target[:, tap * mid : (tap + 1) * mid] = value.astype(narrow_type)
        else:
            fold_store(target, tap, parts, value)

    first_parts, eight_parts = {}, {}
    turned_y = y[...].T
    total_grad[...] = jnp.zeros_like(total_grad)
    smooth_back(0)
    for tap in range(4):
        a, b = tap // 2, tap % 2
        cols = slice(tap * mid, (tap + 1) * mid)
        rows = slice(tap * tokens, (tap + 1) * tokens)
        parts = []
        for pair in range(2):
            sides = []
            for side in range(2):
                pieces = []
                for i in range(strip_rows):
                    at = (4 * i + 2 * a + pair) * levels.cols[0] + 2 * b + side
                    pieces.append(get_strided(spread, at, width, 4))
                upstream = jnp.concatenate(pieces, axis=0)
                sides.append(reduced_back(0, upstream, (4 * tap + 2 * pair + side) * tokens))
            both = jnp.concatenate(sides, axis=1)
            half = source_zero.shape[1] // 2
            product = dot_tn(both, source_zero[rows, pair * half : (pair + 1) * half])
            if tap == 0 and pair == 0:
                four_sum[...] = product
            else:
                four_sum[...] += product
            parts.append(dot_nn(both, lat_four[...]).astype(narrow_type))
        second_low = jnp.concatenate(parts, axis=1)
        sums[3:4, :] += column_sum(second_low.astype(wide_type))
        product = dot_tn(second_low, active[rows, :])
        if tap == 0:
            second_sum[...] = product
        else:
            second_sum[...] += product
        active_grad = dot_nn(second_low, second[...])
        hat, inverse = norm_parts(first_map[:, cols])
        gain = vec[base + 1 : base + 2, :mid]
        normed = hat * gain + vec[base + 2 : base + 3, :mid]
        normed_grad = active_grad * gelu_slope(normed)
        sums[1:2, :mid] += column_sum(normed_grad * hat)
        sums[2:3, :mid] += column_sum(normed_grad)
        first_low = norm_back(hat, inverse, normed_grad * gain).astype(narrow_type)
        sums[0:1, :mid] += column_sum(first_low.astype(wide_type))
        keep_tap(first_grad, tap, first_parts, dot_nn(turned_y, first_low))
        total_grad[...] += dot_nt(first_low, first[:, cols])
    second_grad[...] = second_sum[...].astype(narrow_type)
    quarter = lat_four.shape[1] // 2
    lat_four_grad[...] = (
        four_sum[:channels, :quarter] + four_sum[channels:, quarter:]
    ).astype(narrow_type)
    smooth_back(1)
    for tap in range(4):
        a, b = tap // 2, tap % 2
        cols = slice(tap * mid, (tap + 1) * mid)
        rows = slice(tap * tokens, (tap + 1) * tokens)
        pieces = []
        for i in range(strip_rows):
            at = (2 * i + a) * levels.cols[1] + b
            pieces.append(get_strided(spread, at, width, 2))
        upstream = jnp.concatenate(pieces, axis=0)
        low = reduced_back(1, upstream, levels.at[1] + tap * tokens)
        product = dot_tn(low, source_one[rows, :])
        if tap == 0:
            eight_sum[...] = product
        else:
            eight_sum[...] += product
        eight_low = dot_nn(low, lat_eight[...]).astype(narrow_type)
        sums[4:5, :mid] += column_sum(eight_low.astype(wide_type))
        keep_tap(eight_grad, tap, eight_parts, dot_nn(turned_y, eight_low))
        total_grad[...] += dot_nt(eight_low, eight[:, cols])
    lat_eight_grad[...] = eight_sum[...].astype(narrow_type)
    smooth_back(2)
    low = reduced_back(2, join_parts(spread, 0, tokens), levels.at[2])
    lat_sixteen_grad[...] = dot_tn(low, y[...]).astype(narrow_type)
    total_grad[...] += dot_nn(low, lat_sixteen[...])
    smooth_back(3)
    low = reduced_back(3, join_parts(spread, 0, tokens // 4), levels.at[3])
    lat_thirty_grad[...] = dot_tn(low, pooled[...]).astype(narrow_type)
    pooled_grad = dot_nn(low, lat_thirty[...]) * 0.25
    count = width // 2
    for i in range(strip_rows // 2):
        piece = pooled_grad[i * count : (i + 1) * count]
        for a in range(2):
            for b in range(2):
                at = (2 * i + a) * width + b
                put_strided(pool_grad, at, count, 2, piece)
    y_grad[...] = (total_grad[...] + join_parts(pool_grad, 0, tokens)).astype(narrow_type)


def level_back(levels, strip_rows, width, base, operands, devices):
    tokens, model = operands[10].shape
    channels = operands[0].shape[1]
    smooth, first, second, eight, four_pair, lat_eight, lat_sixteen, lat_thirty = operands[12:]
    biggest = (levels.rows[0] + 2) * levels.cols[0]

    def shape(rows, cols, kind=narrow_type):
        return jax.ShapeDtypeStruct((rows, cols), kind)

    outs = [
        shape(tokens, model),
        shape(16, model, wide_type),
        shape(smooth.shape[0] * smooth.shape[1], smooth.shape[2]),
        shape(*first.shape),
        shape(*second.shape),
        shape(*eight.shape),
        shape(channels, four_pair.shape[1] // 2),
        shape(*lat_eight.shape),
        shape(*lat_sixteen.shape),
        shape(*lat_thirty.shape),
    ]
    if devices:
        folded = (devices, first.shape[0] // devices * 4, first.shape[1] // 4)
        outs[3] = jax.ShapeDtypeStruct(folded, narrow_type)
        outs[5] = jax.ShapeDtypeStruct(folded, narrow_type)
    return pl.pallas_call(
        partial(level_back_kernel, levels, strip_rows, width, base),
        out_shape=outs,
        in_specs=vmem_specs(len(operands)),
        out_specs=vmem_specs(len(outs)),
        scratch_shapes=[
            pltpu.VMEM((biggest + 16, channels), wide_type),
            pltpu.VMEM((biggest, 3 * channels), narrow_type),
            pltpu.VMEM((channels // lanes, levels.rows[0] * levels.cols[0], lanes), wide_type),
            pltpu.VMEM(second.shape, wide_type),
            pltpu.VMEM(four_pair.shape, wide_type),
            pltpu.VMEM(lat_eight.shape, wide_type),
            pltpu.VMEM((tokens, model), wide_type),
            pltpu.VMEM((model // lanes, tokens, lanes), wide_type),
        ],
        compiler_params=pltpu.CompilerParams(vmem_limit_bytes=62 << 20),
        name="level_back",
    )(*operands)


def own_rows(values, count):
    return lax.dynamic_slice_in_dim(values, lax.axis_index("scale") * count, count, axis=1)


def level_weight(scale_level, strip_rows, cotans, anchors, roi_mask):
    region = own_rows(roi_mask, strip_rows)
    if scale_level < 3:
        factor = (4, 2, 1)[scale_level]
        region = jnp.repeat(jnp.repeat(region, factor, axis=1), factor, axis=2)
        count = factor * strip_rows
    else:
        region = region[:, ::2, ::2]
        count = strip_rows // 2
    anchor = own_rows(anchors[scale_level], count)
    cotangent = own_rows(cotans[scale_level], count)
    return (anchor + region).astype(narrow_type)[..., None] * cotangent


def on_device(
    block_input,
    pre_gain,
    pre_shift,
    qkv_weight,
    qv_bias,
    rel_rows,
    rel_cols,
    proj_weight,
    proj_bias,
    mid_gain,
    mid_shift,
    fc1_weight,
    fc1_bias,
    fc2_weight,
    fc2_bias,
    deconv_first,
    first_bias,
    upnorm_gain,
    upnorm_shift,
    deconv_second,
    second_bias,
    deconv_eight,
    eight_bias,
    lateral_four,
    lateral_eight,
    lateral_sixteen,
    lateral_thirty,
    lateral_gain,
    lateral_shift,
    smooth_weight,
    output_gain,
    grad_four,
    grad_eight,
    grad_sixteen,
    grad_thirty,
    anchor_four,
    anchor_eight,
    anchor_sixteen,
    anchor_thirty,
    roi_mask,
):
    _, strip_rows, width, model = block_input.shape
    head_size = rel_rows.shape[1]
    tokens = strip_rows * width
    height = strip_rows * lax.axis_size(("rows", "scale"))
    channels = smooth_weight.shape[2]
    ff = fc1_weight.shape[1]
    mid = first_bias.shape[0]
    quarter = second_bias.shape[0]
    levels = Levels(strip_rows, width)
    devices = lax.axis_size(("img", "rows", "scale"))
    fused = devices if (model // devices) % 8 == 0 and height <= 16 else 0
    x_own = block_input.reshape(tokens, model)
    x_all = gather_strips(x_own, 2)

    def wide_rows(vector):
        vector = vector.reshape(-1, vector.shape[-1]).astype(wide_type)
        if vector.shape[-1] > model:
            return vector.reshape(-1, model)
        return jnp.pad(vector, ((0, 0), (0, model - vector.shape[-1])))

    base = 8 + ff // model
    vec = jnp.concatenate(
        [
            wide_rows(part)
            for part in (
                pre_gain,
                pre_shift,
                qv_bias[:model],
                qv_bias[model:],
                proj_bias,
                mid_gain,
                mid_shift,
                fc2_bias,
                fc1_bias,
                first_bias,
                upnorm_gain,
                upnorm_shift,
                jnp.tile(second_bias, 4),
                eight_bias,
                lateral_gain,
                lateral_shift,
                output_gain,
            )
        ],
        axis=0,
    )
    vec = jnp.pad(vec, ((0, -vec.shape[0] % 8), (0, 0)))

    def padded_table(table):
        return jnp.pad(table, ((0, lanes - table.shape[0]), (0, 0)))

    turned = jnp.concatenate(
        [padded_table(rel_cols[::-1]), padded_table(rel_rows[::-1])], axis=0
    ).T
    none = jnp.zeros_like(turned)
    tables = jnp.concatenate(
        [jnp.concatenate([turned, none], axis=1), jnp.concatenate([none, turned], axis=1)], axis=0
    )
    plain = jnp.concatenate([padded_table(rel_cols), padded_table(rel_rows)], axis=0)
    blank = jnp.zeros_like(plain)
    rel_all = jnp.concatenate(
        [jnp.concatenate([plain, blank], axis=1), jnp.concatenate([blank, plain], axis=1)], axis=0
    )
    token = jnp.arange(height * width, dtype=jnp.int32)[:, None]
    lane = jnp.arange(lanes, dtype=jnp.int32)[None, :]
    key_row, key_col = token // width, token % width
    hot_col = (lane % width == key_col) & (lane < 2 * width)
    hot_row = (lane % height == key_row) & (lane < 2 * height)
    hot = jnp.concatenate([hot_col, hot_row], axis=1).astype(narrow_type)
    hot_turned = jnp.concatenate(
        [lane == width - 1 - key_col, lane == height - 1 - key_row], axis=1
    ).astype(narrow_type)
    lat_four_pair = jnp.concatenate(
        [
            jnp.concatenate([lateral_four, jnp.zeros_like(lateral_four)], axis=1),
            jnp.concatenate([jnp.zeros_like(lateral_four), lateral_four], axis=1),
        ],
        axis=0,
    )
    anchors = (anchor_four, anchor_eight, anchor_sixteen, anchor_thirty)
    cotans = (grad_four, grad_eight, grad_sixteen, grad_thirty)
    weight = jnp.concatenate(
        [
            level_weight(level, strip_rows, cotans, anchors, roi_mask).reshape(-1, channels)
            for level in range(4)
        ],
        axis=0,
    )
    (
        q_all,
        k_all,
        v_all,
        attended,
        attended_wide,
        log_norm,
        middle,
        normed_mid,
        hidden_pre,
        hidden,
        result,
    ) = block_forward(
        height,
        width,
        tokens,
        x_all,
        vec,
        qkv_weight,
        tables,
        hot,
        proj_weight,
        fc1_weight,
        fc2_weight,
    )
    lateral, top, bottom, first_map, active, source_zero, source_one, pooled, reduced = (
        level_sources(
            levels,
            strip_rows,
            width,
            base,
            result,
            vec,
            deconv_first,
            deconv_second,
            deconv_eight,
            (lat_four_pair, lateral_eight, lateral_sixteen, lateral_thirty),
        )
    )
    above, below = exchange_edges(top, bottom, 1)
    grads, top, bottom, slabs, gain_sums = smooth_levels(
        levels, base, lateral, above, below, weight, smooth_weight, vec
    )
    above, below = exchange_edges(top, bottom, 1)
    (
        result_grad,
        level_sums,
        smooth_grad,
        first_grad,
        second_grad,
        eight_grad,
        lat_four_grad,
        lat_eight_grad,
        lat_sixteen_grad,
        lat_thirty_grad,
    ) = level_back(
        levels,
        strip_rows,
        width,
        base,
        (
            grads,
            above,
            below,
            slabs,
            reduced,
            first_map,
            active,
            source_zero,
            source_one,
            pooled,
            result,
            vec,
            smooth_weight,
            deconv_first,
            deconv_second,
            deconv_eight,
            lat_four_pair,
            lateral_eight,
            lateral_sixteen,
            lateral_thirty,
        ),
        fused,
    )
    (
        middle_grad,
        attended_grad,
        stats,
        stat_rows,
        block_sums,
        fc1_sum,
        proj_grad,
        fc1_grad,
        fc2_grad,
    ) = block_backward(
        result_grad,
        (hidden_pre, hidden, normed_mid, middle, attended, attended_wide),
        log_norm,
        vec,
        proj_weight,
        fc1_weight,
        fc2_weight,
        fused,
    )
    operands = (
        x_own,
        q_all,
        k_all,
        v_all,
        attended_grad,
        stats,
        stat_rows,
        middle_grad,
        vec,
        tables,
        rel_all,
        hot,
        hot_turned,
        qkv_weight,
    )
    small_operands = (block_sums, fc1_sum, level_sums, gain_sums)
    rest_grads = (
        proj_grad,
        second_grad,
        lat_sixteen_grad,
        lat_thirty_grad,
        lat_eight_grad,
        lat_four_grad,
    )
    rest_names = ("proj", "second", "lat_sixteen", "lat_thirty", "lat_eight", "lat_four")
    rest, rest_fold = fold_chunks(rest_grads, mid)
    if fused:
        arrays = (
            smooth_grad.reshape(devices, -1, channels),
            first_grad,
            eight_grad,
            fc1_grad,
            fc2_grad.reshape(devices, -1, model),
            rest,
        )
        shapes = [array.shape for array in arrays]
        shapes.append((devices, model // devices * (3 * model // mid), mid))
        halves = {}
        for source, begin, size in cut_rows(shapes):
            halves.setdefault(source, []).append((source, begin, size))
        pieces = [
            halves[0][0],
            (1, 0, shapes[1][1]),
            halves[0][1],
            (2, 0, shapes[2][1]),
            halves[3][0],
            halves[5][0],
            halves[4][0],
            halves[5][1],
            halves[3][1],
            halves[4][1],
            halves[6][0],
            halves[6][1],
        ]
        plan = ReducePlan(shapes, pieces, near=(6,))
        shares = []
        names = []

        def share(name, source, places, size):
            flat = jax.ShapeDtypeStruct((size // devices // lanes, lanes), wide_type)
            shares.append((flat, (source, places)))
            names.append(name)

        def folded(source, rows, columns, begin=0):
            own, width_in = rows // devices, shapes[source][2]
            tiles = columns // lanes
            return [
                (begin + f * own, own, f * width_in // lanes, tiles)
                for f in range(max(columns // width_in, 1))
            ]

        share("smooth", 0, folded(0, smooth_grad.shape[0], channels), smooth_grad.size)
        share("first", 1, folded(1, *deconv_first.shape), deconv_first.size)
        share("eight", 2, folded(2, *deconv_eight.shape), deconv_eight.size)
        share("fc1", 3, folded(3, *fc1_weight.shape), fc1_weight.size)
        share("fc2", 4, folded(4, *fc2_weight.shape), fc2_weight.size)
        at = 0
        for name, grad, (own, columns, folds) in zip(rest_names, rest_grads, rest_fold):
            if columns % lanes == 0:
                share(name, 5, folded(5, *grad.shape, begin=at), grad.size)
            else:
                flat = jax.ShapeDtypeStruct((own, mid), wide_type)
                shares.append((flat, (5, [(at, own, 0, 0)])))
                names.append(name)
            at += own * folds
        share("qkv", 6, folded(6, *qkv_weight.shape), qkv_weight.size)
        got = attention_backward(
            height, width, operands, small_operands, arrays, plan, shares, 0
        )
        input_grad, sums, rel_sum = got[:3]
        weight_sums = dict(zip(names, got[3:]))
        narrow = weight_sums["lat_four"]
        weight_sums["lat_four"] = narrow[:, :quarter]
        weight_sums = {name: value.reshape(-1) for name, value in weight_sums.items()}
    else:
        input_grad, mix_sums, rel_sum, qkv_grad = attention_backward(
            height, width, operands, (), (), None, (), 0
        )
        packed, folds, names = [], [], []
        for grads_in, columns, called in (
            ((smooth_grad,), channels, ("smooth",)),
            ((first_grad, eight_grad), model, ("first", "eight")),
            ((fc1_grad,), model, ("fc1",)),
            ((fc2_grad,), model, ("fc2",)),
            ((qkv_grad,), mid, ("qkv",)),
        ):
            stacked, fold = fold_chunks(grads_in, columns)
            packed.append(stacked)
            folds.append(fold)
            names += called
        gain_rows = jnp.pad(gain_sums, ((0, 0), (0, model - channels)))
        small_in = (
            jnp.concatenate(
                [mix_sums, block_sums, fc1_sum.reshape(-1, model), level_sums, gain_rows]
            ),
            rel_sum,
        )
        got, small = last_reduce([*packed, rest], pack_small(small_in), 3)
        sums, rel_sum = unpack_small(small, small_in)
        flat = []
        for summed, fold in zip(got, (*folds, rest_fold)):
            flat += unfold_chunks(summed, fold)
        weight_sums = dict(zip((*names, *rest_names), flat))
    small = (
        sums[3],
        sums[4],
        jnp.concatenate([sums[0], sums[2]]),
        rel_sum[: rel_rows.shape[0], head_size : 2 * head_size],
        rel_sum[: rel_cols.shape[0], :head_size],
        sums[8],
        sums[9],
        sums[10],
        sums[16:20].reshape(-1),
        sums[11],
        sums[20, :mid],
        sums[21, :mid],
        sums[22, :mid],
        jnp.sum(sums[23].reshape(4, quarter), axis=0),
        sums[24, :mid],
        sums[25:29, :channels],
        sums[29:33, :channels],
        sums[36:40, :channels],
    )
    return (
        result.reshape(block_input.shape),
        input_grad.reshape(block_input.shape),
        small[0],
        small[1],
        weight_sums["qkv"],
        small[2],
        small[3],
        small[4],
        weight_sums["proj"],
        small[5],
        small[6],
        small[7],
        weight_sums["fc1"],
        small[8],
        weight_sums["fc2"],
        small[9],
        weight_sums["first"],
        small[10],
        small[11],
        small[12],
        weight_sums["second"],
        small[13],
        weight_sums["eight"],
        small[14],
        weight_sums["lat_four"],
        weight_sums["lat_eight"],
        weight_sums["lat_sixteen"],
        weight_sums["lat_thirty"],
        small[15],
        small[16],
        weight_sums["smooth"],
        small[17],
    )


def solution(mesh):
    in_specs = (
        P("img", ("rows", "scale"), None, None),
        P(),
        P(),
        P(),
        P(),
        P(),
        P(),
        P(),
        P(),
        P(),
        P(),
        P(),
        P(),
        P(),
        P(),
        P(),
        P(),
        P(),
        P(),
        P(),
        P(),
        P(),
        P(),
        P(),
        P(),
        P(),
        P(),
        P(),
        P(),
        P(),
        P(),
        P("img", "rows", None, None),
        P("img", "rows", None, None),
        P("img", "rows", None, None),
        P("img", "rows", None, None),
        P("img", "rows", None),
        P("img", "rows", None),
        P("img", "rows", None),
        P("img", "rows", None),
        P("img", "rows", None),
    )
    out_specs = (
        P("img", ("rows", "scale"), None, None),
        P("img", ("rows", "scale"), None, None),
        P(),
        P(),
        P(("img", "rows", "scale")),
        P(),
        P(),
        P(),
        P(("img", "rows", "scale")),
        P(),
        P(),
        P(),
        P(("img", "rows", "scale")),
        P(),
        P(("img", "rows", "scale")),
        P(),
        P(("img", "rows", "scale")),
        P(),
        P(),
        P(),
        P(("img", "rows", "scale")),
        P(),
        P(("img", "rows", "scale")),
        P(),
        P(("img", "rows", "scale")),
        P(("img", "rows", "scale")),
        P(("img", "rows", "scale")),
        P(("img", "rows", "scale")),
        P(),
        P(),
        P(("img", "rows", "scale")),
        P(),
    )
    return jax.shard_map(
        on_device, mesh=mesh, in_specs=in_specs, out_specs=out_specs, check_vma=False
    )
```

```python
from functools import partial

import jax
import jax.numpy as jnp
from jax import lax
from jax.experimental import pallas as pl
from jax.experimental.pallas import tpu as pltpu
from jax.sharding import PartitionSpec as P

norm_eps = 1e-06
wide_type = jnp.float32
narrow_type = jnp.bfloat16

MESH_ID = pl.DeviceIdType.MESH
lanes = 128


def axis_bits(size):
    bits = []
    step = 1
    while step < size:
        bits.append(step)
        step *= 2
    return bits


def bit_partner(axis, step):
    here = lax.axis_index(axis)
    bit = lax.rem(lax.div(here, step), 2)
    return {axis: here + step - 2 * step * bit}, bit


def halving_dims():
    dims = []
    for axis in ("img", "rows", "scale"):
        for step in reversed(axis_bits(lax.axis_size(axis))):
            dims.append((axis, step))
    return dims


class ReducePlan:
    def __init__(self, shapes, pieces, near=()):
        self.dims = halving_dims()
        self.stages = len(self.dims)
        core = self.dims.index(("img", 1))
        plane = [i for i, d in enumerate(self.dims) if d[0] == "img" and i != core]
        across = [i for i, d in enumerate(self.dims) if d[0] == "rows"]
        along = [i for i, d in enumerate(self.dims) if d[0] == "scale"][::-1]
        orders = {
            "x": [core] + across + plane + along,
            "y": [core] + plane + across + along,
            "z": [core] + along[:1] + plane + across + along[1:],
        }
        self.shapes = shapes
        self.near = near
        self.groups = [[core], across + plane, along]
        self.pieces, self.spans, self.entries, self.events = [], [], [], []
        for source, begin, size, first, entry, start, waves in pieces:
            self.pieces.append((source, begin, size, shapes[source][-1], orders[first]))
            self.spans.append((start, start + len(waves)))
            self.entries.append(entry)
            self.events.append(waves)
        self.staging = sorted(
            {
                piece[2:4]
                for piece, span in zip(self.pieces, self.spans)
                if piece[0] not in near and span[0] == 0
            }
        )

    def lead(self, t):
        return (2,) * (self.stages - max(self.spans[t][0], 1))

    def left(self, t):
        _, _, rows, columns, _ = self.pieces[t]
        return (2,) * (self.stages - self.spans[t][1]) + (rows, columns)

    def scratch(self):
        out = []
        for t, (_, _, rows, columns, _) in enumerate(self.pieces):
            out.append(pltpu.VMEM(self.lead(t) + (rows, columns), narrow_type))
        for t, (_, _, rows, columns, _) in enumerate(self.pieces):
            start, stop = self.spans[t]
            for stage in range(max(start, 1), stop):
                lead = (2,) * (self.stages - 1 - stage)
                out.append(pltpu.VMEM(lead + (rows, columns), narrow_type))
        for shape in self.staging:
            out.append(pltpu.VMEM((2,) * (self.stages - 1) + shape, narrow_type))
        count = len(self.pieces)
        out += [pltpu.SemaphoreType.DMA((count, self.stages))] * 2
        out += [pltpu.SemaphoreType.DMA((count,))]
        return out

    def calls(self):
        out = {}
        for stage in reversed(range(self.stages)):
            for t, (start, stop) in enumerate(self.spans):
                if start <= stage < stop:
                    out.setdefault(self.events[t][stage - start], []).append((t, stage))
        return out

    def waves(self):
        return max(self.calls()) + 1

    def shaped(self, arrays):
        out = []
        for array in arrays:
            if len(array.shape) == 3 and array.shape[0] == 2**self.stages:
                array = array.reshape((2,) * self.stages + array.shape[1:])
            out.append(array)
        return out

    def sums(self):
        return [jax.ShapeDtypeStruct(shape[1:], wide_type) for shape in self.shapes]


class Reducer:
    def __init__(self, plan, sources, outs, scratch):
        self.plan, self.sources, self.outs = plan, sources, outs
        count = len(plan.pieces)
        scratch = list(scratch)
        self.held, scratch = scratch[:count], scratch[count:]
        self.landed = []
        for start, stop in plan.spans:
            size = stop - max(start, 1)
            stages = range(max(start, 1), stop)
            self.landed.append(dict(zip(stages, scratch[:size])))
            scratch = scratch[size:]
        self.staging = dict(zip(plan.staging, scratch))
        self.send_sem, self.recv_sem, self.local_sem = scratch[len(plan.staging) :]
        self.partners = [bit_partner(axis, step) for axis, step in plan.dims]
        users = {shape: [] for shape in plan.staging}
        self.following = {}
        for t in sorted(range(count), key=lambda t: plan.events[t][0]):
            piece = plan.pieces[t]
            if piece[0] in plan.near or plan.spans[t][0]:
                continue
            used = users[piece[2:4]]
            if used:
                self.following[used[-1]] = t
            used.append(t)
        self.first_local = [used[0] for used in users.values()]
        self.todo = plan.calls()
        self.riders = {}

    def greet(self, barrier, groups=False):
        devices = [partner for partner, _ in self.partners]
        if groups:
            devices += [
                self.across(group, mask)
                for group in self.plan.groups
                for mask in range(1, 2 ** len(group))
                if mask & (mask - 1)
            ]
        for device in devices:
            pl.semaphore_signal(barrier, inc=1, device_id=device, device_id_type=MESH_ID)
        return len(devices)

    def across(self, group, mask):
        device = {}
        for i, dim in enumerate(group):
            axis, step = self.plan.dims[dim]
            if mask >> i & 1:
                here = device.get(axis, lax.axis_index(axis))
                device[axis] = here + step - 2 * step * self.partners[dim][1]
        return device

    def index(self, taken, current, keep, gone=()):
        out = []
        for dim in range(self.plan.stages):
            bit = self.partners[dim][1]
            if dim in gone:
                continue
            if dim in taken:
                out.append(bit)
            elif dim == current:
                out.append(bit if keep else 1 - bit)
            else:
                out.append(slice(None))
        return tuple(out)

    def gone(self, t):
        return self.plan.pieces[t][4][: max(self.plan.spans[t][0], 1)]

    def copy(self, t, stage):
        source, begin, rows, _, order = self.plan.pieces[t]
        if stage == 0:
            index = self.index((), order[0], False)
            view = self.sources[source].at[index + (pl.ds(begin, rows),)]
            target = self.held[t]
        else:
            index = self.index(order[:stage], order[stage], False, self.gone(t))
            view = self.held[t].at[index]
            target = self.landed[t][stage]
        return pltpu.make_async_remote_copy(
            src_ref=view,
            dst_ref=target,
            send_sem=self.send_sem.at[t, stage],
            recv_sem=self.recv_sem.at[t, stage],
            device_id=self.partners[order[stage]][0],
            device_id_type=MESH_ID,
        )

    def local(self, t):
        source, begin, rows, columns, order = self.plan.pieces[t]
        if self.plan.spans[t][0]:
            view, target = self.sources[source], self.held[t]
        else:
            index = self.index((), order[0], True)
            view = self.sources[source].at[index + (pl.ds(begin, rows),)]
            target = self.staging[(rows, columns)]
        return pltpu.make_async_copy(view, target, self.local_sem.at[t])

    def each(self, lead, action):
        total = 1
        for size in lead:
            total *= size

        def body(step, carry):
            place, left = [], step
            for size in reversed(lead):
                place.append(lax.rem(left, size))
                left = lax.div(left, size)
            action(tuple(reversed(place)))
            return carry

        if lead:
            lax.fori_loop(0, total, body, 0)
        else:
            action(())

    def add(self, target, arrived, begin=0):
        lead, rows = target.shape[:-2], target.shape[-2]
        arrived = arrived.at[(slice(None),) * len(lead) + (pl.ds(begin, rows),)]

        def action(place):
            target[place] = target[place] + arrived[place]

        self.each(lead, action)

    def start(self):
        for t, span in enumerate(self.plan.spans):
            if span[0]:
                self.local(t).start()
            elif self.plan.pieces[t][0] not in self.plan.near:
                self.copy(t, 0).start()
        for t in self.first_local:
            self.local(t).start()
        for t, span in enumerate(self.plan.spans):
            if span[0]:
                self.local(t).wait()

    def start_near(self, source):
        for t in range(len(self.plan.pieces)):
            if self.plan.pieces[t][0] == source:
                self.copy(t, 0).start()

    def event(self, t, stage):
        source, begin, rows, columns, order = self.plan.pieces[t]
        self.copy(t, stage).wait_recv()
        if stage == 0 and source in self.plan.near:
            own = self.sources[source].at[self.index((), order[0], True)]
            self.add(self.held[t], own, begin)
        elif stage == 0:
            self.local(t).wait()
            self.add(self.held[t], self.staging[(rows, columns)])
            if t in self.following:
                self.local(self.following[t]).start()
        else:
            index = self.index(order[:stage], order[stage], True, self.gone(t))
            self.add(self.held[t].at[index], self.landed[t][stage])
        if t in self.riders:
            self.riders[t].step()
        if stage + 1 < self.plan.spans[t][1]:
            self.copy(t, stage + 1).start()
        elif stage + 1 < self.plan.stages:
            kept = self.held[t].at[self.index(order[: stage + 1], -1, True, self.gone(t))]
            out = self.outs[source][t]

            def action(place):
                out[place] = kept[place]

            self.each(kept.shape[:-2], action)
        else:
            index = self.index(order, -1, True, self.gone(t))
            self.emit(source, begin, self.held[t][index].astype(wide_type))

    def emit(self, source, begin, value):
        out = self.outs[source]
        if not isinstance(out, list):
            out[begin : begin + value.shape[0], :] = value
            return
        for first, count, tile, tiles, ref in out:
            low, high = max(first, begin), min(first + count, begin + value.shape[0])
            if low < high:
                part = value[low - begin : high - begin]
                if tiles == 0:
                    ref[low - first : high - first, :] = part
                for c in range(min(tiles, part.shape[1] // lanes)):
                    here = part[:, c * lanes : (c + 1) * lanes]
                    at = (low - first) * tiles + tile + c
                    ref[pl.ds(at, high - low, stride=tiles), :] = here

    def wave(self, number):
        for t, span in enumerate(self.plan.spans):
            if span[0] and self.plan.entries[t] == number:
                self.copy(t, span[0]).start()
        for t, stage in self.todo.get(number, ()):
            self.event(t, stage)

    def finish(self):
        for t, (start, stop) in enumerate(self.plan.spans):
            for stage in range(start, stop):
                self.copy(t, stage).wait_send()


class SmallReduce:
    def __init__(self, reducer, groups, total, landed, send_sem, recv_sem):
        self.reducer, self.total, self.landed = reducer, total, landed
        self.send_sem, self.recv_sem = send_sem, recv_sem
        self.groups = groups
        self.stage = 0

    @staticmethod
    def sizes(groups):
        sizes = [2 ** len(group) for group in groups]
        return sizes, [sum(sizes[:i]) for i in range(len(sizes) + 1)]

    def copies(self):
        group = self.groups[self.stage]
        sizes, at = self.sizes(self.groups)
        place = sum(self.reducer.partners[dim][1] * 2**i for i, dim in enumerate(group))
        return place, [
            pltpu.make_async_remote_copy(
                src_ref=self.total,
                dst_ref=self.landed.at[at[self.stage] + place],
                send_sem=self.send_sem.at[at[self.stage] + mask],
                recv_sem=self.recv_sem.at[at[self.stage] + mask],
                device_id=self.reducer.across(group, mask),
                device_id_type=MESH_ID,
            )
            for mask in range(1, sizes[self.stage])
        ]

    def start(self):
        place, copies = self.copies()
        for copy in copies:
            copy.start()
        sizes, at = self.sizes(self.groups)
        self.landed[at[self.stage] + place] = self.total[...]

    def step(self):
        if self.stage == len(self.groups):
            return
        for copy in self.copies()[1]:
            copy.wait()
        sizes, at = self.sizes(self.groups)
        total = self.landed[at[self.stage]]
        for i in range(1, sizes[self.stage]):
            total = total + self.landed[at[self.stage] + i]
        self.total[...] = total
        self.stage += 1
        if self.stage < len(self.groups):
            self.start()


class StripGather:
    def __init__(self, owns, wholes, send_sem, recv_sem):
        self.owns, self.wholes = owns, wholes
        self.send_sem, self.recv_sem = send_sem, recv_sem
        self.deep, self.wide = lax.axis_size("scale"), lax.axis_size("rows")
        self.here, self.line = lax.axis_index("scale"), lax.axis_index("rows")

    @staticmethod
    def slots():
        deep, wide = lax.axis_size("scale"), lax.axis_size("rows")
        return 2 * (deep - 1) + (wide - 1) * (2 * deep - 1)

    def greet(self, barrier):
        waits = self.wide - 1
        for k in range(1, self.wide):
            device = {"rows": lax.rem(self.line + k, self.wide)}
            pl.semaphore_signal(barrier, inc=1, device_id=device, device_id_type=MESH_ID)

        @pl.when(self.here > 0)
        def _():
            device = {"scale": self.here - 1}
            pl.semaphore_signal(barrier, inc=1, device_id=device, device_id_type=MESH_ID)

        @pl.when(self.here < self.deep - 1)
        def _():
            device = {"scale": self.here + 1}
            pl.semaphore_signal(barrier, inc=1, device_id=device, device_id_type=MESH_ID)

        more = jnp.where(self.here > 0, 1, 0) + jnp.where(self.here < self.deep - 1, 1, 0)
        return waits + more

    def copies(self, block, slot, device):
        out = []
        for i, whole in enumerate(self.wholes):
            view = whole.at[self.line * self.deep + block]
            out.append(
                pltpu.make_async_remote_copy(
                    src_ref=view,
                    dst_ref=view,
                    send_sem=self.send_sem.at[slot, i],
                    recv_sem=self.recv_sem.at[slot, i],
                    device_id=device,
                    device_id_type=MESH_ID,
                )
            )
        return out

    def along(self, step, right):
        if right:
            block, device = self.here - step, {"scale": jnp.minimum(self.here + 1, self.deep - 1)}
            sent = (block >= 0) & (self.here < self.deep - 1)
            got = self.here - 1 - step >= 0
            return block, step, device, sent, got
        block, device = self.here + step, {"scale": jnp.maximum(self.here - 1, 0)}
        sent = (block < self.deep) & (self.here > 0)
        got = self.here + 1 + step < self.deep
        return block, self.deep - 1 + step, device, sent, got

    def across(self, block, kind, action):
        base = 2 * (self.deep - 1)
        for k in range(1, self.wide):
            slot = base + (k - 1) * (2 * self.deep - 1) + kind
            device = {"rows": lax.rem(self.line + k, self.wide)}
            for copy in self.copies(block, slot, device):
                action(copy)

    def start(self):
        for own, whole in zip(self.owns, self.wholes):
            whole[self.line * self.deep + self.here] = own[...]
        for right in (True, False):
            block, slot, device, sent, _ = self.along(0, right)

            @pl.when(sent)
            def _():
                for copy in self.copies(block, slot, device):
                    copy.start()

        self.across(self.here, 0, lambda copy: copy.start())

    def step(self, number):
        for right in (True, False):
            _, slot, device, _, got = self.along(number, right)
            block = self.here - 1 - number if right else self.here + 1 + number

            @pl.when(got)
            def _():
                for copy in self.copies(block, slot, device):
                    copy.wait_recv()
                kind = 1 + 2 * number + (0 if right else 1)
                self.across(block, kind, lambda copy: copy.start())

            if number + 1 < self.deep - 1:
                later, slot, device, sent, _ = self.along(number + 1, right)

                @pl.when(sent)
                def _():
                    for copy in self.copies(later, slot, device):
                        copy.start()

    def finish(self):
        self.across(self.here, 0, lambda copy: copy.wait())
        for number in range(self.deep - 1):
            for right in (True, False):
                _, _, _, _, got = self.along(number, right)
                block = self.here - 1 - number if right else self.here + 1 + number
                kind = 1 + 2 * number + (0 if right else 1)

                @pl.when(got)
                def _():
                    self.across(block, kind, lambda copy: copy.wait())

                sent_block, slot, device, sent, _ = self.along(number, right)

                @pl.when(sent)
                def _():
                    for copy in self.copies(sent_block, slot, device):
                        copy.wait_send()


def fold_chunks(grads, width):
    devices = lax.axis_size(("img", "rows", "scale"))
    cut, plan = [], []
    for grad in grads:
        rows, columns = grad.shape
        own = rows // devices
        chunk = grad.astype(narrow_type).reshape(devices, own, columns)
        folds = max(columns // width, 1)
        if columns < width:
            chunk = jnp.pad(chunk, ((0, 0), (0, 0), (0, width - columns)))
        cut += [chunk[:, :, f * width : (f + 1) * width] for f in range(folds)]
        plan.append((own, columns, folds))
    stacked = jnp.concatenate(cut, axis=1) if len(cut) > 1 else cut[0]
    extra = -stacked.shape[1] % 16
    if extra:
        stacked = jnp.pad(stacked, ((0, 0), (0, extra), (0, 0)))
    return stacked, plan


def unfold_chunks(summed, plan):
    at, out = 0, []
    for own, columns, folds in plan:
        parts = []
        for _ in range(folds):
            parts.append(summed[at : at + own, : min(columns, summed.shape[1])])
            at += own
        whole = jnp.concatenate(parts, axis=1) if folds > 1 else parts[0]
        out.append(whole.reshape(-1))
    return out


def last_reduce_kernel(plan, count, refs):
    sources, small_in = refs[:count], refs[count]
    outs, small_out = refs[count + 1 : 2 * count + 1], refs[2 * count + 1]
    scratch = refs[2 * count + 2 :]
    small_held, small_landed, small_send, small_recv = scratch[:4]
    reducer = Reducer(plan, sources, outs, scratch[4:])
    barrier = pltpu.get_barrier_semaphore()
    pl.semaphore_wait(barrier, reducer.greet(barrier))

    def small_copy(stage):
        return pltpu.make_async_remote_copy(
            src_ref=small_held,
            dst_ref=small_landed.at[stage],
            send_sem=small_send.at[stage],
            recv_sem=small_recv.at[stage],
            device_id=reducer.partners[plan.pieces[0][4][stage]][0],
            device_id_type=MESH_ID,
        )

    small_held[...] = small_in[...]
    reducer.start()
    small_copy(0).start()
    for number in range(plan.waves()):
        reducer.wave(number)
        if number < plan.stages:
            small_copy(number).wait()
            small_held[...] = small_held[...] + small_landed[number]
            if number + 1 < plan.stages:
                small_copy(number + 1).start()
    small_out[...] = small_held[...]
    reducer.finish()


def cut_rows(shapes):
    out = []
    stages = len(halving_dims())
    for source, (_, rows, _) in enumerate(shapes):
        first = -(-rows // 32) * 16
        waves = tuple(source + stage + (1 if stage else 0) for stage in range(stages))
        out.append((source, 0, first, "x", source, 0, waves))
        if first < rows:
            out.append((source, first, rows - first, "y", source, 0, waves))
    return out


def last_reduce(arrays, small, call_id):
    shapes = [array.shape for array in arrays]
    plan = ReducePlan(shapes, cut_rows(shapes))
    count = len(arrays)

    def body(*refs):
        last_reduce_kernel(plan, count, refs)

    vmem = pl.BlockSpec(memory_space=pltpu.VMEM)
    got = pl.pallas_call(
        body,
        out_shape=plan.sums() + [jax.ShapeDtypeStruct(small.shape, wide_type)],
        in_specs=[pl.BlockSpec(memory_space=pl.ANY)] * count + [vmem],
        out_specs=[vmem] * (count + 1),
        scratch_shapes=[
            pltpu.VMEM(small.shape, wide_type),
            pltpu.VMEM((plan.stages,) + small.shape, wide_type),
            pltpu.SemaphoreType.DMA((plan.stages,)),
            pltpu.SemaphoreType.DMA((plan.stages,)),
        ]
        + plan.scratch(),
        compiler_params=pltpu.CompilerParams(
            collective_id=call_id, has_side_effects=True, vmem_limit_bytes=60 << 20
        ),
        name="last_reduce",
    )(*plan.shaped(arrays), small)
    return got[:count], got[count]


def pack_small(parts):
    flat = jnp.concatenate([part.reshape(-1) for part in parts])
    unit = 8 * lanes
    total = -(-flat.shape[0] // unit) * unit
    return jnp.pad(flat, (0, total - flat.shape[0])).reshape(-1, lanes)


def unpack_small(packed, parts):
    flat = packed.reshape(-1)
    out, at = [], 0
    for part in parts:
        out.append(flat[at : at + part.size].reshape(part.shape))
        at += part.size
    return out


def gather_kernel(own, whole, send_sem, recv_sem):
    gather = StripGather([own], [whole], send_sem, recv_sem)
    barrier = pltpu.get_barrier_semaphore()
    pl.semaphore_wait(barrier, gather.greet(barrier))
    gather.start()
    for number in range(gather.deep - 1):
        gather.step(number)
    gather.finish()


def gather_strips(own, call_id):
    strips = lax.axis_size(("rows", "scale"))
    slots = StripGather.slots()
    return pl.pallas_call(
        gather_kernel,
        out_shape=jax.ShapeDtypeStruct((strips,) + own.shape, own.dtype),
        in_specs=[pl.BlockSpec(memory_space=pltpu.VMEM)],
        out_specs=pl.BlockSpec(memory_space=pltpu.VMEM),
        scratch_shapes=[
            pltpu.SemaphoreType.DMA((slots, 1)),
            pltpu.SemaphoreType.DMA((slots, 1)),
        ],
        compiler_params=pltpu.CompilerParams(collective_id=call_id, has_side_effects=True),
        name="gather_strips",
    )(own)


def dot_nn(left, right):
    return lax.dot_general(left, right, (((1,), (0,)), ((), ())), preferred_element_type=wide_type)


def dot_nt(left, right):
    return lax.dot_general(left, right, (((1,), (1,)), ((), ())), preferred_element_type=wide_type)


def dot_tn(left, right):
    return lax.dot_general(left, right, (((0,), (0,)), ((), ())), preferred_element_type=wide_type)


def norm_parts(values):
    centre = values - jnp.mean(values, axis=-1, keepdims=True)
    inverse = lax.rsqrt(jnp.mean(centre * centre, axis=-1, keepdims=True) + norm_eps)
    return centre * inverse, inverse


def norm_back(hat, inverse, hat_grad):
    inner = jnp.mean(hat_grad * hat, axis=-1, keepdims=True)
    return inverse * (hat_grad - jnp.mean(hat_grad, axis=-1, keepdims=True) - hat * inner)


def normal_cdf(values):
    return 0.5 + 0.5 * lax.erf(values * (0.5**0.5))


def gelu_slope(values):
    density = jnp.exp(-0.5 * values * values) * (0.5 / jnp.pi) ** 0.5
    return normal_cdf(values) + values * density


def lane_ids(shape):
    return lax.broadcasted_iota(jnp.int32, shape, len(shape) - 1)


def column_sum(values):
    return jnp.sum(values, axis=0, keepdims=True)


def half_mask(half, head_size, value):
    lane = lane_ids((1, 2 * head_size))
    inside = (lane >= half * head_size) & (lane < (half + 1) * head_size)
    return jnp.where(inside, value, 0.0).astype(narrow_type)


def split_lanes(values, used):
    lane = lane_ids(values.shape)
    twice = jnp.where(lane < used, values, pltpu.roll(values, used, 1))
    near = twice.astype(narrow_type).astype(wide_type)
    both = jnp.where(lane < used, near, twice - near)
    return jnp.where(lane < 2 * used, both, 0.0).astype(narrow_type)


def place_cols(tab, width):
    by_col = pltpu.roll(tab, lanes - (width - 1), 1, stride=1, stride_axis=0)
    return split_lanes(by_col, width)


def place_rows(tab, row, height):
    by_row = pltpu.roll(tab, lax.rem(lanes - (height - 1) + row, lanes), 1)
    return split_lanes(by_row, height)


def both_halves(values, head_size, scale):
    masked = [values * half_mask(half, head_size, scale) for half in range(2)]
    return jnp.concatenate(masked, axis=0)


def own_extra(tab, strip_rows, width, height):
    out = []
    for half in range(2):
        for i in range(strip_rows):
            piece = tab[i * width : (i + 1) * width, 2 * half * lanes : 2 * (half + 1) * lanes]
            row = strip_index() * strip_rows + i
            cols = place_cols(piece[:, :lanes], width)
            out.append(jnp.concatenate([cols, place_rows(piece[:, lanes:], row, height)], axis=1))
    return jnp.concatenate(out, axis=0)


def strip_index():
    return lax.axis_index("rows") * lax.axis_size("scale") + lax.axis_index("scale")


def block_forward_kernel(
    height,
    width,
    x_all,
    vec,
    qkv_weight,
    tables,
    hot,
    proj_hbm,
    fc1_hbm,
    fc2_hbm,
    q_all,
    k_all,
    v_all,
    attended,
    attended_wide,
    log_norm,
    middle,
    normed_mid,
    hidden_pre,
    hidden,
    result,
    proj,
    fc1,
    fc2,
    sems,
):
    model = x_all.shape[2]
    tokens = middle.shape[0]
    strip_rows = tokens // width
    head_size = lanes // 2
    copies = [
        pltpu.make_async_copy(source, target, sems.at[i])
        for i, (source, target) in enumerate(((proj_hbm, proj), (fc1_hbm, fc1), (fc2_hbm, fc2)))
    ]
    for copy in copies:
        copy.start()
    start = pl.multiple_of(strip_index() * tokens, tokens)

    def mix(step, carry):
        at = pl.ds(pl.multiple_of(step * tokens, tokens), tokens)
        hat, _ = norm_parts(x_all[step].astype(wide_type))
        normed = (hat * vec[0:1, :] + vec[1:2, :]).astype(narrow_type)
        mixed = dot_nn(normed, qkv_weight[...])
        q_all[at, :] = (mixed[:, :model] + vec[2:3, :]).astype(narrow_type)
        k_all[at, :] = mixed[:, model : 2 * model].astype(narrow_type)
        v_all[at, :] = (mixed[:, 2 * model :] + vec[3:4, :]).astype(narrow_type)
        return carry

    lax.fori_loop(0, x_all.shape[0], mix, 0)
    log_norm[...] = jnp.zeros_like(log_norm)
    lane = lane_ids((tokens, lanes))

    def pair_step(pair, carry):
        cols = pl.ds(pl.multiple_of(pair * lanes, lanes), lanes)
        queries = q_all[pl.ds(start, tokens), cols]
        values = v_all[:, cols]
        keys = jnp.concatenate([k_all[:, cols], hot[...]], axis=1)
        extra = own_extra(dot_nn(queries, tables[...]), strip_rows, width, height)
        masked = both_halves(queries, head_size, head_size**-0.5)
        scores = dot_nt(jnp.concatenate([masked, extra], axis=1), keys)
        peak = jnp.max(scores, axis=-1, keepdims=True)
        raised = jnp.exp(scores - peak)
        total = jnp.sum(raised, axis=-1, keepdims=True)
        probs = (raised * (1.0 / total)).astype(narrow_type)
        out = dot_nn(probs, values)
        mixed = (out[:tokens], out[tokens:])
        norm = peak + jnp.log(total)
        kept = jnp.where(lane == 2 * pair, norm[:tokens], log_norm[...])
        log_norm[...] = jnp.where(lane == 2 * pair + 1, norm[tokens:], kept)
        joined = jnp.where(lane < head_size, mixed[0], mixed[1])
        attended_wide[:, cols] = joined
        attended[:, cols] = joined.astype(narrow_type)
        return carry

    lax.fori_loop(0, model // lanes, pair_step, 0)
    copies[0].wait()
    inputs = x_all[strip_index()].astype(wide_type)
    centre = inputs + (dot_nn(attended[...], proj[...]) + vec[4:5, :])
    middle[...] = centre
    hat, _ = norm_parts(centre)
    normed_low = (hat * vec[5:6, :] + vec[6:7, :]).astype(narrow_type)
    normed_mid[...] = normed_low
    copies[1].wait()
    copies[2].wait()
    result_wide = centre + vec[7:8, :]
    for j in range(fc1.shape[1] // model):
        cols = slice(j * model, (j + 1) * model)
        pre = dot_nn(normed_mid[...], fc1[:, cols]) + vec[8 + j : 9 + j, :]
        hidden_pre[:, cols] = pre
        low = (pre * normal_cdf(pre)).astype(narrow_type)
        hidden[:, cols] = low
        result_wide = result_wide + dot_nn(low, fc2[cols, :])
    result[...] = result_wide.astype(narrow_type)


def vmem_specs(count):
    return [pl.BlockSpec(memory_space=pltpu.VMEM)] * count


def any_specs(count):
    return [pl.BlockSpec(memory_space=pl.ANY)] * count


def block_forward(height, width, tokens, x_all, vec, qkv_weight, tables, hot, proj, fc1, fc2):
    model = x_all.shape[2]
    total = x_all.shape[0] * tokens
    ff = fc1.shape[1]

    def shape(rows, cols, kind):
        return jax.ShapeDtypeStruct((rows, cols), kind)

    outs = [
        shape(total, model, narrow_type),
        shape(total, model, narrow_type),
        shape(total, model, narrow_type),
        shape(tokens, model, narrow_type),
        shape(tokens, model, wide_type),
        shape(tokens, lanes, wide_type),
        shape(tokens, model, wide_type),
        shape(tokens, model, narrow_type),
        shape(tokens, ff, wide_type),
        shape(tokens, ff, narrow_type),
        shape(tokens, model, narrow_type),
    ]
    return pl.pallas_call(
        partial(block_forward_kernel, height, width),
        out_shape=outs,
        in_specs=vmem_specs(5) + any_specs(3),
        out_specs=vmem_specs(len(outs)),
        scratch_shapes=[
            pltpu.VMEM(proj.shape, narrow_type),
            pltpu.VMEM(fc1.shape, narrow_type),
            pltpu.VMEM(fc2.shape, narrow_type),
            pltpu.SemaphoreType.DMA((3,)),
        ],
        compiler_params=pltpu.CompilerParams(vmem_limit_bytes=60 << 20),
        name="block_forward",
    )(x_all, vec, qkv_weight, tables, hot, proj, fc1, fc2)


def fold_store(target, number, parts, value):
    devices = target.shape[0]
    own = value.shape[0] // devices
    parts[number] = value.reshape(devices, own, value.shape[1])
    if number % 2:
        both = jnp.concatenate([parts.pop(number - 1), parts.pop(number)], axis=1)
        begin = (number - 1) * own
        target[:, begin : begin + 2 * own, :] = both.astype(narrow_type)


def block_backward_kernel(
    result_grad,
    hidden_pre,
    hidden,
    normed_mid,
    middle,
    attended,
    attended_wide,
    log_norm,
    vec,
    proj_far,
    fc1_far,
    fc2_far,
    middle_grad,
    attended_grad,
    stats,
    stat_rows,
    sums,
    fc1_sum,
    proj_grad,
    fc1_out,
    fc2_out,
    proj,
    fc1,
    fc2,
    fc1_grad,
    fc2_grad,
    sems,
):
    width = middle.shape[1]
    blocks = hidden.shape[1] // width
    fc1_in, fc2_in, fc2_back = [], [], []
    for j in range(blocks):
        part = slice(j * width, (j + 1) * width)
        fc1_in.append(
            pltpu.make_async_copy(fc1_far.at[:, part], fc1.at[:, part], sems.at[0, j])
        )
        fc2_in.append(pltpu.make_async_copy(fc2_far.at[part], fc2.at[part], sems.at[1, j]))
        fc2_back.append(pltpu.make_async_copy(fc2_grad.at[part], fc2_out.at[part], sems.at[2, j]))
        fc2_in[j].start()
        fc1_in[j].start()
    proj_in = pltpu.make_async_copy(proj_far, proj, sems.at[3, 0])
    proj_in.start()
    fc1_back = []
    if len(fc1_out.shape) == 3:
        rows = fc1_out.shape[1] // 2
        for j in range(2):
            part = slice(j * rows, (j + 1) * rows)
            fc1_back.append(
                pltpu.make_async_copy(fc1_grad.at[:, part], fc1_out.at[:, part], sems.at[4, j])
            )
    else:
        fc1_back.append(pltpu.make_async_copy(fc1_grad, fc1_out, sems.at[4, 0]))
    model = middle.shape[1]
    ff = hidden.shape[1]
    grad_low = result_grad[...]
    grad_wide = grad_low.astype(wide_type)
    back = jnp.zeros(middle.shape, wide_type)
    normed_turned = normed_mid[...].T
    parts = {}
    for j in range(ff // model):
        cols = slice(j * model, (j + 1) * model)
        pre = hidden_pre[:, cols]
        fc2_in[j].wait()
        pre_grad = dot_nt(grad_low, fc2[cols, :]) * gelu_slope(pre)
        pre_low = pre_grad.astype(narrow_type)
        fc1_sum[:, cols] = column_sum(pre_low.astype(wide_type))
        fc1_in[j].wait()
        back = back + dot_nt(pre_low, fc1[:, cols])
        part = dot_nn(normed_turned, pre_low)
        if len(fc1_grad.shape) == 2:
            fc1_grad[:, cols] = part.astype(narrow_type)
        else:
            fold_store(fc1_grad, j, parts, part)
        fc2_grad[cols, :] = dot_nn(hidden[:, cols].T, grad_low).astype(narrow_type)
        fc2_back[j].start()
        if len(fc1_back) == 2 and j % 2:
            fc1_back[j // 2].start()
    if len(fc1_back) == 1:
        fc1_back[0].start()
    proj_in.wait()
    hat, inverse = norm_parts(middle[...])
    gain_grad = column_sum(back * hat)
    shift_grad = column_sum(back)
    centre_grad = grad_wide + norm_back(hat, inverse, back * vec[5:6, :])
    middle_grad[...] = centre_grad
    branch_low = centre_grad.astype(narrow_type)
    sums[0:1, :] = column_sum(branch_low.astype(wide_type))
    sums[1:2, :] = gain_grad
    sums[2:3, :] = shift_grad
    sums[3:4, :] = column_sum(grad_wide)
    sums[4:8, :] = jnp.zeros((4, model), wide_type)
    attended_turned = attended[...].T
    if len(proj_grad.shape) == 2:
        proj_grad[...] = dot_nn(attended_turned, branch_low).astype(narrow_type)
    else:
        half = model // 2
        for j in range(2):
            part = dot_nn(attended_turned, branch_low[:, j * half : (j + 1) * half])
            fold_store(proj_grad, j, parts, part)
    out_grad = dot_nt(branch_low, proj[...]).astype(narrow_type)
    attended_grad[...] = out_grad
    product = out_grad.astype(wide_type) * attended_wide[...]
    near = product.astype(narrow_type)
    rest = (product - near.astype(wide_type)).astype(narrow_type)
    head_size = lanes // 2
    channel = lax.broadcasted_iota(jnp.int32, (model, lanes), 0)
    head = lax.broadcasted_iota(jnp.int32, (model, lanes), 1)
    member = (lax.div(channel, head_size) == head - 16).astype(wide_type).astype(narrow_type)
    delta = dot_nn(near, member) + dot_nn(rest, member)
    both = jnp.where(lane_ids(delta.shape) < 16, log_norm[...], delta)
    stats[...] = both
    stat_rows[...] = both.T[:32, :]
    for copy in fc1_back + fc2_back:
        copy.wait()


def share_outs(plan, shares, refs):
    outs = [[] for _ in plan.shapes]
    for ref, share in zip(refs, shares):
        for source, places in share if isinstance(share, list) else [share]:
            for place in places:
                outs[source].append(place + (ref,))
    return outs


def block_backward(result_grad, kept, log_norm, vec, proj, fc1, fc2, devices):
    hidden_pre, hidden, normed_mid, middle, attended, attended_wide = kept
    tokens, model = middle.shape
    ff = fc1.shape[1]

    def shape(rows, cols, kind):
        return jax.ShapeDtypeStruct((rows, cols), kind)

    outs = [
        shape(tokens, model, wide_type),
        shape(tokens, model, narrow_type),
        shape(tokens, lanes, wide_type),
        shape(32, tokens, wide_type),
        shape(8, model, wide_type),
        shape(1, ff, wide_type),
        shape(model, model, narrow_type),
        shape(model, ff, narrow_type),
        shape(ff, model, narrow_type),
    ]
    if devices:
        outs[6] = jax.ShapeDtypeStruct((devices, model // devices * 2, model // 2), narrow_type)
        outs[7] = jax.ShapeDtypeStruct((devices, model // devices * (ff // model), model), narrow_type)
    return pl.pallas_call(
        block_backward_kernel,
        out_shape=outs,
        in_specs=vmem_specs(9) + any_specs(3),
        out_specs=vmem_specs(len(outs) - 2) + any_specs(2),
        scratch_shapes=[
            pltpu.VMEM(proj.shape, narrow_type),
            pltpu.VMEM(fc1.shape, narrow_type),
            pltpu.VMEM(fc2.shape, narrow_type),
            pltpu.VMEM(outs[7].shape, narrow_type),
            pltpu.VMEM(outs[8].shape, narrow_type),
            pltpu.SemaphoreType.DMA((5, ff // model)),
        ],
        compiler_params=pltpu.CompilerParams(vmem_limit_bytes=60 << 20),
        name="block_backward",
    )(
        result_grad,
        hidden_pre,
        hidden,
        normed_mid,
        middle,
        attended,
        attended_wide,
        log_norm,
        vec,
        proj,
        fc1,
        fc2,
    )


def small_groups(plan):
    return [[[dim] for dim in plan.pieces[t][4]] for t in plan.riders]


def attention_backward_kernel(height, width, plan, shares, refs):
    (
        x_own,
        q_all,
        k_all,
        v_all,
        grad_own,
        own_stats,
        stat_own,
        middle_grad,
        vec,
        tables,
        rel_all,
        hot,
        hot_turned,
        qkv_weight,
    ) = refs[:14]
    refs = refs[14:]
    if plan is None:
        input_grad, sums, rel_sum, weight_grad = refs[:4]
        scratch = refs[4:]
    else:
        block_sums, fc1_sum, level_sums, gain_sums = refs[:4]
        count = len(plan.shapes) - 2
        sources = refs[4 : 4 + count]
        input_grad, sums_out, early_out, rel_out = refs[4 + count : 8 + count]
        flat = refs[8 + count : 8 + count + len(shares)]
        scratch = refs[8 + count + len(shares) :]
        near_query, near_rest, sums, early, rel_sum = scratch[:5]
        small_scratch, scratch = scratch[5:14], scratch[14:]
        outs = share_outs(plan, shares, flat)
    joined, wide_tab, cols_extra, rows_extra, grad_all, stat_all, stat_rows, rel_grad = scratch[:8]
    gather = StripGather([grad_own, stat_own], [grad_all, stat_all], scratch[8], scratch[9])
    total, model = q_all.shape
    tokens = x_own.shape[0]
    strip_rows = tokens // width
    head_size = lanes // 2
    scale = head_size**-0.5
    strip = strip_index()
    strips = grad_all.shape[0]
    own = pl.ds(pl.multiple_of(strip * tokens, tokens), tokens)
    pairs = model // lanes
    barrier = pltpu.get_barrier_semaphore()
    greeted = gather.greet(barrier)
    if plan is not None:
        reducer = Reducer(plan, (*sources, near_query, near_rest), outs, scratch[10:])
        greeted = greeted + reducer.greet(barrier)
        late_sums, early_sums, rel_sums = [
            SmallReduce(reducer, groups, total, *small_scratch[3 * i : 3 * i + 3])
            for i, (groups, total) in enumerate(zip(small_groups(plan), (sums, early, rel_sum)))
        ]
        reducer.riders = dict(zip(plan.riders, (late_sums, early_sums, rel_sums)))
    if plan is not None:
        early[0:4, :] = block_sums[0:4, :]
        size = early.shape[1]
        for j in range(fc1_sum.shape[1] // size):
            early[4 + j : 5 + j, :] = fc1_sum[:, j * size : (j + 1) * size]
        mid, channels = size // 2, gain_sums.shape[1]
        early[8:9, :mid], early[8:9, mid:] = level_sums[0:1, :mid], level_sums[1:2, :mid]
        early[9:10, :mid], early[9:10, mid:] = level_sums[2:3, :mid], level_sums[4:5, :mid]
        early[10:11, :] = level_sums[3:4, :]
        early[11:15, :channels] = level_sums[5:9, :channels]
        early[11:15, channels : 2 * channels] = level_sums[9:13, :channels]
        early[11:15, 2 * channels :] = gain_sums[0:4, :]
        early[15:16, :] = jnp.zeros((1, size), wide_type)
    pl.semaphore_wait(barrier, greeted)
    gather.start()
    if plan is not None:
        early_sums.start()
        reducer.start()

    rel_grad[...] = jnp.zeros_like(rel_grad)
    lane = lane_ids((tokens, lanes))

    def own_queries(pair):
        cols = slice(pair * lanes, (pair + 1) * lanes)
        queries = q_all[own, cols]
        keys = k_all[:, cols]
        extra = own_extra(dot_nn(queries, tables[...]), strip_rows, width, height)
        masked = both_halves(queries, head_size, scale)
        keys_hot = jnp.concatenate([keys, hot[...]], axis=1)
        scores = dot_nt(jnp.concatenate([masked, extra], axis=1), keys_hot)
        norms, means = [], []
        for half in range(2):
            head = 2 * pair + half
            stats = own_stats[...]
            norms.append(jnp.sum(jnp.where(lane == head, stats, 0.0), axis=-1, keepdims=True))
            means.append(jnp.sum(jnp.where(lane == 16 + head, stats, 0.0), axis=-1, keepdims=True))
        probs = jnp.exp(scores - jnp.concatenate(norms, axis=0))
        prob_grad = dot_nt(both_halves(grad_own[:, cols], head_size, 1.0), v_all[:, cols])
        score_grad = probs * (prob_grad - jnp.concatenate(means, axis=0))
        keys_turned = jnp.concatenate([keys, hot_turned[...]], axis=1)
        back = dot_nn(score_grad.astype(narrow_type), keys_turned)
        offsets = []
        for half in range(2):
            parts = []
            for i in range(strip_rows):
                at = half * tokens + i * width
                piece = back[at : at + width]
                by_col = pltpu.roll(piece[:, lanes : 2 * lanes], 0, 1, stride=1, stride_axis=0)
                by_row = pltpu.roll(piece[:, 2 * lanes :], strip * strip_rows + i, 1)
                parts.append(jnp.concatenate([by_col, by_row], axis=1))
            offsets.append(jnp.concatenate(parts, axis=0))
        off = jnp.concatenate(offsets, axis=1).astype(narrow_type)
        plain = jnp.where(lane < head_size, back[:tokens, :lanes], back[tokens:, :lanes])
        query_grad = plain * scale + dot_nn(off, rel_all[...])
        joined[:, cols] = query_grad.astype(narrow_type)
        rel_grad[...] += dot_tn(off, queries)

    def own_keys(pair):
        at = pair * lanes
        cols = slice(at, at + lanes)
        all_queries = q_all[:, cols]
        wide_tab[...] = dot_nn(all_queries, tables[...])

        def widen(row, inner):
            rows = pl.ds(pl.multiple_of(row * width, width), width)
            for half in range(2):
                begin = 2 * half * lanes
                cols_extra[half, rows, :] = place_cols(wide_tab[rows, begin : begin + lanes], width)
                piece = wide_tab[rows, begin + lanes : begin + 2 * lanes]
                rows_extra[half, rows, :] = place_rows(piece, row, height)
            return inner

        lax.fori_loop(0, height, widen, 0)
        all_grads = grad_all[:, :, cols].reshape(total, lanes)
        hot_own = hot[own, :]
        blank = jnp.zeros((tokens, lanes), narrow_type)
        hot_col, hot_row = hot_own[:, :lanes], hot_own[:, lanes:]
        keys = both_halves(k_all[own, cols], head_size, scale)
        left = jnp.concatenate(
            [
                jnp.concatenate([hot_col, blank, hot_row, blank], axis=1),
                jnp.concatenate([blank, hot_col, blank, hot_row], axis=1),
            ],
            axis=0,
        )
        right = jnp.concatenate(
            [all_queries, cols_extra[0], cols_extra[1], rows_extra[0], rows_extra[1]], axis=1
        )
        scores = dot_nt(jnp.concatenate([keys, left], axis=1), right)
        prob_grad = dot_nt(both_halves(v_all[own, cols], head_size, 1.0), all_grads)
        probs, score_grads = [], []
        for half in range(2):
            head = 2 * pair + half
            here = slice(half * tokens, (half + 1) * tokens)
            prob = jnp.exp(scores[here] - stat_rows[head : head + 1, :])
            probs.append(prob.astype(narrow_type))
            score_grad = prob * (prob_grad[here] - stat_rows[16 + head : 17 + head, :])
            score_grads.append(score_grad.astype(narrow_type))
        key_both = dot_nn(jnp.concatenate(score_grads, axis=0), all_queries)
        value_both = dot_nn(jnp.concatenate(probs, axis=0), all_grads)
        key_grad = jnp.where(lane < head_size, key_both[:tokens], key_both[tokens:]) * scale
        value_grad = jnp.where(lane < head_size, value_both[:tokens], value_both[tokens:])
        joined[:, model + at : model + at + lanes] = key_grad.astype(narrow_type)
        joined[:, 2 * model + at : 2 * model + at + lanes] = value_grad.astype(narrow_type)

    hat, inverse = norm_parts(x_own[...].astype(wide_type))
    normed_turned = (hat * vec[0:1, :] + vec[1:2, :]).astype(narrow_type).T
    steps = gather.deep - 1
    progress = [0]

    def advance():
        if plan is not None:
            reducer.wave(progress[0])
            progress[0] += 1

    def near_grads(near, first):
        fold = near.shape[-1]
        own_count = model // 2**plan.stages
        lead = (slice(None),) * plan.stages
        parts = {}
        for f in range(near.shape[-2] // own_count):
            begin = first + f * fold
            value = dot_nn(normed_turned, joined[:, begin : begin + fold])
            parts[f] = value.reshape((2,) * plan.stages + (own_count, fold))
            if f % 2:
                both = jnp.concatenate([parts.pop(f - 1), parts.pop(f)], axis=plan.stages)
                rows = slice((f - 1) * own_count, (f + 1) * own_count)
                near[lead + (rows,)] = both.astype(narrow_type)

    advance()
    for pair in range(pairs):
        own_queries(pair)
        if pair < steps:
            gather.step(pair)
        advance()
    turned = pltpu.roll(rel_grad[2 * lanes :, :], head_size, 1)
    both = rel_grad[: 2 * lanes, :] + turned
    low = lane_ids((lanes, lanes)) < head_size
    rel_sum[...] = jnp.where(low, both[:lanes], pltpu.roll(both[lanes:], head_size, 1))
    if plan is not None:
        near_grads(near_query, 0)
        rel_sums.start()
        reducer.start_near(len(plan.shapes) - 2)
    gather.finish()
    for block in range(strips):
        stat_rows[:, block * tokens : (block + 1) * tokens] = stat_all[block]
    for pair in range(pairs):
        own_keys(pair)
        advance()
    if plan is not None:
        near_grads(near_rest, model)
        reducer.start_near(len(plan.shapes) - 1)
    back = jnp.zeros((tokens, model), wide_type)
    for j in range(3):
        cols = slice(j * model, (j + 1) * model)
        part = joined[:, cols]
        sums[j : j + 1, :] = column_sum(part.astype(wide_type))
        back = back + dot_nt(part, qkv_weight[:, cols])
        if plan is None:
            weight_grad[:, cols] = dot_nn(normed_turned, part).astype(narrow_type)
    sums[3:4, :] = column_sum(back * hat)
    sums[4:5, :] = column_sum(back)
    sums[5:8, :] = jnp.zeros((3, model), wide_type)
    if plan is not None:
        late_sums.start()
    input_grad[...] = middle_grad[...] + norm_back(hat, inverse, back * vec[0:1, :])
    if plan is None:
        return
    while progress[0] < plan.waves():
        advance()
    for small in (early_sums, rel_sums, late_sums):
        while small.stage < len(small.groups):
            small.step()
    sums_out[...] = sums[...]
    early_out[...] = early[...]
    rel_out[...] = rel_sum[...]
    reducer.finish()


def attention_backward(height, width, operands, small, arrays, plan, shares, call_id):
    tokens, model = operands[0].shape
    total = operands[1].shape[0]
    strips = total // tokens
    slots = StripGather.slots()

    def shape(rows, cols, kind):
        return jax.ShapeDtypeStruct((rows, cols), kind)

    outs = [shape(tokens, model, wide_type)]
    scratch = []
    extra = []
    if plan is None:
        outs += [
            shape(8, model, wide_type),
            shape(lanes, lanes, wide_type),
            shape(model, 3 * model, narrow_type),
        ]
    else:
        smalls = [(8, model), (16, model), (lanes, lanes)]
        outs += [shape(*dims, wide_type) for dims in smalls]
        outs += [flat for flat, _ in shares]
        shares = [share for _, share in shares]
        stages = plan.stages
        scratch += [
            pltpu.VMEM((2,) * stages + dims[1:], narrow_type) for dims in plan.shapes[-2:]
        ]
        scratch += [pltpu.VMEM(dims, wide_type) for dims in smalls]
        for dims, groups in zip(smalls, small_groups(plan)):
            slots_small = SmallReduce.sizes(groups)[1][-1]
            scratch += [
                pltpu.VMEM((slots_small,) + dims, wide_type),
                pltpu.SemaphoreType.DMA((slots_small,)),
                pltpu.SemaphoreType.DMA((slots_small,)),
            ]
        extra = plan.scratch()
    scratch += [
        pltpu.VMEM((tokens, 3 * model), narrow_type),
        pltpu.VMEM((total, 4 * lanes), wide_type),
        pltpu.VMEM((2, total, lanes), narrow_type),
        pltpu.VMEM((2, total, lanes), narrow_type),
        pltpu.VMEM((strips, tokens, model), narrow_type),
        pltpu.VMEM((strips, 32, tokens), wide_type),
        pltpu.VMEM((32, total), wide_type),
        pltpu.VMEM((4 * lanes, lanes), wide_type),
        pltpu.SemaphoreType.DMA((slots, 2)),
        pltpu.SemaphoreType.DMA((slots, 2)),
    ]

    def body(*refs):
        attention_backward_kernel(height, width, plan, shares, refs)

    given = operands + (small if plan is not None else ())
    far = plan.shaped(arrays) if plan is not None else []
    return pl.pallas_call(
        body,
        out_shape=outs,
        in_specs=vmem_specs(len(given)) + any_specs(len(far)),
        out_specs=vmem_specs(len(outs)),
        scratch_shapes=scratch + extra,
        compiler_params=pltpu.CompilerParams(
            collective_id=call_id, has_side_effects=True, vmem_limit_bytes=62 << 20
        ),
        name="attention_backward",
    )(*given, *far)


def finish_kernel(widths, refs):
    count = len(widths) - 1
    input_grad, late, early, rel_sum = refs[:4]
    flats = refs[4 : 4 + count]
    out = refs[4 + count :]
    sums = jnp.concatenate([late[...], early[...]], axis=0)
    out[0][...] = input_grad[...]
    for source, target in zip(flats, out[1 : 1 + count]):
        target[...] = source[: target.shape[0], : target.shape[1]]
    vectors, tables = out[1 + count : -5], out[-5:]
    for target, (rows, begin, size) in zip(vectors, widths[-1]):
        for j, row in enumerate(rows):
            value = sums[row : row + 1, begin : begin + size]
            if target.shape[0] < size:
                quarter = target.shape[0]
                parts = [value[:, k * quarter : (k + 1) * quarter] for k in range(size // quarter)]
                value = sum(parts[1:], parts[0])
            target[j * size : j * size + value.shape[1]] = value[0]
    half = rel_sum.shape[1] // 2
    rows, cols, lateral_gain, lateral_shift, output_gain = tables
    cols[...] = rel_sum[...].T[:half, : cols.shape[1]]
    rows[...] = rel_sum[: rows.shape[0], half:]
    channels = output_gain.shape[1]
    for k, table in enumerate((lateral_gain, lateral_shift, output_gain)):
        table[...] = sums[19:23, k * channels : (k + 1) * channels]


def finish(input_grad, smalls, flats, shapes, vectors, table_shapes):
    def wide(shape):
        return jax.ShapeDtypeStruct(shape, wide_type)

    outs = [wide(input_grad.shape)] + [wide(shape) for shape in shapes]
    for _, _, _, length in vectors:
        outs.append(wide((length,)))
    outs += [wide(shape) for shape in table_shapes]
    widths = [None] * len(flats) + [[vector[:3] for vector in vectors]]

    def body(*refs):
        finish_kernel(widths, refs)

    given = (input_grad, *smalls, *flats)
    return pl.pallas_call(
        body,
        out_shape=outs,
        in_specs=vmem_specs(len(given)),
        out_specs=vmem_specs(len(outs)),
        name="finish",
    )(*given)


class Levels:
    def __init__(self, strip_rows, width):
        self.rows = (4 * strip_rows, 2 * strip_rows, strip_rows, strip_rows // 2)
        self.cols = (4 * width, 2 * width, width, width // 2)
        self.at, self.edge_at, self.wide_at = [], [], []
        total = edge = wide = 0
        for rows, cols in zip(self.rows, self.cols):
            self.at.append(total)
            self.edge_at.append(edge)
            self.wide_at.append(wide)
            total += rows * cols
            edge += cols
            wide += (rows + 2) * cols
        self.total, self.edge, self.wide = total, edge, wide


def put_strided(target, at, count, stride, value):
    for part in range(target.shape[0]):
        target[part, pl.ds(at, count, stride=stride), :] = value[:, part * lanes : (part + 1) * lanes]


def get_strided(source, at, count, stride):
    parts = [source[part, pl.ds(at, count, stride=stride), :] for part in range(source.shape[0])]
    return jnp.concatenate(parts, axis=1)


def join_parts(source, begin, end):
    return jnp.concatenate([source[part, begin:end, :] for part in range(source.shape[0])], axis=1)


def store_edges(levels, level, source, offset, top, bottom):
    rows, cols = levels.rows[level], levels.cols[level]
    at = levels.edge_at[level]
    top[at : at + cols, :] = source[offset : offset + cols, :]
    last = offset + (rows - 1) * cols
    bottom[at : at + cols, :] = source[last : last + cols, :]


def level_source_kernel(
    levels,
    strip_rows,
    width,
    base,
    y,
    vec,
    first,
    second,
    eight,
    lat_four,
    lat_eight,
    lat_sixteen,
    lat_thirty,
    lateral,
    top,
    bottom,
    first_map,
    active,
    source_zero,
    source_one,
    pooled,
    reduced,
    spread_zero,
    spread_one,
    wide_y,
):
    tokens, model = y.shape
    out = lat_sixteen.shape[0]
    mid = first.shape[1] // 4
    values = y[...]

    def finish(level, value, at):
        reduced[at : at + value.shape[0], :] = value
        hat, _ = norm_parts(value)
        gain = vec[base + 5 + level : base + 6 + level, :out]
        shift = vec[base + 9 + level : base + 10 + level, :out]
        return hat * gain + shift

    for tap in range(4):
        a, b = tap // 2, tap % 2
        cols = slice(tap * mid, (tap + 1) * mid)
        rows = slice(tap * tokens, (tap + 1) * tokens)
        mapped = dot_nn(values, first[:, cols]) + vec[base : base + 1, :mid]
        first_map[:, cols] = mapped
        hat, _ = norm_parts(mapped)
        normed = hat * vec[base + 1 : base + 2, :mid] + vec[base + 2 : base + 3, :mid]
        act = (normed * normal_cdf(normed)).astype(narrow_type)
        active[rows, :] = act
        source = (dot_nt(act, second[...]) + vec[base + 3 : base + 4, :]).astype(narrow_type)
        source_zero[rows, :] = source
        half = source.shape[1] // 2
        for pair in range(2):
            both = dot_nt(source[:, pair * half : (pair + 1) * half], lat_four[...])
            for side in range(2):
                place = (4 * tap + 2 * pair + side) * tokens
                value = finish(0, both[:, side * out : (side + 1) * out], place)
                for i in range(strip_rows):
                    at = (4 * i + 2 * a + pair) * levels.cols[0] + 2 * b + side
                    put_strided(spread_zero, at, width, 4, value[i * width : (i + 1) * width])
        mapped = dot_nn(values, eight[:, cols]) + vec[base + 4 : base + 5, :mid]
        source = mapped.astype(narrow_type)
        source_one[rows, :] = source
        value = finish(1, dot_nt(source, lat_eight[...]), levels.at[1] + tap * tokens)
        for i in range(strip_rows):
            at = (2 * i + a) * levels.cols[1] + b
            put_strided(spread_one, at, width, 2, value[i * width : (i + 1) * width])
    for target, begin, end in ((spread_zero, 0, levels.at[1]), (spread_one, *levels.at[1:3])):
        joined = join_parts(target, 0, end - begin)
        lateral[begin:end, :] = joined.astype(narrow_type)
    value = finish(2, dot_nt(values, lat_sixteen[...]), levels.at[2])
    lateral[levels.at[2] : levels.at[3], :] = value.astype(narrow_type)
    for part in range(model // lanes):
        wide_y[part] = values[:, part * lanes : (part + 1) * lanes].astype(wide_type)
    quarter = width // 2
    for i in range(strip_rows // 2):
        summed = 0.0
        for a in range(2):
            for b in range(2):
                at = (2 * i + a) * width + b
                summed = summed + get_strided(wide_y, at, quarter, 2)
        pooled[i * quarter : (i + 1) * quarter, :] = (summed * 0.25).astype(narrow_type)
    value = finish(3, dot_nt(pooled[...], lat_thirty[...]), levels.at[3])
    lateral[levels.at[3] : levels.total, :] = value.astype(narrow_type)
    for level in range(4):
        store_edges(levels, level, lateral, levels.at[level], top, bottom)


def level_sources(levels, strip_rows, width, base, y, vec, first, second, eight, laterals):
    tokens, model = y.shape
    out = laterals[2].shape[0]

    def shape(rows, cols, kind):
        return jax.ShapeDtypeStruct((rows, cols), kind)

    mid = first.shape[1] // 4
    outs = [
        shape(levels.total, out, narrow_type),
        shape(levels.edge, out, narrow_type),
        shape(levels.edge, out, narrow_type),
        shape(tokens, 4 * mid, wide_type),
        shape(4 * tokens, mid, narrow_type),
        shape(4 * tokens, second.shape[0], narrow_type),
        shape(4 * tokens, mid, narrow_type),
        shape(tokens // 4, model, narrow_type),
        shape(levels.total, out, wide_type),
    ]
    return pl.pallas_call(
        partial(level_source_kernel, levels, strip_rows, width, base),
        out_shape=outs,
        in_specs=vmem_specs(9),
        out_specs=vmem_specs(len(outs)),
        scratch_shapes=[
            pltpu.VMEM((out // lanes, levels.at[1], lanes), wide_type),
            pltpu.VMEM((out // lanes, levels.at[2] - levels.at[1], lanes), wide_type),
            pltpu.VMEM((model // lanes, tokens, lanes), wide_type),
        ],
        compiler_params=pltpu.CompilerParams(vmem_limit_bytes=60 << 20),
        name="level_sources",
    )(y, vec, first, second, eight, *laterals)


class EdgeExchange:
    def __init__(self, top, bottom, above, below, send_sem, recv_sem):
        strip, scale = strip_index(), lax.axis_size("scale")
        count = lax.axis_size("rows") * scale

        def place(index):
            return {"rows": lax.div(index, scale), "scale": lax.rem(index, scale)}

        self.has_up, self.has_down = strip > 0, strip < count - 1
        self.up = place(jnp.maximum(strip - 1, 0))
        self.down = place(jnp.minimum(strip + 1, count - 1))
        self.above, self.below = above, below

        def send(source, target, i, device):
            return pltpu.make_async_remote_copy(
                src_ref=source,
                dst_ref=target,
                send_sem=send_sem.at[i],
                recv_sem=recv_sem.at[i],
                device_id=device,
                device_id_type=MESH_ID,
            )

        self.lower = send(bottom, above, 0, self.down)
        self.upper = send(top, below, 1, self.up)

    def start(self, reducer=None):
        barrier = pltpu.get_barrier_semaphore()
        others = 0 if reducer is None else reducer.greet(barrier)

        @pl.when(self.has_up)
        def _():
            pl.semaphore_signal(barrier, inc=1, device_id=self.up, device_id_type=MESH_ID)

        @pl.when(self.has_down)
        def _():
            pl.semaphore_signal(barrier, inc=1, device_id=self.down, device_id_type=MESH_ID)

        @pl.when(jnp.logical_not(self.has_up))
        def _():
            self.above[...] = jnp.zeros_like(self.above)

        @pl.when(jnp.logical_not(self.has_down))
        def _():
            self.below[...] = jnp.zeros_like(self.below)

        peers = jnp.where(self.has_up, 1, 0) + jnp.where(self.has_down, 1, 0)
        pl.semaphore_wait(barrier, peers + others)

        @pl.when(self.has_down)
        def _():
            self.lower.start()

        @pl.when(self.has_up)
        def _():
            self.upper.start()

    def arrive(self):
        @pl.when(self.has_down)
        def _():
            self.lower.wait_send()
            self.upper.wait_recv()

        @pl.when(self.has_up)
        def _():
            self.upper.wait_send()
            self.lower.wait_recv()


def tile_start(index):
    return index if isinstance(index, int) else pl.multiple_of(index, 32)


def widen_rows(levels, level, source, at, first, count, padded, slab, offset):
    cols = levels.cols[level]
    channels = source.shape[1]
    size = count * cols
    padded[8 : 8 + size, :] = source[at : at + size, :].astype(wide_type)
    block = min(256, size)

    def step(i, carry):
        begin = tile_start(i * block)
        got = padded[pl.ds(begin, block + 16), :]
        col = lax.rem(begin + lax.broadcasted_iota(jnp.int32, (block, channels), 0), cols)
        left = jnp.where(col > 0, got[7 : 7 + block], 0.0)
        right = jnp.where(col < cols - 1, got[9 : 9 + block], 0.0)
        joined = jnp.concatenate([left, got[8 : 8 + block], right], axis=1)
        slab[pl.ds(tile_start(offset + first * cols + begin), block), :] = joined.astype(narrow_type)
        return carry

    if size == block:
        step(0, 0)
    else:
        lax.fori_loop(0, size // block, step, 0)


def widen_own(levels, level, source, padded, slab, offset):
    rows = levels.rows[level]
    widen_rows(levels, level, source, levels.at[level], 1, rows, padded, slab, offset)


def widen_edges(levels, level, above, below, padded, slab, offset):
    at, rows = levels.edge_at[level], levels.rows[level]
    widen_rows(levels, level, above, at, 0, 1, padded, slab, offset)
    widen_rows(levels, level, below, at, rows + 1, 1, padded, slab, offset)


def inner_first(size, block, cols, step, arrive):
    count = size // block
    if count > 2 and block >= cols:
        lax.fori_loop(1, count - 1, step, 0)
        arrive()
        step(0, 0)
        step(count - 1, 0)
    else:
        arrive()
        lax.fori_loop(0, count, step, 0)


def smooth_kernel(
    levels,
    base,
    lateral,
    edge_top,
    edge_bottom,
    weight,
    smooth,
    vec,
    grads,
    top,
    bottom,
    slabs,
    gain_sums,
    padded,
    above,
    below,
    send_sem,
    recv_sem,
):
    channels = lateral.shape[1]
    edges = EdgeExchange(edge_top, edge_bottom, above, below, send_sem, recv_sem)
    edges.start()
    gain_sums[...] = jnp.zeros_like(gain_sums)
    for level in range(4):
        rows, cols = levels.rows[level], levels.cols[level]
        offset = levels.wide_at[level]
        widen_own(levels, level, lateral, padded, slabs, offset)

        def arrive():
            if level == 0:
                edges.arrive()
            widen_edges(levels, level, above, below, padded, slabs, offset)

        size = rows * cols
        block = min(256, size)
        gain = vec[base + 13 + level : base + 14 + level, :channels]

        def step(i, carry):
            begin = tile_start(i * block)
            total = None
            for a in range(3):
                window = slabs[pl.ds(tile_start(offset + a * cols + begin), block), :]
                part = dot_nn(
                    window, smooth[level, 3 * a * channels : 3 * (a + 1) * channels, :]
                )
                total = part if total is None else total + part
            hat, inverse = norm_parts(total)
            here = pl.ds(tile_start(levels.at[level] + begin), block)
            upstream = weight[here, :].astype(wide_type)
            gain_sums[level : level + 1, :] += column_sum(upstream * hat)
            grads[here, :] = norm_back(hat, inverse, upstream * gain).astype(narrow_type)
            return carry

        inner_first(size, block, cols, step, arrive)
        store_edges(levels, level, grads, levels.at[level], top, bottom)


def edge_scratch(edge):
    return [
        pltpu.VMEM(edge.shape, narrow_type),
        pltpu.VMEM(edge.shape, narrow_type),
        pltpu.SemaphoreType.DMA((2,)),
        pltpu.SemaphoreType.DMA((2,)),
    ]


def smooth_levels(levels, base, lateral, edges, weight, smooth, vec, call_id):
    channels = lateral.shape[1]
    biggest = levels.rows[0] * levels.cols[0]
    outs = [
        jax.ShapeDtypeStruct(lateral.shape, narrow_type),
        jax.ShapeDtypeStruct(edges[0].shape, narrow_type),
        jax.ShapeDtypeStruct(edges[0].shape, narrow_type),
        jax.ShapeDtypeStruct((levels.wide, 3 * channels), narrow_type),
        jax.ShapeDtypeStruct((8, channels), wide_type),
    ]
    return pl.pallas_call(
        partial(smooth_kernel, levels, base),
        out_shape=outs,
        in_specs=vmem_specs(6),
        out_specs=vmem_specs(len(outs)),
        scratch_shapes=[pltpu.VMEM((biggest + 16, channels), wide_type)] + edge_scratch(edges[0]),
        compiler_params=pltpu.CompilerParams(
            collective_id=call_id, has_side_effects=True, vmem_limit_bytes=60 << 20
        ),
        name="smooth_levels",
    )(lateral, *edges, weight, smooth, vec)


def level_back_kernel(levels, strip_rows, width, base, plan, refs):
    (
        grads,
        edge_top,
        edge_bottom,
        slabs,
        reduced,
        first_map,
        active,
        source_zero,
        source_one,
        pooled,
        y,
        vec,
        smooth,
        first,
        second,
        eight,
        lat_four,
        lat_eight,
        lat_sixteen,
        lat_thirty,
    ) = refs[:20]
    y_grad, sums, smooth_grad, first_grad, eight_grad = refs[20:25]
    if plan is not None:
        rest_grad, scratch = refs[25], refs[26:]
        count = len(plan.pieces)
        left, scratch = scratch[:count], scratch[count:]
    else:
        rest_grad, scratch = None, refs[30:]
        second_grad, lat_four_grad, lat_eight_grad, lat_sixteen_grad, lat_thirty_grad = refs[25:30]
    padded, slab, spread, second_sum, four_sum, eight_sum, total_grad, pool_grad = scratch[:8]
    above, below, send_sem, recv_sem = scratch[8:12]
    tokens, model = y.shape
    channels = grads.shape[1]
    mid = first.shape[1] // 4
    edges = EdgeExchange(edge_top, edge_bottom, above, below, send_sem, recv_sem)
    if plan is not None:
        outs = [dict(enumerate(left))]
        devices = 2**plan.stages
        own = smooth_grad.shape[-2]
        reducer = Reducer(plan, [smooth_grad], outs, scratch[12:])
        edges.start(reducer)
    else:
        edges.start()
    sums[...] = jnp.zeros_like(sums)

    def smooth_weights(level):
        rows, cols = levels.rows[level], levels.cols[level]
        size = rows * cols
        turned = grads[levels.at[level] : levels.at[level] + size, :].T
        for a in range(3):
            begin = levels.wide_at[level] + a * cols
            for b in range(3):
                part = dot_nn(turned, slabs[begin : begin + size, b * channels : (b + 1) * channels])
                part = part.T.astype(narrow_type)
                at = (level * 9 + 3 * a + b) * channels
                if plan is None:
                    smooth_grad[at : at + channels, :] = part
                    continue
                done = 0
                while done < channels:
                    device, row = divmod(at + done, own)
                    count = min(channels - done, own - row)
                    lead = tuple((device >> (plan.stages - 1 - d)) & 1 for d in range(plan.stages))
                    smooth_grad[lead + (slice(row, row + count),)] = part[done : done + count]
                    done += count

    def smooth_back(level):
        rows, cols = levels.rows[level], levels.cols[level]
        size = rows * cols
        widen_own(levels, level, grads, padded, slab, 0)
        block = min(256, size)

        def arrive():
            if level == 0:
                if plan is not None:
                    reducer.wave(0)
                edges.arrive()
            widen_edges(levels, level, above, below, padded, slab, 0)

        def step(i, carry):
            begin = tile_start(i * block)
            total = None
            for a in range(3):
                for b in range(3):
                    window = slab[
                        pl.ds(tile_start((2 - a) * cols + begin), block),
                        (2 - b) * channels : (3 - b) * channels,
                    ]
                    tap = (3 * a + b) * channels
                    part = dot_nt(window, smooth[level, tap : tap + channels, :])
                    total = part if total is None else total + part
            for part in range(channels // lanes):
                here = total[:, part * lanes : (part + 1) * lanes]
                spread[part, pl.ds(begin, block), :] = here
            return carry

        inner_first(size, block, cols, step, arrive)

    def reduced_back(level, upstream, at):
        hat, inverse = norm_parts(reduced[at : at + upstream.shape[0], :])
        gain = vec[base + 5 + level : base + 6 + level, :channels]
        sums[5 + level : 6 + level, :channels] += column_sum(upstream * hat)
        sums[9 + level : 10 + level, :channels] += column_sum(upstream)
        return norm_back(hat, inverse, upstream * gain).astype(narrow_type)

    def keep_tap(target, tap, parts, value):
        if len(target.shape) == 2:
            target[:, tap * mid : (tap + 1) * mid] = value.astype(narrow_type)
        else:
            fold_store(target, tap, parts, value)

    first_parts, eight_parts = {}, {}
    turned_y = y[...].T
    total_grad[...] = jnp.zeros_like(total_grad)
    for level in range(4):
        smooth_weights(level)
    if plan is not None:
        reducer.start_near(0)
    smooth_back(0)
    for tap in range(4):
        a, b = tap // 2, tap % 2
        cols = slice(tap * mid, (tap + 1) * mid)
        rows = slice(tap * tokens, (tap + 1) * tokens)
        parts = []
        for pair in range(2):
            sides = []
            for side in range(2):
                pieces = []
                for i in range(strip_rows):
                    at = (4 * i + 2 * a + pair) * levels.cols[0] + 2 * b + side
                    pieces.append(get_strided(spread, at, width, 4))
                upstream = jnp.concatenate(pieces, axis=0)
                sides.append(reduced_back(0, upstream, (4 * tap + 2 * pair + side) * tokens))
            both = jnp.concatenate(sides, axis=1)
            half = source_zero.shape[1] // 2
            product = dot_tn(both, source_zero[rows, pair * half : (pair + 1) * half])
            if tap == 0 and pair == 0:
                four_sum[...] = product
            else:
                four_sum[...] += product
            parts.append(dot_nn(both, lat_four[...]).astype(narrow_type))
        second_low = jnp.concatenate(parts, axis=1)
        sums[3:4, :] += column_sum(second_low.astype(wide_type))
        product = dot_tn(second_low, active[rows, :])
        if tap == 0:
            second_sum[...] = product
        else:
            second_sum[...] += product
        active_grad = dot_nn(second_low, second[...])
        hat, inverse = norm_parts(first_map[:, cols])
        gain = vec[base + 1 : base + 2, :mid]
        normed = hat * gain + vec[base + 2 : base + 3, :mid]
        normed_grad = active_grad * gelu_slope(normed)
        sums[1:2, :mid] += column_sum(normed_grad * hat)
        sums[2:3, :mid] += column_sum(normed_grad)
        first_low = norm_back(hat, inverse, normed_grad * gain).astype(narrow_type)
        sums[0:1, :mid] += column_sum(first_low.astype(wide_type))
        keep_tap(first_grad, tap, first_parts, dot_nn(turned_y, first_low))
        total_grad[...] += dot_nt(first_low, first[:, cols])
    quarter = lat_four.shape[1] // 2
    if rest_grad is None:
        second_grad[...] = second_sum[...].astype(narrow_type)
        lat_four_grad[...] = (
            four_sum[:channels, :quarter] + four_sum[channels:, quarter:]
        ).astype(narrow_type)
    smooth_back(1)
    for tap in range(4):
        a, b = tap // 2, tap % 2
        cols = slice(tap * mid, (tap + 1) * mid)
        rows = slice(tap * tokens, (tap + 1) * tokens)
        pieces = []
        for i in range(strip_rows):
            at = (2 * i + a) * levels.cols[1] + b
            pieces.append(get_strided(spread, at, width, 2))
        upstream = jnp.concatenate(pieces, axis=0)
        low = reduced_back(1, upstream, levels.at[1] + tap * tokens)
        product = dot_tn(low, source_one[rows, :])
        if tap == 0:
            eight_sum[...] = product
        else:
            eight_sum[...] += product
        eight_low = dot_nn(low, lat_eight[...]).astype(narrow_type)
        sums[4:5, :mid] += column_sum(eight_low.astype(wide_type))
        keep_tap(eight_grad, tap, eight_parts, dot_nn(turned_y, eight_low))
        total_grad[...] += dot_nt(eight_low, eight[:, cols])
    if rest_grad is None:
        lat_eight_grad[...] = eight_sum[...].astype(narrow_type)
    smooth_back(2)
    low = reduced_back(2, join_parts(spread, 0, tokens), levels.at[2])
    sixteen = dot_tn(low, y[...])
    if rest_grad is None:
        lat_sixteen_grad[...] = sixteen.astype(narrow_type)
    total_grad[...] += dot_nn(low, lat_sixteen[...])
    smooth_back(3)
    low = reduced_back(3, join_parts(spread, 0, tokens // 4), levels.at[3])
    thirty = dot_tn(low, pooled[...])
    if rest_grad is None:
        lat_thirty_grad[...] = thirty.astype(narrow_type)
    else:
        count = rest_grad.shape[0]
        turned = pltpu.roll(four_sum[channels:, :], quarter, 1)
        both = four_sum[:channels, :] + turned
        four = jnp.where(lane_ids(both.shape) < quarter, both, 0.0)
        for part in range(mid // lanes):
            here = slice(part * lanes, (part + 1) * lanes)
            pieces = [second_sum[:, here]]
            for value in (sixteen, thirty):
                for half in range(2):
                    at = half * mid + part * lanes
                    pieces.append(value[:, at : at + lanes])
            pieces += [eight_sum[:, here], four[:, here]]
            pieces = [piece.reshape(count, piece.shape[0] // count, lanes) for piece in pieces]
            used = sum(piece.shape[1] for piece in pieces)
            pieces.append(jnp.zeros((count, rest_grad.shape[1] - used, lanes), wide_type))
            rest_grad[:, :, here] = jnp.concatenate(pieces, axis=1).astype(narrow_type)
    pooled_grad = dot_nn(low, lat_thirty[...]) * 0.25
    count = width // 2
    for i in range(strip_rows // 2):
        piece = pooled_grad[i * count : (i + 1) * count]
        for a in range(2):
            for b in range(2):
                at = (2 * i + a) * width + b
                put_strided(pool_grad, at, count, 2, piece)
    y_grad[...] = (total_grad[...] + join_parts(pool_grad, 0, tokens)).astype(narrow_type)
    if plan is not None:
        for number in range(1, plan.waves()):
            reducer.wave(number)
        reducer.finish()


def level_back(levels, strip_rows, width, base, operands, devices, plan, call_id):
    tokens, model = operands[10].shape
    channels = operands[0].shape[1]
    smooth, first, second, eight, four_pair, lat_eight, lat_sixteen, lat_thirty = operands[12:]
    biggest = (levels.rows[0] + 2) * levels.cols[0]

    def shape(rows, cols, kind=narrow_type):
        return jax.ShapeDtypeStruct((rows, cols), kind)

    outs = [
        shape(tokens, model),
        shape(16, model, wide_type),
        shape(smooth.shape[0] * smooth.shape[1], smooth.shape[2]),
    ]
    if devices:
        own = smooth.shape[0] * smooth.shape[1] // devices
        outs[2] = jax.ShapeDtypeStruct((2,) * plan.stages + (own, smooth.shape[2]), narrow_type)
        mid = first.shape[1] // 4
        folded = (devices, first.shape[0] // devices * 4, mid)
        rows = second.shape[0] // devices + channels // devices * 6
        rest = (devices, -(-rows // 16) * 16, mid)
        outs += [jax.ShapeDtypeStruct(dims, narrow_type) for dims in (folded, folded, rest)]
        outs += [jax.ShapeDtypeStruct(plan.left(t), narrow_type) for t in range(len(plan.pieces))]
    else:
        outs += [
            shape(*first.shape),
            shape(*eight.shape),
            shape(*second.shape),
            shape(channels, four_pair.shape[1] // 2),
            shape(*lat_eight.shape),
            shape(*lat_sixteen.shape),
            shape(*lat_thirty.shape),
        ]

    def body(*refs):
        level_back_kernel(levels, strip_rows, width, base, plan, refs)

    return pl.pallas_call(
        body,
        out_shape=outs,
        in_specs=vmem_specs(len(operands)),
        out_specs=vmem_specs(len(outs)),
        scratch_shapes=[
            pltpu.VMEM((biggest + 16, channels), wide_type),
            pltpu.VMEM((biggest, 3 * channels), narrow_type),
            pltpu.VMEM((channels // lanes, levels.rows[0] * levels.cols[0], lanes), wide_type),
            pltpu.VMEM(second.shape, wide_type),
            pltpu.VMEM(four_pair.shape, wide_type),
            pltpu.VMEM(lat_eight.shape, wide_type),
            pltpu.VMEM((tokens, model), wide_type),
            pltpu.VMEM((model // lanes, tokens, lanes), wide_type),
        ]
        + edge_scratch(operands[1])
        + ([] if plan is None else plan.scratch()),
        compiler_params=pltpu.CompilerParams(
            collective_id=call_id, has_side_effects=True, vmem_limit_bytes=62 << 20
        ),
        name="level_back",
    )(*operands)


def own_rows(values, count):
    return lax.dynamic_slice_in_dim(values, lax.axis_index("scale") * count, count, axis=1)


def level_weight(scale_level, strip_rows, cotans, anchors, roi_mask):
    region = own_rows(roi_mask, strip_rows)
    if scale_level < 3:
        factor = (4, 2, 1)[scale_level]
        region = jnp.repeat(jnp.repeat(region, factor, axis=1), factor, axis=2)
        count = factor * strip_rows
    else:
        region = region[:, ::2, ::2]
        count = strip_rows // 2
    anchor = own_rows(anchors[scale_level], count)
    cotangent = own_rows(cotans[scale_level], count)
    return (anchor + region).astype(narrow_type)[..., None] * cotangent


def on_device(
    block_input,
    pre_gain,
    pre_shift,
    qkv_weight,
    qv_bias,
    rel_rows,
    rel_cols,
    proj_weight,
    proj_bias,
    mid_gain,
    mid_shift,
    fc1_weight,
    fc1_bias,
    fc2_weight,
    fc2_bias,
    deconv_first,
    first_bias,
    upnorm_gain,
    upnorm_shift,
    deconv_second,
    second_bias,
    deconv_eight,
    eight_bias,
    lateral_four,
    lateral_eight,
    lateral_sixteen,
    lateral_thirty,
    lateral_gain,
    lateral_shift,
    smooth_weight,
    output_gain,
    grad_four,
    grad_eight,
    grad_sixteen,
    grad_thirty,
    anchor_four,
    anchor_eight,
    anchor_sixteen,
    anchor_thirty,
    roi_mask,
):
    _, strip_rows, width, model = block_input.shape
    head_size = rel_rows.shape[1]
    tokens = strip_rows * width
    height = strip_rows * lax.axis_size(("rows", "scale"))
    channels = smooth_weight.shape[2]
    ff = fc1_weight.shape[1]
    mid = first_bias.shape[0]
    quarter = second_bias.shape[0]
    levels = Levels(strip_rows, width)
    devices = lax.axis_size(("img", "rows", "scale"))
    fused = devices if (model // devices) % 8 == 0 and height <= 16 else 0
    x_own = block_input.reshape(tokens, model)
    x_all = gather_strips(x_own, 2)

    def wide_rows(vector):
        vector = vector.reshape(-1, vector.shape[-1]).astype(wide_type)
        if vector.shape[-1] > model:
            return vector.reshape(-1, model)
        return jnp.pad(vector, ((0, 0), (0, model - vector.shape[-1])))

    base = 8 + ff // model
    vec = jnp.concatenate(
        [
            wide_rows(part)
            for part in (
                pre_gain,
                pre_shift,
                qv_bias[:model],
                qv_bias[model:],
                proj_bias,
                mid_gain,
                mid_shift,
                fc2_bias,
                fc1_bias,
                first_bias,
                upnorm_gain,
                upnorm_shift,
                jnp.tile(second_bias, 4),
                eight_bias,
                lateral_gain,
                lateral_shift,
                output_gain,
            )
        ],
        axis=0,
    )
    vec = jnp.pad(vec, ((0, -vec.shape[0] % 8), (0, 0)))

    def padded_table(table):
        return jnp.pad(table, ((0, lanes - table.shape[0]), (0, 0)))

    turned = jnp.concatenate(
        [padded_table(rel_cols[::-1]), padded_table(rel_rows[::-1])], axis=0
    ).T
    none = jnp.zeros_like(turned)
    tables = jnp.concatenate(
        [jnp.concatenate([turned, none], axis=1), jnp.concatenate([none, turned], axis=1)], axis=0
    )
    plain = jnp.concatenate([padded_table(rel_cols), padded_table(rel_rows)], axis=0)
    blank = jnp.zeros_like(plain)
    rel_all = jnp.concatenate(
        [jnp.concatenate([plain, blank], axis=1), jnp.concatenate([blank, plain], axis=1)], axis=0
    )
    token = jnp.arange(height * width, dtype=jnp.int32)[:, None]
    lane = jnp.arange(lanes, dtype=jnp.int32)[None, :]
    key_row, key_col = token // width, token % width
    hot_col = (lane % width == key_col) & (lane < 2 * width)
    hot_row = (lane % height == key_row) & (lane < 2 * height)
    hot = jnp.concatenate([hot_col, hot_row], axis=1).astype(narrow_type)
    hot_turned = jnp.concatenate(
        [lane == width - 1 - key_col, lane == height - 1 - key_row], axis=1
    ).astype(narrow_type)
    lat_four_pair = jnp.concatenate(
        [
            jnp.concatenate([lateral_four, jnp.zeros_like(lateral_four)], axis=1),
            jnp.concatenate([jnp.zeros_like(lateral_four), lateral_four], axis=1),
        ],
        axis=0,
    )
    anchors = (anchor_four, anchor_eight, anchor_sixteen, anchor_thirty)
    cotans = (grad_four, grad_eight, grad_sixteen, grad_thirty)
    weight = jnp.concatenate(
        [
            level_weight(level, strip_rows, cotans, anchors, roi_mask).reshape(-1, channels)
            for level in range(4)
        ],
        axis=0,
    )
    (
        q_all,
        k_all,
        v_all,
        attended,
        attended_wide,
        log_norm,
        middle,
        normed_mid,
        hidden_pre,
        hidden,
        result,
    ) = block_forward(
        height,
        width,
        tokens,
        x_all,
        vec,
        qkv_weight,
        tables,
        hot,
        proj_weight,
        fc1_weight,
        fc2_weight,
    )
    lateral, top, bottom, first_map, active, source_zero, source_one, pooled, reduced = (
        level_sources(
            levels,
            strip_rows,
            width,
            base,
            result,
            vec,
            deconv_first,
            deconv_second,
            deconv_eight,
            (lat_four_pair, lateral_eight, lateral_sixteen, lateral_thirty),
        )
    )
    grads, top, bottom, slabs, gain_sums = smooth_levels(
        levels, base, lateral, (top, bottom), weight, smooth_weight, vec, 1
    )
    smooth_plan = None
    if fused:
        rows = smooth_weight.shape[0] * smooth_weight.shape[1] // devices
        smooth_shape = (devices, rows, channels)
        stages = len(halving_dims())
        cut = -(-rows // 32) * 16
        smooth_cuts = [(0, 0, cut, "x"), (0, cut, rows - cut, "y")]
        smooth_plan = ReducePlan(
            [smooth_shape], [piece + (0, 0, (0, 1)) for piece in smooth_cuts], near=(0,)
        )
    (
        result_grad,
        level_sums,
        smooth_grad,
        first_grad,
        eight_grad,
        *rest_grads,
    ) = level_back(
        levels,
        strip_rows,
        width,
        base,
        (
            grads,
            top,
            bottom,
            slabs,
            reduced,
            first_map,
            active,
            source_zero,
            source_one,
            pooled,
            result,
            vec,
            smooth_weight,
            deconv_first,
            deconv_second,
            deconv_eight,
            lat_four_pair,
            lateral_eight,
            lateral_sixteen,
            lateral_thirty,
        ),
        fused,
        smooth_plan,
        4,
    )
    names, final = [], []

    def share(shares, shapes, name, source, weight_in, begin=0):
        rows, columns = weight_in
        own, width_in = rows // devices, shapes[source][-1]
        names.append(name)
        if columns % lanes:
            flat = jax.ShapeDtypeStruct((own, width_in), wide_type)
            places = [(begin, own, 0, 0)]
            final.append((own, columns))
        else:
            tiles = columns // lanes
            flat = jax.ShapeDtypeStruct((own * tiles, lanes), wide_type)
            places = [
                (begin + f * own, own, f * width_in // lanes, tiles)
                for f in range(max(columns // width_in, 1))
            ]
            final.append((own * tiles, lanes))
        shares.append((flat, (source, places)))
        return begin + own * max(columns // width_in, 1)

    if fused:
        rest_grad, *smooth_left = rest_grads
    (
        middle_grad,
        attended_grad,
        stats,
        stat_rows,
        block_sums,
        fc1_sum,
        proj_grad,
        fc1_grad,
        fc2_grad,
    ) = block_backward(
        result_grad,
        (hidden_pre, hidden, normed_mid, middle, attended, attended_wide),
        log_norm,
        vec,
        proj_weight,
        fc1_weight,
        fc2_weight,
        fused,
    )
    operands = (
        x_own,
        q_all,
        k_all,
        v_all,
        attended_grad,
        stats,
        stat_rows,
        middle_grad,
        vec,
        tables,
        rel_all,
        hot,
        hot_turned,
        qkv_weight,
    )
    small_operands = (block_sums, fc1_sum, level_sums, gain_sums)
    if fused:
        arrays = (
            fc1_grad,
            fc2_grad.reshape(devices, -1, model),
            proj_grad,
            first_grad,
            eight_grad,
            rest_grad,
            *smooth_left,
        )
        shapes = [array.shape for array in arrays]
        query, keys = len(shapes), len(shapes) + 1
        own = model // devices
        shapes.append((devices, own * (model // mid), mid))
        shapes.append((devices, own * (2 * model // mid), mid))

        def half(source, part):
            size = shapes[source][1]
            first = -(-size // 32) * 16
            return (source, 0, first) if part == 0 else (source, first, size - first)

        def whole(source):
            return (source, 0, shapes[source][-2])

        pieces = [
            (6, *smooth_cuts[0][1:], 0, 2, (2, 4, 6)),
            (7, *smooth_cuts[1][1:], 6, 2, (9, 12, 20)),
            (*whole(query), "x", 0, 0, (8, 10, 14, 23, 27)),
            (*whole(2), "x", 0, 0, (10, 15, 32, 36, 40)),
            (*half(0, 0), "y", 0, 0, (1, 5, 7, 9, 11)),
            (*half(0, 1), "z", 0, 0, (5, 8, 10, 12, 17)),
            (*whole(4), "z", 0, 0, (7, 11, 18, 24, 28)),
            (*half(1, 0), "y", 0, 0, (3, 7, 9, 12, 16)),
            (*whole(3), "y", 0, 0, (6, 9, 11, 13, 22)),
            (*half(1, 1), "y", 0, 0, (9, 12, 19, 26, 31)),
            (*whole(5), "y", 0, 0, (13, 25, 30, 34, 38)),
            (*half(keys, 0), "x", 0, 0, (13, 21, 35, 39, 42)),
            (*half(keys, 1), "y", 0, 0, (13, 29, 33, 37, 41)),
        ]
        plan = ReducePlan(shapes, pieces, near=(query, keys))
        plan.riders = (12, 4, 2)
        shares = []
        tiles = channels // lanes
        names.append("smooth")
        final.append((rows * tiles, lanes))
        flat = jax.ShapeDtypeStruct((rows * tiles, lanes), wide_type)
        places = [(0, rows, 0, tiles)]
        shares.append((flat, [(6, places), (7, places)]))
        share(shares, shapes, "first", 3, deconv_first.shape)
        share(shares, shapes, "eight", 4, deconv_eight.shape)
        share(shares, shapes, "fc1", 0, fc1_weight.shape)
        share(shares, shapes, "fc2", 1, fc2_weight.shape)
        share(shares, shapes, "proj", 2, proj_weight.shape)
        at = 0
        for name, weight_in in (
            ("second", deconv_second),
            ("lat_sixteen", lateral_sixteen),
            ("lat_thirty", lateral_thirty),
            ("lat_eight", lateral_eight),
            ("lat_four", lateral_four),
        ):
            at = share(shares, shapes, name, 5, weight_in.shape, at)
        tiles = 3 * model // lanes
        names.append("qkv")
        final.append((own * tiles, lanes))
        flat = jax.ShapeDtypeStruct((own * tiles, lanes), wide_type)
        folds = [(own, f * mid // lanes, tiles) for f in range(3 * model // mid)]
        count = model // mid
        of_query = [(f * own, *fold) for f, fold in enumerate(folds[:count])]
        of_keys = [(f * own, *fold) for f, fold in enumerate(folds[count:])]
        shares.append((flat, [(query, of_query), (keys, of_keys)]))
        got = attention_backward(
            height, width, operands, small_operands, arrays, plan, shares, 0
        )
        vectors = (
            ((3,), 0, model, model),
            ((4,), 0, model, model),
            ((0, 2), 0, model, 2 * model),
            ((8,), 0, model, model),
            ((9,), 0, model, model),
            ((10,), 0, model, model),
            ((12, 13, 14, 15), 0, model, ff),
            ((11,), 0, model, model),
            ((16,), 0, mid, mid),
            ((16,), mid, mid, mid),
            ((17,), 0, mid, mid),
            ((18,), 0, model, quarter),
            ((17,), mid, mid, mid),
        )
        tables_out = (rel_rows.shape, rel_cols.shape[::-1]) + (lateral_gain.shape,) * 3
        input_grad, *got = finish(got[0], got[1:4], got[4:], final, vectors, tables_out)
        weight_sums = {name: value.reshape(-1) for name, value in zip(names, got)}
        small = got[len(names) :]
        small = (
            *small[:3],
            small[-5],
            small[-4].T,
            *small[3:13],
            *small[-3:],
        )
    else:
        input_grad, mix_sums, rel_sum, qkv_grad = attention_backward(
            height, width, operands, (), (), None, (), 0
        )
        second_grad, four_grad, lat_eight_grad, lat_sixteen_grad, lat_thirty_grad = rest_grads
        packed, folds = [], []
        for grads_in, columns, called in (
            ((smooth_grad,), channels, ("smooth",)),
            ((first_grad, eight_grad), model, ("first", "eight")),
            ((fc1_grad,), model, ("fc1",)),
            ((fc2_grad,), model, ("fc2",)),
            ((qkv_grad,), mid, ("qkv",)),
            (
                (
                    proj_grad,
                    second_grad,
                    lat_sixteen_grad,
                    lat_thirty_grad,
                    lat_eight_grad,
                    four_grad,
                ),
                mid,
                ("proj", "second", "lat_sixteen", "lat_thirty", "lat_eight", "lat_four"),
            ),
        ):
            stacked, fold = fold_chunks(grads_in, columns)
            packed.append(stacked)
            folds.append(fold)
            names += called
        gain_rows = jnp.pad(gain_sums, ((0, 0), (0, model - channels)))
        small_in = (
            jnp.concatenate(
                [mix_sums, block_sums, fc1_sum.reshape(-1, model), level_sums, gain_rows]
            ),
            rel_sum,
        )
        got, small = last_reduce(packed, pack_small(small_in), 3)
        sums, rel_sum = unpack_small(small, small_in)
        flat = []
        for summed, fold in zip(got, folds):
            flat += unfold_chunks(summed, fold)
        weight_sums = dict(zip(names, flat))
        small = (
            sums[3],
            sums[4],
            jnp.concatenate([sums[0], sums[2]]),
            rel_sum[: rel_rows.shape[0], head_size : 2 * head_size],
            rel_sum[: rel_cols.shape[0], :head_size],
            sums[8],
            sums[9],
            sums[10],
            sums[16:20].reshape(-1),
            sums[11],
            sums[20, :mid],
            sums[21, :mid],
            sums[22, :mid],
            jnp.sum(sums[23].reshape(4, quarter), axis=0),
            sums[24, :mid],
            sums[25:29, :channels],
            sums[29:33, :channels],
            sums[36:40, :channels],
        )
    return (
        result.reshape(block_input.shape),
        input_grad.reshape(block_input.shape),
        small[0],
        small[1],
        weight_sums["qkv"],
        small[2],
        small[3],
        small[4],
        weight_sums["proj"],
        small[5],
        small[6],
        small[7],
        weight_sums["fc1"],
        small[8],
        weight_sums["fc2"],
        small[9],
        weight_sums["first"],
        small[10],
        small[11],
        small[12],
        weight_sums["second"],
        small[13],
        weight_sums["eight"],
        small[14],
        weight_sums["lat_four"],
        weight_sums["lat_eight"],
        weight_sums["lat_sixteen"],
        weight_sums["lat_thirty"],
        small[15],
        small[16],
        weight_sums["smooth"],
        small[17],
    )


def solution(mesh):
    in_specs = (
        P("img", ("rows", "scale"), None, None),
        P(),
        P(),
        P(),
        P(),
        P(),
        P(),
        P(),
        P(),
        P(),
        P(),
        P(),
        P(),
        P(),
        P(),
        P(),
        P(),
        P(),
        P(),
        P(),
        P(),
        P(),
        P(),
        P(),
        P(),
        P(),
        P(),
        P(),
        P(),
        P(),
        P(),
        P("img", "rows", None, None),
        P("img", "rows", None, None),
        P("img", "rows", None, None),
        P("img", "rows", None, None),
        P("img", "rows", None),
        P("img", "rows", None),
        P("img", "rows", None),
        P("img", "rows", None),
        P("img", "rows", None),
    )
    out_specs = (
        P("img", ("rows", "scale"), None, None),
        P("img", ("rows", "scale"), None, None),
        P(),
        P(),
        P(("img", "rows", "scale")),
        P(),
        P(),
        P(),
        P(("img", "rows", "scale")),
        P(),
        P(),
        P(),
        P(("img", "rows", "scale")),
        P(),
        P(("img", "rows", "scale")),
        P(),
        P(("img", "rows", "scale")),
        P(),
        P(),
        P(),
        P(("img", "rows", "scale")),
        P(),
        P(("img", "rows", "scale")),
        P(),
        P(("img", "rows", "scale")),
        P(("img", "rows", "scale")),
        P(("img", "rows", "scale")),
        P(("img", "rows", "scale")),
        P(),
        P(),
        P(("img", "rows", "scale")),
        P(),
    )
    return jax.shard_map(
        on_device, mesh=mesh, in_specs=in_specs, out_specs=out_specs, check_vma=False
    )
```

```python
from functools import partial

import jax
import jax.numpy as jnp
from jax import lax
from jax.experimental import pallas as pl
from jax.experimental.pallas import tpu as pltpu
from jax.sharding import PartitionSpec as P

norm_eps = 1e-06
wide_type = jnp.float32
narrow_type = jnp.bfloat16

MESH_ID = pl.DeviceIdType.MESH
lanes = 128


def axis_bits(size):
    bits = []
    step = 1
    while step < size:
        bits.append(step)
        step *= 2
    return bits


def bit_partner(axis, step):
    here = lax.axis_index(axis)
    bit = lax.rem(lax.div(here, step), 2)
    return {axis: here + step - 2 * step * bit}, bit


def halving_dims():
    dims = []
    for axis in ("img", "rows", "scale"):
        for step in reversed(axis_bits(lax.axis_size(axis))):
            dims.append((axis, step))
    return dims


class ReducePlan:
    def __init__(self, shapes, pieces, near=()):
        self.dims = halving_dims()
        self.stages = len(self.dims)
        core = self.dims.index(("img", 1))
        plane = [i for i, d in enumerate(self.dims) if d[0] == "img" and i != core]
        across = [i for i, d in enumerate(self.dims) if d[0] == "rows"]
        along = [i for i, d in enumerate(self.dims) if d[0] == "scale"][::-1]
        orders = {
            "x": [core] + across + plane + along,
            "y": [core] + plane + across + along,
            "z": [core] + along[:1] + plane + across + along[1:],
        }
        self.shapes = shapes
        self.near = near
        self.groups = [[core], across + plane, along]
        self.pieces, self.spans, self.entries, self.events = [], [], [], []
        for source, begin, size, first, entry, start, waves in pieces:
            self.pieces.append((source, begin, size, shapes[source][-1], orders[first]))
            self.spans.append((start, start + len(waves)))
            self.entries.append(entry)
            self.events.append(waves)
        self.staging = sorted(
            {
                piece[2:4]
                for piece, span in zip(self.pieces, self.spans)
                if piece[0] not in near and span[0] == 0
            }
        )

    def lead(self, t):
        return (2,) * (self.stages - max(self.spans[t][0], 1))

    def left(self, t):
        _, _, rows, columns, _ = self.pieces[t]
        return (2,) * (self.stages - self.spans[t][1]) + (rows, columns)

    def scratch(self):
        out = []
        for t, (_, _, rows, columns, _) in enumerate(self.pieces):
            out.append(pltpu.VMEM(self.lead(t) + (rows, columns), narrow_type))
        for t, (_, _, rows, columns, _) in enumerate(self.pieces):
            start, stop = self.spans[t]
            for stage in range(max(start, 1), stop):
                lead = (2,) * (self.stages - 1 - stage)
                out.append(pltpu.VMEM(lead + (rows, columns), narrow_type))
        for shape in self.staging:
            out.append(pltpu.VMEM((2,) * (self.stages - 1) + shape, narrow_type))
        count = len(self.pieces)
        out += [pltpu.SemaphoreType.DMA((count, self.stages))] * 2
        out += [pltpu.SemaphoreType.DMA((count,))]
        return out

    def calls(self):
        out = {}
        for stage in reversed(range(self.stages)):
            for t, (start, stop) in enumerate(self.spans):
                if start <= stage < stop:
                    out.setdefault(self.events[t][stage - start], []).append((t, stage))
        return out

    def waves(self):
        return max(self.calls()) + 1

    def shaped(self, arrays):
        out = []
        for array in arrays:
            if len(array.shape) == 3 and array.shape[0] == 2**self.stages:
                array = array.reshape((2,) * self.stages + array.shape[1:])
            out.append(array)
        return out

    def sums(self):
        return [jax.ShapeDtypeStruct(shape[1:], wide_type) for shape in self.shapes]


class Reducer:
    def __init__(self, plan, sources, outs, scratch):
        self.plan, self.sources, self.outs = plan, sources, outs
        count = len(plan.pieces)
        scratch = list(scratch)
        self.held, scratch = scratch[:count], scratch[count:]
        self.landed = []
        for start, stop in plan.spans:
            size = stop - max(start, 1)
            stages = range(max(start, 1), stop)
            self.landed.append(dict(zip(stages, scratch[:size])))
            scratch = scratch[size:]
        self.staging = dict(zip(plan.staging, scratch))
        self.send_sem, self.recv_sem, self.local_sem = scratch[len(plan.staging) :]
        self.partners = [bit_partner(axis, step) for axis, step in plan.dims]
        users = {shape: [] for shape in plan.staging}
        self.following = {}
        for t in sorted(range(count), key=lambda t: plan.events[t][0]):
            piece = plan.pieces[t]
            if piece[0] in plan.near or plan.spans[t][0]:
                continue
            used = users[piece[2:4]]
            if used:
                self.following[used[-1]] = t
            used.append(t)
        self.first_local = [used[0] for used in users.values()]
        self.todo = plan.calls()
        self.riders = {}

    def greet(self, barrier, groups=False):
        devices = [partner for partner, _ in self.partners]
        if groups:
            devices += [
                self.across(group, mask)
                for group in self.plan.groups
                for mask in range(1, 2 ** len(group))
                if mask & (mask - 1)
            ]
        for device in devices:
            pl.semaphore_signal(barrier, inc=1, device_id=device, device_id_type=MESH_ID)
        return len(devices)

    def across(self, group, mask):
        device = {}
        for i, dim in enumerate(group):
            axis, step = self.plan.dims[dim]
            if mask >> i & 1:
                here = device.get(axis, lax.axis_index(axis))
                device[axis] = here + step - 2 * step * self.partners[dim][1]
        return device

    def index(self, taken, current, keep, gone=()):
        out = []
        for dim in range(self.plan.stages):
            bit = self.partners[dim][1]
            if dim in gone:
                continue
            if dim in taken:
                out.append(bit)
            elif dim == current:
                out.append(bit if keep else 1 - bit)
            else:
                out.append(slice(None))
        return tuple(out)

    def gone(self, t):
        return self.plan.pieces[t][4][: max(self.plan.spans[t][0], 1)]

    def copy(self, t, stage):
        source, begin, rows, _, order = self.plan.pieces[t]
        if stage == 0:
            index = self.index((), order[0], False)
            view = self.sources[source].at[index + (pl.ds(begin, rows),)]
            target = self.held[t]
        else:
            index = self.index(order[:stage], order[stage], False, self.gone(t))
            view = self.held[t].at[index]
            target = self.landed[t][stage]
        return pltpu.make_async_remote_copy(
            src_ref=view,
            dst_ref=target,
            send_sem=self.send_sem.at[t, stage],
            recv_sem=self.recv_sem.at[t, stage],
            device_id=self.partners[order[stage]][0],
            device_id_type=MESH_ID,
        )

    def local(self, t):
        source, begin, rows, columns, order = self.plan.pieces[t]
        if self.plan.spans[t][0]:
            view, target = self.sources[source], self.held[t]
        else:
            index = self.index((), order[0], True)
            view = self.sources[source].at[index + (pl.ds(begin, rows),)]
            target = self.staging[(rows, columns)]
        return pltpu.make_async_copy(view, target, self.local_sem.at[t])

    def each(self, lead, action):
        total = 1
        for size in lead:
            total *= size

        def body(step, carry):
            place, left = [], step
            for size in reversed(lead):
                place.append(lax.rem(left, size))
                left = lax.div(left, size)
            action(tuple(reversed(place)))
            return carry

        if lead:
            lax.fori_loop(0, total, body, 0)
        else:
            action(())

    def add(self, target, arrived, begin=0):
        lead, rows = target.shape[:-2], target.shape[-2]
        arrived = arrived.at[(slice(None),) * len(lead) + (pl.ds(begin, rows),)]

        def action(place):
            target[place] = target[place] + arrived[place]

        self.each(lead, action)

    def start(self):
        for t, span in enumerate(self.plan.spans):
            if span[0]:
                self.local(t).start()
            elif self.plan.pieces[t][0] not in self.plan.near:
                self.copy(t, 0).start()
        for t in self.first_local:
            self.local(t).start()
        for t, span in enumerate(self.plan.spans):
            if span[0]:
                self.local(t).wait()

    def start_near(self, source):
        for t in range(len(self.plan.pieces)):
            if self.plan.pieces[t][0] == source:
                self.copy(t, 0).start()

    def event(self, t, stage):
        source, begin, rows, columns, order = self.plan.pieces[t]
        self.copy(t, stage).wait_recv()
        if stage == 0 and source in self.plan.near:
            own = self.sources[source].at[self.index((), order[0], True)]
            self.add(self.held[t], own, begin)
        elif stage == 0:
            self.local(t).wait()
            self.add(self.held[t], self.staging[(rows, columns)])
            if t in self.following:
                self.local(self.following[t]).start()
        else:
            index = self.index(order[:stage], order[stage], True, self.gone(t))
            self.add(self.held[t].at[index], self.landed[t][stage])
        if t in self.riders:
            self.riders[t].step()
        if stage + 1 < self.plan.spans[t][1]:
            self.copy(t, stage + 1).start()
        elif stage + 1 < self.plan.stages:
            kept = self.held[t].at[self.index(order[: stage + 1], -1, True, self.gone(t))]
            out = self.outs[source][t]

            def action(place):
                out[place] = kept[place]

            self.each(kept.shape[:-2], action)
        else:
            index = self.index(order, -1, True, self.gone(t))
            self.emit(source, begin, self.held[t][index].astype(wide_type))

    def emit(self, source, begin, value):
        out = self.outs[source]
        if not isinstance(out, list):
            out[begin : begin + value.shape[0], :] = value
            return
        for first, count, tile, tiles, ref in out:
            low, high = max(first, begin), min(first + count, begin + value.shape[0])
            if low < high:
                part = value[low - begin : high - begin]
                if tiles == 0:
                    ref[low - first : high - first, :] = part
                for c in range(min(tiles, part.shape[1] // lanes)):
                    here = part[:, c * lanes : (c + 1) * lanes]
                    at = (low - first) * tiles + tile + c
                    ref[pl.ds(at, high - low, stride=tiles), :] = here

    def wave(self, number):
        for t, span in enumerate(self.plan.spans):
            if span[0] and self.plan.entries[t] == number:
                self.copy(t, span[0]).start()
        for t, stage in self.todo.get(number, ()):
            self.event(t, stage)

    def finish(self):
        for t, (start, stop) in enumerate(self.plan.spans):
            for stage in range(start, stop):
                self.copy(t, stage).wait_send()


class SmallReduce:
    def __init__(self, reducer, groups, total, landed, send_sem, recv_sem):
        self.reducer, self.total, self.landed = reducer, total, landed
        self.send_sem, self.recv_sem = send_sem, recv_sem
        self.groups = groups
        self.stage = 0

    @staticmethod
    def sizes(groups):
        sizes = [2 ** len(group) for group in groups]
        return sizes, [sum(sizes[:i]) for i in range(len(sizes) + 1)]

    def copies(self):
        group = self.groups[self.stage]
        sizes, at = self.sizes(self.groups)
        place = sum(self.reducer.partners[dim][1] * 2**i for i, dim in enumerate(group))
        return place, [
            pltpu.make_async_remote_copy(
                src_ref=self.total,
                dst_ref=self.landed.at[at[self.stage] + place],
                send_sem=self.send_sem.at[at[self.stage] + mask],
                recv_sem=self.recv_sem.at[at[self.stage] + mask],
                device_id=self.reducer.across(group, mask),
                device_id_type=MESH_ID,
            )
            for mask in range(1, sizes[self.stage])
        ]

    def start(self):
        place, copies = self.copies()
        for copy in copies:
            copy.start()
        sizes, at = self.sizes(self.groups)
        self.landed[at[self.stage] + place] = self.total[...]

    def step(self):
        if self.stage == len(self.groups):
            return
        for copy in self.copies()[1]:
            copy.wait()
        sizes, at = self.sizes(self.groups)
        total = self.landed[at[self.stage]]
        for i in range(1, sizes[self.stage]):
            total = total + self.landed[at[self.stage] + i]
        self.total[...] = total
        self.stage += 1
        if self.stage < len(self.groups):
            self.start()


class StripGather:
    def __init__(self, owns, wholes, send_sem, recv_sem):
        self.owns, self.wholes = owns, wholes
        self.send_sem, self.recv_sem = send_sem, recv_sem
        self.deep, self.wide = lax.axis_size("scale"), lax.axis_size("rows")
        self.here, self.line = lax.axis_index("scale"), lax.axis_index("rows")

    @staticmethod
    def slots():
        deep, wide = lax.axis_size("scale"), lax.axis_size("rows")
        return 2 * (deep - 1) + (wide - 1) * (2 * deep - 1)

    def greet(self, barrier):
        waits = self.wide - 1
        for k in range(1, self.wide):
            device = {"rows": lax.rem(self.line + k, self.wide)}
            pl.semaphore_signal(barrier, inc=1, device_id=device, device_id_type=MESH_ID)

        @pl.when(self.here > 0)
        def _():
            device = {"scale": self.here - 1}
            pl.semaphore_signal(barrier, inc=1, device_id=device, device_id_type=MESH_ID)

        @pl.when(self.here < self.deep - 1)
        def _():
            device = {"scale": self.here + 1}
            pl.semaphore_signal(barrier, inc=1, device_id=device, device_id_type=MESH_ID)

        more = jnp.where(self.here > 0, 1, 0) + jnp.where(self.here < self.deep - 1, 1, 0)
        return waits + more

    def copies(self, block, slot, device):
        out = []
        for i, whole in enumerate(self.wholes):
            view = whole.at[self.line * self.deep + block]
            out.append(
                pltpu.make_async_remote_copy(
                    src_ref=view,
                    dst_ref=view,
                    send_sem=self.send_sem.at[slot, i],
                    recv_sem=self.recv_sem.at[slot, i],
                    device_id=device,
                    device_id_type=MESH_ID,
                )
            )
        return out

    def along(self, step, right):
        if right:
            block, device = self.here - step, {"scale": jnp.minimum(self.here + 1, self.deep - 1)}
            sent = (block >= 0) & (self.here < self.deep - 1)
            got = self.here - 1 - step >= 0
            return block, step, device, sent, got
        block, device = self.here + step, {"scale": jnp.maximum(self.here - 1, 0)}
        sent = (block < self.deep) & (self.here > 0)
        got = self.here + 1 + step < self.deep
        return block, self.deep - 1 + step, device, sent, got

    def across(self, block, kind, action):
        base = 2 * (self.deep - 1)
        for k in range(1, self.wide):
            slot = base + (k - 1) * (2 * self.deep - 1) + kind
            device = {"rows": lax.rem(self.line + k, self.wide)}
            for copy in self.copies(block, slot, device):
                action(copy)

    def start(self):
        for own, whole in zip(self.owns, self.wholes):
            whole[self.line * self.deep + self.here] = own[...]
        for right in (True, False):
            block, slot, device, sent, _ = self.along(0, right)

            @pl.when(sent)
            def _():
                for copy in self.copies(block, slot, device):
                    copy.start()

        self.across(self.here, 0, lambda copy: copy.start())

    def step(self, number):
        for right in (True, False):
            _, slot, device, _, got = self.along(number, right)
            block = self.here - 1 - number if right else self.here + 1 + number

            @pl.when(got)
            def _():
                for copy in self.copies(block, slot, device):
                    copy.wait_recv()
                kind = 1 + 2 * number + (0 if right else 1)
                self.across(block, kind, lambda copy: copy.start())

            if number + 1 < self.deep - 1:
                later, slot, device, sent, _ = self.along(number + 1, right)

                @pl.when(sent)
                def _():
                    for copy in self.copies(later, slot, device):
                        copy.start()

    def finish(self):
        self.across(self.here, 0, lambda copy: copy.wait())
        for number in range(self.deep - 1):
            for right in (True, False):
                _, _, _, _, got = self.along(number, right)
                block = self.here - 1 - number if right else self.here + 1 + number
                kind = 1 + 2 * number + (0 if right else 1)

                @pl.when(got)
                def _():
                    self.across(block, kind, lambda copy: copy.wait())

                sent_block, slot, device, sent, _ = self.along(number, right)

                @pl.when(sent)
                def _():
                    for copy in self.copies(sent_block, slot, device):
                        copy.wait_send()


def fold_chunks(grads, width):
    devices = lax.axis_size(("img", "rows", "scale"))
    cut, plan = [], []
    for grad in grads:
        rows, columns = grad.shape
        own = rows // devices
        chunk = grad.astype(narrow_type).reshape(devices, own, columns)
        folds = max(columns // width, 1)
        if columns < width:
            chunk = jnp.pad(chunk, ((0, 0), (0, 0), (0, width - columns)))
        cut += [chunk[:, :, f * width : (f + 1) * width] for f in range(folds)]
        plan.append((own, columns, folds))
    stacked = jnp.concatenate(cut, axis=1) if len(cut) > 1 else cut[0]
    extra = -stacked.shape[1] % 16
    if extra:
        stacked = jnp.pad(stacked, ((0, 0), (0, extra), (0, 0)))
    return stacked, plan


def unfold_chunks(summed, plan):
    at, out = 0, []
    for own, columns, folds in plan:
        parts = []
        for _ in range(folds):
            parts.append(summed[at : at + own, : min(columns, summed.shape[1])])
            at += own
        whole = jnp.concatenate(parts, axis=1) if folds > 1 else parts[0]
        out.append(whole.reshape(-1))
    return out


def last_reduce_kernel(plan, count, refs):
    sources, small_in = refs[:count], refs[count]
    outs, small_out = refs[count + 1 : 2 * count + 1], refs[2 * count + 1]
    scratch = refs[2 * count + 2 :]
    small_held, small_landed, small_send, small_recv = scratch[:4]
    reducer = Reducer(plan, sources, outs, scratch[4:])
    barrier = pltpu.get_barrier_semaphore()
    pl.semaphore_wait(barrier, reducer.greet(barrier))

    def small_copy(stage):
        return pltpu.make_async_remote_copy(
            src_ref=small_held,
            dst_ref=small_landed.at[stage],
            send_sem=small_send.at[stage],
            recv_sem=small_recv.at[stage],
            device_id=reducer.partners[plan.pieces[0][4][stage]][0],
            device_id_type=MESH_ID,
        )

    small_held[...] = small_in[...]
    reducer.start()
    small_copy(0).start()
    for number in range(plan.waves()):
        reducer.wave(number)
        if number < plan.stages:
            small_copy(number).wait()
            small_held[...] = small_held[...] + small_landed[number]
            if number + 1 < plan.stages:
                small_copy(number + 1).start()
    small_out[...] = small_held[...]
    reducer.finish()


def cut_rows(shapes):
    out = []
    stages = len(halving_dims())
    for source, (_, rows, _) in enumerate(shapes):
        first = -(-rows // 32) * 16
        waves = tuple(source + stage + (1 if stage else 0) for stage in range(stages))
        out.append((source, 0, first, "x", source, 0, waves))
        if first < rows:
            out.append((source, first, rows - first, "y", source, 0, waves))
    return out


def last_reduce(arrays, small, call_id):
    shapes = [array.shape for array in arrays]
    plan = ReducePlan(shapes, cut_rows(shapes))
    count = len(arrays)

    def body(*refs):
        last_reduce_kernel(plan, count, refs)

    vmem = pl.BlockSpec(memory_space=pltpu.VMEM)
    got = pl.pallas_call(
        body,
        out_shape=plan.sums() + [jax.ShapeDtypeStruct(small.shape, wide_type)],
        in_specs=[pl.BlockSpec(memory_space=pl.ANY)] * count + [vmem],
        out_specs=[vmem] * (count + 1),
        scratch_shapes=[
            pltpu.VMEM(small.shape, wide_type),
            pltpu.VMEM((plan.stages,) + small.shape, wide_type),
            pltpu.SemaphoreType.DMA((plan.stages,)),
            pltpu.SemaphoreType.DMA((plan.stages,)),
        ]
        + plan.scratch(),
        compiler_params=pltpu.CompilerParams(
            collective_id=call_id, has_side_effects=True, vmem_limit_bytes=60 << 20
        ),
        name="last_reduce",
    )(*plan.shaped(arrays), small)
    return got[:count], got[count]


def pack_small(parts):
    flat = jnp.concatenate([part.reshape(-1) for part in parts])
    unit = 8 * lanes
    total = -(-flat.shape[0] // unit) * unit
    return jnp.pad(flat, (0, total - flat.shape[0])).reshape(-1, lanes)


def unpack_small(packed, parts):
    flat = packed.reshape(-1)
    out, at = [], 0
    for part in parts:
        out.append(flat[at : at + part.size].reshape(part.shape))
        at += part.size
    return out


def dot_nn(left, right):
    return lax.dot_general(left, right, (((1,), (0,)), ((), ())), preferred_element_type=wide_type)


def dot_nt(left, right):
    return lax.dot_general(left, right, (((1,), (1,)), ((), ())), preferred_element_type=wide_type)


def dot_tn(left, right):
    return lax.dot_general(left, right, (((0,), (0,)), ((), ())), preferred_element_type=wide_type)


def norm_parts(values):
    centre = values - jnp.mean(values, axis=-1, keepdims=True)
    inverse = lax.rsqrt(jnp.mean(centre * centre, axis=-1, keepdims=True) + norm_eps)
    return centre * inverse, inverse


def norm_back(hat, inverse, hat_grad):
    inner = jnp.mean(hat_grad * hat, axis=-1, keepdims=True)
    return inverse * (hat_grad - jnp.mean(hat_grad, axis=-1, keepdims=True) - hat * inner)


def normal_cdf(values):
    return 0.5 + 0.5 * lax.erf(values * (0.5**0.5))


def gelu_slope(values):
    density = jnp.exp(-0.5 * values * values) * (0.5 / jnp.pi) ** 0.5
    return normal_cdf(values) + values * density


def lane_ids(shape):
    return lax.broadcasted_iota(jnp.int32, shape, len(shape) - 1)


def column_sum(values):
    return jnp.sum(values, axis=0, keepdims=True)


def half_mask(half, head_size, value):
    lane = lane_ids((1, 2 * head_size))
    inside = (lane >= half * head_size) & (lane < (half + 1) * head_size)
    return jnp.where(inside, value, 0.0).astype(narrow_type)


def split_lanes(values, used):
    lane = lane_ids(values.shape)
    twice = jnp.where(lane < used, values, pltpu.roll(values, used, 1))
    near = twice.astype(narrow_type).astype(wide_type)
    both = jnp.where(lane < used, near, twice - near)
    return jnp.where(lane < 2 * used, both, 0.0).astype(narrow_type)


def place_cols(tab, width):
    by_col = pltpu.roll(tab, lanes - (width - 1), 1, stride=1, stride_axis=0)
    return split_lanes(by_col, width)


def place_rows(tab, row, height):
    by_row = pltpu.roll(tab, lax.rem(lanes - (height - 1) + row, lanes), 1)
    return split_lanes(by_row, height)


def both_halves(values, head_size, scale):
    masked = [values * half_mask(half, head_size, scale) for half in range(2)]
    return jnp.concatenate(masked, axis=0)


def own_extra(tab, strip_rows, width, height):
    out = []
    for half in range(2):
        for i in range(strip_rows):
            piece = tab[i * width : (i + 1) * width, 2 * half * lanes : 2 * (half + 1) * lanes]
            row = strip_index() * strip_rows + i
            cols = place_cols(piece[:, :lanes], width)
            out.append(jnp.concatenate([cols, place_rows(piece[:, lanes:], row, height)], axis=1))
    return jnp.concatenate(out, axis=0)


def strip_index():
    return lax.axis_index("rows") * lax.axis_size("scale") + lax.axis_index("scale")


def block_forward_kernel(height, width, count, refs):
    x_own, refs = refs[0], refs[1:]
    small, refs = refs[: count + 3], refs[count + 3 :]
    qkv_hbm, proj_hbm, fc1_hbm, fc2_hbm = refs[:4]
    prepared, refs = refs[4:10], refs[10:]
    (
        q_all,
        k_all,
        v_all,
        attended,
        attended_wide,
        log_norm,
        middle,
        normed_mid,
        hidden_pre,
        hidden,
        result,
    ) = refs[:11]
    qkv_weight, proj, fc1, fc2, sems, x_all, table, send_sem, recv_sem = refs[11:]
    vec, tables, _, hot, _, _ = prepared
    model = x_all.shape[2]
    tokens = middle.shape[0]
    strip_rows = tokens // width
    head_size = lanes // 2
    copies = [
        pltpu.make_async_copy(source, target, sems.at[i])
        for i, (source, target) in enumerate(
            ((proj_hbm, proj), (fc1_hbm, fc1), (fc2_hbm, fc2), (qkv_hbm, qkv_weight))
        )
    ]
    for copy in reversed(copies):
        copy.start()
    gather = StripGather([x_own], [x_all], send_sem, recv_sem)
    barrier = pltpu.get_barrier_semaphore()
    pl.semaphore_wait(barrier, gather.greet(barrier))
    gather.start()
    prepare_kernel(height, width, count, (*small, *prepared, table))
    copies[3].wait()
    start = pl.multiple_of(strip_index() * tokens, tokens)

    def mix(begin, blocks):
        at = pl.ds(pl.multiple_of(begin * tokens, tokens), blocks * tokens)
        inputs = x_all[pl.ds(begin, blocks)].reshape(blocks * tokens, model)
        hat, _ = norm_parts(inputs.astype(wide_type))
        normed = (hat * vec[0:1, :] + vec[1:2, :]).astype(narrow_type)
        mixed = dot_nn(normed, qkv_weight[...])
        q_all[at, :] = (mixed[:, :model] + vec[2:3, :]).astype(narrow_type)
        k_all[at, :] = mixed[:, model : 2 * model].astype(narrow_type)
        v_all[at, :] = (mixed[:, 2 * model :] + vec[3:4, :]).astype(narrow_type)

    for number in range(gather.deep - 1):
        gather.step(number)
    line = gather.line * gather.deep
    mix(line, gather.deep)
    gather.finish()

    def others(step, carry):
        mix(lax.rem(gather.line + 1 + step, gather.wide) * gather.deep, gather.deep)
        return carry

    lax.fori_loop(0, gather.wide - 1, others, 0)
    log_norm[...] = jnp.zeros_like(log_norm)
    lane = lane_ids((tokens, lanes))

    def pair_step(pair, carry):
        cols = pl.ds(pl.multiple_of(pair * lanes, lanes), lanes)
        queries = q_all[pl.ds(start, tokens), cols]
        values = v_all[:, cols]
        keys = jnp.concatenate([k_all[:, cols], hot[...]], axis=1)
        extra = own_extra(dot_nn(queries, tables[...]), strip_rows, width, height)
        masked = both_halves(queries, head_size, head_size**-0.5)
        scores = dot_nt(jnp.concatenate([masked, extra], axis=1), keys)
        peak = jnp.max(scores, axis=-1, keepdims=True)
        raised = jnp.exp(scores - peak)
        total = jnp.sum(raised, axis=-1, keepdims=True)
        probs = (raised * (1.0 / total)).astype(narrow_type)
        out = dot_nn(probs, values)
        mixed = (out[:tokens], out[tokens:])
        norm = peak + jnp.log(total)
        kept = jnp.where(lane == 2 * pair, norm[:tokens], log_norm[...])
        log_norm[...] = jnp.where(lane == 2 * pair + 1, norm[tokens:], kept)
        joined = jnp.where(lane < head_size, mixed[0], mixed[1])
        attended_wide[:, cols] = joined
        attended[:, cols] = joined.astype(narrow_type)
        return carry

    lax.fori_loop(0, model // lanes, pair_step, 0)
    copies[0].wait()
    inputs = x_all[strip_index()].astype(wide_type)
    centre = inputs + (dot_nn(attended[...], proj[...]) + vec[4:5, :])
    middle[...] = centre
    hat, _ = norm_parts(centre)
    normed_low = (hat * vec[5:6, :] + vec[6:7, :]).astype(narrow_type)
    normed_mid[...] = normed_low
    copies[1].wait()
    copies[2].wait()
    result_wide = centre + vec[7:8, :]
    for j in range(fc1.shape[1] // model):
        cols = slice(j * model, (j + 1) * model)
        pre = dot_nn(normed_mid[...], fc1[:, cols]) + vec[8 + j : 9 + j, :]
        hidden_pre[:, cols] = pre
        low = (pre * normal_cdf(pre)).astype(narrow_type)
        hidden[:, cols] = low
        result_wide = result_wide + dot_nn(low, fc2[cols, :])
    result[...] = result_wide.astype(narrow_type)


def vmem_specs(count):
    return [pl.BlockSpec(memory_space=pltpu.VMEM)] * count


def any_specs(count):
    return [pl.BlockSpec(memory_space=pl.ANY)] * count


def block_forward(height, width, x_own, vectors, turned, weights, call_id):
    tokens, model = x_own.shape
    total = height * width
    ff = weights[2].shape[1]
    slots = StripGather.slots()

    def shape(rows, cols, kind):
        return jax.ShapeDtypeStruct((rows, cols), kind)

    outs = [
        shape(total, model, narrow_type),
        shape(total, model, narrow_type),
        shape(total, model, narrow_type),
        shape(tokens, model, narrow_type),
        shape(tokens, model, wide_type),
        shape(tokens, lanes, wide_type),
        shape(tokens, model, wide_type),
        shape(tokens, model, narrow_type),
        shape(tokens, ff, wide_type),
        shape(tokens, ff, narrow_type),
        shape(tokens, model, narrow_type),
    ]
    outs = prepared_shapes(height, width, model, vectors, turned[2]) + outs
    small = (*vectors, *turned)

    def body(*refs):
        block_forward_kernel(height, width, len(vectors), refs)

    return pl.pallas_call(
        body,
        out_shape=outs,
        in_specs=vmem_specs(1 + len(small)) + any_specs(4),
        out_specs=vmem_specs(len(outs)),
        scratch_shapes=[pltpu.VMEM(weight.shape, narrow_type) for weight in weights]
        + [
            pltpu.SemaphoreType.DMA((4,)),
            pltpu.VMEM((total // tokens, tokens, model), narrow_type),
            pltpu.VMEM((lanes, lanes), wide_type),
            pltpu.SemaphoreType.DMA((slots, 1)),
            pltpu.SemaphoreType.DMA((slots, 1)),
        ],
        compiler_params=pltpu.CompilerParams(
            collective_id=call_id, has_side_effects=True, vmem_limit_bytes=60 << 20
        ),
        name="block_forward",
    )(x_own, *small, *weights)


def fold_store(target, number, parts, value):
    devices = target.shape[0]
    own = value.shape[0] // devices
    parts[number] = value.reshape(devices, own, value.shape[1])
    if number % 2:
        both = jnp.concatenate([parts.pop(number - 1), parts.pop(number)], axis=1)
        begin = (number - 1) * own
        target[:, begin : begin + 2 * own, :] = both.astype(narrow_type)


def block_backward_kernel(
    result_grad,
    hidden_pre,
    hidden,
    normed_mid,
    middle,
    attended,
    attended_wide,
    log_norm,
    vec,
    proj_far,
    fc1_far,
    fc2_far,
    middle_grad,
    attended_grad,
    stats,
    stat_rows,
    sums,
    fc1_sum,
    proj_grad,
    fc1_out,
    fc2_out,
    proj,
    fc1,
    fc2,
    fc1_grad,
    fc2_grad,
    sems,
):
    width = middle.shape[1]
    blocks = hidden.shape[1] // width
    fc1_in, fc2_in, fc2_back = [], [], []
    for j in range(blocks):
        part = slice(j * width, (j + 1) * width)
        fc1_in.append(
            pltpu.make_async_copy(fc1_far.at[:, part], fc1.at[:, part], sems.at[0, j])
        )
        fc2_in.append(pltpu.make_async_copy(fc2_far.at[part], fc2.at[part], sems.at[1, j]))
        fc2_back.append(pltpu.make_async_copy(fc2_grad.at[part], fc2_out.at[part], sems.at[2, j]))
        fc2_in[j].start()
        fc1_in[j].start()
    proj_in = pltpu.make_async_copy(proj_far, proj, sems.at[3, 0])
    proj_in.start()
    fc1_back = []
    if len(fc1_out.shape) == 3:
        rows = fc1_out.shape[1] // 2
        for j in range(2):
            part = slice(j * rows, (j + 1) * rows)
            fc1_back.append(
                pltpu.make_async_copy(fc1_grad.at[:, part], fc1_out.at[:, part], sems.at[4, j])
            )
    else:
        fc1_back.append(pltpu.make_async_copy(fc1_grad, fc1_out, sems.at[4, 0]))
    model = middle.shape[1]
    ff = hidden.shape[1]
    grad_low = result_grad[...]
    grad_wide = grad_low.astype(wide_type)
    back = jnp.zeros(middle.shape, wide_type)
    normed_turned = normed_mid[...].T
    parts = {}
    for j in range(ff // model):
        cols = slice(j * model, (j + 1) * model)
        pre = hidden_pre[:, cols]
        fc2_in[j].wait()
        pre_grad = dot_nt(grad_low, fc2[cols, :]) * gelu_slope(pre)
        pre_low = pre_grad.astype(narrow_type)
        fc1_sum[:, cols] = column_sum(pre_low.astype(wide_type))
        fc1_in[j].wait()
        back = back + dot_nt(pre_low, fc1[:, cols])
        part = dot_nn(normed_turned, pre_low)
        if len(fc1_grad.shape) == 2:
            fc1_grad[:, cols] = part.astype(narrow_type)
        else:
            fold_store(fc1_grad, j, parts, part)
        fc2_grad[cols, :] = dot_nn(hidden[:, cols].T, grad_low).astype(narrow_type)
        fc2_back[j].start()
        if len(fc1_back) == 2 and j % 2:
            fc1_back[j // 2].start()
    if len(fc1_back) == 1:
        fc1_back[0].start()
    proj_in.wait()
    hat, inverse = norm_parts(middle[...])
    gain_grad = column_sum(back * hat)
    shift_grad = column_sum(back)
    centre_grad = grad_wide + norm_back(hat, inverse, back * vec[5:6, :])
    middle_grad[...] = centre_grad
    branch_low = centre_grad.astype(narrow_type)
    sums[0:1, :] = column_sum(branch_low.astype(wide_type))
    sums[1:2, :] = gain_grad
    sums[2:3, :] = shift_grad
    sums[3:4, :] = column_sum(grad_wide)
    sums[4:8, :] = jnp.zeros((4, model), wide_type)
    attended_turned = attended[...].T
    if len(proj_grad.shape) == 2:
        proj_grad[...] = dot_nn(attended_turned, branch_low).astype(narrow_type)
    else:
        half = model // 2
        for j in range(2):
            part = dot_nn(attended_turned, branch_low[:, j * half : (j + 1) * half])
            fold_store(proj_grad, j, parts, part)
    out_grad = dot_nt(branch_low, proj[...]).astype(narrow_type)
    attended_grad[...] = out_grad
    product = out_grad.astype(wide_type) * attended_wide[...]
    near = product.astype(narrow_type)
    rest = (product - near.astype(wide_type)).astype(narrow_type)
    head_size = lanes // 2
    channel = lax.broadcasted_iota(jnp.int32, (model, lanes), 0)
    head = lax.broadcasted_iota(jnp.int32, (model, lanes), 1)
    member = (lax.div(channel, head_size) == head - 16).astype(wide_type).astype(narrow_type)
    delta = dot_nn(near, member) + dot_nn(rest, member)
    both = jnp.where(lane_ids(delta.shape) < 16, log_norm[...], delta)
    stats[...] = both
    stat_rows[...] = both.T[:32, :]
    for copy in fc1_back + fc2_back:
        copy.wait()


def share_outs(plan, shares, refs):
    outs = [[] for _ in plan.shapes]
    for ref, share in zip(refs, shares):
        for source, places in share if isinstance(share, list) else [share]:
            for place in places:
                outs[source].append(place + (ref,))
    return outs


def block_backward(result_grad, kept, log_norm, vec, proj, fc1, fc2, devices):
    hidden_pre, hidden, normed_mid, middle, attended, attended_wide = kept
    tokens, model = middle.shape
    ff = fc1.shape[1]

    def shape(rows, cols, kind):
        return jax.ShapeDtypeStruct((rows, cols), kind)

    outs = [
        shape(tokens, model, wide_type),
        shape(tokens, model, narrow_type),
        shape(tokens, lanes, wide_type),
        shape(32, tokens, wide_type),
        shape(8, model, wide_type),
        shape(1, ff, wide_type),
        shape(model, model, narrow_type),
        shape(model, ff, narrow_type),
        shape(ff, model, narrow_type),
    ]
    if devices:
        outs[6] = jax.ShapeDtypeStruct((devices, model // devices * 2, model // 2), narrow_type)
        outs[7] = jax.ShapeDtypeStruct((devices, model // devices * (ff // model), model), narrow_type)
    return pl.pallas_call(
        block_backward_kernel,
        out_shape=outs,
        in_specs=vmem_specs(9) + any_specs(3),
        out_specs=vmem_specs(len(outs) - 2) + any_specs(2),
        scratch_shapes=[
            pltpu.VMEM(proj.shape, narrow_type),
            pltpu.VMEM(fc1.shape, narrow_type),
            pltpu.VMEM(fc2.shape, narrow_type),
            pltpu.VMEM(outs[7].shape, narrow_type),
            pltpu.VMEM(outs[8].shape, narrow_type),
            pltpu.SemaphoreType.DMA((5, ff // model)),
        ],
        compiler_params=pltpu.CompilerParams(vmem_limit_bytes=60 << 20),
        name="block_backward",
    )(
        result_grad,
        hidden_pre,
        hidden,
        normed_mid,
        middle,
        attended,
        attended_wide,
        log_norm,
        vec,
        proj,
        fc1,
        fc2,
    )


def small_groups(plan):
    return [[[dim] for dim in plan.pieces[t][4]] for t in plan.riders]


def attention_backward_kernel(height, width, plan, shares, refs):
    (
        x_own,
        q_all,
        k_all,
        v_all,
        grad_own,
        own_stats,
        stat_own,
        middle_grad,
        vec,
        tables,
        rel_all,
        hot,
        hot_turned,
        qkv_weight,
    ) = refs[:14]
    refs = refs[14:]
    if plan is None:
        input_grad, sums, rel_sum, weight_grad = refs[:4]
        scratch = refs[4:]
    else:
        block_sums, fc1_sum, level_sums, gain_sums = refs[:4]
        count = len(plan.shapes) - 2
        sources = refs[4 : 4 + count]
        input_grad, sums_out, early_out, rel_out = refs[4 + count : 8 + count]
        flat = refs[8 + count : 8 + count + len(shares)]
        scratch = refs[8 + count + len(shares) :]
        near_query, near_rest, sums, early, rel_sum = scratch[:5]
        small_scratch, scratch = scratch[5:14], scratch[14:]
        outs = share_outs(plan, shares, flat)
    joined, wide_tab, cols_extra, rows_extra, grad_all, stat_all, stat_rows, rel_grad = scratch[:8]
    gather = StripGather([grad_own, stat_own], [grad_all, stat_all], scratch[8], scratch[9])
    total, model = q_all.shape
    tokens = x_own.shape[0]
    strip_rows = tokens // width
    head_size = lanes // 2
    scale = head_size**-0.5
    strip = strip_index()
    strips = grad_all.shape[0]
    own = pl.ds(pl.multiple_of(strip * tokens, tokens), tokens)
    pairs = model // lanes
    barrier = pltpu.get_barrier_semaphore()
    greeted = gather.greet(barrier)
    if plan is not None:
        reducer = Reducer(plan, (*sources, near_query, near_rest), outs, scratch[10:])
        greeted = greeted + reducer.greet(barrier)
        late_sums, early_sums, rel_sums = [
            SmallReduce(reducer, groups, total, *small_scratch[3 * i : 3 * i + 3])
            for i, (groups, total) in enumerate(zip(small_groups(plan), (sums, early, rel_sum)))
        ]
        reducer.riders = dict(zip(plan.riders, (late_sums, early_sums, rel_sums)))
    if plan is not None:
        early[0:4, :] = block_sums[0:4, :]
        size = early.shape[1]
        for j in range(fc1_sum.shape[1] // size):
            early[4 + j : 5 + j, :] = fc1_sum[:, j * size : (j + 1) * size]
        mid, channels = size // 2, gain_sums.shape[1]
        early[8:9, :mid], early[8:9, mid:] = level_sums[0:1, :mid], level_sums[1:2, :mid]
        early[9:10, :mid], early[9:10, mid:] = level_sums[2:3, :mid], level_sums[4:5, :mid]
        early[10:11, :] = level_sums[3:4, :]
        early[11:15, :channels] = level_sums[5:9, :channels]
        early[11:15, channels : 2 * channels] = level_sums[9:13, :channels]
        early[11:15, 2 * channels :] = gain_sums[0:4, :]
        early[15:16, :] = jnp.zeros((1, size), wide_type)
    pl.semaphore_wait(barrier, greeted)
    gather.start()
    if plan is not None:
        early_sums.start()
        reducer.start()

    rel_grad[...] = jnp.zeros_like(rel_grad)
    lane = lane_ids((tokens, lanes))

    def own_queries(pair):
        cols = slice(pair * lanes, (pair + 1) * lanes)
        queries = q_all[own, cols]
        keys = k_all[:, cols]
        extra = own_extra(dot_nn(queries, tables[...]), strip_rows, width, height)
        masked = both_halves(queries, head_size, scale)
        keys_hot = jnp.concatenate([keys, hot[...]], axis=1)
        scores = dot_nt(jnp.concatenate([masked, extra], axis=1), keys_hot)
        norms, means = [], []
        for half in range(2):
            head = 2 * pair + half
            stats = own_stats[...]
            norms.append(jnp.sum(jnp.where(lane == head, stats, 0.0), axis=-1, keepdims=True))
            means.append(jnp.sum(jnp.where(lane == 16 + head, stats, 0.0), axis=-1, keepdims=True))
        probs = jnp.exp(scores - jnp.concatenate(norms, axis=0))
        prob_grad = dot_nt(both_halves(grad_own[:, cols], head_size, 1.0), v_all[:, cols])
        score_grad = probs * (prob_grad - jnp.concatenate(means, axis=0))
        keys_turned = jnp.concatenate([keys, hot_turned[...]], axis=1)
        back = dot_nn(score_grad.astype(narrow_type), keys_turned)
        offsets = []
        for half in range(2):
            parts = []
            for i in range(strip_rows):
                at = half * tokens + i * width
                piece = back[at : at + width]
                by_col = pltpu.roll(piece[:, lanes : 2 * lanes], 0, 1, stride=1, stride_axis=0)
                by_row = pltpu.roll(piece[:, 2 * lanes :], strip * strip_rows + i, 1)
                parts.append(jnp.concatenate([by_col, by_row], axis=1))
            offsets.append(jnp.concatenate(parts, axis=0))
        off = jnp.concatenate(offsets, axis=1).astype(narrow_type)
        plain = jnp.where(lane < head_size, back[:tokens, :lanes], back[tokens:, :lanes])
        query_grad = plain * scale + dot_nn(off, rel_all[...])
        joined[:, cols] = query_grad.astype(narrow_type)
        rel_grad[...] += dot_tn(off, queries)

    def own_keys(pair):
        at = pair * lanes
        cols = slice(at, at + lanes)
        all_queries = q_all[:, cols]
        wide_tab[...] = dot_nn(all_queries, tables[...])

        def widen(row, inner):
            rows = pl.ds(pl.multiple_of(row * width, width), width)
            for half in range(2):
                begin = 2 * half * lanes
                cols_extra[half, rows, :] = place_cols(wide_tab[rows, begin : begin + lanes], width)
                piece = wide_tab[rows, begin + lanes : begin + 2 * lanes]
                rows_extra[half, rows, :] = place_rows(piece, row, height)
            return inner

        lax.fori_loop(0, height, widen, 0)
        all_grads = grad_all[:, :, cols].reshape(total, lanes)
        hot_own = hot[own, :]
        blank = jnp.zeros((tokens, lanes), narrow_type)
        hot_col, hot_row = hot_own[:, :lanes], hot_own[:, lanes:]
        keys = both_halves(k_all[own, cols], head_size, scale)
        left = jnp.concatenate(
            [
                jnp.concatenate([hot_col, blank, hot_row, blank], axis=1),
                jnp.concatenate([blank, hot_col, blank, hot_row], axis=1),
            ],
            axis=0,
        )
        right = jnp.concatenate(
            [all_queries, cols_extra[0], cols_extra[1], rows_extra[0], rows_extra[1]], axis=1
        )
        scores = dot_nt(jnp.concatenate([keys, left], axis=1), right)
        prob_grad = dot_nt(both_halves(v_all[own, cols], head_size, 1.0), all_grads)
        probs, score_grads = [], []
        for half in range(2):
            head = 2 * pair + half
            here = slice(half * tokens, (half + 1) * tokens)
            prob = jnp.exp(scores[here] - stat_rows[head : head + 1, :])
            probs.append(prob.astype(narrow_type))
            score_grad = prob * (prob_grad[here] - stat_rows[16 + head : 17 + head, :])
            score_grads.append(score_grad.astype(narrow_type))
        key_both = dot_nn(jnp.concatenate(score_grads, axis=0), all_queries)
        value_both = dot_nn(jnp.concatenate(probs, axis=0), all_grads)
        key_grad = jnp.where(lane < head_size, key_both[:tokens], key_both[tokens:]) * scale
        value_grad = jnp.where(lane < head_size, value_both[:tokens], value_both[tokens:])
        joined[:, model + at : model + at + lanes] = key_grad.astype(narrow_type)
        joined[:, 2 * model + at : 2 * model + at + lanes] = value_grad.astype(narrow_type)

    hat, inverse = norm_parts(x_own[...].astype(wide_type))
    normed_turned = (hat * vec[0:1, :] + vec[1:2, :]).astype(narrow_type).T
    steps = gather.deep - 1
    progress = [0]

    def advance():
        if plan is not None:
            reducer.wave(progress[0])
            progress[0] += 1

    def near_grads(near, first):
        fold = near.shape[-1]
        own_count = model // 2**plan.stages
        lead = (slice(None),) * plan.stages
        parts = {}
        for f in range(near.shape[-2] // own_count):
            begin = first + f * fold
            value = dot_nn(normed_turned, joined[:, begin : begin + fold])
            parts[f] = value.reshape((2,) * plan.stages + (own_count, fold))
            if f % 2:
                both = jnp.concatenate([parts.pop(f - 1), parts.pop(f)], axis=plan.stages)
                rows = slice((f - 1) * own_count, (f + 1) * own_count)
                near[lead + (rows,)] = both.astype(narrow_type)

    advance()
    for pair in range(pairs):
        own_queries(pair)
        if pair < steps:
            gather.step(pair)
        advance()
    turned = pltpu.roll(rel_grad[2 * lanes :, :], head_size, 1)
    both = rel_grad[: 2 * lanes, :] + turned
    low = lane_ids((lanes, lanes)) < head_size
    rel_sum[...] = jnp.where(low, both[:lanes], pltpu.roll(both[lanes:], head_size, 1))
    if plan is not None:
        near_grads(near_query, 0)
        rel_sums.start()
        reducer.start_near(len(plan.shapes) - 2)
    gather.finish()
    for block in range(strips):
        stat_rows[:, block * tokens : (block + 1) * tokens] = stat_all[block]
    for pair in range(pairs):
        own_keys(pair)
        advance()
    if plan is not None:
        near_grads(near_rest, model)
        reducer.start_near(len(plan.shapes) - 1)
    back = jnp.zeros((tokens, model), wide_type)
    for j in range(3):
        cols = slice(j * model, (j + 1) * model)
        part = joined[:, cols]
        sums[j : j + 1, :] = column_sum(part.astype(wide_type))
        back = back + dot_nt(part, qkv_weight[:, cols])
        if plan is None:
            weight_grad[:, cols] = dot_nn(normed_turned, part).astype(narrow_type)
    sums[3:4, :] = column_sum(back * hat)
    sums[4:5, :] = column_sum(back)
    sums[5:8, :] = jnp.zeros((3, model), wide_type)
    if plan is not None:
        late_sums.start()
    input_grad[...] = middle_grad[...] + norm_back(hat, inverse, back * vec[0:1, :])
    if plan is None:
        return
    while progress[0] < plan.waves():
        advance()
    for small in (early_sums, rel_sums, late_sums):
        while small.stage < len(small.groups):
            small.step()
    sums_out[...] = sums[...]
    early_out[...] = early[...]
    rel_out[...] = rel_sum[...]
    reducer.finish()


def attention_backward(height, width, operands, small, arrays, plan, shares, call_id):
    tokens, model = operands[0].shape
    total = operands[1].shape[0]
    strips = total // tokens
    slots = StripGather.slots()

    def shape(rows, cols, kind):
        return jax.ShapeDtypeStruct((rows, cols), kind)

    outs = [shape(tokens, model, wide_type)]
    scratch = []
    extra = []
    if plan is None:
        outs += [
            shape(8, model, wide_type),
            shape(lanes, lanes, wide_type),
            shape(model, 3 * model, narrow_type),
        ]
    else:
        smalls = [(8, model), (16, model), (lanes, lanes)]
        outs += [shape(*dims, wide_type) for dims in smalls]
        outs += [flat for flat, _ in shares]
        shares = [share for _, share in shares]
        stages = plan.stages
        scratch += [
            pltpu.VMEM((2,) * stages + dims[1:], narrow_type) for dims in plan.shapes[-2:]
        ]
        scratch += [pltpu.VMEM(dims, wide_type) for dims in smalls]
        for dims, groups in zip(smalls, small_groups(plan)):
            slots_small = SmallReduce.sizes(groups)[1][-1]
            scratch += [
                pltpu.VMEM((slots_small,) + dims, wide_type),
                pltpu.SemaphoreType.DMA((slots_small,)),
                pltpu.SemaphoreType.DMA((slots_small,)),
            ]
        extra = plan.scratch()
    scratch += [
        pltpu.VMEM((tokens, 3 * model), narrow_type),
        pltpu.VMEM((total, 4 * lanes), wide_type),
        pltpu.VMEM((2, total, lanes), narrow_type),
        pltpu.VMEM((2, total, lanes), narrow_type),
        pltpu.VMEM((strips, tokens, model), narrow_type),
        pltpu.VMEM((strips, 32, tokens), wide_type),
        pltpu.VMEM((32, total), wide_type),
        pltpu.VMEM((4 * lanes, lanes), wide_type),
        pltpu.SemaphoreType.DMA((slots, 2)),
        pltpu.SemaphoreType.DMA((slots, 2)),
    ]

    def body(*refs):
        attention_backward_kernel(height, width, plan, shares, refs)

    given = operands + (small if plan is not None else ())
    far = plan.shaped(arrays) if plan is not None else []
    return pl.pallas_call(
        body,
        out_shape=outs,
        in_specs=vmem_specs(len(given)) + any_specs(len(far)),
        out_specs=vmem_specs(len(outs)),
        scratch_shapes=scratch + extra,
        compiler_params=pltpu.CompilerParams(
            collective_id=call_id, has_side_effects=True, vmem_limit_bytes=62 << 20
        ),
        name="attention_backward",
    )(*given, *far)


def finish_kernel(widths, refs):
    count = len(widths) - 1
    result, input_grad, late, early, rel_sum = refs[:5]
    flats = refs[5 : 5 + count]
    out = refs[5 + count :]
    out[0][...] = result[...]
    out = out[1:]
    sums = jnp.concatenate([late[...], early[...]], axis=0)
    out[0][...] = input_grad[...]
    for source, target in zip(flats, out[1 : 1 + count]):
        target[...] = source[: target.shape[0], : target.shape[1]]
    vectors, tables = out[1 + count : -5], out[-5:]
    for target, (rows, begin, size) in zip(vectors, widths[-1]):
        for j, row in enumerate(rows):
            value = sums[row : row + 1, begin : begin + size]
            if target.shape[0] < size:
                quarter = target.shape[0]
                parts = [value[:, k * quarter : (k + 1) * quarter] for k in range(size // quarter)]
                value = sum(parts[1:], parts[0])
            target[j * size : j * size + value.shape[1]] = value[0]
    half = rel_sum.shape[1] // 2
    rows, cols, lateral_gain, lateral_shift, output_gain = tables
    cols[...] = rel_sum[...].T[:half, : cols.shape[1]]
    rows[...] = rel_sum[: rows.shape[0], half:]
    channels = output_gain.shape[1]
    for k, table in enumerate((lateral_gain, lateral_shift, output_gain)):
        table[...] = sums[19:23, k * channels : (k + 1) * channels]


def finish(result, input_grad, smalls, flats, shapes, vectors, table_shapes):
    def wide(shape):
        return jax.ShapeDtypeStruct(shape, wide_type)

    outs = [jax.ShapeDtypeStruct(result.shape, narrow_type), wide(input_grad.shape)]
    outs += [wide(shape) for shape in shapes]
    for _, _, _, length in vectors:
        outs.append(wide((length,)))
    outs += [wide(shape) for shape in table_shapes]
    widths = [None] * len(flats) + [[vector[:3] for vector in vectors]]

    def body(*refs):
        finish_kernel(widths, refs)

    given = (result, input_grad, *smalls, *flats)
    return pl.pallas_call(
        body,
        out_shape=outs,
        in_specs=vmem_specs(len(given)),
        out_specs=vmem_specs(len(outs)),
        name="finish",
    )(*given)


def prepare_kernel(height, width, count, refs):
    vectors, (rel_rows, rel_cols, four) = refs[:count], refs[count : count + 3]
    vec, tables, rel_all, hot, hot_turned, four_pair, table = refs[count + 3 :]
    model = vec.shape[1]
    vec[...] = jnp.zeros_like(vec)
    at = 0
    for source in vectors:
        value = source[...].astype(wide_type)
        if len(source.shape) == 2:
            vec[at : at + value.shape[0], : value.shape[1]] = value
            at += value.shape[0]
            continue
        value = value.reshape(1, value.shape[0])
        size = value.shape[1]
        for begin in range(0, size, model):
            part = value[:, begin : begin + model]
            vec[at : at + 1, : part.shape[1]] = part
            at += 1
    half = lanes // 2
    tables[...] = jnp.zeros_like(tables)
    for i, source in enumerate((rel_cols, rel_rows)):
        size = source.shape[1]
        table[...] = jnp.zeros_like(table)
        table[:half, :size] = source[...].astype(wide_type)
        plain = table[...].T
        rel_all[i * lanes : (i + 1) * lanes, :] = plain.astype(narrow_type)
        moved = pltpu.roll(plain, half, 1).astype(narrow_type)
        rel_all[(2 + i) * lanes : (3 + i) * lanes, :] = moved
        row = lax.broadcasted_iota(jnp.int32, (lanes, lanes), 0)
        col = lax.broadcasted_iota(jnp.int32, (lanes, lanes), 1)
        mirror = (row + col == size - 1).astype(wide_type).astype(narrow_type)
        turned = dot_nn(table[...].astype(narrow_type), mirror)[:half].astype(narrow_type)
        tables[:half, i * lanes : (i + 1) * lanes] = turned
        tables[half:, (2 + i) * lanes : (3 + i) * lanes] = turned
    total = hot.shape[0]
    token = lax.broadcasted_iota(jnp.int32, (total, lanes), 0)
    lane = lax.broadcasted_iota(jnp.int32, (total, lanes), 1)
    key_row, key_col = lax.div(token, width), lax.rem(token, width)
    by_col = (lax.rem(lane, width) == key_col) & (lane < 2 * width)
    by_row = (lax.rem(lane, height) == key_row) & (lane < 2 * height)
    for i, (plain, turned) in enumerate(
        ((by_col, lane == width - 1 - key_col), (by_row, lane == height - 1 - key_row))
    ):
        here = slice(i * lanes, (i + 1) * lanes)
        hot[:, here] = plain.astype(wide_type).astype(narrow_type)
        hot_turned[:, here] = turned.astype(wide_type).astype(narrow_type)
    cols, rows = four.shape
    value = four[...].astype(wide_type).T.astype(narrow_type)
    four_pair[...] = jnp.zeros_like(four_pair)
    four_pair[:rows, :cols] = value
    four_pair[rows:, cols:] = value


def prepared_shapes(height, width, model, vectors, four):
    rows = 0
    for vector in vectors:
        rows += vector.shape[0] if len(vector.shape) == 2 else -(-vector.shape[0] // model)
    rows = -(-rows // 8) * 8
    total = height * width

    def shape(rows_out, cols, kind=narrow_type):
        return jax.ShapeDtypeStruct((rows_out, cols), kind)

    return [
        shape(rows, model, wide_type),
        shape(lanes, 4 * lanes),
        shape(4 * lanes, lanes),
        shape(total, 2 * lanes),
        shape(total, 2 * lanes),
        shape(2 * four.shape[1], 2 * four.shape[0]),
    ]


class Levels:
    def __init__(self, strip_rows, width):
        self.rows = (4 * strip_rows, 2 * strip_rows, strip_rows, strip_rows // 2)
        self.cols = (4 * width, 2 * width, width, width // 2)
        self.at, self.edge_at, self.wide_at = [], [], []
        total = edge = wide = 0
        for rows, cols in zip(self.rows, self.cols):
            self.at.append(total)
            self.edge_at.append(edge)
            self.wide_at.append(wide)
            total += rows * cols
            edge += cols
            wide += (rows + 2) * cols
        self.total, self.edge, self.wide = total, edge, wide


def put_strided(target, at, count, stride, value):
    for part in range(target.shape[0]):
        target[part, pl.ds(at, count, stride=stride), :] = value[:, part * lanes : (part + 1) * lanes]


def get_strided(source, at, count, stride):
    parts = [source[part, pl.ds(at, count, stride=stride), :] for part in range(source.shape[0])]
    return jnp.concatenate(parts, axis=1)


def join_parts(source, begin, end):
    return jnp.concatenate([source[part, begin:end, :] for part in range(source.shape[0])], axis=1)


def store_edges(levels, level, source, offset, top, bottom):
    rows, cols = levels.rows[level], levels.cols[level]
    at = levels.edge_at[level]
    top[at : at + cols, :] = source[offset : offset + cols, :]
    last = offset + (rows - 1) * cols
    bottom[at : at + cols, :] = source[last : last + cols, :]


def four_times(vec, row):
    value = vec[row : row + 1, :]
    quarter = value.shape[1] // 4
    low = jnp.where(lane_ids(value.shape) < quarter, value, 0.0)
    twice = low + pltpu.roll(low, quarter, 1)
    return twice + pltpu.roll(twice, 2 * quarter, 1)


def level_source_kernel(
    levels,
    strip_rows,
    width,
    base,
    y,
    vec,
    first,
    second,
    eight,
    lat_four,
    lat_eight,
    lat_sixteen,
    lat_thirty,
    lateral,
    top,
    bottom,
    first_map,
    active,
    source_zero,
    source_one,
    pooled,
    reduced,
    spread_zero,
    spread_one,
    wide_y,
):
    tokens, model = y.shape
    out = lat_sixteen.shape[0]
    mid = first.shape[1] // 4
    values = y[...]

    def finish(level, value, at):
        reduced[at : at + value.shape[0], :] = value
        hat, _ = norm_parts(value)
        gain = vec[base + 5 + level : base + 6 + level, :out]
        shift = vec[base + 9 + level : base + 10 + level, :out]
        return hat * gain + shift

    for tap in range(4):
        a, b = tap // 2, tap % 2
        cols = slice(tap * mid, (tap + 1) * mid)
        rows = slice(tap * tokens, (tap + 1) * tokens)
        mapped = dot_nn(values, first[:, cols]) + vec[base : base + 1, :mid]
        first_map[:, cols] = mapped
        hat, _ = norm_parts(mapped)
        normed = hat * vec[base + 1 : base + 2, :mid] + vec[base + 2 : base + 3, :mid]
        act = (normed * normal_cdf(normed)).astype(narrow_type)
        active[rows, :] = act
        source = (dot_nt(act, second[...]) + four_times(vec, base + 3)).astype(narrow_type)
        source_zero[rows, :] = source
        half = source.shape[1] // 2
        for pair in range(2):
            both = dot_nt(source[:, pair * half : (pair + 1) * half], lat_four[...])
            for side in range(2):
                place = (4 * tap + 2 * pair + side) * tokens
                value = finish(0, both[:, side * out : (side + 1) * out], place)
                for i in range(strip_rows):
                    at = (4 * i + 2 * a + pair) * levels.cols[0] + 2 * b + side
                    put_strided(spread_zero, at, width, 4, value[i * width : (i + 1) * width])
        mapped = dot_nn(values, eight[:, cols]) + vec[base + 4 : base + 5, :mid]
        source = mapped.astype(narrow_type)
        source_one[rows, :] = source
        value = finish(1, dot_nt(source, lat_eight[...]), levels.at[1] + tap * tokens)
        for i in range(strip_rows):
            at = (2 * i + a) * levels.cols[1] + b
            put_strided(spread_one, at, width, 2, value[i * width : (i + 1) * width])
    for target, begin, end in ((spread_zero, 0, levels.at[1]), (spread_one, *levels.at[1:3])):
        joined = join_parts(target, 0, end - begin)
        lateral[begin:end, :] = joined.astype(narrow_type)
    value = finish(2, dot_nt(values, lat_sixteen[...]), levels.at[2])
    lateral[levels.at[2] : levels.at[3], :] = value.astype(narrow_type)
    for part in range(model // lanes):
        wide_y[part] = values[:, part * lanes : (part + 1) * lanes].astype(wide_type)
    quarter = width // 2
    for i in range(strip_rows // 2):
        summed = 0.0
        for a in range(2):
            for b in range(2):
                at = (2 * i + a) * width + b
                summed = summed + get_strided(wide_y, at, quarter, 2)
        pooled[i * quarter : (i + 1) * quarter, :] = (summed * 0.25).astype(narrow_type)
    value = finish(3, dot_nt(pooled[...], lat_thirty[...]), levels.at[3])
    lateral[levels.at[3] : levels.total, :] = value.astype(narrow_type)
    for level in range(4):
        store_edges(levels, level, lateral, levels.at[level], top, bottom)


class EdgeExchange:
    def __init__(self, top, bottom, above, below, send_sem, recv_sem):
        strip, scale = strip_index(), lax.axis_size("scale")
        count = lax.axis_size("rows") * scale

        def place(index):
            return {"rows": lax.div(index, scale), "scale": lax.rem(index, scale)}

        self.has_up, self.has_down = strip > 0, strip < count - 1
        self.up = place(jnp.maximum(strip - 1, 0))
        self.down = place(jnp.minimum(strip + 1, count - 1))
        self.above, self.below = above, below

        def send(source, target, i, device):
            return pltpu.make_async_remote_copy(
                src_ref=source,
                dst_ref=target,
                send_sem=send_sem.at[i],
                recv_sem=recv_sem.at[i],
                device_id=device,
                device_id_type=MESH_ID,
            )

        self.lower = send(bottom, above, 0, self.down)
        self.upper = send(top, below, 1, self.up)

    def greet(self, barrier):
        @pl.when(self.has_up)
        def _():
            pl.semaphore_signal(barrier, inc=1, device_id=self.up, device_id_type=MESH_ID)

        @pl.when(self.has_down)
        def _():
            pl.semaphore_signal(barrier, inc=1, device_id=self.down, device_id_type=MESH_ID)

        return jnp.where(self.has_up, 1, 0) + jnp.where(self.has_down, 1, 0)

    def send(self):
        @pl.when(jnp.logical_not(self.has_up))
        def _():
            self.above[...] = jnp.zeros_like(self.above)

        @pl.when(jnp.logical_not(self.has_down))
        def _():
            self.below[...] = jnp.zeros_like(self.below)

        @pl.when(self.has_down)
        def _():
            self.lower.start()

        @pl.when(self.has_up)
        def _():
            self.upper.start()

    def arrive(self):
        @pl.when(self.has_down)
        def _():
            self.lower.wait_send()
            self.upper.wait_recv()

        @pl.when(self.has_up)
        def _():
            self.upper.wait_send()
            self.lower.wait_recv()


def tile_start(index):
    return index if isinstance(index, int) else pl.multiple_of(index, 32)


def widen_rows(levels, level, source, at, first, count, padded, slab, offset):
    cols = levels.cols[level]
    channels = source.shape[1]
    size = count * cols
    padded[8 : 8 + size, :] = source[at : at + size, :].astype(wide_type)
    block = min(256, size)

    def step(i, carry):
        begin = tile_start(i * block)
        got = padded[pl.ds(begin, block + 16), :]
        col = lax.rem(begin + lax.broadcasted_iota(jnp.int32, (block, channels), 0), cols)
        left = jnp.where(col > 0, got[7 : 7 + block], 0.0)
        right = jnp.where(col < cols - 1, got[9 : 9 + block], 0.0)
        joined = jnp.concatenate([left, got[8 : 8 + block], right], axis=1)
        slab[pl.ds(tile_start(offset + first * cols + begin), block), :] = joined.astype(narrow_type)
        return carry

    if size == block:
        step(0, 0)
    else:
        lax.fori_loop(0, size // block, step, 0)


def widen_own(levels, level, source, padded, slab, offset):
    rows = levels.rows[level]
    widen_rows(levels, level, source, levels.at[level], 1, rows, padded, slab, offset)


def widen_edges(levels, level, above, below, padded, slab, offset):
    at, rows = levels.edge_at[level], levels.rows[level]
    widen_rows(levels, level, above, at, 0, 1, padded, slab, offset)
    widen_rows(levels, level, below, at, rows + 1, 1, padded, slab, offset)


def inner_first(size, block, cols, step, arrive):
    count = size // block
    if count > 2 and block >= cols:
        lax.fori_loop(1, count - 1, step, 0)
        arrive()
        step(0, 0)
        step(count - 1, 0)
    else:
        arrive()
        lax.fori_loop(0, count, step, 0)


def smooth_kernel(
    levels,
    base,
    lateral,
    edges,
    weight,
    smooth,
    vec,
    grads,
    top,
    bottom,
    slabs,
    gain_sums,
    padded,
):
    channels = lateral.shape[1]
    above, below = edges.above, edges.below
    gain_sums[...] = jnp.zeros_like(gain_sums)
    for level in range(4):
        rows, cols = levels.rows[level], levels.cols[level]
        offset = levels.wide_at[level]
        widen_own(levels, level, lateral, padded, slabs, offset)

        def arrive():
            if level == 0:
                edges.arrive()
            widen_edges(levels, level, above, below, padded, slabs, offset)

        size = rows * cols
        block = min(256, size)
        gain = vec[base + 13 + level : base + 14 + level, :channels]

        def step(i, carry):
            begin = tile_start(i * block)
            total = None
            for a in range(3):
                window = slabs[pl.ds(tile_start(offset + a * cols + begin), block), :]
                part = dot_nn(
                    window, smooth[level, 3 * a * channels : 3 * (a + 1) * channels, :]
                )
                total = part if total is None else total + part
            hat, inverse = norm_parts(total)
            here = pl.ds(tile_start(levels.at[level] + begin), block)
            upstream = weight[here, :].astype(wide_type)
            gain_sums[level : level + 1, :] += column_sum(upstream * hat)
            grads[here, :] = norm_back(hat, inverse, upstream * gain).astype(narrow_type)
            return carry

        inner_first(size, block, cols, step, arrive)
        store_edges(levels, level, grads, levels.at[level], top, bottom)


def level_back_kernel(levels, strip_rows, width, base, reducer, edges, given, outs, scratch, done):
    (
        grads,
        slabs,
        reduced,
        first_map,
        active,
        source_zero,
        source_one,
        pooled,
        y,
        vec,
        smooth,
        first,
        second,
        eight,
        lat_four,
        lat_eight,
        lat_sixteen,
        lat_thirty,
    ) = given
    y_grad, sums, smooth_grad, first_grad, eight_grad, *rest = outs
    if reducer is not None:
        (rest_grad,) = rest
        plan, own = reducer.plan, smooth_grad.shape[-2]
    else:
        rest_grad, plan = None, None
        second_grad, lat_four_grad, lat_eight_grad, lat_sixteen_grad, lat_thirty_grad = rest
    padded, slab, spread, second_sum, four_sum, eight_sum, total_grad, pool_grad = scratch
    tokens, model = y.shape
    channels = grads.shape[1]
    mid = first.shape[1] // 4
    above, below = edges.above, edges.below
    sums[...] = jnp.zeros_like(sums)

    def smooth_weights(level):
        rows, cols = levels.rows[level], levels.cols[level]
        size = rows * cols
        turned = grads[levels.at[level] : levels.at[level] + size, :].T
        for a in range(3):
            begin = levels.wide_at[level] + a * cols
            for b in range(3):
                part = dot_nn(turned, slabs[begin : begin + size, b * channels : (b + 1) * channels])
                part = part.T.astype(narrow_type)
                at = (level * 9 + 3 * a + b) * channels
                if plan is None:
                    smooth_grad[at : at + channels, :] = part
                    continue
                done = 0
                while done < channels:
                    device, row = divmod(at + done, own)
                    count = min(channels - done, own - row)
                    lead = tuple((device >> (plan.stages - 1 - d)) & 1 for d in range(plan.stages))
                    smooth_grad[lead + (slice(row, row + count),)] = part[done : done + count]
                    done += count

    def smooth_back(level):
        rows, cols = levels.rows[level], levels.cols[level]
        size = rows * cols
        widen_own(levels, level, grads, padded, slab, 0)
        block = min(256, size)

        def arrive():
            if level == 0:
                if plan is not None:
                    reducer.wave(0)
                edges.arrive()
            widen_edges(levels, level, above, below, padded, slab, 0)

        def step(i, carry):
            begin = tile_start(i * block)
            total = None
            for a in range(3):
                for b in range(3):
                    window = slab[
                        pl.ds(tile_start((2 - a) * cols + begin), block),
                        (2 - b) * channels : (3 - b) * channels,
                    ]
                    tap = (3 * a + b) * channels
                    part = dot_nt(window, smooth[level, tap : tap + channels, :])
                    total = part if total is None else total + part
            for part in range(channels // lanes):
                here = total[:, part * lanes : (part + 1) * lanes]
                spread[part, pl.ds(begin, block), :] = here
            return carry

        inner_first(size, block, cols, step, arrive)

    def reduced_back(level, upstream, at):
        hat, inverse = norm_parts(reduced[at : at + upstream.shape[0], :])
        gain = vec[base + 5 + level : base + 6 + level, :channels]
        sums[5 + level : 6 + level, :channels] += column_sum(upstream * hat)
        sums[9 + level : 10 + level, :channels] += column_sum(upstream)
        return norm_back(hat, inverse, upstream * gain).astype(narrow_type)

    def keep_tap(target, tap, parts, value):
        if len(target.shape) == 2:
            target[:, tap * mid : (tap + 1) * mid] = value.astype(narrow_type)
        else:
            fold_store(target, tap, parts, value)

    first_parts, eight_parts = {}, {}
    turned_y = y[...].T
    total_grad[...] = jnp.zeros_like(total_grad)
    for level in range(4):
        smooth_weights(level)
    if plan is not None:
        reducer.start_near(0)
    smooth_back(0)
    for tap in range(4):
        a, b = tap // 2, tap % 2
        cols = slice(tap * mid, (tap + 1) * mid)
        rows = slice(tap * tokens, (tap + 1) * tokens)
        parts = []
        for pair in range(2):
            sides = []
            for side in range(2):
                pieces = []
                for i in range(strip_rows):
                    at = (4 * i + 2 * a + pair) * levels.cols[0] + 2 * b + side
                    pieces.append(get_strided(spread, at, width, 4))
                upstream = jnp.concatenate(pieces, axis=0)
                sides.append(reduced_back(0, upstream, (4 * tap + 2 * pair + side) * tokens))
            both = jnp.concatenate(sides, axis=1)
            half = source_zero.shape[1] // 2
            product = dot_tn(both, source_zero[rows, pair * half : (pair + 1) * half])
            if tap == 0 and pair == 0:
                four_sum[...] = product
            else:
                four_sum[...] += product
            parts.append(dot_nn(both, lat_four[...]).astype(narrow_type))
        second_low = jnp.concatenate(parts, axis=1)
        sums[3:4, :] += column_sum(second_low.astype(wide_type))
        product = dot_tn(second_low, active[rows, :])
        if tap == 0:
            second_sum[...] = product
        else:
            second_sum[...] += product
        active_grad = dot_nn(second_low, second[...])
        hat, inverse = norm_parts(first_map[:, cols])
        gain = vec[base + 1 : base + 2, :mid]
        normed = hat * gain + vec[base + 2 : base + 3, :mid]
        normed_grad = active_grad * gelu_slope(normed)
        sums[1:2, :mid] += column_sum(normed_grad * hat)
        sums[2:3, :mid] += column_sum(normed_grad)
        first_low = norm_back(hat, inverse, normed_grad * gain).astype(narrow_type)
        sums[0:1, :mid] += column_sum(first_low.astype(wide_type))
        keep_tap(first_grad, tap, first_parts, dot_nn(turned_y, first_low))
        total_grad[...] += dot_nt(first_low, first[:, cols])
    done(first_grad)
    quarter = lat_four.shape[1] // 2
    if rest_grad is None:
        second_grad[...] = second_sum[...].astype(narrow_type)
        lat_four_grad[...] = (
            four_sum[:channels, :quarter] + four_sum[channels:, quarter:]
        ).astype(narrow_type)
    smooth_back(1)
    for tap in range(4):
        a, b = tap // 2, tap % 2
        cols = slice(tap * mid, (tap + 1) * mid)
        rows = slice(tap * tokens, (tap + 1) * tokens)
        pieces = []
        for i in range(strip_rows):
            at = (2 * i + a) * levels.cols[1] + b
            pieces.append(get_strided(spread, at, width, 2))
        upstream = jnp.concatenate(pieces, axis=0)
        low = reduced_back(1, upstream, levels.at[1] + tap * tokens)
        product = dot_tn(low, source_one[rows, :])
        if tap == 0:
            eight_sum[...] = product
        else:
            eight_sum[...] += product
        eight_low = dot_nn(low, lat_eight[...]).astype(narrow_type)
        sums[4:5, :mid] += column_sum(eight_low.astype(wide_type))
        keep_tap(eight_grad, tap, eight_parts, dot_nn(turned_y, eight_low))
        total_grad[...] += dot_nt(eight_low, eight[:, cols])
    done(eight_grad)
    if rest_grad is None:
        lat_eight_grad[...] = eight_sum[...].astype(narrow_type)
    smooth_back(2)
    low = reduced_back(2, join_parts(spread, 0, tokens), levels.at[2])
    sixteen = dot_tn(low, y[...])
    if rest_grad is None:
        lat_sixteen_grad[...] = sixteen.astype(narrow_type)
    total_grad[...] += dot_nn(low, lat_sixteen[...])
    smooth_back(3)
    low = reduced_back(3, join_parts(spread, 0, tokens // 4), levels.at[3])
    thirty = dot_tn(low, pooled[...])
    if rest_grad is None:
        lat_thirty_grad[...] = thirty.astype(narrow_type)
    else:
        count = rest_grad.shape[0]
        turned = pltpu.roll(four_sum[channels:, :], quarter, 1)
        both = four_sum[:channels, :] + turned
        four = jnp.where(lane_ids(both.shape) < quarter, both, 0.0)
        for part in range(mid // lanes):
            here = slice(part * lanes, (part + 1) * lanes)
            pieces = [second_sum[:, here]]
            for value in (sixteen, thirty):
                for half in range(2):
                    at = half * mid + part * lanes
                    pieces.append(value[:, at : at + lanes])
            pieces += [eight_sum[:, here], four[:, here]]
            pieces = [piece.reshape(count, piece.shape[0] // count, lanes) for piece in pieces]
            used = sum(piece.shape[1] for piece in pieces)
            pieces.append(jnp.zeros((count, rest_grad.shape[1] - used, lanes), wide_type))
            rest_grad[:, :, here] = jnp.concatenate(pieces, axis=1).astype(narrow_type)
    for target in rest:
        done(target)
    pooled_grad = dot_nn(low, lat_thirty[...]) * 0.25
    count = width // 2
    for i in range(strip_rows // 2):
        piece = pooled_grad[i * count : (i + 1) * count]
        for a in range(2):
            for b in range(2):
                at = (2 * i + a) * width + b
                put_strided(pool_grad, at, count, 2, piece)
    y_grad[...] = (total_grad[...] + join_parts(pool_grad, 0, tokens)).astype(narrow_type)
    if plan is not None:
        for number in range(1, plan.waves()):
            reducer.wave(number)


def region_weights(levels, strip_rows, width, roi, anchors, weight):
    scale = lax.axis_index("scale")
    channels = weight.shape[1]
    ones = jnp.ones((1, channels), narrow_type)

    def own(rows, count):
        shape = (count, rows.shape[0])
        wanted = lax.broadcasted_iota(jnp.int32, shape, 0) + scale * count
        pick = (lax.broadcasted_iota(jnp.int32, shape, 1) == wanted).astype(wide_type)
        rows = rows.astype(wide_type).astype(narrow_type)
        return dot_nn(pick.astype(narrow_type), rows)

    region = own(roi[0], strip_rows).astype(narrow_type)
    for level in range(4):
        rows, cols = levels.rows[level], levels.cols[level]
        shape = (width, cols)
        patch = lax.broadcasted_iota(jnp.int32, shape, 0)
        cell = lax.broadcasted_iota(jnp.int32, shape, 1)
        cell = lax.div(cell, cols // width) if level < 3 else 2 * cell
        spread = (patch == cell).astype(wide_type).astype(narrow_type)
        regions = dot_nn(region, spread)
        positives = own(anchors[level][0], rows)
        for row in range(rows):
            patch_row = row * strip_rows // rows
            factor = positives[row : row + 1] + regions[patch_row : patch_row + 1]
            wide = dot_tn(factor.astype(narrow_type), ones)
            at = levels.at[level] + row * cols
            here = slice(at, at + cols)
            weight[here, :] = (weight[here, :].astype(wide_type) * wide).astype(narrow_type)


def pyramid_kernel(levels, strip_rows, width, base, plan, count, refs):
    y, vec, roi, *anchors = refs[:7]
    far, cotans, refs = refs[7:15], refs[15:19], refs[19:]
    y_grad, sums, gain_sums = refs[:3]
    far_outs, left, scratch = refs[3 : 3 + count], [], refs[3 + count :]
    if plan is not None:
        left, scratch = scratch[: len(plan.pieces)], scratch[len(plan.pieces) :]
    near, scratch = scratch[:9], scratch[9:]
    near_outs, scratch = scratch[:count], scratch[count:]
    sems, smooth_grad = scratch[:2]
    lateral, first_map, active, source_zero, source_one, pooled, reduced = scratch[2:9]
    grads, slabs, spread_one = scratch[9:12]
    edge_refs, scratch = scratch[12:24], scratch[24:]
    work, scratch = scratch[:8], scratch[8:]
    copies = [
        pltpu.make_async_copy(source, target, sems.at[i])
        for i, (source, target) in enumerate(zip(far, near))
    ]
    weight = near[8]
    given = []
    for level, source in enumerate(cotans):
        rows, cols = levels.rows[level], levels.cols[level]
        for row in range(rows):
            at = levels.at[level] + row * cols
            view = source.at[0, lax.axis_index("scale") * rows + row]
            semaphore = sems.at[9 + count + len(given)]
            given.append(pltpu.make_async_copy(view, weight.at[at : at + cols], semaphore))
    for copy in copies + given:
        copy.start()
    first, second, lat_four, eight, lat_eight, lat_sixteen, lat_thirty, smooth, weight = near
    edges, edges_back = [EdgeExchange(*edge_refs[6 * i : 6 * i + 6]) for i in range(2)]
    barrier = pltpu.get_barrier_semaphore()
    greeted = edges.greet(barrier)
    reducer = None
    if plan is not None:
        reducer = Reducer(plan, [smooth_grad], [dict(enumerate(left))], scratch)
        greeted = greeted + reducer.greet(barrier)
    for copy in copies[:7]:
        copy.wait()
    padded, _, spread, _, _, _, _, pool_grad = work
    top, bottom = edge_refs[:2]
    level_source_kernel(
        levels,
        strip_rows,
        width,
        base,
        y,
        vec,
        first,
        second,
        eight,
        lat_four,
        lat_eight,
        lat_sixteen,
        lat_thirty,
        lateral,
        top,
        bottom,
        first_map,
        active,
        source_zero,
        source_one,
        pooled,
        reduced,
        spread,
        spread_one,
        pool_grad,
    )
    pl.semaphore_wait(barrier, greeted)
    edges.send()
    for copy in copies[7:] + given:
        copy.wait()
    region_weights(levels, strip_rows, width, roi, anchors, weight)
    top, bottom = edge_refs[6:8]
    smooth_kernel(
        levels,
        base,
        lateral,
        edges,
        weight,
        smooth,
        vec,
        grads,
        top,
        bottom,
        slabs,
        gain_sums,
        padded,
    )
    edges_back.send()
    backs = []

    def done(target):
        for i, near_out in enumerate(near_outs):
            if near_out is target:
                backs.append(pltpu.make_async_copy(target, far_outs[i], sems.at[9 + i]))
                backs[-1].start()

    given = (grads, slabs, reduced, first_map, active, source_zero, source_one, pooled, y, vec)
    weights = (smooth, first, second, eight, lat_four, lat_eight, lat_sixteen, lat_thirty)
    outs = (y_grad, sums, smooth_grad, *near_outs)
    if plan is None:
        outs = (y_grad, sums, near_outs[-1], *near_outs[:-1])
    level_back_kernel(
        levels, strip_rows, width, base, reducer, edges_back, given + weights, outs, work, done
    )
    if plan is None:
        done(near_outs[-1])
    for copy in backs:
        copy.wait()
    if plan is not None:
        reducer.finish()


def pyramid(levels, strip_rows, width, base, y, vec, maps, weights, cotans, devices, plan, call_id):
    first, second, four_pair, eight, lat_eight, lat_sixteen, lat_thirty, smooth = weights
    tokens, model = y.shape
    channels = smooth.shape[2]
    mid = first.shape[1] // 4

    def shape(rows, cols, kind=narrow_type):
        return jax.ShapeDtypeStruct((rows, cols), kind)

    outs = [shape(tokens, model), shape(16, model, wide_type), shape(8, channels, wide_type)]
    total = smooth.shape[0] * smooth.shape[1]
    if devices:
        folded = (devices, first.shape[0] // devices * 4, mid)
        rows = second.shape[0] // devices + channels // devices * 6
        rest = (devices, -(-rows // 16) * 16, mid)
        far = [jax.ShapeDtypeStruct(dims, narrow_type) for dims in (folded, folded, rest)]
        smooth_dims = (2,) * plan.stages + (total // devices, channels)
        left = [jax.ShapeDtypeStruct(plan.left(t), narrow_type) for t in range(len(plan.pieces))]
    else:
        far = [
            shape(*first.shape),
            shape(*eight.shape),
            shape(*second.shape),
            shape(channels, four_pair.shape[1] // 2),
            shape(*lat_eight.shape),
            shape(*lat_sixteen.shape),
            shape(*lat_thirty.shape),
            shape(total, channels),
        ]
        smooth_dims = (16, lanes)
        left = []
    count = len(far)

    def body(*refs):
        pyramid_kernel(levels, strip_rows, width, base, plan, count, refs)

    def vmem(rows, cols, kind=narrow_type):
        return pltpu.VMEM((rows, cols), kind)

    size = levels.rows[0] * levels.cols[0]
    edge = [vmem(levels.edge, channels)] * 4 + [pltpu.SemaphoreType.DMA((2,))] * 2
    scratch = [pltpu.VMEM(weight_in.shape, narrow_type) for weight_in in weights]
    scratch.append(vmem(levels.total, channels))
    scratch += [pltpu.VMEM(out.shape, narrow_type) for out in far]
    scratch += [
        pltpu.SemaphoreType.DMA((9 + count + sum(levels.rows),)),
        pltpu.VMEM(smooth_dims, narrow_type),
        vmem(levels.total, channels),
        vmem(tokens, 4 * mid, wide_type),
        vmem(4 * tokens, mid),
        vmem(4 * tokens, second.shape[0]),
        vmem(4 * tokens, mid),
        vmem(tokens // 4, model),
        vmem(levels.total, channels, wide_type),
        vmem(levels.total, channels),
        vmem(levels.wide, 3 * channels),
        pltpu.VMEM((channels // lanes, levels.at[2] - levels.at[1], lanes), wide_type),
    ]
    scratch += edge + edge
    scratch += [
        vmem(size + 16, channels, wide_type),
        vmem(size + 2 * levels.cols[0], 3 * channels),
        pltpu.VMEM((channels // lanes, size, lanes), wide_type),
        pltpu.VMEM(second.shape, wide_type),
        pltpu.VMEM(four_pair.shape, wide_type),
        pltpu.VMEM(lat_eight.shape, wide_type),
        vmem(tokens, model, wide_type),
        pltpu.VMEM((model // lanes, tokens, lanes), wide_type),
    ]
    if plan is not None:
        scratch += plan.scratch()
    return pl.pallas_call(
        body,
        out_shape=outs + far + left,
        in_specs=vmem_specs(2 + len(maps)) + any_specs(len(weights) + len(cotans)),
        out_specs=vmem_specs(3) + any_specs(count) + vmem_specs(len(left)),
        scratch_shapes=scratch,
        compiler_params=pltpu.CompilerParams(
            collective_id=call_id, has_side_effects=True, vmem_limit_bytes=62 << 20
        ),
        name="pyramid",
    )(y, vec, *maps, *weights, *cotans)


def on_device(
    block_input,
    pre_gain,
    pre_shift,
    qkv_weight,
    qv_bias,
    rel_rows,
    rel_cols,
    proj_weight,
    proj_bias,
    mid_gain,
    mid_shift,
    fc1_weight,
    fc1_bias,
    fc2_weight,
    fc2_bias,
    deconv_first,
    first_bias,
    upnorm_gain,
    upnorm_shift,
    deconv_second,
    second_bias,
    deconv_eight,
    eight_bias,
    lateral_four,
    lateral_eight,
    lateral_sixteen,
    lateral_thirty,
    lateral_gain,
    lateral_shift,
    smooth_weight,
    output_gain,
    grad_four,
    grad_eight,
    grad_sixteen,
    grad_thirty,
    anchor_four,
    anchor_eight,
    anchor_sixteen,
    anchor_thirty,
    roi_mask,
):
    _, strip_rows, width, model = block_input.shape
    head_size = rel_rows.shape[1]
    tokens = strip_rows * width
    height = strip_rows * lax.axis_size(("rows", "scale"))
    channels = smooth_weight.shape[2]
    ff = fc1_weight.shape[1]
    mid = first_bias.shape[0]
    quarter = second_bias.shape[0]
    levels = Levels(strip_rows, width)
    devices = lax.axis_size(("img", "rows", "scale"))
    fused = devices if (model // devices) % 8 == 0 and height <= 16 else 0
    x_own = block_input.reshape(tokens, model)

    base = 8 + ff // model
    (
        vec,
        tables,
        rel_all,
        hot,
        hot_turned,
        lat_four_pair,
        q_all,
        k_all,
        v_all,
        attended,
        attended_wide,
        log_norm,
        middle,
        normed_mid,
        hidden_pre,
        hidden,
        result,
    ) = block_forward(
        height,
        width,
        x_own,
        (
            pre_gain,
            pre_shift,
            qv_bias,
            proj_bias,
            mid_gain,
            mid_shift,
            fc2_bias,
            fc1_bias,
            first_bias,
            upnorm_gain,
            upnorm_shift,
            second_bias,
            eight_bias,
            lateral_gain,
            lateral_shift,
            output_gain,
        ),
        (rel_rows.T, rel_cols.T, lateral_four.T),
        (qkv_weight, proj_weight, fc1_weight, fc2_weight),
        2,
    )
    smooth_plan = None
    if fused:
        rows = smooth_weight.shape[0] * smooth_weight.shape[1] // devices
        smooth_shape = (devices, rows, channels)
        stages = len(halving_dims())
        cut = -(-rows // 32) * 16
        smooth_cuts = [(0, 0, cut, "x"), (0, cut, rows - cut, "y")]
        smooth_plan = ReducePlan(
            [smooth_shape], [piece + (0, 0, (0, 1)) for piece in smooth_cuts], near=(0,)
        )
    result_grad, level_sums, gain_sums, first_grad, eight_grad, *rest_grads = pyramid(
        levels,
        strip_rows,
        width,
        base,
        result,
        vec,
        (roi_mask, anchor_four, anchor_eight, anchor_sixteen, anchor_thirty),
        (
            deconv_first,
            deconv_second,
            lat_four_pair,
            deconv_eight,
            lateral_eight,
            lateral_sixteen,
            lateral_thirty,
            smooth_weight,
        ),
        (grad_four, grad_eight, grad_sixteen, grad_thirty),
        fused,
        smooth_plan,
        1,
    )
    if fused:
        smooth_rows = smooth_weight.shape[0] * smooth_weight.shape[1] // devices
    else:
        *rest_grads, smooth_grad = rest_grads
    names, final = [], []

    def share(shares, shapes, name, source, weight_in, begin=0):
        rows, columns = weight_in
        own, width_in = rows // devices, shapes[source][-1]
        names.append(name)
        if columns % lanes:
            flat = jax.ShapeDtypeStruct((own, width_in), wide_type)
            places = [(begin, own, 0, 0)]
            final.append((own, columns))
        else:
            tiles = columns // lanes
            flat = jax.ShapeDtypeStruct((own * tiles, lanes), wide_type)
            places = [
                (begin + f * own, own, f * width_in // lanes, tiles)
                for f in range(max(columns // width_in, 1))
            ]
            final.append((own * tiles, lanes))
        shares.append((flat, (source, places)))
        return begin + own * max(columns // width_in, 1)

    if fused:
        rest_grad, *smooth_left = rest_grads
    (
        middle_grad,
        attended_grad,
        stats,
        stat_rows,
        block_sums,
        fc1_sum,
        proj_grad,
        fc1_grad,
        fc2_grad,
    ) = block_backward(
        result_grad,
        (hidden_pre, hidden, normed_mid, middle, attended, attended_wide),
        log_norm,
        vec,
        proj_weight,
        fc1_weight,
        fc2_weight,
        fused,
    )
    operands = (
        x_own,
        q_all,
        k_all,
        v_all,
        attended_grad,
        stats,
        stat_rows,
        middle_grad,
        vec,
        tables,
        rel_all,
        hot,
        hot_turned,
        qkv_weight,
    )
    small_operands = (block_sums, fc1_sum, level_sums, gain_sums)
    if fused:
        arrays = (
            fc1_grad,
            fc2_grad.reshape(devices, -1, model),
            proj_grad,
            first_grad,
            eight_grad,
            rest_grad,
            *smooth_left,
        )
        shapes = [array.shape for array in arrays]
        query, keys = len(shapes), len(shapes) + 1
        own = model // devices
        shapes.append((devices, own * (model // mid), mid))
        shapes.append((devices, own * (2 * model // mid), mid))

        def half(source, part):
            size = shapes[source][1]
            first = -(-size // 32) * 16
            return (source, 0, first) if part == 0 else (source, first, size - first)

        def whole(source):
            return (source, 0, shapes[source][-2])

        pieces = [
            (6, *smooth_cuts[0][1:], 0, 2, (2, 4, 6)),
            (7, *smooth_cuts[1][1:], 6, 2, (9, 12, 18)),
            (*whole(3), "z", 0, 0, (5, 8, 11, 13, 22)),
            (*whole(4), "z", 0, 0, (7, 11, 15, 29, 37)),
            (*half(1, 1), "y", 0, 0, (1, 5, 7, 9, 12)),
            (*whole(5), "x", 0, 0, (8, 12, 19, 23, 30)),
            (*whole(query), "z", 0, 0, (11, 14, 28, 34, 39)),
            (*whole(2), "x", 0, 0, (11, 17, 31, 36, 41)),
            (*half(0, 1), "y", 0, 0, (3, 7, 10, 12, 16)),
            (*half(1, 0), "y", 0, 0, (6, 10, 12, 20, 26)),
            (*half(0, 0), "y", 0, 0, (9, 12, 21, 27, 33)),
            (*half(keys, 0), "x", 0, 0, (13, 25, 35, 40, 43)),
            (*half(keys, 1), "y", 0, 0, (13, 24, 32, 38, 42)),
        ]
        plan = ReducePlan(shapes, pieces, near=(query, keys))
        plan.riders = (12, 4, 6)
        shares = []
        tiles = channels // lanes
        names.append("smooth")
        final.append((rows * tiles, lanes))
        flat = jax.ShapeDtypeStruct((rows * tiles, lanes), wide_type)
        places = [(0, rows, 0, tiles)]
        shares.append((flat, [(6, places), (7, places)]))
        share(shares, shapes, "first", 3, deconv_first.shape)
        share(shares, shapes, "eight", 4, deconv_eight.shape)
        share(shares, shapes, "fc1", 0, fc1_weight.shape)
        share(shares, shapes, "fc2", 1, fc2_weight.shape)
        share(shares, shapes, "proj", 2, proj_weight.shape)
        at = 0
        for name, weight_in in (
            ("second", deconv_second),
            ("lat_sixteen", lateral_sixteen),
            ("lat_thirty", lateral_thirty),
            ("lat_eight", lateral_eight),
            ("lat_four", lateral_four),
        ):
            at = share(shares, shapes, name, 5, weight_in.shape, at)
        tiles = 3 * model // lanes
        names.append("qkv")
        final.append((own * tiles, lanes))
        flat = jax.ShapeDtypeStruct((own * tiles, lanes), wide_type)
        folds = [(own, f * mid // lanes, tiles) for f in range(3 * model // mid)]
        count = model // mid
        of_query = [(f * own, *fold) for f, fold in enumerate(folds[:count])]
        of_keys = [(f * own, *fold) for f, fold in enumerate(folds[count:])]
        shares.append((flat, [(query, of_query), (keys, of_keys)]))
        got = attention_backward(
            height, width, operands, small_operands, arrays, plan, shares, 0
        )
        vectors = (
            ((3,), 0, model, model),
            ((4,), 0, model, model),
            ((0, 2), 0, model, 2 * model),
            ((8,), 0, model, model),
            ((9,), 0, model, model),
            ((10,), 0, model, model),
            ((12, 13, 14, 15), 0, model, ff),
            ((11,), 0, model, model),
            ((16,), 0, mid, mid),
            ((16,), mid, mid, mid),
            ((17,), 0, mid, mid),
            ((18,), 0, model, quarter),
            ((17,), mid, mid, mid),
        )
        tables_out = (rel_rows.shape, rel_cols.shape[::-1]) + (lateral_gain.shape,) * 3
        result, input_grad, *got = finish(
            result, got[0], got[1:4], got[4:], final, vectors, tables_out
        )
        weight_sums = {name: value.reshape(-1) for name, value in zip(names, got)}
        small = got[len(names) :]
        small = (
            *small[:3],
            small[-5],
            small[-4].T,
            *small[3:13],
            *small[-3:],
        )
    else:
        input_grad, mix_sums, rel_sum, qkv_grad = attention_backward(
            height, width, operands, (), (), None, (), 0
        )
        second_grad, four_grad, lat_eight_grad, lat_sixteen_grad, lat_thirty_grad = rest_grads
        packed, folds = [], []
        for grads_in, columns, called in (
            ((smooth_grad,), channels, ("smooth",)),
            ((first_grad, eight_grad), model, ("first", "eight")),
            ((fc1_grad,), model, ("fc1",)),
            ((fc2_grad,), model, ("fc2",)),
            ((qkv_grad,), mid, ("qkv",)),
            (
                (
                    proj_grad,
                    second_grad,
                    lat_sixteen_grad,
                    lat_thirty_grad,
                    lat_eight_grad,
                    four_grad,
                ),
                mid,
                ("proj", "second", "lat_sixteen", "lat_thirty", "lat_eight", "lat_four"),
            ),
        ):
            stacked, fold = fold_chunks(grads_in, columns)
            packed.append(stacked)
            folds.append(fold)
            names += called
        gain_rows = jnp.pad(gain_sums, ((0, 0), (0, model - channels)))
        small_in = (
            jnp.concatenate(
                [mix_sums, block_sums, fc1_sum.reshape(-1, model), level_sums, gain_rows]
            ),
            rel_sum,
        )
        got, small = last_reduce(packed, pack_small(small_in), 3)
        sums, rel_sum = unpack_small(small, small_in)
        flat = []
        for summed, fold in zip(got, folds):
            flat += unfold_chunks(summed, fold)
        weight_sums = dict(zip(names, flat))
        small = (
            sums[3],
            sums[4],
            jnp.concatenate([sums[0], sums[2]]),
            rel_sum[: rel_rows.shape[0], head_size : 2 * head_size],
            rel_sum[: rel_cols.shape[0], :head_size],
            sums[8],
            sums[9],
            sums[10],
            sums[16:20].reshape(-1),
            sums[11],
            sums[20, :mid],
            sums[21, :mid],
            sums[22, :mid],
            jnp.sum(sums[23].reshape(4, quarter), axis=0),
            sums[24, :mid],
            sums[25:29, :channels],
            sums[29:33, :channels],
            sums[36:40, :channels],
        )
    return (
        result.reshape(block_input.shape),
        input_grad.reshape(block_input.shape),
        small[0],
        small[1],
        weight_sums["qkv"],
        small[2],
        small[3],
        small[4],
        weight_sums["proj"],
        small[5],
        small[6],
        small[7],
        weight_sums["fc1"],
        small[8],
        weight_sums["fc2"],
        small[9],
        weight_sums["first"],
        small[10],
        small[11],
        small[12],
        weight_sums["second"],
        small[13],
        weight_sums["eight"],
        small[14],
        weight_sums["lat_four"],
        weight_sums["lat_eight"],
        weight_sums["lat_sixteen"],
        weight_sums["lat_thirty"],
        small[15],
        small[16],
        weight_sums["smooth"],
        small[17],
    )


def solution(mesh):
    in_specs = (
        P("img", ("rows", "scale"), None, None),
        P(),
        P(),
        P(),
        P(),
        P(),
        P(),
        P(),
        P(),
        P(),
        P(),
        P(),
        P(),
        P(),
        P(),
        P(),
        P(),
        P(),
        P(),
        P(),
        P(),
        P(),
        P(),
        P(),
        P(),
        P(),
        P(),
        P(),
        P(),
        P(),
        P(),
        P("img", "rows", None, None),
        P("img", "rows", None, None),
        P("img", "rows", None, None),
        P("img", "rows", None, None),
        P("img", "rows", None),
        P("img", "rows", None),
        P("img", "rows", None),
        P("img", "rows", None),
        P("img", "rows", None),
    )
    out_specs = (
        P("img", ("rows", "scale"), None, None),
        P("img", ("rows", "scale"), None, None),
        P(),
        P(),
        P(("img", "rows", "scale")),
        P(),
        P(),
        P(),
        P(("img", "rows", "scale")),
        P(),
        P(),
        P(),
        P(("img", "rows", "scale")),
        P(),
        P(("img", "rows", "scale")),
        P(),
        P(("img", "rows", "scale")),
        P(),
        P(),
        P(),
        P(("img", "rows", "scale")),
        P(),
        P(("img", "rows", "scale")),
        P(),
        P(("img", "rows", "scale")),
        P(("img", "rows", "scale")),
        P(("img", "rows", "scale")),
        P(("img", "rows", "scale")),
        P(),
        P(),
        P(("img", "rows", "scale")),
        P(),
    )
    return jax.shard_map(
        on_device, mesh=mesh, in_specs=in_specs, out_specs=out_specs, check_vma=False
    )
```

```python
from functools import partial

import jax
import jax.numpy as jnp
from jax import lax
from jax.experimental import pallas as pl
from jax.experimental.pallas import tpu as pltpu
from jax.sharding import PartitionSpec as P

norm_eps = 1e-06
wide_type = jnp.float32
narrow_type = jnp.bfloat16

MESH_ID = pl.DeviceIdType.MESH
lanes = 128


def axis_bits(size):
    bits = []
    step = 1
    while step < size:
        bits.append(step)
        step *= 2
    return bits


def bit_partner(axis, step):
    here = lax.axis_index(axis)
    bit = lax.rem(lax.div(here, step), 2)
    return {axis: here + step - 2 * step * bit}, bit


def halving_dims():
    dims = []
    for axis in ("img", "rows", "scale"):
        for step in reversed(axis_bits(lax.axis_size(axis))):
            dims.append((axis, step))
    return dims


class ReducePlan:
    def __init__(self, shapes, pieces, near=()):
        self.dims = halving_dims()
        self.stages = len(self.dims)
        core = self.dims.index(("img", 1))
        plane = [i for i, d in enumerate(self.dims) if d[0] == "img" and i != core]
        across = [i for i, d in enumerate(self.dims) if d[0] == "rows"]
        along = [i for i, d in enumerate(self.dims) if d[0] == "scale"][::-1]
        orders = {
            "x": [core] + across + plane + along,
            "y": [core] + plane + across + along,
            "z": [core] + along[:1] + plane + across + along[1:],
        }
        self.shapes = shapes
        self.near = near
        self.groups = [[core], across + plane, along]
        self.pieces, self.spans, self.entries, self.events = [], [], [], []
        for source, begin, size, first, entry, start, waves in pieces:
            self.pieces.append((source, begin, size, shapes[source][-1], orders[first]))
            self.spans.append((start, start + len(waves)))
            self.entries.append(entry)
            self.events.append(waves)
        self.staging = sorted(
            {
                piece[2:4]
                for piece, span in zip(self.pieces, self.spans)
                if piece[0] not in near and span[0] == 0
            }
        )

    def lead(self, t):
        return (2,) * (self.stages - max(self.spans[t][0], 1))

    def left(self, t):
        _, _, rows, columns, _ = self.pieces[t]
        return (2,) * (self.stages - self.spans[t][1]) + (rows, columns)

    def scratch(self):
        out = []
        for t, (_, _, rows, columns, _) in enumerate(self.pieces):
            out.append(pltpu.VMEM(self.lead(t) + (rows, columns), narrow_type))
        for t, (_, _, rows, columns, _) in enumerate(self.pieces):
            start, stop = self.spans[t]
            for stage in range(max(start, 1), stop):
                lead = (2,) * (self.stages - 1 - stage)
                out.append(pltpu.VMEM(lead + (rows, columns), narrow_type))
        for shape in self.staging:
            out.append(pltpu.VMEM((2,) * (self.stages - 1) + shape, narrow_type))
        count = len(self.pieces)
        out += [pltpu.SemaphoreType.DMA((count, self.stages))] * 2
        out += [pltpu.SemaphoreType.DMA((count,))]
        return out

    def calls(self):
        out = {}
        for stage in reversed(range(self.stages)):
            for t, (start, stop) in enumerate(self.spans):
                if start <= stage < stop:
                    out.setdefault(self.events[t][stage - start], []).append((t, stage))
        return out

    def waves(self):
        return max(self.calls()) + 1

    def shaped(self, arrays):
        out = []
        for array in arrays:
            if len(array.shape) == 3 and array.shape[0] == 2**self.stages:
                array = array.reshape((2,) * self.stages + array.shape[1:])
            out.append(array)
        return out

    def sums(self):
        return [jax.ShapeDtypeStruct(shape[1:], wide_type) for shape in self.shapes]


class Reducer:
    def __init__(self, plan, sources, outs, scratch):
        self.plan, self.sources, self.outs = plan, sources, outs
        count = len(plan.pieces)
        scratch = list(scratch)
        self.held, scratch = scratch[:count], scratch[count:]
        self.landed = []
        for start, stop in plan.spans:
            size = stop - max(start, 1)
            stages = range(max(start, 1), stop)
            self.landed.append(dict(zip(stages, scratch[:size])))
            scratch = scratch[size:]
        self.staging = dict(zip(plan.staging, scratch))
        self.send_sem, self.recv_sem, self.local_sem = scratch[len(plan.staging) :]
        self.partners = [bit_partner(axis, step) for axis, step in plan.dims]
        users = {shape: [] for shape in plan.staging}
        self.following = {}
        for t in sorted(range(count), key=lambda t: plan.events[t][0]):
            piece = plan.pieces[t]
            if piece[0] in plan.near or plan.spans[t][0]:
                continue
            used = users[piece[2:4]]
            if used:
                self.following[used[-1]] = t
            used.append(t)
        self.first_local = [used[0] for used in users.values()]
        self.todo = plan.calls()
        self.riders = {}

    def greet(self, barrier, groups=False):
        devices = [partner for partner, _ in self.partners]
        if groups:
            devices += [
                self.across(group, mask)
                for group in self.plan.groups
                for mask in range(1, 2 ** len(group))
                if mask & (mask - 1)
            ]
        for device in devices:
            pl.semaphore_signal(barrier, inc=1, device_id=device, device_id_type=MESH_ID)
        return len(devices)

    def across(self, group, mask):
        device = {}
        for i, dim in enumerate(group):
            axis, step = self.plan.dims[dim]
            if mask >> i & 1:
                here = device.get(axis, lax.axis_index(axis))
                device[axis] = here + step - 2 * step * self.partners[dim][1]
        return device

    def index(self, taken, current, keep, gone=()):
        out = []
        for dim in range(self.plan.stages):
            bit = self.partners[dim][1]
            if dim in gone:
                continue
            if dim in taken:
                out.append(bit)
            elif dim == current:
                out.append(bit if keep else 1 - bit)
            else:
                out.append(slice(None))
        return tuple(out)

    def gone(self, t):
        return self.plan.pieces[t][4][: max(self.plan.spans[t][0], 1)]

    def copy(self, t, stage):
        source, begin, rows, _, order = self.plan.pieces[t]
        if stage == 0:
            index = self.index((), order[0], False)
            view = self.sources[source].at[index + (pl.ds(begin, rows),)]
            target = self.held[t]
        else:
            index = self.index(order[:stage], order[stage], False, self.gone(t))
            view = self.held[t].at[index]
            target = self.landed[t][stage]
        return pltpu.make_async_remote_copy(
            src_ref=view,
            dst_ref=target,
            send_sem=self.send_sem.at[t, stage],
            recv_sem=self.recv_sem.at[t, stage],
            device_id=self.partners[order[stage]][0],
            device_id_type=MESH_ID,
        )

    def local(self, t):
        source, begin, rows, columns, order = self.plan.pieces[t]
        if self.plan.spans[t][0]:
            view, target = self.sources[source], self.held[t]
        else:
            index = self.index((), order[0], True)
            view = self.sources[source].at[index + (pl.ds(begin, rows),)]
            target = self.staging[(rows, columns)]
        return pltpu.make_async_copy(view, target, self.local_sem.at[t])

    def each(self, lead, action):
        total = 1
        for size in lead:
            total *= size

        def body(step, carry):
            place, left = [], step
            for size in reversed(lead):
                place.append(lax.rem(left, size))
                left = lax.div(left, size)
            action(tuple(reversed(place)))
            return carry

        if lead:
            lax.fori_loop(0, total, body, 0)
        else:
            action(())

    def add(self, target, arrived, begin=0):
        lead, rows = target.shape[:-2], target.shape[-2]
        arrived = arrived.at[(slice(None),) * len(lead) + (pl.ds(begin, rows),)]

        def action(place):
            target[place] = target[place] + arrived[place]

        self.each(lead, action)

    def start(self):
        for t, span in enumerate(self.plan.spans):
            if span[0]:
                self.local(t).start()
            elif self.plan.pieces[t][0] not in self.plan.near:
                self.copy(t, 0).start()
        for t in self.first_local:
            self.local(t).start()
        for t, span in enumerate(self.plan.spans):
            if span[0]:
                self.local(t).wait()

    def start_near(self, source):
        for t in range(len(self.plan.pieces)):
            if self.plan.pieces[t][0] == source:
                self.copy(t, 0).start()

    def event(self, t, stage):
        source, begin, rows, columns, order = self.plan.pieces[t]
        self.copy(t, stage).wait_recv()
        if stage == 0 and source in self.plan.near:
            own = self.sources[source].at[self.index((), order[0], True)]
            self.add(self.held[t], own, begin)
        elif stage == 0:
            self.local(t).wait()
            self.add(self.held[t], self.staging[(rows, columns)])
            if t in self.following:
                self.local(self.following[t]).start()
        else:
            index = self.index(order[:stage], order[stage], True, self.gone(t))
            self.add(self.held[t].at[index], self.landed[t][stage])
        if t in self.riders:
            self.riders[t].step()
        if stage + 1 < self.plan.spans[t][1]:
            self.copy(t, stage + 1).start()
        elif stage + 1 < self.plan.stages:
            kept = self.held[t].at[self.index(order[: stage + 1], -1, True, self.gone(t))]
            out = self.outs[source][t]

            def action(place):
                out[place] = kept[place]

            self.each(kept.shape[:-2], action)
        else:
            index = self.index(order, -1, True, self.gone(t))
            self.emit(source, begin, self.held[t][index].astype(wide_type))

    def emit(self, source, begin, value):
        out = self.outs[source]
        if not isinstance(out, list):
            out[begin : begin + value.shape[0], :] = value
            return
        for first, count, tile, tiles, ref in out:
            low, high = max(first, begin), min(first + count, begin + value.shape[0])
            if low < high:
                part = value[low - begin : high - begin]
                if tiles == 0:
                    ref[low - first : high - first, :] = part
                for c in range(min(tiles, part.shape[1] // lanes)):
                    here = part[:, c * lanes : (c + 1) * lanes]
                    at = (low - first) * tiles + tile + c
                    ref[pl.ds(at, high - low, stride=tiles), :] = here

    def wave(self, number):
        for t, span in enumerate(self.plan.spans):
            if span[0] and self.plan.entries[t] == number:
                self.copy(t, span[0]).start()
        for t, stage in self.todo.get(number, ()):
            self.event(t, stage)

    def finish(self):
        for t, (start, stop) in enumerate(self.plan.spans):
            for stage in range(start, stop):
                self.copy(t, stage).wait_send()


class SmallReduce:
    def __init__(self, reducer, groups, total, landed, send_sem, recv_sem):
        self.reducer, self.total, self.landed = reducer, total, landed
        self.send_sem, self.recv_sem = send_sem, recv_sem
        self.groups = groups
        self.stage = 0

    @staticmethod
    def sizes(groups):
        sizes = [2 ** len(group) for group in groups]
        return sizes, [sum(sizes[:i]) for i in range(len(sizes) + 1)]

    def copies(self):
        group = self.groups[self.stage]
        sizes, at = self.sizes(self.groups)
        place = sum(self.reducer.partners[dim][1] * 2**i for i, dim in enumerate(group))
        return place, [
            pltpu.make_async_remote_copy(
                src_ref=self.total,
                dst_ref=self.landed.at[at[self.stage] + place],
                send_sem=self.send_sem.at[at[self.stage] + mask],
                recv_sem=self.recv_sem.at[at[self.stage] + mask],
                device_id=self.reducer.across(group, mask),
                device_id_type=MESH_ID,
            )
            for mask in range(1, sizes[self.stage])
        ]

    def start(self):
        place, copies = self.copies()
        for copy in copies:
            copy.start()
        sizes, at = self.sizes(self.groups)
        self.landed[at[self.stage] + place] = self.total[...]

    def step(self):
        if self.stage == len(self.groups):
            return
        for copy in self.copies()[1]:
            copy.wait()
        sizes, at = self.sizes(self.groups)
        total = self.landed[at[self.stage]]
        for i in range(1, sizes[self.stage]):
            total = total + self.landed[at[self.stage] + i]
        self.total[...] = total
        self.stage += 1
        if self.stage < len(self.groups):
            self.start()


class StripGather:
    def __init__(self, owns, wholes, send_sem, recv_sem):
        self.owns, self.wholes = owns, wholes
        self.send_sem, self.recv_sem = send_sem, recv_sem
        self.deep, self.wide = lax.axis_size("scale"), lax.axis_size("rows")
        self.here, self.line = lax.axis_index("scale"), lax.axis_index("rows")

    @staticmethod
    def slots():
        deep, wide = lax.axis_size("scale"), lax.axis_size("rows")
        return 2 * (deep - 1) + (wide - 1) * (2 * deep - 1)

    def greet(self, barrier):
        waits = self.wide - 1
        for k in range(1, self.wide):
            device = {"rows": lax.rem(self.line + k, self.wide)}
            pl.semaphore_signal(barrier, inc=1, device_id=device, device_id_type=MESH_ID)

        @pl.when(self.here > 0)
        def _():
            device = {"scale": self.here - 1}
            pl.semaphore_signal(barrier, inc=1, device_id=device, device_id_type=MESH_ID)

        @pl.when(self.here < self.deep - 1)
        def _():
            device = {"scale": self.here + 1}
            pl.semaphore_signal(barrier, inc=1, device_id=device, device_id_type=MESH_ID)

        more = jnp.where(self.here > 0, 1, 0) + jnp.where(self.here < self.deep - 1, 1, 0)
        return waits + more

    def copies(self, block, slot, device):
        out = []
        for i, whole in enumerate(self.wholes):
            view = whole.at[self.line * self.deep + block]
            out.append(
                pltpu.make_async_remote_copy(
                    src_ref=view,
                    dst_ref=view,
                    send_sem=self.send_sem.at[slot, i],
                    recv_sem=self.recv_sem.at[slot, i],
                    device_id=device,
                    device_id_type=MESH_ID,
                )
            )
        return out

    def along(self, step, right):
        if right:
            block, device = self.here - step, {"scale": jnp.minimum(self.here + 1, self.deep - 1)}
            sent = (block >= 0) & (self.here < self.deep - 1)
            got = self.here - 1 - step >= 0
            return block, step, device, sent, got
        block, device = self.here + step, {"scale": jnp.maximum(self.here - 1, 0)}
        sent = (block < self.deep) & (self.here > 0)
        got = self.here + 1 + step < self.deep
        return block, self.deep - 1 + step, device, sent, got

    def across(self, block, kind, action):
        base = 2 * (self.deep - 1)
        for k in range(1, self.wide):
            slot = base + (k - 1) * (2 * self.deep - 1) + kind
            device = {"rows": lax.rem(self.line + k, self.wide)}
            for copy in self.copies(block, slot, device):
                action(copy)

    def start(self):
        for own, whole in zip(self.owns, self.wholes):
            whole[self.line * self.deep + self.here] = own[...]
        for right in (True, False):
            block, slot, device, sent, _ = self.along(0, right)

            @pl.when(sent)
            def _():
                for copy in self.copies(block, slot, device):
                    copy.start()

        self.across(self.here, 0, lambda copy: copy.start())

    def step(self, number):
        for right in (True, False):
            _, slot, device, _, got = self.along(number, right)
            block = self.here - 1 - number if right else self.here + 1 + number

            @pl.when(got)
            def _():
                for copy in self.copies(block, slot, device):
                    copy.wait_recv()
                kind = 1 + 2 * number + (0 if right else 1)
                self.across(block, kind, lambda copy: copy.start())

            if number + 1 < self.deep - 1:
                later, slot, device, sent, _ = self.along(number + 1, right)

                @pl.when(sent)
                def _():
                    for copy in self.copies(later, slot, device):
                        copy.start()

    def finish(self):
        self.across(self.here, 0, lambda copy: copy.wait())
        for number in range(self.deep - 1):
            for right in (True, False):
                _, _, _, _, got = self.along(number, right)
                block = self.here - 1 - number if right else self.here + 1 + number
                kind = 1 + 2 * number + (0 if right else 1)

                @pl.when(got)
                def _():
                    self.across(block, kind, lambda copy: copy.wait())

                sent_block, slot, device, sent, _ = self.along(number, right)

                @pl.when(sent)
                def _():
                    for copy in self.copies(sent_block, slot, device):
                        copy.wait_send()


def fold_chunks(grads, width):
    devices = lax.axis_size(("img", "rows", "scale"))
    cut, plan = [], []
    for grad in grads:
        rows, columns = grad.shape
        own = rows // devices
        chunk = grad.astype(narrow_type).reshape(devices, own, columns)
        folds = max(columns // width, 1)
        if columns < width:
            chunk = jnp.pad(chunk, ((0, 0), (0, 0), (0, width - columns)))
        cut += [chunk[:, :, f * width : (f + 1) * width] for f in range(folds)]
        plan.append((own, columns, folds))
    stacked = jnp.concatenate(cut, axis=1) if len(cut) > 1 else cut[0]
    extra = -stacked.shape[1] % 16
    if extra:
        stacked = jnp.pad(stacked, ((0, 0), (0, extra), (0, 0)))
    return stacked, plan


def unfold_chunks(summed, plan):
    at, out = 0, []
    for own, columns, folds in plan:
        parts = []
        for _ in range(folds):
            parts.append(summed[at : at + own, : min(columns, summed.shape[1])])
            at += own
        whole = jnp.concatenate(parts, axis=1) if folds > 1 else parts[0]
        out.append(whole.reshape(-1))
    return out


def last_reduce_kernel(plan, count, refs):
    sources, small_in = refs[:count], refs[count]
    outs, small_out = refs[count + 1 : 2 * count + 1], refs[2 * count + 1]
    scratch = refs[2 * count + 2 :]
    small_held, small_landed, small_send, small_recv = scratch[:4]
    reducer = Reducer(plan, sources, outs, scratch[4:])
    barrier = pltpu.get_barrier_semaphore()
    pl.semaphore_wait(barrier, reducer.greet(barrier))

    def small_copy(stage):
        return pltpu.make_async_remote_copy(
            src_ref=small_held,
            dst_ref=small_landed.at[stage],
            send_sem=small_send.at[stage],
            recv_sem=small_recv.at[stage],
            device_id=reducer.partners[plan.pieces[0][4][stage]][0],
            device_id_type=MESH_ID,
        )

    small_held[...] = small_in[...]
    reducer.start()
    small_copy(0).start()
    for number in range(plan.waves()):
        reducer.wave(number)
        if number < plan.stages:
            small_copy(number).wait()
            small_held[...] = small_held[...] + small_landed[number]
            if number + 1 < plan.stages:
                small_copy(number + 1).start()
    small_out[...] = small_held[...]
    reducer.finish()


def cut_rows(shapes):
    out = []
    stages = len(halving_dims())
    for source, (_, rows, _) in enumerate(shapes):
        first = -(-rows // 32) * 16
        waves = tuple(source + stage + (1 if stage else 0) for stage in range(stages))
        out.append((source, 0, first, "x", source, 0, waves))
        if first < rows:
            out.append((source, first, rows - first, "y", source, 0, waves))
    return out


def last_reduce(arrays, small, call_id):
    shapes = [array.shape for array in arrays]
    plan = ReducePlan(shapes, cut_rows(shapes))
    count = len(arrays)

    def body(*refs):
        last_reduce_kernel(plan, count, refs)

    vmem = pl.BlockSpec(memory_space=pltpu.VMEM)
    got = pl.pallas_call(
        body,
        out_shape=plan.sums() + [jax.ShapeDtypeStruct(small.shape, wide_type)],
        in_specs=[pl.BlockSpec(memory_space=pl.ANY)] * count + [vmem],
        out_specs=[vmem] * (count + 1),
        scratch_shapes=[
            pltpu.VMEM(small.shape, wide_type),
            pltpu.VMEM((plan.stages,) + small.shape, wide_type),
            pltpu.SemaphoreType.DMA((plan.stages,)),
            pltpu.SemaphoreType.DMA((plan.stages,)),
        ]
        + plan.scratch(),
        compiler_params=pltpu.CompilerParams(
            collective_id=call_id, has_side_effects=True, vmem_limit_bytes=60 << 20
        ),
        name="last_reduce",
    )(*plan.shaped(arrays), small)
    return got[:count], got[count]


def pack_small(parts):
    flat = jnp.concatenate([part.reshape(-1) for part in parts])
    unit = 8 * lanes
    total = -(-flat.shape[0] // unit) * unit
    return jnp.pad(flat, (0, total - flat.shape[0])).reshape(-1, lanes)


def unpack_small(packed, parts):
    flat = packed.reshape(-1)
    out, at = [], 0
    for part in parts:
        out.append(flat[at : at + part.size].reshape(part.shape))
        at += part.size
    return out


def dot_nn(left, right):
    return lax.dot_general(left, right, (((1,), (0,)), ((), ())), preferred_element_type=wide_type)


def dot_nt(left, right):
    return lax.dot_general(left, right, (((1,), (1,)), ((), ())), preferred_element_type=wide_type)


def dot_tn(left, right):
    return lax.dot_general(left, right, (((0,), (0,)), ((), ())), preferred_element_type=wide_type)


def norm_parts(values):
    centre = values - jnp.mean(values, axis=-1, keepdims=True)
    inverse = lax.rsqrt(jnp.mean(centre * centre, axis=-1, keepdims=True) + norm_eps)
    return centre * inverse, inverse


def norm_back(hat, inverse, hat_grad):
    inner = jnp.mean(hat_grad * hat, axis=-1, keepdims=True)
    return inverse * (hat_grad - jnp.mean(hat_grad, axis=-1, keepdims=True) - hat * inner)


def normal_cdf(values):
    return 0.5 + 0.5 * lax.erf(values * (0.5**0.5))


def gelu_slope(values):
    density = jnp.exp(-0.5 * values * values) * (0.5 / jnp.pi) ** 0.5
    return normal_cdf(values) + values * density


def lane_ids(shape):
    return lax.broadcasted_iota(jnp.int32, shape, len(shape) - 1)


def column_sum(values):
    return jnp.sum(values, axis=0, keepdims=True)


def half_mask(half, head_size, value):
    lane = lane_ids((1, 2 * head_size))
    inside = (lane >= half * head_size) & (lane < (half + 1) * head_size)
    return jnp.where(inside, value, 0.0).astype(narrow_type)


def split_lanes(values, used):
    lane = lane_ids(values.shape)
    twice = jnp.where(lane < used, values, pltpu.roll(values, used, 1))
    near = twice.astype(narrow_type).astype(wide_type)
    both = jnp.where(lane < used, near, twice - near)
    return jnp.where(lane < 2 * used, both, 0.0).astype(narrow_type)


def place_cols(tab, width):
    by_col = pltpu.roll(tab, lanes - (width - 1), 1, stride=1, stride_axis=0)
    return split_lanes(by_col, width)


def place_rows(tab, row, height):
    by_row = pltpu.roll(tab, lax.rem(lanes - (height - 1) + row, lanes), 1)
    return split_lanes(by_row, height)


def both_halves(values, head_size, scale):
    masked = [values * half_mask(half, head_size, scale) for half in range(2)]
    return jnp.concatenate(masked, axis=0)


def own_extra(tab, strip_rows, width, height):
    out = []
    for half in range(2):
        for i in range(strip_rows):
            piece = tab[i * width : (i + 1) * width, 2 * half * lanes : 2 * (half + 1) * lanes]
            row = strip_index() * strip_rows + i
            cols = place_cols(piece[:, :lanes], width)
            out.append(jnp.concatenate([cols, place_rows(piece[:, lanes:], row, height)], axis=1))
    return jnp.concatenate(out, axis=0)


def strip_index():
    return lax.axis_index("rows") * lax.axis_size("scale") + lax.axis_index("scale")


def block_forward_kernel(height, width, count, refs):
    x_own, refs = refs[0], refs[1:]
    small, refs = refs[: count + 3], refs[count + 3 :]
    qkv_hbm, proj_hbm, fc1_hbm, fc2_hbm = refs[:4]
    prepared, refs = refs[4:10], refs[10:]
    (
        q_all,
        k_all,
        v_all,
        attended,
        attended_wide,
        log_norm,
        middle,
        normed_mid,
        hidden_pre,
        hidden,
        result,
    ) = refs[:11]
    qkv_weight, proj, fc1, fc2, sems, x_all, table, extras, send_sem, recv_sem = refs[11:]
    vec, tables, _, hot, _, _ = prepared
    model = x_all.shape[2]
    tokens = middle.shape[0]
    strip_rows = tokens // width
    head_size = lanes // 2
    copies = [
        pltpu.make_async_copy(source, target, sems.at[i])
        for i, (source, target) in enumerate(
            ((proj_hbm, proj), (fc1_hbm, fc1), (fc2_hbm, fc2), (qkv_hbm, qkv_weight))
        )
    ]
    for copy in reversed(copies):
        copy.start()
    gather = StripGather([x_own], [x_all], send_sem, recv_sem)
    barrier = pltpu.get_barrier_semaphore()
    pl.semaphore_wait(barrier, gather.greet(barrier))
    gather.start()
    prepare_kernel(height, width, count, (*small, *prepared, table))
    copies[3].wait()
    start = pl.multiple_of(strip_index() * tokens, tokens)

    def mix(begin, blocks):
        at = pl.ds(pl.multiple_of(begin * tokens, tokens), blocks * tokens)
        inputs = x_all[pl.ds(begin, blocks)].reshape(blocks * tokens, model)
        hat, _ = norm_parts(inputs.astype(wide_type))
        normed = (hat * vec[0:1, :] + vec[1:2, :]).astype(narrow_type)
        mixed = dot_nn(normed, qkv_weight[...])
        q_all[at, :] = (mixed[:, :model] + vec[2:3, :]).astype(narrow_type)
        k_all[at, :] = mixed[:, model : 2 * model].astype(narrow_type)
        v_all[at, :] = (mixed[:, 2 * model :] + vec[3:4, :]).astype(narrow_type)

    for number in range(gather.deep - 1):
        gather.step(number)
    line = gather.line * gather.deep
    mix(line, gather.deep)
    for pair in range(model // lanes):
        queries = q_all[pl.ds(start, tokens), pair * lanes : (pair + 1) * lanes]
        extras[pair] = own_extra(dot_nn(queries, tables[...]), strip_rows, width, height)
    gather.finish()

    def others(step, carry):
        mix(lax.rem(gather.line + 1 + step, gather.wide) * gather.deep, gather.deep)
        return carry

    lax.fori_loop(0, gather.wide - 1, others, 0)
    log_norm[...] = jnp.zeros_like(log_norm)
    lane = lane_ids((tokens, lanes))

    def pair_step(pair):
        cols = slice(pair * lanes, (pair + 1) * lanes)
        queries = q_all[pl.ds(start, tokens), cols]
        values = v_all[:, cols]
        keys = jnp.concatenate([k_all[:, cols], hot[...]], axis=1)
        masked = both_halves(queries, head_size, head_size**-0.5)
        scores = dot_nt(jnp.concatenate([masked, extras[pair]], axis=1), keys)
        peak = jnp.max(scores, axis=-1, keepdims=True)
        raised = jnp.exp(scores - peak)
        total = jnp.sum(raised, axis=-1, keepdims=True)
        probs = (raised * (1.0 / total)).astype(narrow_type)
        out = dot_nn(probs, values)
        mixed = (out[:tokens], out[tokens:])
        norm = peak + jnp.log(total)
        kept = jnp.where(lane == 2 * pair, norm[:tokens], log_norm[...])
        log_norm[...] = jnp.where(lane == 2 * pair + 1, norm[tokens:], kept)
        joined = jnp.where(lane < head_size, mixed[0], mixed[1])
        attended_wide[:, cols] = joined
        attended[:, cols] = joined.astype(narrow_type)

    for pair in range(model // lanes):
        pair_step(pair)
    copies[0].wait()
    inputs = x_all[strip_index()].astype(wide_type)
    centre = inputs + (dot_nn(attended[...], proj[...]) + vec[4:5, :])
    middle[...] = centre
    hat, _ = norm_parts(centre)
    normed_low = (hat * vec[5:6, :] + vec[6:7, :]).astype(narrow_type)
    normed_mid[...] = normed_low
    copies[1].wait()
    copies[2].wait()
    result_wide = centre + vec[7:8, :]
    for j in range(fc1.shape[1] // model):
        cols = slice(j * model, (j + 1) * model)
        pre = dot_nn(normed_mid[...], fc1[:, cols]) + vec[8 + j : 9 + j, :]
        hidden_pre[:, cols] = pre
        low = (pre * normal_cdf(pre)).astype(narrow_type)
        hidden[:, cols] = low
        result_wide = result_wide + dot_nn(low, fc2[cols, :])
    result[...] = result_wide.astype(narrow_type)


def vmem_specs(count):
    return [pl.BlockSpec(memory_space=pltpu.VMEM)] * count


def any_specs(count):
    return [pl.BlockSpec(memory_space=pl.ANY)] * count


def block_forward(height, width, x_own, vectors, turned, weights, call_id):
    tokens, model = x_own.shape
    total = height * width
    ff = weights[2].shape[1]
    slots = StripGather.slots()

    def shape(rows, cols, kind):
        return jax.ShapeDtypeStruct((rows, cols), kind)

    outs = [
        shape(total, model, narrow_type),
        shape(total, model, narrow_type),
        shape(total, model, narrow_type),
        shape(tokens, model, narrow_type),
        shape(tokens, model, wide_type),
        shape(tokens, lanes, wide_type),
        shape(tokens, model, wide_type),
        shape(tokens, model, narrow_type),
        shape(tokens, ff, wide_type),
        shape(tokens, ff, narrow_type),
        shape(tokens, model, narrow_type),
    ]
    outs = prepared_shapes(height, width, model, vectors, turned[2]) + outs
    small = (*vectors, *turned)

    def body(*refs):
        block_forward_kernel(height, width, len(vectors), refs)

    return pl.pallas_call(
        body,
        out_shape=outs,
        in_specs=vmem_specs(1 + len(small)) + any_specs(4),
        out_specs=vmem_specs(len(outs)),
        scratch_shapes=[pltpu.VMEM(weight.shape, narrow_type) for weight in weights]
        + [
            pltpu.SemaphoreType.DMA((4,)),
            pltpu.VMEM((total // tokens, tokens, model), narrow_type),
            pltpu.VMEM((lanes, lanes), wide_type),
            pltpu.VMEM((model // lanes, 2 * tokens, 2 * lanes), narrow_type),
            pltpu.SemaphoreType.DMA((slots, 1)),
            pltpu.SemaphoreType.DMA((slots, 1)),
        ],
        compiler_params=pltpu.CompilerParams(
            collective_id=call_id, has_side_effects=True, vmem_limit_bytes=60 << 20
        ),
        name="block_forward",
    )(x_own, *small, *weights)


def fold_store(target, number, parts, value):
    devices = target.shape[0]
    own = value.shape[0] // devices
    parts[number] = value.reshape(devices, own, value.shape[1])
    if number % 2:
        both = jnp.concatenate([parts.pop(number - 1), parts.pop(number)], axis=1)
        begin = (number - 1) * own
        target[:, begin : begin + 2 * own, :] = both.astype(narrow_type)


def block_backward_kernel(whole, refs):
    (
        result_grad,
        hidden_pre,
        hidden,
        normed_mid,
        middle,
        attended,
        attended_wide,
        log_norm,
        vec,
        proj_far,
        fc1_far,
        fc2_far,
        middle_grad,
        attended_grad,
        stats,
        stat_rows,
        sums,
        fc1_sum,
        pre_out,
        branch_out,
    ) = refs[:20]
    refs = refs[20:]
    if whole:
        proj_grad, fc1_grad, fc2_grad = refs[:3]
        refs = refs[3:]
    proj, fc1, fc2, sems = refs
    width = middle.shape[1]
    blocks = hidden.shape[1] // width
    fc1_in, fc2_in = [], []
    for j in range(blocks):
        part = slice(j * width, (j + 1) * width)
        fc1_in.append(
            pltpu.make_async_copy(fc1_far.at[:, part], fc1.at[:, part], sems.at[0, j])
        )
        fc2_in.append(pltpu.make_async_copy(fc2_far.at[part], fc2.at[part], sems.at[1, j]))
        fc2_in[j].start()
        fc1_in[j].start()
    proj_in = pltpu.make_async_copy(proj_far, proj, sems.at[2, 0])
    proj_in.start()
    model = middle.shape[1]
    ff = hidden.shape[1]
    grad_low = result_grad[...]
    grad_wide = grad_low.astype(wide_type)
    back = jnp.zeros(middle.shape, wide_type)
    for j in range(ff // model):
        cols = slice(j * model, (j + 1) * model)
        pre = hidden_pre[:, cols]
        fc2_in[j].wait()
        pre_grad = dot_nt(grad_low, fc2[cols, :]) * gelu_slope(pre)
        pre_low = pre_grad.astype(narrow_type)
        fc1_sum[:, cols] = column_sum(pre_low.astype(wide_type))
        fc1_in[j].wait()
        back = back + dot_nt(pre_low, fc1[:, cols])
        pre_out[:, cols] = pre_low
        if whole:
            part = dot_nn(normed_mid[...].T, pre_low)
            fc1_grad[:, cols] = part.astype(narrow_type)
            fc2_grad[cols, :] = dot_nn(hidden[:, cols].T, grad_low).astype(narrow_type)
    proj_in.wait()
    hat, inverse = norm_parts(middle[...])
    gain_grad = column_sum(back * hat)
    shift_grad = column_sum(back)
    centre_grad = grad_wide + norm_back(hat, inverse, back * vec[5:6, :])
    middle_grad[...] = centre_grad
    branch_low = centre_grad.astype(narrow_type)
    sums[0:1, :] = column_sum(branch_low.astype(wide_type))
    sums[1:2, :] = gain_grad
    sums[2:3, :] = shift_grad
    sums[3:4, :] = column_sum(grad_wide)
    sums[4:8, :] = jnp.zeros((4, model), wide_type)
    branch_out[...] = branch_low
    if whole:
        proj_grad[...] = dot_nn(attended[...].T, branch_low).astype(narrow_type)
    out_grad = dot_nt(branch_low, proj[...]).astype(narrow_type)
    attended_grad[...] = out_grad
    product = out_grad.astype(wide_type) * attended_wide[...]
    near = product.astype(narrow_type)
    rest = (product - near.astype(wide_type)).astype(narrow_type)
    head_size = lanes // 2
    channel = lax.broadcasted_iota(jnp.int32, (model, lanes), 0)
    head = lax.broadcasted_iota(jnp.int32, (model, lanes), 1)
    member = (lax.div(channel, head_size) == head - 16).astype(wide_type).astype(narrow_type)
    delta = dot_nn(near, member) + dot_nn(rest, member)
    both = jnp.where(lane_ids(delta.shape) < 16, log_norm[...], delta)
    stats[...] = both
    stat_rows[...] = both.T[:32, :]


def share_outs(plan, shares, refs):
    outs = [[] for _ in plan.shapes]
    for ref, share in zip(refs, shares):
        for source, places in share if isinstance(share, list) else [share]:
            for place in places:
                outs[source].append(place + (ref,))
    return outs


def block_backward(result_grad, kept, log_norm, vec, proj, fc1, fc2, devices):
    hidden_pre, hidden, normed_mid, middle, attended, attended_wide = kept
    tokens, model = middle.shape
    ff = fc1.shape[1]

    def shape(rows, cols, kind):
        return jax.ShapeDtypeStruct((rows, cols), kind)

    outs = [
        shape(tokens, model, wide_type),
        shape(tokens, model, narrow_type),
        shape(tokens, lanes, wide_type),
        shape(32, tokens, wide_type),
        shape(8, model, wide_type),
        shape(1, ff, wide_type),
        shape(tokens, ff, narrow_type),
        shape(tokens, model, narrow_type),
    ]
    whole = not devices
    if whole:
        outs += [
            shape(model, model, narrow_type),
            shape(model, ff, narrow_type),
            shape(ff, model, narrow_type),
        ]

    def body(*refs):
        block_backward_kernel(whole, refs)

    return pl.pallas_call(
        body,
        out_shape=outs,
        in_specs=vmem_specs(9) + any_specs(3),
        out_specs=vmem_specs(len(outs)),
        scratch_shapes=[
            pltpu.VMEM(proj.shape, narrow_type),
            pltpu.VMEM(fc1.shape, narrow_type),
            pltpu.VMEM(fc2.shape, narrow_type),
            pltpu.SemaphoreType.DMA((3, ff // model)),
        ],
        compiler_params=pltpu.CompilerParams(vmem_limit_bytes=60 << 20),
        name="block_backward",
    )(
        result_grad,
        hidden_pre,
        hidden,
        normed_mid,
        middle,
        attended,
        attended_wide,
        log_norm,
        vec,
        proj,
        fc1,
        fc2,
    )


def small_groups(plan):
    return [[[dim] for dim in plan.pieces[t][4]] for t in plan.riders]


def attention_backward_kernel(height, width, plan, shares, refs):
    (
        x_own,
        q_all,
        k_all,
        v_all,
        grad_own,
        own_stats,
        stat_own,
        middle_grad,
        vec,
        tables,
        rel_all,
        hot,
        hot_turned,
        qkv_weight,
    ) = refs[:14]
    refs = refs[14:]
    if plan is None:
        input_grad, sums, rel_sum, weight_grad = refs[:4]
        scratch = refs[4:]
    else:
        block_sums, fc1_sum, level_sums, gain_sums = refs[:4]
        normed_mid, pre_grad, hidden, result_grad, attended, branch_grad = refs[4:10]
        refs = refs[10:]
        count = len(plan.shapes) - len(plan.near)
        sources, refs = refs[:count], refs[count:]
        input_grad, sums_out, early_out, rel_out = refs[:4]
        flat = refs[4 : 4 + len(shares)]
        scratch = refs[4 + len(shares) :]
        near_fc1, near_fc2, near_proj, near_query, near_rest, sums, early, rel_sum = scratch[:8]
        small_scratch, scratch = scratch[8:17], scratch[17:]
        near_block = (near_fc1, near_fc2, near_proj)
        outs = share_outs(plan, shares, flat)
    joined, wide_tab, cols_extra, rows_extra, grad_all, stat_all, stat_rows, rel_grad = scratch[:8]
    gather = StripGather([grad_own, stat_own], [grad_all, stat_all], scratch[8], scratch[9])
    total, model = q_all.shape
    tokens = x_own.shape[0]
    strip_rows = tokens // width
    head_size = lanes // 2
    scale = head_size**-0.5
    strip = strip_index()
    strips = grad_all.shape[0]
    own = pl.ds(pl.multiple_of(strip * tokens, tokens), tokens)
    pairs = model // lanes
    barrier = pltpu.get_barrier_semaphore()
    greeted = gather.greet(barrier)
    if plan is not None:
        arrays = (*near_block, *sources, near_query, near_rest)
        reducer = Reducer(plan, arrays, outs, scratch[10:])
        greeted = greeted + reducer.greet(barrier)
        late_sums, early_sums, rel_sums = [
            SmallReduce(reducer, groups, total, *small_scratch[3 * i : 3 * i + 3])
            for i, (groups, total) in enumerate(zip(small_groups(plan), (sums, early, rel_sum)))
        ]
        reducer.riders = dict(zip(plan.riders, (late_sums, early_sums, rel_sums)))
    if plan is not None:
        early[0:4, :] = block_sums[0:4, :]
        size = early.shape[1]
        for j in range(fc1_sum.shape[1] // size):
            early[4 + j : 5 + j, :] = fc1_sum[:, j * size : (j + 1) * size]
        mid, channels = size // 2, gain_sums.shape[1]
        early[8:9, :mid], early[8:9, mid:] = level_sums[0:1, :mid], level_sums[1:2, :mid]
        early[9:10, :mid], early[9:10, mid:] = level_sums[2:3, :mid], level_sums[4:5, :mid]
        early[10:11, :] = level_sums[3:4, :]
        early[11:15, :channels] = level_sums[5:9, :channels]
        early[11:15, channels : 2 * channels] = level_sums[9:13, :channels]
        early[11:15, 2 * channels :] = gain_sums[0:4, :]
        early[15:16, :] = jnp.zeros((1, size), wide_type)
    pl.semaphore_wait(barrier, greeted)
    gather.start()
    if plan is not None:
        early_sums.start()
        reducer.start()

    rel_grad[...] = jnp.zeros_like(rel_grad)
    lane = lane_ids((tokens, lanes))

    def own_queries(pair):
        cols = slice(pair * lanes, (pair + 1) * lanes)
        queries = q_all[own, cols]
        keys = k_all[:, cols]
        extra = own_extra(dot_nn(queries, tables[...]), strip_rows, width, height)
        masked = both_halves(queries, head_size, scale)
        keys_hot = jnp.concatenate([keys, hot[...]], axis=1)
        scores = dot_nt(jnp.concatenate([masked, extra], axis=1), keys_hot)
        norms, means = [], []
        for half in range(2):
            head = 2 * pair + half
            stats = own_stats[...]
            norms.append(jnp.sum(jnp.where(lane == head, stats, 0.0), axis=-1, keepdims=True))
            means.append(jnp.sum(jnp.where(lane == 16 + head, stats, 0.0), axis=-1, keepdims=True))
        probs = jnp.exp(scores - jnp.concatenate(norms, axis=0))
        prob_grad = dot_nt(both_halves(grad_own[:, cols], head_size, 1.0), v_all[:, cols])
        score_grad = probs * (prob_grad - jnp.concatenate(means, axis=0))
        keys_turned = jnp.concatenate([keys, hot_turned[...]], axis=1)
        back = dot_nn(score_grad.astype(narrow_type), keys_turned)
        offsets = []
        for half in range(2):
            parts = []
            for i in range(strip_rows):
                at = half * tokens + i * width
                piece = back[at : at + width]
                by_col = pltpu.roll(piece[:, lanes : 2 * lanes], 0, 1, stride=1, stride_axis=0)
                by_row = pltpu.roll(piece[:, 2 * lanes :], strip * strip_rows + i, 1)
                parts.append(jnp.concatenate([by_col, by_row], axis=1))
            offsets.append(jnp.concatenate(parts, axis=0))
        off = jnp.concatenate(offsets, axis=1).astype(narrow_type)
        plain = jnp.where(lane < head_size, back[:tokens, :lanes], back[tokens:, :lanes])
        query_grad = plain * scale + dot_nn(off, rel_all[...])
        joined[:, cols] = query_grad.astype(narrow_type)
        rel_grad[...] += dot_tn(off, queries)

    def own_keys(pair):
        at = pair * lanes
        cols = slice(at, at + lanes)
        all_queries = q_all[:, cols]
        wide_tab[...] = dot_nn(all_queries, tables[...])

        def widen(row, inner):
            rows = pl.ds(pl.multiple_of(row * width, width), width)
            for half in range(2):
                begin = 2 * half * lanes
                cols_extra[half, rows, :] = place_cols(wide_tab[rows, begin : begin + lanes], width)
                piece = wide_tab[rows, begin + lanes : begin + 2 * lanes]
                rows_extra[half, rows, :] = place_rows(piece, row, height)
            return inner

        lax.fori_loop(0, height, widen, 0)
        all_grads = grad_all[:, :, cols].reshape(total, lanes)
        hot_own = hot[own, :]
        blank = jnp.zeros((tokens, lanes), narrow_type)
        hot_col, hot_row = hot_own[:, :lanes], hot_own[:, lanes:]
        keys = both_halves(k_all[own, cols], head_size, scale)
        left = jnp.concatenate(
            [
                jnp.concatenate([hot_col, blank, hot_row, blank], axis=1),
                jnp.concatenate([blank, hot_col, blank, hot_row], axis=1),
            ],
            axis=0,
        )
        right = jnp.concatenate(
            [all_queries, cols_extra[0], cols_extra[1], rows_extra[0], rows_extra[1]], axis=1
        )
        scores = dot_nt(jnp.concatenate([keys, left], axis=1), right)
        prob_grad = dot_nt(both_halves(v_all[own, cols], head_size, 1.0), all_grads)
        probs, score_grads = [], []
        for half in range(2):
            head = 2 * pair + half
            here = slice(half * tokens, (half + 1) * tokens)
            prob = jnp.exp(scores[here] - stat_rows[head : head + 1, :])
            probs.append(prob.astype(narrow_type))
            score_grad = prob * (prob_grad[here] - stat_rows[16 + head : 17 + head, :])
            score_grads.append(score_grad.astype(narrow_type))
        key_both = dot_nn(jnp.concatenate(score_grads, axis=0), all_queries)
        value_both = dot_nn(jnp.concatenate(probs, axis=0), all_grads)
        key_grad = jnp.where(lane < head_size, key_both[:tokens], key_both[tokens:]) * scale
        value_grad = jnp.where(lane < head_size, value_both[:tokens], value_both[tokens:])
        joined[:, model + at : model + at + lanes] = key_grad.astype(narrow_type)
        joined[:, 2 * model + at : 2 * model + at + lanes] = value_grad.astype(narrow_type)

    hat, inverse = norm_parts(x_own[...].astype(wide_type))
    normed_turned = (hat * vec[0:1, :] + vec[1:2, :]).astype(narrow_type).T
    steps = gather.deep - 1
    progress = [0]

    def advance():
        if plan is not None:
            reducer.wave(progress[0])
            progress[0] += 1

    def near_grads(near, left, right, first):
        fold = near.shape[-1]
        own_count = left.shape[0] // 2**plan.stages
        lead = (slice(None),) * plan.stages
        parts = {}
        for f in range(near.shape[-2] // own_count):
            begin = first + f * fold
            value = dot_nn(left, right[:, begin : begin + fold])
            parts[f] = value.reshape((2,) * plan.stages + (own_count, fold))
            if f % 2:
                both = jnp.concatenate([parts.pop(f - 1), parts.pop(f)], axis=plan.stages)
                rows = slice((f - 1) * own_count, (f + 1) * own_count)
                near[lead + (rows,)] = both.astype(narrow_type)

    def near_second():
        blocks = hidden.shape[1] // model
        grads = result_grad[...]
        bits = len(axis_bits(blocks))
        for j in range(blocks):
            value = dot_nn(hidden[:, j * model : (j + 1) * model].T, grads).astype(narrow_type)
            lead = tuple((j >> (bits - 1 - d)) & 1 for d in range(bits))
            near_fc2[lead] = value.reshape(near_fc2.shape[bits:])

    if plan is not None:
        near_second()
        reducer.start_near(1)
    advance()
    for pair in range(pairs):
        own_queries(pair)
        if pair < steps:
            gather.step(pair)
        if plan is not None and pair == 1:
            near_grads(near_fc1, normed_mid[...].T, pre_grad, 0)
            reducer.start_near(0)
        if plan is not None and pair == 3:
            near_grads(near_proj, attended[...].T, branch_grad, 0)
            reducer.start_near(2)
        advance()
    turned = pltpu.roll(rel_grad[2 * lanes :, :], head_size, 1)
    both = rel_grad[: 2 * lanes, :] + turned
    low = lane_ids((lanes, lanes)) < head_size
    rel_sum[...] = jnp.where(low, both[:lanes], pltpu.roll(both[lanes:], head_size, 1))
    if plan is not None:
        near_grads(near_query, normed_turned, joined, 0)
        rel_sums.start()
        reducer.start_near(len(plan.shapes) - 2)
    gather.finish()
    for block in range(strips):
        stat_rows[:, block * tokens : (block + 1) * tokens] = stat_all[block]
    for pair in range(pairs):
        own_keys(pair)
        advance()
    if plan is not None:
        near_grads(near_rest, normed_turned, joined, model)
        reducer.start_near(len(plan.shapes) - 1)
    back = jnp.zeros((tokens, model), wide_type)
    for j in range(3):
        cols = slice(j * model, (j + 1) * model)
        part = joined[:, cols]
        sums[j : j + 1, :] = column_sum(part.astype(wide_type))
        back = back + dot_nt(part, qkv_weight[:, cols])
        if plan is None:
            weight_grad[:, cols] = dot_nn(normed_turned, part).astype(narrow_type)
    sums[3:4, :] = column_sum(back * hat)
    sums[4:5, :] = column_sum(back)
    sums[5:8, :] = jnp.zeros((3, model), wide_type)
    if plan is not None:
        late_sums.start()
    input_grad[...] = middle_grad[...] + norm_back(hat, inverse, back * vec[0:1, :])
    if plan is None:
        return
    while progress[0] < plan.waves():
        advance()
    for small in (early_sums, rel_sums, late_sums):
        while small.stage < len(small.groups):
            small.step()
    sums_out[...] = sums[...]
    early_out[...] = early[...]
    rel_out[...] = rel_sum[...]
    reducer.finish()


def attention_backward(height, width, operands, small, arrays, plan, shares, call_id):
    tokens, model = operands[0].shape
    total = operands[1].shape[0]
    strips = total // tokens
    slots = StripGather.slots()

    def shape(rows, cols, kind):
        return jax.ShapeDtypeStruct((rows, cols), kind)

    outs = [shape(tokens, model, wide_type)]
    scratch = []
    extra = []
    if plan is None:
        outs += [
            shape(8, model, wide_type),
            shape(lanes, lanes, wide_type),
            shape(model, 3 * model, narrow_type),
        ]
    else:
        smalls = [(8, model), (16, model), (lanes, lanes)]
        outs += [shape(*dims, wide_type) for dims in smalls]
        outs += [flat for flat, _ in shares]
        shares = [share for _, share in shares]
        stages = plan.stages
        scratch += [
            pltpu.VMEM((2,) * stages + plan.shapes[i][1:], narrow_type) for i in plan.near
        ]
        scratch += [pltpu.VMEM(dims, wide_type) for dims in smalls]
        for dims, groups in zip(smalls, small_groups(plan)):
            slots_small = SmallReduce.sizes(groups)[1][-1]
            scratch += [
                pltpu.VMEM((slots_small,) + dims, wide_type),
                pltpu.SemaphoreType.DMA((slots_small,)),
                pltpu.SemaphoreType.DMA((slots_small,)),
            ]
        extra = plan.scratch()
    scratch += [
        pltpu.VMEM((tokens, 3 * model), narrow_type),
        pltpu.VMEM((total, 4 * lanes), wide_type),
        pltpu.VMEM((2, total, lanes), narrow_type),
        pltpu.VMEM((2, total, lanes), narrow_type),
        pltpu.VMEM((strips, tokens, model), narrow_type),
        pltpu.VMEM((strips, 32, tokens), wide_type),
        pltpu.VMEM((32, total), wide_type),
        pltpu.VMEM((4 * lanes, lanes), wide_type),
        pltpu.SemaphoreType.DMA((slots, 2)),
        pltpu.SemaphoreType.DMA((slots, 2)),
    ]

    def body(*refs):
        attention_backward_kernel(height, width, plan, shares, refs)

    given = operands + (small if plan is not None else ())
    far = plan.shaped(arrays) if plan is not None else []
    return pl.pallas_call(
        body,
        out_shape=outs,
        in_specs=vmem_specs(len(given)) + any_specs(len(far)),
        out_specs=vmem_specs(len(outs)),
        scratch_shapes=scratch + extra,
        compiler_params=pltpu.CompilerParams(
            collective_id=call_id, has_side_effects=True, vmem_limit_bytes=62 << 20
        ),
        name="attention_backward",
    )(*given, *far)


def finish_kernel(widths, refs):
    count = len(widths) - 1
    result, input_grad, late, early, rel_sum = refs[:5]
    flats = refs[5 : 5 + count]
    out = refs[5 + count :]
    out[0][...] = result[...]
    out = out[1:]
    sums = jnp.concatenate([late[...], early[...]], axis=0)
    out[0][...] = input_grad[...]
    for source, target in zip(flats, out[1 : 1 + count]):
        if source.shape == target.shape:
            target[...] = source[...]
            continue
        half = lanes // 2
        low = lane_ids((1, lanes)) < half
        for k in range(source.shape[0] // 2):
            upper, lower = source[2 * k : 2 * k + 1, :], source[2 * k + 1 : 2 * k + 2, :]
            begin, rest = lower[:, :lanes], lower[:, lanes : 2 * lanes]
            target[3 * k : 3 * k + 1, :] = upper[:, :lanes]
            begin = pltpu.roll(begin, half, 1)
            target[3 * k + 1 : 3 * k + 2, :] = jnp.where(low, upper[:, lanes : 2 * lanes], begin)
            target[3 * k + 2 : 3 * k + 3, :] = jnp.where(low, begin, pltpu.roll(rest, half, 1))
    vectors, tables = out[1 + count : -5], out[-5:]
    for target, (rows, begin, size) in zip(vectors, widths[-1]):
        for j, row in enumerate(rows):
            value = sums[row : row + 1, begin : begin + size]
            if target.shape[0] < size:
                quarter = target.shape[0]
                parts = [value[:, k * quarter : (k + 1) * quarter] for k in range(size // quarter)]
                value = sum(parts[1:], parts[0])
            target[j * size : j * size + value.shape[1]] = value[0]
    half = rel_sum.shape[1] // 2
    rows, cols, lateral_gain, lateral_shift, output_gain = tables
    cols[...] = rel_sum[...].T[:half, : cols.shape[1]]
    rows[...] = rel_sum[: rows.shape[0], half:]
    channels = output_gain.shape[1]
    for k, table in enumerate((lateral_gain, lateral_shift, output_gain)):
        table[...] = sums[19:23, k * channels : (k + 1) * channels]


def finish(result, input_grad, smalls, flats, shapes, vectors, table_shapes):
    def wide(shape):
        return jax.ShapeDtypeStruct(shape, wide_type)

    outs = [jax.ShapeDtypeStruct(result.shape, narrow_type), wide(input_grad.shape)]
    outs += [wide(shape) for shape in shapes]
    for _, _, _, length in vectors:
        outs.append(wide((length,)))
    outs += [wide(shape) for shape in table_shapes]
    widths = [None] * len(flats) + [[vector[:3] for vector in vectors]]

    def body(*refs):
        finish_kernel(widths, refs)

    given = (result, input_grad, *smalls, *flats)
    return pl.pallas_call(
        body,
        out_shape=outs,
        in_specs=vmem_specs(len(given)),
        out_specs=vmem_specs(len(outs)),
        name="finish",
    )(*given)


def prepare_kernel(height, width, count, refs):
    vectors, (rel_rows, rel_cols, four) = refs[:count], refs[count : count + 3]
    vec, tables, rel_all, hot, hot_turned, four_pair, table = refs[count + 3 :]
    model = vec.shape[1]
    vec[...] = jnp.zeros_like(vec)
    at = 0
    for source in vectors:
        value = source[...].astype(wide_type)
        if len(source.shape) == 2:
            vec[at : at + value.shape[0], : value.shape[1]] = value
            at += value.shape[0]
            continue
        value = value.reshape(1, value.shape[0])
        size = value.shape[1]
        for begin in range(0, size, model):
            part = value[:, begin : begin + model]
            vec[at : at + 1, : part.shape[1]] = part
            at += 1
    half = lanes // 2
    tables[...] = jnp.zeros_like(tables)
    for i, source in enumerate((rel_cols, rel_rows)):
        table[...] = jnp.zeros_like(table)
        if i == 0:
            size = source.shape[1]
            table[:half, :size] = source[...].astype(wide_type)
            plain = table[...].T
        else:
            size = source.shape[0]
            table[:size, :half] = source[...].astype(wide_type)
            plain = table[...]
        rel_all[i * lanes : (i + 1) * lanes, :] = plain.astype(narrow_type)
        moved = pltpu.roll(plain, half, 1).astype(narrow_type)
        rel_all[(2 + i) * lanes : (3 + i) * lanes, :] = moved
        row = lax.broadcasted_iota(jnp.int32, (lanes, lanes), 0)
        col = lax.broadcasted_iota(jnp.int32, (lanes, lanes), 1)
        mirror = (row + col == size - 1).astype(wide_type).astype(narrow_type)
        turned = dot_tn(plain.astype(narrow_type), mirror)[:half].astype(narrow_type)
        tables[:half, i * lanes : (i + 1) * lanes] = turned
        tables[half:, (2 + i) * lanes : (3 + i) * lanes] = turned
    total = hot.shape[0]
    token = lax.broadcasted_iota(jnp.int32, (total, lanes), 0)
    lane = lax.broadcasted_iota(jnp.int32, (total, lanes), 1)
    key_row, key_col = lax.div(token, width), lax.rem(token, width)
    by_col = (lax.rem(lane, width) == key_col) & (lane < 2 * width)
    by_row = (lax.rem(lane, height) == key_row) & (lane < 2 * height)
    for i, (plain, turned) in enumerate(
        ((by_col, lane == width - 1 - key_col), (by_row, lane == height - 1 - key_row))
    ):
        here = slice(i * lanes, (i + 1) * lanes)
        hot[:, here] = plain.astype(wide_type).astype(narrow_type)
        hot_turned[:, here] = turned.astype(wide_type).astype(narrow_type)
    cols, rows = four.shape
    value = four[...].astype(wide_type).T.astype(narrow_type)
    four_pair[...] = jnp.zeros_like(four_pair)
    four_pair[:rows, :cols] = value
    four_pair[rows:, cols:] = value


def prepared_shapes(height, width, model, vectors, four):
    rows = 0
    for vector in vectors:
        rows += vector.shape[0] if len(vector.shape) == 2 else -(-vector.shape[0] // model)
    rows = -(-rows // 8) * 8
    total = height * width

    def shape(rows_out, cols, kind=narrow_type):
        return jax.ShapeDtypeStruct((rows_out, cols), kind)

    return [
        shape(rows, model, wide_type),
        shape(lanes, 4 * lanes),
        shape(4 * lanes, lanes),
        shape(total, 2 * lanes),
        shape(total, 2 * lanes),
        shape(2 * four.shape[1], 2 * four.shape[0]),
    ]


class Levels:
    def __init__(self, strip_rows, width):
        self.rows = (4 * strip_rows, 2 * strip_rows, strip_rows, strip_rows // 2)
        self.cols = (4 * width, 2 * width, width, width // 2)
        self.at, self.edge_at, self.wide_at = [], [], []
        total = edge = wide = 0
        for rows, cols in zip(self.rows, self.cols):
            self.at.append(total)
            self.edge_at.append(edge)
            self.wide_at.append(wide)
            total += rows * cols
            edge += cols
            wide += (rows + 2) * cols
        self.total, self.edge, self.wide = total, edge, wide


def put_strided(target, at, count, stride, value):
    for part in range(target.shape[0]):
        target[part, pl.ds(at, count, stride=stride), :] = value[:, part * lanes : (part + 1) * lanes]


def get_strided(source, at, count, stride):
    parts = [source[part, pl.ds(at, count, stride=stride), :] for part in range(source.shape[0])]
    return jnp.concatenate(parts, axis=1)


def join_parts(source, begin, end):
    return jnp.concatenate([source[part, begin:end, :] for part in range(source.shape[0])], axis=1)


def store_edges(levels, level, source, offset, top, bottom):
    rows, cols = levels.rows[level], levels.cols[level]
    at = levels.edge_at[level]
    top[at : at + cols, :] = source[offset : offset + cols, :]
    last = offset + (rows - 1) * cols
    bottom[at : at + cols, :] = source[last : last + cols, :]


def four_times(vec, row):
    value = vec[row : row + 1, :]
    quarter = value.shape[1] // 4
    low = jnp.where(lane_ids(value.shape) < quarter, value, 0.0)
    twice = low + pltpu.roll(low, quarter, 1)
    return twice + pltpu.roll(twice, 2 * quarter, 1)


def level_source_kernel(
    levels,
    strip_rows,
    width,
    base,
    y,
    vec,
    first,
    second,
    eight,
    lat_four,
    lat_eight,
    lat_sixteen,
    lat_thirty,
    lateral,
    top,
    bottom,
    first_map,
    active,
    source_zero,
    source_one,
    pooled,
    reduced,
    spread_zero,
    spread_one,
    wide_y,
    first_ready,
):
    tokens, model = y.shape
    out = lat_sixteen.shape[0]
    mid = first.shape[1] // 4
    values = y[...]

    def finish(level, value, at):
        reduced[at : at + value.shape[0], :] = value
        hat, _ = norm_parts(value)
        gain = vec[base + 5 + level : base + 6 + level, :out]
        shift = vec[base + 9 + level : base + 10 + level, :out]
        return hat * gain + shift

    for tap in range(4):
        a, b = tap // 2, tap % 2
        cols = slice(tap * mid, (tap + 1) * mid)
        rows = slice(tap * tokens, (tap + 1) * tokens)
        mapped = dot_nn(values, first[:, cols]) + vec[base : base + 1, :mid]
        first_map[:, cols] = mapped
        hat, _ = norm_parts(mapped)
        normed = hat * vec[base + 1 : base + 2, :mid] + vec[base + 2 : base + 3, :mid]
        active[rows, :] = (normed * normal_cdf(normed)).astype(narrow_type)
    source = dot_nt(active[...], second[...]) + four_times(vec, base + 3)
    source_zero[...] = source.astype(narrow_type)
    half = source_zero.shape[1] // 2
    for pair in range(2):
        both = dot_nt(source_zero[:, pair * half : (pair + 1) * half], lat_four[...])
        for tap in range(4):
            a, b = tap // 2, tap % 2
            for side in range(2):
                place = (4 * tap + 2 * pair + side) * tokens
                part = both[tap * tokens : (tap + 1) * tokens, side * out : (side + 1) * out]
                value = finish(0, part, place)
                for i in range(strip_rows):
                    at = (4 * i + 2 * a + pair) * levels.cols[0] + 2 * b + side
                    put_strided(spread_zero, at, width, 4, value[i * width : (i + 1) * width])
    lateral[0 : levels.at[1], :] = join_parts(spread_zero, 0, levels.at[1]).astype(narrow_type)
    store_edges(levels, 0, lateral, 0, top, bottom)
    first_ready()
    for tap in range(4):
        a, b = tap // 2, tap % 2
        cols = slice(tap * mid, (tap + 1) * mid)
        rows = slice(tap * tokens, (tap + 1) * tokens)
        mapped = dot_nn(values, eight[:, cols]) + vec[base + 4 : base + 5, :mid]
        source_one[rows, :] = mapped.astype(narrow_type)
    values_one = finish(1, dot_nt(source_one[...], lat_eight[...]), levels.at[1])
    for tap in range(4):
        a, b = tap // 2, tap % 2
        value = values_one[tap * tokens : (tap + 1) * tokens]
        for i in range(strip_rows):
            at = (2 * i + a) * levels.cols[1] + b
            put_strided(spread_one, at, width, 2, value[i * width : (i + 1) * width])
    begin, end = levels.at[1:3]
    lateral[begin:end, :] = join_parts(spread_one, 0, end - begin).astype(narrow_type)
    value = finish(2, dot_nt(values, lat_sixteen[...]), levels.at[2])
    lateral[levels.at[2] : levels.at[3], :] = value.astype(narrow_type)
    for part in range(model // lanes):
        wide_y[part] = values[:, part * lanes : (part + 1) * lanes].astype(wide_type)
    quarter = width // 2
    for i in range(strip_rows // 2):
        summed = 0.0
        for a in range(2):
            for b in range(2):
                at = (2 * i + a) * width + b
                summed = summed + get_strided(wide_y, at, quarter, 2)
        pooled[i * quarter : (i + 1) * quarter, :] = (summed * 0.25).astype(narrow_type)
    value = finish(3, dot_nt(pooled[...], lat_thirty[...]), levels.at[3])
    lateral[levels.at[3] : levels.total, :] = value.astype(narrow_type)
    for level in range(1, 4):
        store_edges(levels, level, lateral, levels.at[level], top, bottom)


class EdgeExchange:
    def __init__(self, levels, top, bottom, above, below, send_sem, recv_sem):
        strip, scale = strip_index(), lax.axis_size("scale")
        count = lax.axis_size("rows") * scale

        def place(index):
            return {"rows": lax.div(index, scale), "scale": lax.rem(index, scale)}

        self.has_up, self.has_down = strip > 0, strip < count - 1
        self.up = place(jnp.maximum(strip - 1, 0))
        self.down = place(jnp.minimum(strip + 1, count - 1))
        self.above, self.below = above, below

        def send(source, target, part, i, device):
            begin = (0, levels.edge_at[1])[part]
            rows = pl.ds(begin, (levels.edge_at[1], levels.edge)[part] - begin)
            return pltpu.make_async_remote_copy(
                src_ref=source.at[rows],
                dst_ref=target.at[rows],
                send_sem=send_sem.at[part, i],
                recv_sem=recv_sem.at[part, i],
                device_id=device,
                device_id_type=MESH_ID,
            )

        self.lower = [send(bottom, above, part, 0, self.down) for part in range(2)]
        self.upper = [send(top, below, part, 1, self.up) for part in range(2)]

    def greet(self, barrier):
        @pl.when(self.has_up)
        def _():
            pl.semaphore_signal(barrier, inc=1, device_id=self.up, device_id_type=MESH_ID)

        @pl.when(self.has_down)
        def _():
            pl.semaphore_signal(barrier, inc=1, device_id=self.down, device_id_type=MESH_ID)

        return jnp.where(self.has_up, 1, 0) + jnp.where(self.has_down, 1, 0)

    def clear(self):
        @pl.when(jnp.logical_not(self.has_up))
        def _():
            self.above[...] = jnp.zeros_like(self.above)

        @pl.when(jnp.logical_not(self.has_down))
        def _():
            self.below[...] = jnp.zeros_like(self.below)

    def send(self, part):
        @pl.when(self.has_down)
        def _():
            self.lower[part].start()

        @pl.when(self.has_up)
        def _():
            self.upper[part].start()

    def arrive(self, part):
        @pl.when(self.has_down)
        def _():
            self.lower[part].wait_send()
            self.upper[part].wait_recv()

        @pl.when(self.has_up)
        def _():
            self.upper[part].wait_send()
            self.lower[part].wait_recv()


def tile_start(index):
    return index if isinstance(index, int) else pl.multiple_of(index, 32)


def widen_rows(levels, level, source, at, first, count, padded, slab, offset):
    cols = levels.cols[level]
    channels = source.shape[1]
    size = count * cols
    padded[8 : 8 + size, :] = source[at : at + size, :].astype(wide_type)
    block = min(256, size)

    def step(i, carry):
        begin = tile_start(i * block)
        got = padded[pl.ds(begin, block + 16), :]
        col = lax.rem(begin + lax.broadcasted_iota(jnp.int32, (block, channels), 0), cols)
        left = jnp.where(col > 0, got[7 : 7 + block], 0.0)
        right = jnp.where(col < cols - 1, got[9 : 9 + block], 0.0)
        joined = jnp.concatenate([left, got[8 : 8 + block], right], axis=1)
        slab[pl.ds(tile_start(offset + first * cols + begin), block), :] = joined.astype(narrow_type)
        return carry

    if size == block:
        step(0, 0)
    else:
        lax.fori_loop(0, size // block, step, 0)


def widen_own(levels, level, source, padded, slab, offset):
    rows = levels.rows[level]
    widen_rows(levels, level, source, levels.at[level], 1, rows, padded, slab, offset)


def widen_edges(levels, level, above, below, padded, slab, offset):
    at, rows = levels.edge_at[level], levels.rows[level]
    widen_rows(levels, level, above, at, 0, 1, padded, slab, offset)
    widen_rows(levels, level, below, at, rows + 1, 1, padded, slab, offset)


def inner_first(size, block, cols, step, arrive):
    count = size // block
    if count > 2 and block >= cols:
        lax.fori_loop(1, count - 1, step, 0)
        arrive()
        step(0, 0)
        step(count - 1, 0)
    else:
        arrive()
        lax.fori_loop(0, count, step, 0)


def smooth_kernel(
    levels,
    base,
    lateral,
    edges,
    weight,
    smooth,
    vec,
    grads,
    top,
    bottom,
    slabs,
    gain_sums,
    padded,
    first_ready,
):
    channels = lateral.shape[1]
    above, below = edges.above, edges.below
    gain_sums[...] = jnp.zeros_like(gain_sums)
    for level in range(4):
        rows, cols = levels.rows[level], levels.cols[level]
        offset = levels.wide_at[level]
        widen_own(levels, level, lateral, padded, slabs, offset)

        def arrive():
            if level < 2:
                edges.arrive(level)
            widen_edges(levels, level, above, below, padded, slabs, offset)

        size = rows * cols
        block = min(256, size)
        gain = vec[base + 13 + level : base + 14 + level, :channels]

        def step(i, carry):
            begin = tile_start(i * block)
            total = None
            for a in range(3):
                window = slabs[pl.ds(tile_start(offset + a * cols + begin), block), :]
                part = dot_nn(
                    window, smooth[level, 3 * a * channels : 3 * (a + 1) * channels, :]
                )
                total = part if total is None else total + part
            hat, inverse = norm_parts(total)
            here = pl.ds(tile_start(levels.at[level] + begin), block)
            upstream = weight[here, :].astype(wide_type)
            gain_sums[level : level + 1, :] += column_sum(upstream * hat)
            grads[here, :] = norm_back(hat, inverse, upstream * gain).astype(narrow_type)
            return carry

        inner_first(size, block, cols, step, arrive)
        store_edges(levels, level, grads, levels.at[level], top, bottom)
        if level == 0:
            first_ready()


def level_back_kernel(levels, strip_rows, width, base, reducer, edges, given, outs, scratch, done):
    (
        grads,
        slabs,
        reduced,
        first_map,
        active,
        source_zero,
        source_one,
        pooled,
        y,
        vec,
        smooth,
        first,
        second,
        eight,
        lat_four,
        lat_eight,
        lat_sixteen,
        lat_thirty,
    ) = given
    y_grad, sums, smooth_grad, first_grad, eight_grad, *rest = outs
    if reducer is not None:
        (rest_grad,) = rest
        plan, own = reducer.plan, smooth_grad.shape[-2]
    else:
        rest_grad, plan = None, None
        second_grad, lat_four_grad, lat_eight_grad, lat_sixteen_grad, lat_thirty_grad = rest
    padded, slab, spread, second_sum, four_sum, eight_sum, total_grad, pool_grad = scratch[:8]
    low_pair, second_low, active_grads = scratch[8:]
    tokens, model = y.shape
    channels = grads.shape[1]
    mid = first.shape[1] // 4
    above, below = edges.above, edges.below
    sums[...] = jnp.zeros_like(sums)

    def smooth_weights(level):
        rows, cols = levels.rows[level], levels.cols[level]
        size = rows * cols
        turned = grads[levels.at[level] : levels.at[level] + size, :].T
        for a in range(3):
            begin = levels.wide_at[level] + a * cols
            for b in range(3):
                part = dot_nn(turned, slabs[begin : begin + size, b * channels : (b + 1) * channels])
                part = part.T.astype(narrow_type)
                at = (level * 9 + 3 * a + b) * channels
                if plan is None:
                    smooth_grad[at : at + channels, :] = part
                    continue
                done = 0
                while done < channels:
                    device, row = divmod(at + done, own)
                    count = min(channels - done, own - row)
                    lead = tuple((device >> (plan.stages - 1 - d)) & 1 for d in range(plan.stages))
                    smooth_grad[lead + (slice(row, row + count),)] = part[done : done + count]
                    done += count

    def smooth_back(level):
        rows, cols = levels.rows[level], levels.cols[level]
        size = rows * cols
        widen_own(levels, level, grads, padded, slab, 0)
        block = min(256, size)

        def arrive():
            if level == 0 and plan is not None:
                reducer.wave(0)
            if level < 2:
                edges.arrive(level)
            widen_edges(levels, level, above, below, padded, slab, 0)

        def step(i, carry):
            begin = tile_start(i * block)
            total = None
            for a in range(3):
                for b in range(3):
                    window = slab[
                        pl.ds(tile_start((2 - a) * cols + begin), block),
                        (2 - b) * channels : (3 - b) * channels,
                    ]
                    tap = (3 * a + b) * channels
                    part = dot_nt(window, smooth[level, tap : tap + channels, :])
                    total = part if total is None else total + part
            for part in range(channels // lanes):
                here = total[:, part * lanes : (part + 1) * lanes]
                spread[part, pl.ds(begin, block), :] = here
            return carry

        inner_first(size, block, cols, step, arrive)

    def reduced_back(level, upstream, at):
        hat, inverse = norm_parts(reduced[at : at + upstream.shape[0], :])
        gain = vec[base + 5 + level : base + 6 + level, :channels]
        sums[5 + level : 6 + level, :channels] += column_sum(upstream * hat)
        sums[9 + level : 10 + level, :channels] += column_sum(upstream)
        return norm_back(hat, inverse, upstream * gain).astype(narrow_type)

    def keep_tap(target, tap, parts, value):
        if len(target.shape) == 2:
            target[:, tap * mid : (tap + 1) * mid] = value.astype(narrow_type)
        else:
            fold_store(target, tap, parts, value)

    first_parts, eight_parts = {}, {}
    turned_y = y[...].T
    total_grad[...] = jnp.zeros_like(total_grad)
    for level in range(4):
        smooth_weights(level)
    if plan is not None:
        reducer.start_near(0)
    smooth_back(0)
    half = source_zero.shape[1] // 2
    for pair in range(2):
        for tap in range(4):
            a, b = tap // 2, tap % 2
            for side in range(2):
                pieces = []
                for i in range(strip_rows):
                    at = (4 * i + 2 * a + pair) * levels.cols[0] + 2 * b + side
                    pieces.append(get_strided(spread, at, width, 4))
                upstream = jnp.concatenate(pieces, axis=0)
                low = reduced_back(0, upstream, (4 * tap + 2 * pair + side) * tokens)
                here = slice(side * channels, (side + 1) * channels)
                low_pair[tap * tokens : (tap + 1) * tokens, here] = low
        own_cols = slice(pair * half, (pair + 1) * half)
        product = dot_tn(low_pair[...], source_zero[:, own_cols])
        if pair == 0:
            four_sum[...] = product
        else:
            four_sum[...] += product
        second_low[:, own_cols] = dot_nn(low_pair[...], lat_four[...]).astype(narrow_type)
    sums[3:4, :] = column_sum(second_low[...].astype(wide_type))
    second_sum[...] = dot_tn(second_low[...], active[...])
    active_grads[...] = dot_nn(second_low[...], second[...])
    for tap in range(4):
        cols = slice(tap * mid, (tap + 1) * mid)
        active_grad = active_grads[tap * tokens : (tap + 1) * tokens, :]
        hat, inverse = norm_parts(first_map[:, cols])
        gain = vec[base + 1 : base + 2, :mid]
        normed = hat * gain + vec[base + 2 : base + 3, :mid]
        normed_grad = active_grad * gelu_slope(normed)
        sums[1:2, :mid] += column_sum(normed_grad * hat)
        sums[2:3, :mid] += column_sum(normed_grad)
        first_low = norm_back(hat, inverse, normed_grad * gain).astype(narrow_type)
        sums[0:1, :mid] += column_sum(first_low.astype(wide_type))
        keep_tap(first_grad, tap, first_parts, dot_nn(turned_y, first_low))
        total_grad[...] += dot_nt(first_low, first[:, cols])
    done(first_grad)
    quarter = lat_four.shape[1] // 2
    if rest_grad is None:
        second_grad[...] = second_sum[...].astype(narrow_type)
        lat_four_grad[...] = (
            four_sum[:channels, :quarter] + four_sum[channels:, quarter:]
        ).astype(narrow_type)
    smooth_back(1)
    pieces = []
    for tap in range(4):
        a, b = tap // 2, tap % 2
        for i in range(strip_rows):
            at = (2 * i + a) * levels.cols[1] + b
            pieces.append(get_strided(spread, at, width, 2))
    low = reduced_back(1, jnp.concatenate(pieces, axis=0), levels.at[1])
    eight_sum[...] = dot_tn(low, source_one[...])
    eight_lows = dot_nn(low, lat_eight[...]).astype(narrow_type)
    for tap in range(4):
        cols = slice(tap * mid, (tap + 1) * mid)
        eight_low = eight_lows[tap * tokens : (tap + 1) * tokens]
        sums[4:5, :mid] += column_sum(eight_low.astype(wide_type))
        keep_tap(eight_grad, tap, eight_parts, dot_nn(turned_y, eight_low))
        total_grad[...] += dot_nt(eight_low, eight[:, cols])
    done(eight_grad)
    if rest_grad is None:
        lat_eight_grad[...] = eight_sum[...].astype(narrow_type)
    smooth_back(2)
    low = reduced_back(2, join_parts(spread, 0, tokens), levels.at[2])
    sixteen = dot_tn(low, y[...])
    if rest_grad is None:
        lat_sixteen_grad[...] = sixteen.astype(narrow_type)
    total_grad[...] += dot_nn(low, lat_sixteen[...])
    smooth_back(3)
    low = reduced_back(3, join_parts(spread, 0, tokens // 4), levels.at[3])
    thirty = dot_tn(low, pooled[...])
    if rest_grad is None:
        lat_thirty_grad[...] = thirty.astype(narrow_type)
    else:
        count = rest_grad.shape[0]
        turned = pltpu.roll(four_sum[channels:, :], quarter, 1)
        both = four_sum[:channels, :] + turned
        four = jnp.where(lane_ids(both.shape) < quarter, both, 0.0)
        for part in range(mid // lanes):
            here = slice(part * lanes, (part + 1) * lanes)
            pieces = [second_sum[:, here]]
            for value in (sixteen, thirty):
                for half in range(2):
                    at = half * mid + part * lanes
                    pieces.append(value[:, at : at + lanes])
            pieces += [eight_sum[:, here], four[:, here]]
            pieces = [piece.reshape(count, piece.shape[0] // count, lanes) for piece in pieces]
            used = sum(piece.shape[1] for piece in pieces)
            pieces.append(jnp.zeros((count, rest_grad.shape[1] - used, lanes), wide_type))
            rest_grad[:, :, here] = jnp.concatenate(pieces, axis=1).astype(narrow_type)
    for target in rest:
        done(target)
    pooled_grad = dot_nn(low, lat_thirty[...]) * 0.25
    count = width // 2
    for i in range(strip_rows // 2):
        piece = pooled_grad[i * count : (i + 1) * count]
        for a in range(2):
            for b in range(2):
                at = (2 * i + a) * width + b
                put_strided(pool_grad, at, count, 2, piece)
    y_grad[...] = (total_grad[...] + join_parts(pool_grad, 0, tokens)).astype(narrow_type)
    if plan is not None:
        for number in range(1, plan.waves()):
            reducer.wave(number)


def region_weights(levels, strip_rows, width, roi, anchors, weight):
    scale = lax.axis_index("scale")
    channels = weight.shape[1]
    ones = jnp.ones((1, channels), narrow_type)

    def own(rows, count):
        shape = (count, rows.shape[0])
        wanted = lax.broadcasted_iota(jnp.int32, shape, 0) + scale * count
        pick = (lax.broadcasted_iota(jnp.int32, shape, 1) == wanted).astype(wide_type)
        rows = rows.astype(wide_type).astype(narrow_type)
        return dot_nn(pick.astype(narrow_type), rows)

    region = own(roi[0], strip_rows).astype(narrow_type)
    for level in range(4):
        rows, cols = levels.rows[level], levels.cols[level]
        shape = (width, cols)
        patch = lax.broadcasted_iota(jnp.int32, shape, 0)
        cell = lax.broadcasted_iota(jnp.int32, shape, 1)
        cell = lax.div(cell, cols // width) if level < 3 else 2 * cell
        spread = (patch == cell).astype(wide_type).astype(narrow_type)
        regions = dot_nn(region, spread)
        positives = own(anchors[level][0], rows)
        for row in range(rows):
            patch_row = row * strip_rows // rows
            factor = positives[row : row + 1] + regions[patch_row : patch_row + 1]
            wide = dot_tn(factor.astype(narrow_type), ones)
            at = levels.at[level] + row * cols
            here = slice(at, at + cols)
            weight[here, :] = (weight[here, :].astype(wide_type) * wide).astype(narrow_type)


def pyramid_kernel(levels, strip_rows, width, base, plan, count, refs):
    y, vec, roi, *anchors = refs[:7]
    far, cotans, refs = refs[7:15], refs[15:19], refs[19:]
    y_grad, sums, gain_sums = refs[:3]
    far_outs, left, scratch = refs[3 : 3 + count], [], refs[3 + count :]
    if plan is not None:
        left, scratch = scratch[: len(plan.pieces)], scratch[len(plan.pieces) :]
    near, scratch = scratch[:9], scratch[9:]
    near_outs, scratch = scratch[:count], scratch[count:]
    sems, smooth_grad = scratch[:2]
    lateral, first_map, active, source_zero, source_one, pooled, reduced = scratch[2:9]
    grads, slabs, spread_one = scratch[9:12]
    edge_refs, scratch = scratch[12:24], scratch[24:]
    work, scratch = scratch[:11], scratch[11:]
    copies = [
        pltpu.make_async_copy(source, target, sems.at[i])
        for i, (source, target) in enumerate(zip(far, near))
    ]
    weight = near[8]
    given = []
    for level, source in enumerate(cotans):
        rows, cols = levels.rows[level], levels.cols[level]
        for row in range(rows):
            at = levels.at[level] + row * cols
            view = source.at[0, lax.axis_index("scale") * rows + row]
            semaphore = sems.at[9 + count + len(given)]
            given.append(pltpu.make_async_copy(view, weight.at[at : at + cols], semaphore))
    for copy in copies + given:
        copy.start()
    first, second, lat_four, eight, lat_eight, lat_sixteen, lat_thirty, smooth, weight = near
    edges, edges_back = [
        EdgeExchange(levels, *edge_refs[6 * i : 6 * i + 6]) for i in range(2)
    ]
    barrier = pltpu.get_barrier_semaphore()
    greeted = edges.greet(barrier)
    reducer = None
    if plan is not None:
        reducer = Reducer(plan, [smooth_grad], [dict(enumerate(left))], scratch)
        greeted = greeted + reducer.greet(barrier)
    for copy in copies[:7]:
        copy.wait()
    padded, _, spread, _, _, _, _, pool_grad = work[:8]
    top, bottom = edge_refs[:2]

    def first_ready():
        pl.semaphore_wait(barrier, greeted)
        edges.clear()
        edges_back.clear()
        edges.send(0)

    level_source_kernel(
        levels,
        strip_rows,
        width,
        base,
        y,
        vec,
        first,
        second,
        eight,
        lat_four,
        lat_eight,
        lat_sixteen,
        lat_thirty,
        lateral,
        top,
        bottom,
        first_map,
        active,
        source_zero,
        source_one,
        pooled,
        reduced,
        spread,
        spread_one,
        pool_grad,
        first_ready,
    )
    edges.send(1)
    for copy in copies[7:] + given:
        copy.wait()
    region_weights(levels, strip_rows, width, roi, anchors, weight)
    top, bottom = edge_refs[6:8]
    smooth_kernel(
        levels,
        base,
        lateral,
        edges,
        weight,
        smooth,
        vec,
        grads,
        top,
        bottom,
        slabs,
        gain_sums,
        padded,
        lambda: edges_back.send(0),
    )
    edges_back.send(1)
    backs = []

    def done(target):
        for i, near_out in enumerate(near_outs):
            if near_out is target:
                backs.append(pltpu.make_async_copy(target, far_outs[i], sems.at[9 + i]))
                backs[-1].start()

    given = (grads, slabs, reduced, first_map, active, source_zero, source_one, pooled, y, vec)
    weights = (smooth, first, second, eight, lat_four, lat_eight, lat_sixteen, lat_thirty)
    outs = (y_grad, sums, smooth_grad, *near_outs)
    if plan is None:
        outs = (y_grad, sums, near_outs[-1], *near_outs[:-1])
    level_back_kernel(
        levels, strip_rows, width, base, reducer, edges_back, given + weights, outs, work, done
    )
    if plan is None:
        done(near_outs[-1])
    for copy in backs:
        copy.wait()
    if plan is not None:
        reducer.finish()


def pyramid(levels, strip_rows, width, base, y, vec, maps, weights, cotans, devices, plan, call_id):
    first, second, four_pair, eight, lat_eight, lat_sixteen, lat_thirty, smooth = weights
    tokens, model = y.shape
    channels = smooth.shape[2]
    mid = first.shape[1] // 4

    def shape(rows, cols, kind=narrow_type):
        return jax.ShapeDtypeStruct((rows, cols), kind)

    outs = [shape(tokens, model), shape(16, model, wide_type), shape(8, channels, wide_type)]
    total = smooth.shape[0] * smooth.shape[1]
    if devices:
        folded = (devices, first.shape[0] // devices * 4, mid)
        rows = second.shape[0] // devices + channels // devices * 6
        rest = (devices, -(-rows // 16) * 16, mid)
        far = [jax.ShapeDtypeStruct(dims, narrow_type) for dims in (folded, folded, rest)]
        smooth_dims = (2,) * plan.stages + (total // devices, channels)
        left = [jax.ShapeDtypeStruct(plan.left(t), narrow_type) for t in range(len(plan.pieces))]
    else:
        far = [
            shape(*first.shape),
            shape(*eight.shape),
            shape(*second.shape),
            shape(channels, four_pair.shape[1] // 2),
            shape(*lat_eight.shape),
            shape(*lat_sixteen.shape),
            shape(*lat_thirty.shape),
            shape(total, channels),
        ]
        smooth_dims = (16, lanes)
        left = []
    count = len(far)

    def body(*refs):
        pyramid_kernel(levels, strip_rows, width, base, plan, count, refs)

    def vmem(rows, cols, kind=narrow_type):
        return pltpu.VMEM((rows, cols), kind)

    size = levels.rows[0] * levels.cols[0]
    edge = [vmem(levels.edge, channels)] * 4 + [pltpu.SemaphoreType.DMA((2, 2))] * 2
    scratch = [pltpu.VMEM(weight_in.shape, narrow_type) for weight_in in weights]
    scratch.append(vmem(levels.total, channels))
    scratch += [pltpu.VMEM(out.shape, narrow_type) for out in far]
    scratch += [
        pltpu.SemaphoreType.DMA((9 + count + sum(levels.rows),)),
        pltpu.VMEM(smooth_dims, narrow_type),
        vmem(levels.total, channels),
        vmem(tokens, 4 * mid, wide_type),
        vmem(4 * tokens, mid),
        vmem(4 * tokens, second.shape[0]),
        vmem(4 * tokens, mid),
        vmem(tokens // 4, model),
        vmem(levels.total, channels, wide_type),
        vmem(levels.total, channels),
        vmem(levels.wide, 3 * channels),
        pltpu.VMEM((channels // lanes, levels.at[2] - levels.at[1], lanes), wide_type),
    ]
    scratch += edge + edge
    scratch += [
        vmem(size + 16, channels, wide_type),
        vmem(size + 2 * levels.cols[0], 3 * channels),
        pltpu.VMEM((channels // lanes, size, lanes), wide_type),
        pltpu.VMEM(second.shape, wide_type),
        pltpu.VMEM(four_pair.shape, wide_type),
        pltpu.VMEM(lat_eight.shape, wide_type),
        vmem(tokens, model, wide_type),
        pltpu.VMEM((model // lanes, tokens, lanes), wide_type),
        vmem(4 * tokens, 2 * channels),
        vmem(4 * tokens, second.shape[0]),
        vmem(4 * tokens, mid, wide_type),
    ]
    if plan is not None:
        scratch += plan.scratch()
    return pl.pallas_call(
        body,
        out_shape=outs + far + left,
        in_specs=vmem_specs(2 + len(maps)) + any_specs(len(weights) + len(cotans)),
        out_specs=vmem_specs(3) + any_specs(count) + vmem_specs(len(left)),
        scratch_shapes=scratch,
        compiler_params=pltpu.CompilerParams(
            collective_id=call_id, has_side_effects=True, vmem_limit_bytes=62 << 20
        ),
        name="pyramid",
    )(y, vec, *maps, *weights, *cotans)


def on_device(
    block_input,
    pre_gain,
    pre_shift,
    qkv_weight,
    qv_bias,
    rel_rows,
    rel_cols,
    proj_weight,
    proj_bias,
    mid_gain,
    mid_shift,
    fc1_weight,
    fc1_bias,
    fc2_weight,
    fc2_bias,
    deconv_first,
    first_bias,
    upnorm_gain,
    upnorm_shift,
    deconv_second,
    second_bias,
    deconv_eight,
    eight_bias,
    lateral_four,
    lateral_eight,
    lateral_sixteen,
    lateral_thirty,
    lateral_gain,
    lateral_shift,
    smooth_weight,
    output_gain,
    grad_four,
    grad_eight,
    grad_sixteen,
    grad_thirty,
    anchor_four,
    anchor_eight,
    anchor_sixteen,
    anchor_thirty,
    roi_mask,
):
    _, strip_rows, width, model = block_input.shape
    head_size = rel_rows.shape[1]
    tokens = strip_rows * width
    height = strip_rows * lax.axis_size(("rows", "scale"))
    channels = smooth_weight.shape[2]
    ff = fc1_weight.shape[1]
    mid = first_bias.shape[0]
    quarter = second_bias.shape[0]
    levels = Levels(strip_rows, width)
    devices = lax.axis_size(("img", "rows", "scale"))
    fused = devices if (model // devices) % 8 == 0 and height <= 16 else 0
    x_own = block_input.reshape(tokens, model)

    base = 8 + ff // model
    (
        vec,
        tables,
        rel_all,
        hot,
        hot_turned,
        lat_four_pair,
        q_all,
        k_all,
        v_all,
        attended,
        attended_wide,
        log_norm,
        middle,
        normed_mid,
        hidden_pre,
        hidden,
        result,
    ) = block_forward(
        height,
        width,
        x_own,
        (
            pre_gain,
            pre_shift,
            qv_bias,
            proj_bias,
            mid_gain,
            mid_shift,
            fc2_bias,
            fc1_bias,
            first_bias,
            upnorm_gain,
            upnorm_shift,
            second_bias,
            eight_bias,
            lateral_gain,
            lateral_shift,
            output_gain,
        ),
        (rel_rows, rel_cols.T, lateral_four.T),
        (qkv_weight, proj_weight, fc1_weight, fc2_weight),
        2,
    )
    smooth_plan = None
    if fused:
        rows = smooth_weight.shape[0] * smooth_weight.shape[1] // devices
        smooth_shape = (devices, rows, channels)
        stages = len(halving_dims())
        cut = -(-rows // 32) * 16
        smooth_cuts = [(0, 0, cut, "x"), (0, cut, rows - cut, "y")]
        smooth_plan = ReducePlan(
            [smooth_shape], [piece + (0, 0, (0, 1)) for piece in smooth_cuts], near=(0,)
        )
    result_grad, level_sums, gain_sums, first_grad, eight_grad, *rest_grads = pyramid(
        levels,
        strip_rows,
        width,
        base,
        result,
        vec,
        (roi_mask, anchor_four, anchor_eight, anchor_sixteen, anchor_thirty),
        (
            deconv_first,
            deconv_second,
            lat_four_pair,
            deconv_eight,
            lateral_eight,
            lateral_sixteen,
            lateral_thirty,
            smooth_weight,
        ),
        (grad_four, grad_eight, grad_sixteen, grad_thirty),
        fused,
        smooth_plan,
        1,
    )
    if fused:
        smooth_rows = smooth_weight.shape[0] * smooth_weight.shape[1] // devices
    else:
        *rest_grads, smooth_grad = rest_grads
    names, final = [], []

    def share(shares, shapes, name, source, weight_in, begin=0):
        rows, columns = weight_in
        own, width_in = rows // devices, shapes[source][-1]
        names.append(name)
        if columns % lanes:
            flat = jax.ShapeDtypeStruct((own, width_in), wide_type)
            places = [(begin, own, 0, 0)]
            final.append((own * columns // lanes, lanes))
        else:
            tiles = columns // lanes
            flat = jax.ShapeDtypeStruct((own * tiles, lanes), wide_type)
            places = [
                (begin + f * own, own, f * width_in // lanes, tiles)
                for f in range(max(columns // width_in, 1))
            ]
            final.append((own * tiles, lanes))
        shares.append((flat, (source, places)))
        return begin + own * max(columns // width_in, 1)

    if fused:
        rest_grad, *smooth_left = rest_grads
    (
        middle_grad,
        attended_grad,
        stats,
        stat_rows,
        block_sums,
        fc1_sum,
        pre_grad,
        branch_grad,
        *block_grads,
    ) = block_backward(
        result_grad,
        (hidden_pre, hidden, normed_mid, middle, attended, attended_wide),
        log_norm,
        vec,
        proj_weight,
        fc1_weight,
        fc2_weight,
        fused,
    )
    operands = (
        x_own,
        q_all,
        k_all,
        v_all,
        attended_grad,
        stats,
        stat_rows,
        middle_grad,
        vec,
        tables,
        rel_all,
        hot,
        hot_turned,
        qkv_weight,
    )
    small_operands = (
        block_sums,
        fc1_sum,
        level_sums,
        gain_sums,
        normed_mid,
        pre_grad,
        hidden,
        result_grad,
        attended,
        branch_grad,
    )
    if fused:
        arrays = (first_grad, eight_grad, rest_grad, *smooth_left)
        own = model // devices
        shapes = [
            (devices, own * (ff // model), model),
            (devices, ff // devices, model),
            (devices, own * (model // mid), mid),
            *(array.shape for array in arrays),
        ]
        query, keys = len(shapes), len(shapes) + 1
        shapes.append((devices, own * (model // mid), mid))
        shapes.append((devices, own * (2 * model // mid), mid))

        def half(source, part):
            size = shapes[source][1]
            first = -(-size // 32) * 16
            return (source, 0, first) if part == 0 else (source, first, size - first)

        def whole(source):
            return (source, 0, shapes[source][-2])

        pieces = [
            (6, *smooth_cuts[0][1:], 0, 2, (2, 4, 6)),
            (7, *smooth_cuts[1][1:], 6, 2, (9, 12, 18)),
            (*whole(3), "z", 0, 0, (5, 8, 11, 13, 22)),
            (*whole(4), "z", 0, 0, (7, 11, 15, 29, 37)),
            (*half(1, 1), "y", 0, 0, (1, 5, 7, 9, 12)),
            (*whole(5), "x", 0, 0, (8, 12, 19, 23, 30)),
            (*whole(query), "z", 0, 0, (11, 14, 28, 34, 39)),
            (*whole(2), "x", 0, 0, (11, 17, 31, 36, 41)),
            (*half(0, 1), "y", 0, 0, (3, 7, 10, 12, 16)),
            (*half(1, 0), "y", 0, 0, (6, 10, 12, 20, 26)),
            (*half(0, 0), "y", 0, 0, (9, 12, 21, 27, 33)),
            (*half(keys, 0), "x", 0, 0, (13, 25, 35, 40, 43)),
            (*half(keys, 1), "y", 0, 0, (13, 24, 32, 38, 42)),
        ]
        plan = ReducePlan(shapes, pieces, near=(0, 1, 2, query, keys))
        plan.riders = (12, 4, 6)
        shares = []
        tiles = channels // lanes
        names.append("smooth")
        final.append((rows * tiles, lanes))
        flat = jax.ShapeDtypeStruct((rows * tiles, lanes), wide_type)
        places = [(0, rows, 0, tiles)]
        shares.append((flat, [(6, places), (7, places)]))
        share(shares, shapes, "first", 3, deconv_first.shape)
        share(shares, shapes, "eight", 4, deconv_eight.shape)
        share(shares, shapes, "fc1", 0, fc1_weight.shape)
        share(shares, shapes, "fc2", 1, fc2_weight.shape)
        share(shares, shapes, "proj", 2, proj_weight.shape)
        at = 0
        for name, weight_in in (
            ("second", deconv_second),
            ("lat_sixteen", lateral_sixteen),
            ("lat_thirty", lateral_thirty),
            ("lat_eight", lateral_eight),
            ("lat_four", lateral_four),
        ):
            at = share(shares, shapes, name, 5, weight_in.shape, at)
        tiles = 3 * model // lanes
        names.append("qkv")
        final.append((own * tiles, lanes))
        flat = jax.ShapeDtypeStruct((own * tiles, lanes), wide_type)
        folds = [(own, f * mid // lanes, tiles) for f in range(3 * model // mid)]
        count = model // mid
        of_query = [(f * own, *fold) for f, fold in enumerate(folds[:count])]
        of_keys = [(f * own, *fold) for f, fold in enumerate(folds[count:])]
        shares.append((flat, [(query, of_query), (keys, of_keys)]))
        got = attention_backward(
            height, width, operands, small_operands, arrays, plan, shares, 0
        )
        vectors = (
            ((3,), 0, model, model),
            ((4,), 0, model, model),
            ((0, 2), 0, model, 2 * model),
            ((8,), 0, model, model),
            ((9,), 0, model, model),
            ((10,), 0, model, model),
            ((12, 13, 14, 15), 0, model, ff),
            ((11,), 0, model, model),
            ((16,), 0, mid, mid),
            ((16,), mid, mid, mid),
            ((17,), 0, mid, mid),
            ((18,), 0, model, quarter),
            ((17,), mid, mid, mid),
        )
        tables_out = (rel_rows.shape, rel_cols.shape[::-1]) + (lateral_gain.shape,) * 3
        result, input_grad, *got = finish(
            result, got[0], got[1:4], got[4:], final, vectors, tables_out
        )
        weight_sums = {name: value.reshape(-1) for name, value in zip(names, got)}
        small = got[len(names) :]
        small = (
            *small[:3],
            small[-5],
            small[-4].T,
            *small[3:13],
            *small[-3:],
        )
    else:
        input_grad, mix_sums, rel_sum, qkv_grad = attention_backward(
            height, width, operands, (), (), None, (), 0
        )
        proj_grad, fc1_grad, fc2_grad = block_grads
        second_grad, four_grad, lat_eight_grad, lat_sixteen_grad, lat_thirty_grad = rest_grads
        packed, folds = [], []
        for grads_in, columns, called in (
            ((smooth_grad,), channels, ("smooth",)),
            ((first_grad, eight_grad), model, ("first", "eight")),
            ((fc1_grad,), model, ("fc1",)),
            ((fc2_grad,), model, ("fc2",)),
            ((qkv_grad,), mid, ("qkv",)),
            (
                (
                    proj_grad,
                    second_grad,
                    lat_sixteen_grad,
                    lat_thirty_grad,
                    lat_eight_grad,
                    four_grad,
                ),
                mid,
                ("proj", "second", "lat_sixteen", "lat_thirty", "lat_eight", "lat_four"),
            ),
        ):
            stacked, fold = fold_chunks(grads_in, columns)
            packed.append(stacked)
            folds.append(fold)
            names += called
        gain_rows = jnp.pad(gain_sums, ((0, 0), (0, model - channels)))
        small_in = (
            jnp.concatenate(
                [mix_sums, block_sums, fc1_sum.reshape(-1, model), level_sums, gain_rows]
            ),
            rel_sum,
        )
        got, small = last_reduce(packed, pack_small(small_in), 3)
        sums, rel_sum = unpack_small(small, small_in)
        flat = []
        for summed, fold in zip(got, folds):
            flat += unfold_chunks(summed, fold)
        weight_sums = dict(zip(names, flat))
        small = (
            sums[3],
            sums[4],
            jnp.concatenate([sums[0], sums[2]]),
            rel_sum[: rel_rows.shape[0], head_size : 2 * head_size],
            rel_sum[: rel_cols.shape[0], :head_size],
            sums[8],
            sums[9],
            sums[10],
            sums[16:20].reshape(-1),
            sums[11],
            sums[20, :mid],
            sums[21, :mid],
            sums[22, :mid],
            jnp.sum(sums[23].reshape(4, quarter), axis=0),
            sums[24, :mid],
            sums[25:29, :channels],
            sums[29:33, :channels],
            sums[36:40, :channels],
        )
    return (
        result.reshape(block_input.shape),
        input_grad.reshape(block_input.shape),
        small[0],
        small[1],
        weight_sums["qkv"],
        small[2],
        small[3],
        small[4],
        weight_sums["proj"],
        small[5],
        small[6],
        small[7],
        weight_sums["fc1"],
        small[8],
        weight_sums["fc2"],
        small[9],
        weight_sums["first"],
        small[10],
        small[11],
        small[12],
        weight_sums["second"],
        small[13],
        weight_sums["eight"],
        small[14],
        weight_sums["lat_four"],
        weight_sums["lat_eight"],
        weight_sums["lat_sixteen"],
        weight_sums["lat_thirty"],
        small[15],
        small[16],
        weight_sums["smooth"],
        small[17],
    )


def solution(mesh):
    in_specs = (
        P("img", ("rows", "scale"), None, None),
        P(),
        P(),
        P(),
        P(),
        P(),
        P(),
        P(),
        P(),
        P(),
        P(),
        P(),
        P(),
        P(),
        P(),
        P(),
        P(),
        P(),
        P(),
        P(),
        P(),
        P(),
        P(),
        P(),
        P(),
        P(),
        P(),
        P(),
        P(),
        P(),
        P(),
        P("img", "rows", None, None),
        P("img", "rows", None, None),
        P("img", "rows", None, None),
        P("img", "rows", None, None),
        P("img", "rows", None),
        P("img", "rows", None),
        P("img", "rows", None),
        P("img", "rows", None),
        P("img", "rows", None),
    )
    out_specs = (
        P("img", ("rows", "scale"), None, None),
        P("img", ("rows", "scale"), None, None),
        P(),
        P(),
        P(("img", "rows", "scale")),
        P(),
        P(),
        P(),
        P(("img", "rows", "scale")),
        P(),
        P(),
        P(),
        P(("img", "rows", "scale")),
        P(),
        P(("img", "rows", "scale")),
        P(),
        P(("img", "rows", "scale")),
        P(),
        P(),
        P(),
        P(("img", "rows", "scale")),
        P(),
        P(("img", "rows", "scale")),
        P(),
        P(("img", "rows", "scale")),
        P(("img", "rows", "scale")),
        P(("img", "rows", "scale")),
        P(("img", "rows", "scale")),
        P(),
        P(),
        P(("img", "rows", "scale")),
        P(),
    )
    return jax.shard_map(
        on_device, mesh=mesh, in_specs=in_specs, out_specs=out_specs, check_vma=False
    )
```

```python
from functools import partial

import jax
import jax.numpy as jnp
from jax import lax
from jax.experimental import pallas as pl
from jax.experimental.pallas import tpu as pltpu
from jax.sharding import PartitionSpec as P

norm_eps = 1e-06
wide_type = jnp.float32
narrow_type = jnp.bfloat16

MESH_ID = pl.DeviceIdType.MESH
lanes = 128


def axis_bits(size):
    bits = []
    step = 1
    while step < size:
        bits.append(step)
        step *= 2
    return bits


def bit_partner(axis, step):
    here = lax.axis_index(axis)
    bit = lax.rem(lax.div(here, step), 2)
    return {axis: here + step - 2 * step * bit}, bit


def halving_dims():
    dims = []
    for axis in ("img", "rows", "scale"):
        for step in reversed(axis_bits(lax.axis_size(axis))):
            dims.append((axis, step))
    return dims


class ReducePlan:
    def __init__(self, shapes, pieces, near=()):
        self.dims = halving_dims()
        self.stages = len(self.dims)
        core = self.dims.index(("img", 1))
        plane = [i for i, d in enumerate(self.dims) if d[0] == "img" and i != core]
        across = [i for i, d in enumerate(self.dims) if d[0] == "rows"]
        along = [i for i, d in enumerate(self.dims) if d[0] == "scale"][::-1]
        orders = {
            "x": [core] + across + plane + along,
            "y": [core] + plane + across + along,
            "z": [core] + along[:1] + plane + across + along[1:],
        }
        self.shapes = shapes
        self.near = near
        self.groups = [[core], across + plane, along]
        self.pieces, self.spans, self.entries, self.events = [], [], [], []
        for source, begin, size, first, entry, start, waves in pieces:
            self.pieces.append((source, begin, size, shapes[source][-1], orders[first]))
            self.spans.append((start, start + len(waves)))
            self.entries.append(entry)
            self.events.append(waves)
        self.staging = sorted(
            {
                piece[2:4]
                for piece, span in zip(self.pieces, self.spans)
                if piece[0] not in near and span[0] == 0
            }
        )

    def lead(self, t):
        return (2,) * (self.stages - max(self.spans[t][0], 1))

    def left(self, t):
        _, _, rows, columns, _ = self.pieces[t]
        return (2,) * (self.stages - self.spans[t][1]) + (rows, columns)

    def scratch(self):
        out = []
        for t, (_, _, rows, columns, _) in enumerate(self.pieces):
            out.append(pltpu.VMEM(self.lead(t) + (rows, columns), narrow_type))
        for t, (_, _, rows, columns, _) in enumerate(self.pieces):
            start, stop = self.spans[t]
            for stage in range(max(start, 1), stop):
                lead = (2,) * (self.stages - 1 - stage)
                out.append(pltpu.VMEM(lead + (rows, columns), narrow_type))
        for shape in self.staging:
            out.append(pltpu.VMEM((2,) * (self.stages - 1) + shape, narrow_type))
        count = len(self.pieces)
        out += [pltpu.SemaphoreType.DMA((count, self.stages))] * 2
        out += [pltpu.SemaphoreType.DMA((count,))]
        return out

    def calls(self):
        out = {}
        for stage in reversed(range(self.stages)):
            for t, (start, stop) in enumerate(self.spans):
                if start <= stage < stop:
                    out.setdefault(self.events[t][stage - start], []).append((t, stage))
        return out

    def waves(self):
        return max(self.calls()) + 1

    def shaped(self, arrays):
        out = []
        for array in arrays:
            if len(array.shape) == 3 and array.shape[0] == 2**self.stages:
                array = array.reshape((2,) * self.stages + array.shape[1:])
            out.append(array)
        return out

    def sums(self):
        return [jax.ShapeDtypeStruct(shape[1:], wide_type) for shape in self.shapes]


class Reducer:
    def __init__(self, plan, sources, outs, scratch):
        self.plan, self.sources, self.outs = plan, sources, outs
        count = len(plan.pieces)
        scratch = list(scratch)
        self.held, scratch = scratch[:count], scratch[count:]
        self.landed = []
        for start, stop in plan.spans:
            size = stop - max(start, 1)
            stages = range(max(start, 1), stop)
            self.landed.append(dict(zip(stages, scratch[:size])))
            scratch = scratch[size:]
        self.staging = dict(zip(plan.staging, scratch))
        self.send_sem, self.recv_sem, self.local_sem = scratch[len(plan.staging) :]
        self.partners = [bit_partner(axis, step) for axis, step in plan.dims]
        users = {shape: [] for shape in plan.staging}
        self.following = {}
        for t in sorted(range(count), key=lambda t: plan.events[t][0]):
            piece = plan.pieces[t]
            if piece[0] in plan.near or plan.spans[t][0]:
                continue
            used = users[piece[2:4]]
            if used:
                self.following[used[-1]] = t
            used.append(t)
        self.first_local = [used[0] for used in users.values()]
        self.todo = plan.calls()
        self.riders = {}

    def greet(self, barrier, groups=False):
        devices = [partner for partner, _ in self.partners]
        if groups:
            devices += [
                self.across(group, mask)
                for group in self.plan.groups
                for mask in range(1, 2 ** len(group))
                if mask & (mask - 1)
            ]
        for device in devices:
            pl.semaphore_signal(barrier, inc=1, device_id=device, device_id_type=MESH_ID)
        return len(devices)

    def across(self, group, mask):
        device = {}
        for i, dim in enumerate(group):
            axis, step = self.plan.dims[dim]
            if mask >> i & 1:
                here = device.get(axis, lax.axis_index(axis))
                device[axis] = here + step - 2 * step * self.partners[dim][1]
        return device

    def index(self, taken, current, keep, gone=()):
        out = []
        for dim in range(self.plan.stages):
            bit = self.partners[dim][1]
            if dim in gone:
                continue
            if dim in taken:
                out.append(bit)
            elif dim == current:
                out.append(bit if keep else 1 - bit)
            else:
                out.append(slice(None))
        return tuple(out)

    def gone(self, t):
        return self.plan.pieces[t][4][: max(self.plan.spans[t][0], 1)]

    def copy(self, t, stage):
        source, begin, rows, _, order = self.plan.pieces[t]
        if stage == 0:
            index = self.index((), order[0], False)
            view = self.sources[source].at[index + (pl.ds(begin, rows),)]
            target = self.held[t]
        else:
            index = self.index(order[:stage], order[stage], False, self.gone(t))
            view = self.held[t].at[index]
            target = self.landed[t][stage]
        return pltpu.make_async_remote_copy(
            src_ref=view,
            dst_ref=target,
            send_sem=self.send_sem.at[t, stage],
            recv_sem=self.recv_sem.at[t, stage],
            device_id=self.partners[order[stage]][0],
            device_id_type=MESH_ID,
        )

    def local(self, t):
        source, begin, rows, columns, order = self.plan.pieces[t]
        if self.plan.spans[t][0]:
            view, target = self.sources[source], self.held[t]
        else:
            index = self.index((), order[0], True)
            view = self.sources[source].at[index + (pl.ds(begin, rows),)]
            target = self.staging[(rows, columns)]
        return pltpu.make_async_copy(view, target, self.local_sem.at[t])

    def each(self, lead, action):
        total = 1
        for size in lead:
            total *= size

        def body(step, carry):
            place, left = [], step
            for size in reversed(lead):
                place.append(lax.rem(left, size))
                left = lax.div(left, size)
            action(tuple(reversed(place)))
            return carry

        if lead:
            lax.fori_loop(0, total, body, 0)
        else:
            action(())

    def add(self, target, arrived, begin=0):
        lead, rows = target.shape[:-2], target.shape[-2]
        arrived = arrived.at[(slice(None),) * len(lead) + (pl.ds(begin, rows),)]

        def action(place):
            target[place] = target[place] + arrived[place]

        self.each(lead, action)

    def start(self):
        for t, span in enumerate(self.plan.spans):
            if span[0]:
                self.local(t).start()
            elif self.plan.pieces[t][0] not in self.plan.near:
                self.copy(t, 0).start()
        for t in self.first_local:
            self.local(t).start()
        for t, span in enumerate(self.plan.spans):
            if span[0]:
                self.local(t).wait()

    def start_near(self, source):
        for t in range(len(self.plan.pieces)):
            if self.plan.pieces[t][0] == source:
                self.copy(t, 0).start()

    def event(self, t, stage):
        source, begin, rows, columns, order = self.plan.pieces[t]
        self.copy(t, stage).wait_recv()
        if stage == 0 and source in self.plan.near:
            own = self.sources[source].at[self.index((), order[0], True)]
            self.add(self.held[t], own, begin)
        elif stage == 0:
            self.local(t).wait()
            self.add(self.held[t], self.staging[(rows, columns)])
            if t in self.following:
                self.local(self.following[t]).start()
        else:
            index = self.index(order[:stage], order[stage], True, self.gone(t))
            self.add(self.held[t].at[index], self.landed[t][stage])
        if t in self.riders:
            self.riders[t].step()
        if stage + 1 < self.plan.spans[t][1]:
            self.copy(t, stage + 1).start()
        elif stage + 1 < self.plan.stages:
            kept = self.held[t].at[self.index(order[: stage + 1], -1, True, self.gone(t))]
            out = self.outs[source][t]

            def action(place):
                out[place] = kept[place]

            self.each(kept.shape[:-2], action)
        else:
            index = self.index(order, -1, True, self.gone(t))
            self.emit(source, begin, self.held[t][index].astype(wide_type))

    def emit(self, source, begin, value):
        out = self.outs[source]
        if not isinstance(out, list):
            out[begin : begin + value.shape[0], :] = value
            return
        for first, count, tile, tiles, ref in out:
            low, high = max(first, begin), min(first + count, begin + value.shape[0])
            if low < high:
                part = value[low - begin : high - begin]
                if tiles == 0:
                    ref[low - first : high - first, :] = part
                for c in range(min(tiles, part.shape[1] // lanes)):
                    here = part[:, c * lanes : (c + 1) * lanes]
                    at = (low - first) * tiles + tile + c
                    ref[pl.ds(at, high - low, stride=tiles), :] = here

    def wave(self, number):
        for t, span in enumerate(self.plan.spans):
            if span[0] and self.plan.entries[t] == number:
                self.copy(t, span[0]).start()
        for t, stage in self.todo.get(number, ()):
            self.event(t, stage)

    def finish(self):
        for t, (start, stop) in enumerate(self.plan.spans):
            for stage in range(start, stop):
                self.copy(t, stage).wait_send()


class SmallReduce:
    def __init__(self, reducer, groups, total, landed, send_sem, recv_sem):
        self.reducer, self.total, self.landed = reducer, total, landed
        self.send_sem, self.recv_sem = send_sem, recv_sem
        self.groups = groups
        self.stage = 0

    @staticmethod
    def sizes(groups):
        sizes = [2 ** len(group) for group in groups]
        return sizes, [sum(sizes[:i]) for i in range(len(sizes) + 1)]

    def copies(self):
        group = self.groups[self.stage]
        sizes, at = self.sizes(self.groups)
        place = sum(self.reducer.partners[dim][1] * 2**i for i, dim in enumerate(group))
        return place, [
            pltpu.make_async_remote_copy(
                src_ref=self.total,
                dst_ref=self.landed.at[at[self.stage] + place],
                send_sem=self.send_sem.at[at[self.stage] + mask],
                recv_sem=self.recv_sem.at[at[self.stage] + mask],
                device_id=self.reducer.across(group, mask),
                device_id_type=MESH_ID,
            )
            for mask in range(1, sizes[self.stage])
        ]

    def start(self):
        place, copies = self.copies()
        for copy in copies:
            copy.start()
        sizes, at = self.sizes(self.groups)
        self.landed[at[self.stage] + place] = self.total[...]

    def step(self):
        if self.stage == len(self.groups):
            return
        for copy in self.copies()[1]:
            copy.wait()
        sizes, at = self.sizes(self.groups)
        total = self.landed[at[self.stage]]
        for i in range(1, sizes[self.stage]):
            total = total + self.landed[at[self.stage] + i]
        self.total[...] = total
        self.stage += 1
        if self.stage < len(self.groups):
            self.start()


class StripGather:
    def __init__(self, owns, wholes, send_sem, recv_sem):
        self.owns, self.wholes = owns, wholes
        self.send_sem, self.recv_sem = send_sem, recv_sem
        self.deep, self.wide = lax.axis_size("scale"), lax.axis_size("rows")
        self.here, self.line = lax.axis_index("scale"), lax.axis_index("rows")

    @staticmethod
    def slots():
        deep, wide = lax.axis_size("scale"), lax.axis_size("rows")
        return 2 * (deep - 1) + (wide - 1) * (2 * deep - 1)

    def greet(self, barrier):
        waits = self.wide - 1
        for k in range(1, self.wide):
            device = {"rows": lax.rem(self.line + k, self.wide)}
            pl.semaphore_signal(barrier, inc=1, device_id=device, device_id_type=MESH_ID)

        @pl.when(self.here > 0)
        def _():
            device = {"scale": self.here - 1}
            pl.semaphore_signal(barrier, inc=1, device_id=device, device_id_type=MESH_ID)

        @pl.when(self.here < self.deep - 1)
        def _():
            device = {"scale": self.here + 1}
            pl.semaphore_signal(barrier, inc=1, device_id=device, device_id_type=MESH_ID)

        more = jnp.where(self.here > 0, 1, 0) + jnp.where(self.here < self.deep - 1, 1, 0)
        return waits + more

    def copies(self, block, slot, device):
        out = []
        for i, whole in enumerate(self.wholes):
            view = whole.at[self.line * self.deep + block]
            out.append(
                pltpu.make_async_remote_copy(
                    src_ref=view,
                    dst_ref=view,
                    send_sem=self.send_sem.at[slot, i],
                    recv_sem=self.recv_sem.at[slot, i],
                    device_id=device,
                    device_id_type=MESH_ID,
                )
            )
        return out

    def along(self, step, right):
        if right:
            block, device = self.here - step, {"scale": jnp.minimum(self.here + 1, self.deep - 1)}
            sent = (block >= 0) & (self.here < self.deep - 1)
            got = self.here - 1 - step >= 0
            return block, step, device, sent, got
        block, device = self.here + step, {"scale": jnp.maximum(self.here - 1, 0)}
        sent = (block < self.deep) & (self.here > 0)
        got = self.here + 1 + step < self.deep
        return block, self.deep - 1 + step, device, sent, got

    def across(self, block, kind, action):
        base = 2 * (self.deep - 1)
        for k in range(1, self.wide):
            slot = base + (k - 1) * (2 * self.deep - 1) + kind
            device = {"rows": lax.rem(self.line + k, self.wide)}
            for copy in self.copies(block, slot, device):
                action(copy)

    def start(self):
        for own, whole in zip(self.owns, self.wholes):
            whole[self.line * self.deep + self.here] = own[...]
        for right in (True, False):
            block, slot, device, sent, _ = self.along(0, right)

            @pl.when(sent)
            def _():
                for copy in self.copies(block, slot, device):
                    copy.start()

        self.across(self.here, 0, lambda copy: copy.start())

    def step(self, number):
        for right in (True, False):
            _, slot, device, _, got = self.along(number, right)
            block = self.here - 1 - number if right else self.here + 1 + number

            @pl.when(got)
            def _():
                for copy in self.copies(block, slot, device):
                    copy.wait_recv()
                kind = 1 + 2 * number + (0 if right else 1)
                self.across(block, kind, lambda copy: copy.start())

            if number + 1 < self.deep - 1:
                later, slot, device, sent, _ = self.along(number + 1, right)

                @pl.when(sent)
                def _():
                    for copy in self.copies(later, slot, device):
                        copy.start()

    def finish(self):
        self.across(self.here, 0, lambda copy: copy.wait())
        for number in range(self.deep - 1):
            for right in (True, False):
                _, _, _, _, got = self.along(number, right)
                block = self.here - 1 - number if right else self.here + 1 + number
                kind = 1 + 2 * number + (0 if right else 1)

                @pl.when(got)
                def _():
                    self.across(block, kind, lambda copy: copy.wait())

                sent_block, slot, device, sent, _ = self.along(number, right)

                @pl.when(sent)
                def _():
                    for copy in self.copies(sent_block, slot, device):
                        copy.wait_send()


def fold_chunks(grads, width):
    devices = lax.axis_size(("img", "rows", "scale"))
    cut, plan = [], []
    for grad in grads:
        rows, columns = grad.shape
        own = rows // devices
        chunk = grad.astype(narrow_type).reshape(devices, own, columns)
        folds = max(columns // width, 1)
        if columns < width:
            chunk = jnp.pad(chunk, ((0, 0), (0, 0), (0, width - columns)))
        cut += [chunk[:, :, f * width : (f + 1) * width] for f in range(folds)]
        plan.append((own, columns, folds))
    stacked = jnp.concatenate(cut, axis=1) if len(cut) > 1 else cut[0]
    extra = -stacked.shape[1] % 16
    if extra:
        stacked = jnp.pad(stacked, ((0, 0), (0, extra), (0, 0)))
    return stacked, plan


def unfold_chunks(summed, plan):
    at, out = 0, []
    for own, columns, folds in plan:
        parts = []
        for _ in range(folds):
            parts.append(summed[at : at + own, : min(columns, summed.shape[1])])
            at += own
        whole = jnp.concatenate(parts, axis=1) if folds > 1 else parts[0]
        out.append(whole.reshape(-1))
    return out


def last_reduce_kernel(plan, count, refs):
    sources, small_in = refs[:count], refs[count]
    outs, small_out = refs[count + 1 : 2 * count + 1], refs[2 * count + 1]
    scratch = refs[2 * count + 2 :]
    small_held, small_landed, small_send, small_recv = scratch[:4]
    reducer = Reducer(plan, sources, outs, scratch[4:])
    barrier = pltpu.get_barrier_semaphore()
    pl.semaphore_wait(barrier, reducer.greet(barrier))

    def small_copy(stage):
        return pltpu.make_async_remote_copy(
            src_ref=small_held,
            dst_ref=small_landed.at[stage],
            send_sem=small_send.at[stage],
            recv_sem=small_recv.at[stage],
            device_id=reducer.partners[plan.pieces[0][4][stage]][0],
            device_id_type=MESH_ID,
        )

    small_held[...] = small_in[...]
    reducer.start()
    small_copy(0).start()
    for number in range(plan.waves()):
        reducer.wave(number)
        if number < plan.stages:
            small_copy(number).wait()
            small_held[...] = small_held[...] + small_landed[number]
            if number + 1 < plan.stages:
                small_copy(number + 1).start()
    small_out[...] = small_held[...]
    reducer.finish()


def cut_rows(shapes):
    out = []
    stages = len(halving_dims())
    for source, (_, rows, _) in enumerate(shapes):
        first = -(-rows // 32) * 16
        waves = tuple(source + stage + (1 if stage else 0) for stage in range(stages))
        out.append((source, 0, first, "x", source, 0, waves))
        if first < rows:
            out.append((source, first, rows - first, "y", source, 0, waves))
    return out


def last_reduce(arrays, small, call_id):
    shapes = [array.shape for array in arrays]
    plan = ReducePlan(shapes, cut_rows(shapes))
    count = len(arrays)

    def body(*refs):
        last_reduce_kernel(plan, count, refs)

    vmem = pl.BlockSpec(memory_space=pltpu.VMEM)
    got = pl.pallas_call(
        body,
        out_shape=plan.sums() + [jax.ShapeDtypeStruct(small.shape, wide_type)],
        in_specs=[pl.BlockSpec(memory_space=pl.ANY)] * count + [vmem],
        out_specs=[vmem] * (count + 1),
        scratch_shapes=[
            pltpu.VMEM(small.shape, wide_type),
            pltpu.VMEM((plan.stages,) + small.shape, wide_type),
            pltpu.SemaphoreType.DMA((plan.stages,)),
            pltpu.SemaphoreType.DMA((plan.stages,)),
        ]
        + plan.scratch(),
        compiler_params=pltpu.CompilerParams(
            collective_id=call_id, has_side_effects=True, vmem_limit_bytes=60 << 20
        ),
        name="last_reduce",
    )(*plan.shaped(arrays), small)
    return got[:count], got[count]


def pack_small(parts):
    flat = jnp.concatenate([part.reshape(-1) for part in parts])
    unit = 8 * lanes
    total = -(-flat.shape[0] // unit) * unit
    return jnp.pad(flat, (0, total - flat.shape[0])).reshape(-1, lanes)


def unpack_small(packed, parts):
    flat = packed.reshape(-1)
    out, at = [], 0
    for part in parts:
        out.append(flat[at : at + part.size].reshape(part.shape))
        at += part.size
    return out


def dot_nn(left, right):
    return lax.dot_general(left, right, (((1,), (0,)), ((), ())), preferred_element_type=wide_type)


def dot_nt(left, right):
    return lax.dot_general(left, right, (((1,), (1,)), ((), ())), preferred_element_type=wide_type)


def dot_tn(left, right):
    return lax.dot_general(left, right, (((0,), (0,)), ((), ())), preferred_element_type=wide_type)


def norm_parts(values):
    centre = values - jnp.mean(values, axis=-1, keepdims=True)
    inverse = lax.rsqrt(jnp.mean(centre * centre, axis=-1, keepdims=True) + norm_eps)
    return centre * inverse, inverse


def norm_back(hat, inverse, hat_grad):
    inner = jnp.mean(hat_grad * hat, axis=-1, keepdims=True)
    return inverse * (hat_grad - jnp.mean(hat_grad, axis=-1, keepdims=True) - hat * inner)


def normal_cdf(values):
    return 0.5 + 0.5 * lax.erf(values * (0.5**0.5))


def gelu_slope(values):
    density = jnp.exp(-0.5 * values * values) * (0.5 / jnp.pi) ** 0.5
    return normal_cdf(values) + values * density


def lane_ids(shape):
    return lax.broadcasted_iota(jnp.int32, shape, len(shape) - 1)


def column_sum(values):
    return jnp.sum(values, axis=0, keepdims=True)


def half_mask(half, head_size, value):
    lane = lane_ids((1, 2 * head_size))
    inside = (lane >= half * head_size) & (lane < (half + 1) * head_size)
    return jnp.where(inside, value, 0.0).astype(narrow_type)


def split_lanes(values, used):
    lane = lane_ids(values.shape)
    twice = jnp.where(lane < used, values, pltpu.roll(values, used, 1))
    near = twice.astype(narrow_type).astype(wide_type)
    both = jnp.where(lane < used, near, twice - near)
    return jnp.where(lane < 2 * used, both, 0.0).astype(narrow_type)


def place_cols(tab, width):
    by_col = pltpu.roll(tab, lanes - (width - 1), 1, stride=1, stride_axis=0)
    return split_lanes(by_col, width)


def place_rows(tab, row, height):
    by_row = pltpu.roll(tab, lax.rem(lanes - (height - 1) + row, lanes), 1)
    return split_lanes(by_row, height)


def both_halves(values, head_size, scale):
    masked = [values * half_mask(half, head_size, scale) for half in range(2)]
    return jnp.concatenate(masked, axis=0)


def own_extra(tab, strip_rows, width, height):
    out = []
    for half in range(2):
        for i in range(strip_rows):
            piece = tab[i * width : (i + 1) * width, 2 * half * lanes : 2 * (half + 1) * lanes]
            row = strip_index() * strip_rows + i
            cols = place_cols(piece[:, :lanes], width)
            out.append(jnp.concatenate([cols, place_rows(piece[:, lanes:], row, height)], axis=1))
    return jnp.concatenate(out, axis=0)


def strip_index():
    return lax.axis_index("rows") * lax.axis_size("scale") + lax.axis_index("scale")


def block_forward_kernel(height, width, count, refs):
    x_own, refs = refs[0], refs[1:]
    small, refs = refs[: count + 3], refs[count + 3 :]
    qkv_hbm, proj_hbm, fc1_hbm, fc2_hbm = refs[:4]
    prepared, refs = refs[4:10], refs[10:]
    (
        q_out,
        k_out,
        v_out,
        attended,
        attended_wide,
        log_norm,
        middle,
        normed_mid,
        hidden_pre,
        hidden,
        result,
    ) = refs[:11]
    qkv_weight, proj, fc1, fc2, sems, x_all, table, extras, send_sem, recv_sem = refs[11:21]
    q_all, k_all, v_all, out_sems = refs[21:]
    vec, tables, _, hot, _, _ = prepared
    model = x_all.shape[2]
    tokens = middle.shape[0]
    strip_rows = tokens // width
    head_size = lanes // 2
    copies = [
        pltpu.make_async_copy(source, target, sems.at[i])
        for i, (source, target) in enumerate(
            ((proj_hbm, proj), (fc1_hbm, fc1), (fc2_hbm, fc2), (qkv_hbm, qkv_weight))
        )
    ]
    for copy in reversed(copies):
        copy.start()
    gather = StripGather([x_own], [x_all], send_sem, recv_sem)
    barrier = pltpu.get_barrier_semaphore()
    pl.semaphore_wait(barrier, gather.greet(barrier))
    gather.start()
    prepare_kernel(height, width, count, (*small, *prepared, table))
    copies[3].wait()
    start = pl.multiple_of(strip_index() * tokens, tokens)

    def mix(begin, blocks):
        at = pl.ds(pl.multiple_of(begin * tokens, tokens), blocks * tokens)
        inputs = x_all[pl.ds(begin, blocks)].reshape(blocks * tokens, model)
        hat, _ = norm_parts(inputs.astype(wide_type))
        normed = (hat * vec[0:1, :] + vec[1:2, :]).astype(narrow_type)
        mixed = dot_nn(normed, qkv_weight[...])
        q_all[at, :] = (mixed[:, :model] + vec[2:3, :]).astype(narrow_type)
        k_all[at, :] = mixed[:, model : 2 * model].astype(narrow_type)
        v_all[at, :] = (mixed[:, 2 * model :] + vec[3:4, :]).astype(narrow_type)

    for number in range(gather.deep - 1):
        gather.step(number)
    line = gather.line * gather.deep
    mix(line, gather.deep)
    for pair in range(model // lanes):
        queries = q_all[pl.ds(start, tokens), pair * lanes : (pair + 1) * lanes]
        extras[pair] = own_extra(dot_nn(queries, tables[...]), strip_rows, width, height)
    gather.finish()

    def others(step, carry):
        mix(lax.rem(gather.line + 1 + step, gather.wide) * gather.deep, gather.deep)
        return carry

    lax.fori_loop(0, gather.wide - 1, others, 0)
    backs = [
        pltpu.make_async_copy(source, target, out_sems.at[i])
        for i, (source, target) in enumerate(((q_all, q_out), (k_all, k_out), (v_all, v_out)))
    ]
    for copy in backs:
        copy.start()
    log_norm[...] = jnp.zeros_like(log_norm)
    lane = lane_ids((tokens, lanes))

    def pair_step(pair):
        cols = slice(pair * lanes, (pair + 1) * lanes)
        queries = q_all[pl.ds(start, tokens), cols]
        values = v_all[:, cols]
        keys = jnp.concatenate([k_all[:, cols], hot[...]], axis=1)
        masked = both_halves(queries, head_size, head_size**-0.5)
        scores = dot_nt(jnp.concatenate([masked, extras[pair]], axis=1), keys)
        peak = jnp.max(scores, axis=-1, keepdims=True)
        raised = jnp.exp(scores - peak)
        total = jnp.sum(raised, axis=-1, keepdims=True)
        probs = (raised * (1.0 / total)).astype(narrow_type)
        out = dot_nn(probs, values)
        mixed = (out[:tokens], out[tokens:])
        norm = peak + jnp.log(total)
        kept = jnp.where(lane == 2 * pair, norm[:tokens], log_norm[...])
        log_norm[...] = jnp.where(lane == 2 * pair + 1, norm[tokens:], kept)
        joined = jnp.where(lane < head_size, mixed[0], mixed[1])
        attended_wide[:, cols] = joined
        attended[:, cols] = joined.astype(narrow_type)

    for pair in range(model // lanes):
        pair_step(pair)
    copies[0].wait()
    inputs = x_all[strip_index()].astype(wide_type)
    centre = inputs + (dot_nn(attended[...], proj[...]) + vec[4:5, :])
    middle[...] = centre
    hat, _ = norm_parts(centre)
    normed_low = (hat * vec[5:6, :] + vec[6:7, :]).astype(narrow_type)
    normed_mid[...] = normed_low
    copies[1].wait()
    copies[2].wait()
    result_wide = centre + vec[7:8, :]
    for j in range(fc1.shape[1] // model):
        cols = slice(j * model, (j + 1) * model)
        pre = dot_nn(normed_mid[...], fc1[:, cols]) + vec[8 + j : 9 + j, :]
        hidden_pre[:, cols] = pre
        low = (pre * normal_cdf(pre)).astype(narrow_type)
        hidden[:, cols] = low
        result_wide = result_wide + dot_nn(low, fc2[cols, :])
    result[...] = result_wide.astype(narrow_type)
    for copy in backs:
        copy.wait()


def vmem_specs(count):
    return [pl.BlockSpec(memory_space=pltpu.VMEM)] * count


def any_specs(count):
    return [pl.BlockSpec(memory_space=pl.ANY)] * count


def block_forward(height, width, x_own, vectors, turned, weights, call_id):
    tokens, model = x_own.shape
    total = height * width
    ff = weights[2].shape[1]
    slots = StripGather.slots()

    def shape(rows, cols, kind):
        return jax.ShapeDtypeStruct((rows, cols), kind)

    outs = [
        shape(total, model, narrow_type),
        shape(total, model, narrow_type),
        shape(total, model, narrow_type),
        shape(tokens, model, narrow_type),
        shape(tokens, model, wide_type),
        shape(tokens, lanes, wide_type),
        shape(tokens, model, wide_type),
        shape(tokens, model, narrow_type),
        shape(tokens, ff, wide_type),
        shape(tokens, ff, narrow_type),
        shape(tokens, model, narrow_type),
    ]
    outs = prepared_shapes(height, width, model, vectors, turned[2]) + outs
    small = (*vectors, *turned)

    def body(*refs):
        block_forward_kernel(height, width, len(vectors), refs)

    return pl.pallas_call(
        body,
        out_shape=outs,
        in_specs=vmem_specs(1 + len(small)) + any_specs(4),
        out_specs=vmem_specs(6) + any_specs(3) + vmem_specs(len(outs) - 9),
        scratch_shapes=[pltpu.VMEM(weight.shape, narrow_type) for weight in weights]
        + [
            pltpu.SemaphoreType.DMA((4,)),
            pltpu.VMEM((total // tokens, tokens, model), narrow_type),
            pltpu.VMEM((lanes, lanes), wide_type),
            pltpu.VMEM((model // lanes, 2 * tokens, 2 * lanes), narrow_type),
            pltpu.SemaphoreType.DMA((slots, 1)),
            pltpu.SemaphoreType.DMA((slots, 1)),
            pltpu.VMEM((total, model), narrow_type),
            pltpu.VMEM((total, model), narrow_type),
            pltpu.VMEM((total, model), narrow_type),
            pltpu.SemaphoreType.DMA((3,)),
        ],
        compiler_params=pltpu.CompilerParams(
            collective_id=call_id, has_side_effects=True, vmem_limit_bytes=60 << 20
        ),
        name="block_forward",
    )(x_own, *small, *weights)


def fold_store(target, number, parts, value):
    devices = target.shape[0]
    own = value.shape[0] // devices
    parts[number] = value.reshape(devices, own, value.shape[1])
    if number % 2:
        both = jnp.concatenate([parts.pop(number - 1), parts.pop(number)], axis=1)
        begin = (number - 1) * own
        target[:, begin : begin + 2 * own, :] = both.astype(narrow_type)


def block_backward_kernel(whole, refs):
    (
        result_grad,
        hidden_pre,
        hidden,
        normed_mid,
        middle,
        attended,
        attended_wide,
        log_norm,
        vec,
        proj_far,
        fc1_far,
        fc2_far,
        middle_grad,
        attended_grad,
        stats,
        stat_rows,
        sums,
        fc1_sum,
        pre_out,
        branch_out,
    ) = refs[:20]
    refs = refs[20:]
    if whole:
        proj_grad, fc1_grad, fc2_grad = refs[:3]
        refs = refs[3:]
    proj, fc1, fc2, sems = refs
    width = middle.shape[1]
    blocks = hidden.shape[1] // width
    fc1_in, fc2_in = [], []
    for j in range(blocks):
        part = slice(j * width, (j + 1) * width)
        fc1_in.append(
            pltpu.make_async_copy(fc1_far.at[:, part], fc1.at[:, part], sems.at[0, j])
        )
        fc2_in.append(pltpu.make_async_copy(fc2_far.at[part], fc2.at[part], sems.at[1, j]))
        fc2_in[j].start()
        fc1_in[j].start()
    proj_in = pltpu.make_async_copy(proj_far, proj, sems.at[2, 0])
    proj_in.start()
    model = middle.shape[1]
    ff = hidden.shape[1]
    grad_low = result_grad[...]
    grad_wide = grad_low.astype(wide_type)
    back = jnp.zeros(middle.shape, wide_type)
    for j in range(ff // model):
        cols = slice(j * model, (j + 1) * model)
        pre = hidden_pre[:, cols]
        fc2_in[j].wait()
        pre_grad = dot_nt(grad_low, fc2[cols, :]) * gelu_slope(pre)
        pre_low = pre_grad.astype(narrow_type)
        fc1_sum[:, cols] = column_sum(pre_low.astype(wide_type))
        fc1_in[j].wait()
        back = back + dot_nt(pre_low, fc1[:, cols])
        pre_out[:, cols] = pre_low
        if whole:
            part = dot_nn(normed_mid[...].T, pre_low)
            fc1_grad[:, cols] = part.astype(narrow_type)
            fc2_grad[cols, :] = dot_nn(hidden[:, cols].T, grad_low).astype(narrow_type)
    proj_in.wait()
    hat, inverse = norm_parts(middle[...])
    gain_grad = column_sum(back * hat)
    shift_grad = column_sum(back)
    centre_grad = grad_wide + norm_back(hat, inverse, back * vec[5:6, :])
    middle_grad[...] = centre_grad
    branch_low = centre_grad.astype(narrow_type)
    sums[0:1, :] = column_sum(branch_low.astype(wide_type))
    sums[1:2, :] = gain_grad
    sums[2:3, :] = shift_grad
    sums[3:4, :] = column_sum(grad_wide)
    sums[4:8, :] = jnp.zeros((4, model), wide_type)
    branch_out[...] = branch_low
    if whole:
        proj_grad[...] = dot_nn(attended[...].T, branch_low).astype(narrow_type)
    out_grad = dot_nt(branch_low, proj[...]).astype(narrow_type)
    attended_grad[...] = out_grad
    product = out_grad.astype(wide_type) * attended_wide[...]
    near = product.astype(narrow_type)
    rest = (product - near.astype(wide_type)).astype(narrow_type)
    head_size = lanes // 2
    channel = lax.broadcasted_iota(jnp.int32, (model, lanes), 0)
    head = lax.broadcasted_iota(jnp.int32, (model, lanes), 1)
    member = (lax.div(channel, head_size) == head - 16).astype(wide_type).astype(narrow_type)
    delta = dot_nn(near, member) + dot_nn(rest, member)
    both = jnp.where(lane_ids(delta.shape) < 16, log_norm[...], delta)
    stats[...] = both
    stat_rows[...] = both.T[:32, :]


def share_outs(plan, shares, refs):
    outs = [[] for _ in plan.shapes]
    for ref, share in zip(refs, shares):
        for source, places in share if isinstance(share, list) else [share]:
            for place in places:
                outs[source].append(place + (ref,))
    return outs


def block_backward(result_grad, kept, log_norm, vec, proj, fc1, fc2, devices):
    hidden_pre, hidden, normed_mid, middle, attended, attended_wide = kept
    tokens, model = middle.shape
    ff = fc1.shape[1]

    def shape(rows, cols, kind):
        return jax.ShapeDtypeStruct((rows, cols), kind)

    outs = [
        shape(tokens, model, wide_type),
        shape(tokens, model, narrow_type),
        shape(tokens, lanes, wide_type),
        shape(32, tokens, wide_type),
        shape(8, model, wide_type),
        shape(1, ff, wide_type),
        shape(tokens, ff, narrow_type),
        shape(tokens, model, narrow_type),
    ]
    whole = not devices
    if whole:
        outs += [
            shape(model, model, narrow_type),
            shape(model, ff, narrow_type),
            shape(ff, model, narrow_type),
        ]

    def body(*refs):
        block_backward_kernel(whole, refs)

    return pl.pallas_call(
        body,
        out_shape=outs,
        in_specs=vmem_specs(9) + any_specs(3),
        out_specs=vmem_specs(len(outs)),
        scratch_shapes=[
            pltpu.VMEM(proj.shape, narrow_type),
            pltpu.VMEM(fc1.shape, narrow_type),
            pltpu.VMEM(fc2.shape, narrow_type),
            pltpu.SemaphoreType.DMA((3, ff // model)),
        ],
        compiler_params=pltpu.CompilerParams(vmem_limit_bytes=60 << 20),
        name="block_backward",
    )(
        result_grad,
        hidden_pre,
        hidden,
        normed_mid,
        middle,
        attended,
        attended_wide,
        log_norm,
        vec,
        proj,
        fc1,
        fc2,
    )


def small_groups(plan):
    return [[[dim] for dim in plan.pieces[t][4]] for t in plan.riders]


def attention_backward_kernel(height, width, plan, shares, refs):
    (
        x_own,
        q_all,
        k_all,
        v_all,
        grad_own,
        own_stats,
        stat_own,
        middle_grad,
        vec,
        tables,
        rel_all,
        hot,
        hot_turned,
        qkv_weight,
    ) = refs[:14]
    refs = refs[14:]
    if plan is None:
        input_grad, sums, rel_sum, weight_grad = refs[:4]
        scratch = refs[4:]
    else:
        block_sums, fc1_sum, level_sums, gain_sums = refs[:4]
        normed_mid, pre_grad, hidden, result_grad, attended, branch_grad = refs[4:10]
        refs = refs[10:]
        count = len(plan.shapes) - len(plan.near)
        sources, refs = refs[:count], refs[count:]
        input_grad, sums_out, early_out, rel_out = refs[:4]
        flat = refs[4 : 4 + len(shares)]
        scratch = refs[4 + len(shares) :]
        near_fc1, near_fc2, near_proj, near_query, near_rest, sums, early, rel_sum = scratch[:8]
        small_scratch, scratch = scratch[8:17], scratch[17:]
        near_block = (near_fc1, near_fc2, near_proj)
        outs = share_outs(plan, shares, flat)
    joined, wide_tab, cols_extra, rows_extra, grad_all, stat_all, stat_rows, rel_grad = scratch[:8]
    gather = StripGather([grad_own, stat_own], [grad_all, stat_all], scratch[8], scratch[9])
    total, model = q_all.shape
    tokens = x_own.shape[0]
    strip_rows = tokens // width
    head_size = lanes // 2
    scale = head_size**-0.5
    strip = strip_index()
    strips = grad_all.shape[0]
    own = pl.ds(pl.multiple_of(strip * tokens, tokens), tokens)
    pairs = model // lanes
    barrier = pltpu.get_barrier_semaphore()
    greeted = gather.greet(barrier)
    if plan is not None:
        arrays = (*near_block, *sources, near_query, near_rest)
        reducer = Reducer(plan, arrays, outs, scratch[10:])
        greeted = greeted + reducer.greet(barrier)
        late_sums, early_sums, rel_sums = [
            SmallReduce(reducer, groups, total, *small_scratch[3 * i : 3 * i + 3])
            for i, (groups, total) in enumerate(zip(small_groups(plan), (sums, early, rel_sum)))
        ]
        reducer.riders = dict(zip(plan.riders, (late_sums, early_sums, rel_sums)))
    if plan is not None:
        early[0:4, :] = block_sums[0:4, :]
        size = early.shape[1]
        for j in range(fc1_sum.shape[1] // size):
            early[4 + j : 5 + j, :] = fc1_sum[:, j * size : (j + 1) * size]
        mid, channels = size // 2, gain_sums.shape[1]
        early[8:9, :mid], early[8:9, mid:] = level_sums[0:1, :mid], level_sums[1:2, :mid]
        early[9:10, :mid], early[9:10, mid:] = level_sums[2:3, :mid], level_sums[4:5, :mid]
        early[10:11, :] = level_sums[3:4, :]
        early[11:15, :channels] = level_sums[5:9, :channels]
        early[11:15, channels : 2 * channels] = level_sums[9:13, :channels]
        early[11:15, 2 * channels :] = gain_sums[0:4, :]
        early[15:16, :] = jnp.zeros((1, size), wide_type)
    pl.semaphore_wait(barrier, greeted)
    gather.start()
    if plan is not None:
        early_sums.start()
        reducer.start()

    rel_grad[...] = jnp.zeros_like(rel_grad)
    lane = lane_ids((tokens, lanes))

    def own_queries(pair):
        cols = slice(pair * lanes, (pair + 1) * lanes)
        queries = q_all[own, cols]
        keys = k_all[:, cols]
        extra = own_extra(dot_nn(queries, tables[...]), strip_rows, width, height)
        masked = both_halves(queries, head_size, scale)
        keys_hot = jnp.concatenate([keys, hot[...]], axis=1)
        scores = dot_nt(jnp.concatenate([masked, extra], axis=1), keys_hot)
        norms, means = [], []
        for half in range(2):
            head = 2 * pair + half
            stats = own_stats[...]
            norms.append(jnp.sum(jnp.where(lane == head, stats, 0.0), axis=-1, keepdims=True))
            means.append(jnp.sum(jnp.where(lane == 16 + head, stats, 0.0), axis=-1, keepdims=True))
        probs = jnp.exp(scores - jnp.concatenate(norms, axis=0))
        prob_grad = dot_nt(both_halves(grad_own[:, cols], head_size, 1.0), v_all[:, cols])
        score_grad = probs * (prob_grad - jnp.concatenate(means, axis=0))
        keys_turned = jnp.concatenate([keys, hot_turned[...]], axis=1)
        back = dot_nn(score_grad.astype(narrow_type), keys_turned)
        offsets = []
        for half in range(2):
            parts = []
            for i in range(strip_rows):
                at = half * tokens + i * width
                piece = back[at : at + width]
                by_col = pltpu.roll(piece[:, lanes : 2 * lanes], 0, 1, stride=1, stride_axis=0)
                by_row = pltpu.roll(piece[:, 2 * lanes :], strip * strip_rows + i, 1)
                parts.append(jnp.concatenate([by_col, by_row], axis=1))
            offsets.append(jnp.concatenate(parts, axis=0))
        off = jnp.concatenate(offsets, axis=1).astype(narrow_type)
        plain = jnp.where(lane < head_size, back[:tokens, :lanes], back[tokens:, :lanes])
        query_grad = plain * scale + dot_nn(off, rel_all[...])
        joined[:, cols] = query_grad.astype(narrow_type)
        rel_grad[...] += dot_tn(off, queries)

    def own_keys(pair):
        at = pair * lanes
        cols = slice(at, at + lanes)
        all_queries = q_all[:, cols]
        wide_tab[...] = dot_nn(all_queries, tables[...])

        def widen(row, inner):
            rows = pl.ds(pl.multiple_of(row * width, width), width)
            for half in range(2):
                begin = 2 * half * lanes
                cols_extra[half, rows, :] = place_cols(wide_tab[rows, begin : begin + lanes], width)
                piece = wide_tab[rows, begin + lanes : begin + 2 * lanes]
                rows_extra[half, rows, :] = place_rows(piece, row, height)
            return inner

        lax.fori_loop(0, height, widen, 0)
        all_grads = grad_all[:, :, cols].reshape(total, lanes)
        hot_own = hot[own, :]
        blank = jnp.zeros((tokens, lanes), narrow_type)
        hot_col, hot_row = hot_own[:, :lanes], hot_own[:, lanes:]
        keys = both_halves(k_all[own, cols], head_size, scale)
        left = jnp.concatenate(
            [
                jnp.concatenate([hot_col, blank, hot_row, blank], axis=1),
                jnp.concatenate([blank, hot_col, blank, hot_row], axis=1),
            ],
            axis=0,
        )
        right = jnp.concatenate(
            [all_queries, cols_extra[0], cols_extra[1], rows_extra[0], rows_extra[1]], axis=1
        )
        scores = dot_nt(jnp.concatenate([keys, left], axis=1), right)
        prob_grad = dot_nt(both_halves(v_all[own, cols], head_size, 1.0), all_grads)
        probs, score_grads = [], []
        for half in range(2):
            head = 2 * pair + half
            here = slice(half * tokens, (half + 1) * tokens)
            prob = jnp.exp(scores[here] - stat_rows[head : head + 1, :])
            probs.append(prob.astype(narrow_type))
            score_grad = prob * (prob_grad[here] - stat_rows[16 + head : 17 + head, :])
            score_grads.append(score_grad.astype(narrow_type))
        key_both = dot_nn(jnp.concatenate(score_grads, axis=0), all_queries)
        value_both = dot_nn(jnp.concatenate(probs, axis=0), all_grads)
        key_grad = jnp.where(lane < head_size, key_both[:tokens], key_both[tokens:]) * scale
        value_grad = jnp.where(lane < head_size, value_both[:tokens], value_both[tokens:])
        joined[:, model + at : model + at + lanes] = key_grad.astype(narrow_type)
        joined[:, 2 * model + at : 2 * model + at + lanes] = value_grad.astype(narrow_type)

    hat, inverse = norm_parts(x_own[...].astype(wide_type))
    normed_turned = (hat * vec[0:1, :] + vec[1:2, :]).astype(narrow_type).T
    steps = gather.deep - 1
    progress = [0]

    def advance():
        if plan is not None:
            reducer.wave(progress[0])
            progress[0] += 1

    def near_grads(near, left, right, first):
        fold = near.shape[-1]
        own_count = left.shape[0] // 2**plan.stages
        lead = (slice(None),) * plan.stages
        parts = {}
        for f in range(near.shape[-2] // own_count):
            begin = first + f * fold
            value = dot_nn(left, right[:, begin : begin + fold])
            parts[f] = value.reshape((2,) * plan.stages + (own_count, fold))
            if f % 2:
                both = jnp.concatenate([parts.pop(f - 1), parts.pop(f)], axis=plan.stages)
                rows = slice((f - 1) * own_count, (f + 1) * own_count)
                near[lead + (rows,)] = both.astype(narrow_type)

    def near_second():
        blocks = hidden.shape[1] // model
        grads = result_grad[...]
        bits = len(axis_bits(blocks))
        for j in range(blocks):
            value = dot_nn(hidden[:, j * model : (j + 1) * model].T, grads).astype(narrow_type)
            lead = tuple((j >> (bits - 1 - d)) & 1 for d in range(bits))
            near_fc2[lead] = value.reshape(near_fc2.shape[bits:])

    if plan is not None:
        near_second()
        reducer.start_near(1)
    advance()
    for pair in range(pairs):
        own_queries(pair)
        if pair < steps:
            gather.step(pair)
        if plan is not None and pair == 1:
            near_grads(near_fc1, normed_mid[...].T, pre_grad, 0)
            reducer.start_near(0)
        if plan is not None and pair == 3:
            near_grads(near_proj, attended[...].T, branch_grad, 0)
            reducer.start_near(2)
        advance()
    turned = pltpu.roll(rel_grad[2 * lanes :, :], head_size, 1)
    both = rel_grad[: 2 * lanes, :] + turned
    low = lane_ids((lanes, lanes)) < head_size
    rel_sum[...] = jnp.where(low, both[:lanes], pltpu.roll(both[lanes:], head_size, 1))
    if plan is not None:
        near_grads(near_query, normed_turned, joined, 0)
        rel_sums.start()
        reducer.start_near(len(plan.shapes) - 2)
    gather.finish()
    for block in range(strips):
        stat_rows[:, block * tokens : (block + 1) * tokens] = stat_all[block]
    for pair in range(pairs):
        own_keys(pair)
        advance()
    if plan is not None:
        near_grads(near_rest, normed_turned, joined, model)
        reducer.start_near(len(plan.shapes) - 1)
    back = jnp.zeros((tokens, model), wide_type)
    for j in range(3):
        cols = slice(j * model, (j + 1) * model)
        part = joined[:, cols]
        sums[j : j + 1, :] = column_sum(part.astype(wide_type))
        back = back + dot_nt(part, qkv_weight[:, cols])
        if plan is None:
            weight_grad[:, cols] = dot_nn(normed_turned, part).astype(narrow_type)
    sums[3:4, :] = column_sum(back * hat)
    sums[4:5, :] = column_sum(back)
    sums[5:8, :] = jnp.zeros((3, model), wide_type)
    if plan is not None:
        late_sums.start()
    input_grad[...] = middle_grad[...] + norm_back(hat, inverse, back * vec[0:1, :])
    if plan is None:
        return
    while progress[0] < plan.waves():
        advance()
    for small in (early_sums, rel_sums, late_sums):
        while small.stage < len(small.groups):
            small.step()
    sums_out[...] = sums[...]
    early_out[...] = early[...]
    rel_out[...] = rel_sum[...]
    reducer.finish()


def attention_backward(height, width, operands, small, arrays, plan, shares, call_id):
    tokens, model = operands[0].shape
    total = operands[1].shape[0]
    strips = total // tokens
    slots = StripGather.slots()

    def shape(rows, cols, kind):
        return jax.ShapeDtypeStruct((rows, cols), kind)

    outs = [shape(tokens, model, wide_type)]
    scratch = []
    extra = []
    if plan is None:
        outs += [
            shape(8, model, wide_type),
            shape(lanes, lanes, wide_type),
            shape(model, 3 * model, narrow_type),
        ]
    else:
        smalls = [(8, model), (16, model), (lanes, lanes)]
        outs += [shape(*dims, wide_type) for dims in smalls]
        outs += [flat for flat, _ in shares]
        shares = [share for _, share in shares]
        stages = plan.stages
        scratch += [
            pltpu.VMEM((2,) * stages + plan.shapes[i][1:], narrow_type) for i in plan.near
        ]
        scratch += [pltpu.VMEM(dims, wide_type) for dims in smalls]
        for dims, groups in zip(smalls, small_groups(plan)):
            slots_small = SmallReduce.sizes(groups)[1][-1]
            scratch += [
                pltpu.VMEM((slots_small,) + dims, wide_type),
                pltpu.SemaphoreType.DMA((slots_small,)),
                pltpu.SemaphoreType.DMA((slots_small,)),
            ]
        extra = plan.scratch()
    scratch += [
        pltpu.VMEM((tokens, 3 * model), narrow_type),
        pltpu.VMEM((total, 4 * lanes), wide_type),
        pltpu.VMEM((2, total, lanes), narrow_type),
        pltpu.VMEM((2, total, lanes), narrow_type),
        pltpu.VMEM((strips, tokens, model), narrow_type),
        pltpu.VMEM((strips, 32, tokens), wide_type),
        pltpu.VMEM((32, total), wide_type),
        pltpu.VMEM((4 * lanes, lanes), wide_type),
        pltpu.SemaphoreType.DMA((slots, 2)),
        pltpu.SemaphoreType.DMA((slots, 2)),
    ]

    def body(*refs):
        attention_backward_kernel(height, width, plan, shares, refs)

    given = operands + (small if plan is not None else ())
    far = plan.shaped(arrays) if plan is not None else []
    return pl.pallas_call(
        body,
        out_shape=outs,
        in_specs=vmem_specs(len(given)) + any_specs(len(far)),
        out_specs=vmem_specs(len(outs)),
        scratch_shapes=scratch + extra,
        compiler_params=pltpu.CompilerParams(
            collective_id=call_id, has_side_effects=True, vmem_limit_bytes=62 << 20
        ),
        name="attention_backward",
    )(*given, *far)


def finish_kernel(widths, refs):
    count = len(widths) - 1
    result, input_grad, late, early, rel_sum = refs[:5]
    flats = refs[5 : 5 + count]
    out = refs[5 + count :]
    out[0][...] = result[...]
    out = out[1:]
    sums = jnp.concatenate([late[...], early[...]], axis=0)
    out[0][...] = input_grad[...]
    for source, target in zip(flats, out[1 : 1 + count]):
        if source.shape == target.shape:
            target[...] = source[...]
            continue
        half = lanes // 2
        low = lane_ids((1, lanes)) < half
        for k in range(source.shape[0] // 2):
            upper, lower = source[2 * k : 2 * k + 1, :], source[2 * k + 1 : 2 * k + 2, :]
            begin, rest = lower[:, :lanes], lower[:, lanes : 2 * lanes]
            target[3 * k : 3 * k + 1, :] = upper[:, :lanes]
            begin = pltpu.roll(begin, half, 1)
            target[3 * k + 1 : 3 * k + 2, :] = jnp.where(low, upper[:, lanes : 2 * lanes], begin)
            target[3 * k + 2 : 3 * k + 3, :] = jnp.where(low, begin, pltpu.roll(rest, half, 1))
    vectors, tables = out[1 + count : -5], out[-5:]
    for target, (rows, begin, size) in zip(vectors, widths[-1]):
        for j, row in enumerate(rows):
            value = sums[row : row + 1, begin : begin + size]
            if target.shape[0] < size:
                quarter = target.shape[0]
                parts = [value[:, k * quarter : (k + 1) * quarter] for k in range(size // quarter)]
                value = sum(parts[1:], parts[0])
            target[j * size : j * size + value.shape[1]] = value[0]
    half = rel_sum.shape[1] // 2
    rows, cols, lateral_gain, lateral_shift, output_gain = tables
    cols[...] = rel_sum[...].T[:half, : cols.shape[1]]
    rows[...] = rel_sum[: rows.shape[0], half:]
    channels = output_gain.shape[1]
    for k, table in enumerate((lateral_gain, lateral_shift, output_gain)):
        table[...] = sums[19:23, k * channels : (k + 1) * channels]


def finish(result, input_grad, smalls, flats, shapes, vectors, table_shapes):
    def wide(shape):
        return jax.ShapeDtypeStruct(shape, wide_type)

    outs = [jax.ShapeDtypeStruct(result.shape, narrow_type), wide(input_grad.shape)]
    outs += [wide(shape) for shape in shapes]
    for _, _, _, length in vectors:
        outs.append(wide((length,)))
    outs += [wide(shape) for shape in table_shapes]
    widths = [None] * len(flats) + [[vector[:3] for vector in vectors]]

    def body(*refs):
        finish_kernel(widths, refs)

    given = (result, input_grad, *smalls, *flats)
    return pl.pallas_call(
        body,
        out_shape=outs,
        in_specs=vmem_specs(len(given)),
        out_specs=vmem_specs(len(outs)),
        name="finish",
    )(*given)


def prepare_kernel(height, width, count, refs):
    vectors, (rel_rows, rel_cols, four) = refs[:count], refs[count : count + 3]
    vec, tables, rel_all, hot, hot_turned, four_pair, table = refs[count + 3 :]
    model = vec.shape[1]
    vec[...] = jnp.zeros_like(vec)
    at = 0
    for source in vectors:
        value = source[...].astype(wide_type)
        if len(source.shape) == 2:
            vec[at : at + value.shape[0], : value.shape[1]] = value
            at += value.shape[0]
            continue
        value = value.reshape(1, value.shape[0])
        size = value.shape[1]
        for begin in range(0, size, model):
            part = value[:, begin : begin + model]
            vec[at : at + 1, : part.shape[1]] = part
            at += 1
    half = lanes // 2
    tables[...] = jnp.zeros_like(tables)
    for i, source in enumerate((rel_cols, rel_rows)):
        table[...] = jnp.zeros_like(table)
        if i == 0:
            size = source.shape[1]
            table[:half, :size] = source[...].astype(wide_type)
            plain = table[...].T
        else:
            size = source.shape[0]
            table[:size, :half] = source[...].astype(wide_type)
            plain = table[...]
        rel_all[i * lanes : (i + 1) * lanes, :] = plain.astype(narrow_type)
        moved = pltpu.roll(plain, half, 1).astype(narrow_type)
        rel_all[(2 + i) * lanes : (3 + i) * lanes, :] = moved
        row = lax.broadcasted_iota(jnp.int32, (lanes, lanes), 0)
        col = lax.broadcasted_iota(jnp.int32, (lanes, lanes), 1)
        mirror = (row + col == size - 1).astype(wide_type).astype(narrow_type)
        turned = dot_tn(plain.astype(narrow_type), mirror)[:half].astype(narrow_type)
        tables[:half, i * lanes : (i + 1) * lanes] = turned
        tables[half:, (2 + i) * lanes : (3 + i) * lanes] = turned
    total = hot.shape[0]
    token = lax.broadcasted_iota(jnp.int32, (total, lanes), 0)
    lane = lax.broadcasted_iota(jnp.int32, (total, lanes), 1)
    key_row, key_col = lax.div(token, width), lax.rem(token, width)
    by_col = (lax.rem(lane, width) == key_col) & (lane < 2 * width)
    by_row = (lax.rem(lane, height) == key_row) & (lane < 2 * height)
    for i, (plain, turned) in enumerate(
        ((by_col, lane == width - 1 - key_col), (by_row, lane == height - 1 - key_row))
    ):
        here = slice(i * lanes, (i + 1) * lanes)
        hot[:, here] = plain.astype(wide_type).astype(narrow_type)
        hot_turned[:, here] = turned.astype(wide_type).astype(narrow_type)
    cols, rows = four.shape
    value = four[...].astype(wide_type).T.astype(narrow_type)
    four_pair[...] = jnp.zeros_like(four_pair)
    four_pair[:rows, :cols] = value
    four_pair[rows:, cols:] = value


def prepared_shapes(height, width, model, vectors, four):
    rows = 0
    for vector in vectors:
        rows += vector.shape[0] if len(vector.shape) == 2 else -(-vector.shape[0] // model)
    rows = -(-rows // 8) * 8
    total = height * width

    def shape(rows_out, cols, kind=narrow_type):
        return jax.ShapeDtypeStruct((rows_out, cols), kind)

    return [
        shape(rows, model, wide_type),
        shape(lanes, 4 * lanes),
        shape(4 * lanes, lanes),
        shape(total, 2 * lanes),
        shape(total, 2 * lanes),
        shape(2 * four.shape[1], 2 * four.shape[0]),
    ]


class Levels:
    def __init__(self, strip_rows, width):
        self.rows = (4 * strip_rows, 2 * strip_rows, strip_rows, strip_rows // 2)
        self.cols = (4 * width, 2 * width, width, width // 2)
        self.at, self.edge_at, self.wide_at = [], [], []
        total = edge = wide = 0
        for rows, cols in zip(self.rows, self.cols):
            self.at.append(total)
            self.edge_at.append(edge)
            self.wide_at.append(wide)
            total += rows * cols
            edge += cols
            wide += (rows + 2) * cols
        self.total, self.edge, self.wide = total, edge, wide


def put_strided(target, at, count, stride, value):
    for part in range(target.shape[0]):
        target[part, pl.ds(at, count, stride=stride), :] = value[:, part * lanes : (part + 1) * lanes]


def get_strided(source, at, count, stride):
    parts = [source[part, pl.ds(at, count, stride=stride), :] for part in range(source.shape[0])]
    return jnp.concatenate(parts, axis=1)


def join_parts(source, begin, end):
    return jnp.concatenate([source[part, begin:end, :] for part in range(source.shape[0])], axis=1)


def store_edges(levels, level, source, offset, top, bottom):
    rows, cols = levels.rows[level], levels.cols[level]
    at = levels.edge_at[level]
    top[at : at + cols, :] = source[offset : offset + cols, :]
    last = offset + (rows - 1) * cols
    bottom[at : at + cols, :] = source[last : last + cols, :]


def four_times(vec, row):
    value = vec[row : row + 1, :]
    quarter = value.shape[1] // 4
    low = jnp.where(lane_ids(value.shape) < quarter, value, 0.0)
    twice = low + pltpu.roll(low, quarter, 1)
    return twice + pltpu.roll(twice, 2 * quarter, 1)


def level_source_kernel(
    levels,
    strip_rows,
    width,
    base,
    y,
    vec,
    first,
    second,
    eight,
    lat_four,
    lat_eight,
    lat_sixteen,
    lat_thirty,
    lateral,
    top,
    bottom,
    first_map,
    active,
    source_zero,
    source_one,
    pooled,
    reduced,
    spread_zero,
    spread_one,
    wide_y,
    first_ready,
):
    tokens, model = y.shape
    out = lat_sixteen.shape[0]
    mid = first.shape[1] // 4
    values = y[...]

    def finish(level, value, at):
        reduced[at : at + value.shape[0], :] = value
        hat, _ = norm_parts(value)
        gain = vec[base + 5 + level : base + 6 + level, :out]
        shift = vec[base + 9 + level : base + 10 + level, :out]
        return hat * gain + shift

    for tap in range(4):
        a, b = tap // 2, tap % 2
        cols = slice(tap * mid, (tap + 1) * mid)
        rows = slice(tap * tokens, (tap + 1) * tokens)
        mapped = dot_nn(values, first[:, cols]) + vec[base : base + 1, :mid]
        first_map[:, cols] = mapped
        hat, _ = norm_parts(mapped)
        normed = hat * vec[base + 1 : base + 2, :mid] + vec[base + 2 : base + 3, :mid]
        active[rows, :] = (normed * normal_cdf(normed)).astype(narrow_type)
    source = dot_nt(active[...], second[...]) + four_times(vec, base + 3)
    source_zero[...] = source.astype(narrow_type)
    half = source_zero.shape[1] // 2
    for pair in range(2):
        both = dot_nt(source_zero[:, pair * half : (pair + 1) * half], lat_four[...])
        for tap in range(4):
            a, b = tap // 2, tap % 2
            for side in range(2):
                place = (4 * tap + 2 * pair + side) * tokens
                part = both[tap * tokens : (tap + 1) * tokens, side * out : (side + 1) * out]
                value = finish(0, part, place)
                for i in range(strip_rows):
                    at = (4 * i + 2 * a + pair) * levels.cols[0] + 2 * b + side
                    put_strided(spread_zero, at, width, 4, value[i * width : (i + 1) * width])
    lateral[0 : levels.at[1], :] = join_parts(spread_zero, 0, levels.at[1]).astype(narrow_type)
    store_edges(levels, 0, lateral, 0, top, bottom)
    first_ready()
    for tap in range(4):
        a, b = tap // 2, tap % 2
        cols = slice(tap * mid, (tap + 1) * mid)
        rows = slice(tap * tokens, (tap + 1) * tokens)
        mapped = dot_nn(values, eight[:, cols]) + vec[base + 4 : base + 5, :mid]
        source_one[rows, :] = mapped.astype(narrow_type)
    values_one = finish(1, dot_nt(source_one[...], lat_eight[...]), levels.at[1])
    for tap in range(4):
        a, b = tap // 2, tap % 2
        value = values_one[tap * tokens : (tap + 1) * tokens]
        for i in range(strip_rows):
            at = (2 * i + a) * levels.cols[1] + b
            put_strided(spread_one, at, width, 2, value[i * width : (i + 1) * width])
    begin, end = levels.at[1:3]
    lateral[begin:end, :] = join_parts(spread_one, 0, end - begin).astype(narrow_type)
    value = finish(2, dot_nt(values, lat_sixteen[...]), levels.at[2])
    lateral[levels.at[2] : levels.at[3], :] = value.astype(narrow_type)
    for part in range(model // lanes):
        wide_y[part] = values[:, part * lanes : (part + 1) * lanes].astype(wide_type)
    quarter = width // 2
    for i in range(strip_rows // 2):
        summed = 0.0
        for a in range(2):
            for b in range(2):
                at = (2 * i + a) * width + b
                summed = summed + get_strided(wide_y, at, quarter, 2)
        pooled[i * quarter : (i + 1) * quarter, :] = (summed * 0.25).astype(narrow_type)
    value = finish(3, dot_nt(pooled[...], lat_thirty[...]), levels.at[3])
    lateral[levels.at[3] : levels.total, :] = value.astype(narrow_type)
    for level in range(1, 4):
        store_edges(levels, level, lateral, levels.at[level], top, bottom)


class EdgeExchange:
    def __init__(self, levels, top, bottom, above, below, send_sem, recv_sem):
        strip, scale = strip_index(), lax.axis_size("scale")
        count = lax.axis_size("rows") * scale

        def place(index):
            return {"rows": lax.div(index, scale), "scale": lax.rem(index, scale)}

        self.has_up, self.has_down = strip > 0, strip < count - 1
        self.up = place(jnp.maximum(strip - 1, 0))
        self.down = place(jnp.minimum(strip + 1, count - 1))
        self.above, self.below = above, below

        def send(source, target, part, i, device):
            begin = (0, levels.edge_at[1])[part]
            rows = pl.ds(begin, (levels.edge_at[1], levels.edge)[part] - begin)
            return pltpu.make_async_remote_copy(
                src_ref=source.at[rows],
                dst_ref=target.at[rows],
                send_sem=send_sem.at[part, i],
                recv_sem=recv_sem.at[part, i],
                device_id=device,
                device_id_type=MESH_ID,
            )

        self.lower = [send(bottom, above, part, 0, self.down) for part in range(2)]
        self.upper = [send(top, below, part, 1, self.up) for part in range(2)]

    def greet(self, barrier):
        @pl.when(self.has_up)
        def _():
            pl.semaphore_signal(barrier, inc=1, device_id=self.up, device_id_type=MESH_ID)

        @pl.when(self.has_down)
        def _():
            pl.semaphore_signal(barrier, inc=1, device_id=self.down, device_id_type=MESH_ID)

        return jnp.where(self.has_up, 1, 0) + jnp.where(self.has_down, 1, 0)

    def clear(self):
        @pl.when(jnp.logical_not(self.has_up))
        def _():
            self.above[...] = jnp.zeros_like(self.above)

        @pl.when(jnp.logical_not(self.has_down))
        def _():
            self.below[...] = jnp.zeros_like(self.below)

    def send(self, part):
        @pl.when(self.has_down)
        def _():
            self.lower[part].start()

        @pl.when(self.has_up)
        def _():
            self.upper[part].start()

    def arrive(self, part):
        @pl.when(self.has_down)
        def _():
            self.lower[part].wait_send()
            self.upper[part].wait_recv()

        @pl.when(self.has_up)
        def _():
            self.upper[part].wait_send()
            self.lower[part].wait_recv()


def tile_start(index):
    return index if isinstance(index, int) else pl.multiple_of(index, 32)


def widen_rows(levels, level, source, at, first, count, padded, slab, offset):
    cols = levels.cols[level]
    channels = source.shape[1]
    size = count * cols
    padded[8 : 8 + size, :] = source[at : at + size, :].astype(wide_type)
    block = min(256, size)

    def step(i, carry):
        begin = tile_start(i * block)
        got = padded[pl.ds(begin, block + 16), :]
        col = lax.rem(begin + lax.broadcasted_iota(jnp.int32, (block, channels), 0), cols)
        left = jnp.where(col > 0, got[7 : 7 + block], 0.0)
        right = jnp.where(col < cols - 1, got[9 : 9 + block], 0.0)
        joined = jnp.concatenate([left, got[8 : 8 + block], right], axis=1)
        slab[pl.ds(tile_start(offset + first * cols + begin), block), :] = joined.astype(narrow_type)
        return carry

    if size == block:
        step(0, 0)
    else:
        lax.fori_loop(0, size // block, step, 0)


def widen_own(levels, level, source, padded, slab, offset):
    rows = levels.rows[level]
    widen_rows(levels, level, source, levels.at[level], 1, rows, padded, slab, offset)


def widen_edges(levels, level, above, below, padded, slab, offset):
    at, rows = levels.edge_at[level], levels.rows[level]
    widen_rows(levels, level, above, at, 0, 1, padded, slab, offset)
    widen_rows(levels, level, below, at, rows + 1, 1, padded, slab, offset)


def inner_first(size, block, cols, step, arrive):
    count = size // block
    if count > 2 and block >= cols:
        lax.fori_loop(1, count - 1, step, 0)
        arrive()
        step(0, 0)
        step(count - 1, 0)
    else:
        arrive()
        lax.fori_loop(0, count, step, 0)


def smooth_kernel(
    levels,
    base,
    lateral,
    edges,
    weight,
    smooth,
    vec,
    grads,
    top,
    bottom,
    slabs,
    gain_sums,
    padded,
    first_ready,
):
    channels = lateral.shape[1]
    above, below = edges.above, edges.below
    gain_sums[...] = jnp.zeros_like(gain_sums)
    for level in range(4):
        rows, cols = levels.rows[level], levels.cols[level]
        offset = levels.wide_at[level]
        widen_own(levels, level, lateral, padded, slabs, offset)

        def arrive():
            if level < 2:
                edges.arrive(level)
            widen_edges(levels, level, above, below, padded, slabs, offset)

        size = rows * cols
        block = min(256, size)
        gain = vec[base + 13 + level : base + 14 + level, :channels]

        def step(i, carry):
            begin = tile_start(i * block)
            total = None
            for a in range(3):
                window = slabs[pl.ds(tile_start(offset + a * cols + begin), block), :]
                part = dot_nn(
                    window, smooth[level, 3 * a * channels : 3 * (a + 1) * channels, :]
                )
                total = part if total is None else total + part
            hat, inverse = norm_parts(total)
            here = pl.ds(tile_start(levels.at[level] + begin), block)
            upstream = weight[here, :].astype(wide_type)
            gain_sums[level : level + 1, :] += column_sum(upstream * hat)
            grads[here, :] = norm_back(hat, inverse, upstream * gain).astype(narrow_type)
            return carry

        inner_first(size, block, cols, step, arrive)
        store_edges(levels, level, grads, levels.at[level], top, bottom)
        if level == 0:
            first_ready()


def level_back_kernel(levels, strip_rows, width, base, reducer, edges, given, outs, scratch, done):
    (
        grads,
        slabs,
        reduced,
        first_map,
        active,
        source_zero,
        source_one,
        pooled,
        y,
        vec,
        smooth,
        first,
        second,
        eight,
        lat_four,
        lat_eight,
        lat_sixteen,
        lat_thirty,
    ) = given
    y_grad, sums, smooth_grad, first_grad, eight_grad, *rest = outs
    if reducer is not None:
        (rest_grad,) = rest
        plan, own = reducer.plan, smooth_grad.shape[-2]
    else:
        rest_grad, plan = None, None
        second_grad, lat_four_grad, lat_eight_grad, lat_sixteen_grad, lat_thirty_grad = rest
    padded, slab, spread, second_sum, four_sum, eight_sum, total_grad, pool_grad = scratch[:8]
    low_pair, second_low, active_grads = scratch[8:]
    tokens, model = y.shape
    channels = grads.shape[1]
    mid = first.shape[1] // 4
    above, below = edges.above, edges.below
    sums[...] = jnp.zeros_like(sums)

    def smooth_weights(level):
        rows, cols = levels.rows[level], levels.cols[level]
        size = rows * cols
        turned = grads[levels.at[level] : levels.at[level] + size, :].T
        for a in range(3):
            begin = levels.wide_at[level] + a * cols
            for b in range(3):
                part = dot_nn(turned, slabs[begin : begin + size, b * channels : (b + 1) * channels])
                part = part.T.astype(narrow_type)
                at = (level * 9 + 3 * a + b) * channels
                if plan is None:
                    smooth_grad[at : at + channels, :] = part
                    continue
                done = 0
                while done < channels:
                    device, row = divmod(at + done, own)
                    count = min(channels - done, own - row)
                    lead = tuple((device >> (plan.stages - 1 - d)) & 1 for d in range(plan.stages))
                    smooth_grad[lead + (slice(row, row + count),)] = part[done : done + count]
                    done += count

    def smooth_back(level):
        rows, cols = levels.rows[level], levels.cols[level]
        size = rows * cols
        widen_own(levels, level, grads, padded, slab, 0)
        block = min(256, size)

        def arrive():
            if level == 0 and plan is not None:
                reducer.wave(0)
            if level < 2:
                edges.arrive(level)
            widen_edges(levels, level, above, below, padded, slab, 0)

        def step(i, carry):
            begin = tile_start(i * block)
            total = None
            for a in range(3):
                for b in range(3):
                    window = slab[
                        pl.ds(tile_start((2 - a) * cols + begin), block),
                        (2 - b) * channels : (3 - b) * channels,
                    ]
                    tap = (3 * a + b) * channels
                    part = dot_nt(window, smooth[level, tap : tap + channels, :])
                    total = part if total is None else total + part
            for part in range(channels // lanes):
                here = total[:, part * lanes : (part + 1) * lanes]
                spread[part, pl.ds(begin, block), :] = here
            return carry

        inner_first(size, block, cols, step, arrive)

    def reduced_back(level, upstream, at):
        hat, inverse = norm_parts(reduced[at : at + upstream.shape[0], :])
        gain = vec[base + 5 + level : base + 6 + level, :channels]
        sums[5 + level : 6 + level, :channels] += column_sum(upstream * hat)
        sums[9 + level : 10 + level, :channels] += column_sum(upstream)
        return norm_back(hat, inverse, upstream * gain).astype(narrow_type)

    def keep_tap(target, tap, parts, value):
        if len(target.shape) == 2:
            target[:, tap * mid : (tap + 1) * mid] = value.astype(narrow_type)
        else:
            fold_store(target, tap, parts, value)

    first_parts, eight_parts = {}, {}
    turned_y = y[...].T
    total_grad[...] = jnp.zeros_like(total_grad)
    for level in range(4):
        smooth_weights(level)
    if plan is not None:
        reducer.start_near(0)
    smooth_back(0)
    half = source_zero.shape[1] // 2
    for pair in range(2):
        for tap in range(4):
            a, b = tap // 2, tap % 2
            for side in range(2):
                pieces = []
                for i in range(strip_rows):
                    at = (4 * i + 2 * a + pair) * levels.cols[0] + 2 * b + side
                    pieces.append(get_strided(spread, at, width, 4))
                upstream = jnp.concatenate(pieces, axis=0)
                low = reduced_back(0, upstream, (4 * tap + 2 * pair + side) * tokens)
                here = slice(side * channels, (side + 1) * channels)
                low_pair[tap * tokens : (tap + 1) * tokens, here] = low
        own_cols = slice(pair * half, (pair + 1) * half)
        product = dot_tn(low_pair[...], source_zero[:, own_cols])
        if pair == 0:
            four_sum[...] = product
        else:
            four_sum[...] += product
        second_low[:, own_cols] = dot_nn(low_pair[...], lat_four[...]).astype(narrow_type)
    sums[3:4, :] = column_sum(second_low[...].astype(wide_type))
    second_sum[...] = dot_tn(second_low[...], active[...])
    active_grads[...] = dot_nn(second_low[...], second[...])
    for tap in range(4):
        cols = slice(tap * mid, (tap + 1) * mid)
        active_grad = active_grads[tap * tokens : (tap + 1) * tokens, :]
        hat, inverse = norm_parts(first_map[:, cols])
        gain = vec[base + 1 : base + 2, :mid]
        normed = hat * gain + vec[base + 2 : base + 3, :mid]
        normed_grad = active_grad * gelu_slope(normed)
        sums[1:2, :mid] += column_sum(normed_grad * hat)
        sums[2:3, :mid] += column_sum(normed_grad)
        first_low = norm_back(hat, inverse, normed_grad * gain).astype(narrow_type)
        sums[0:1, :mid] += column_sum(first_low.astype(wide_type))
        keep_tap(first_grad, tap, first_parts, dot_nn(turned_y, first_low))
        total_grad[...] += dot_nt(first_low, first[:, cols])
    done(first_grad)
    quarter = lat_four.shape[1] // 2
    if rest_grad is None:
        second_grad[...] = second_sum[...].astype(narrow_type)
        lat_four_grad[...] = (
            four_sum[:channels, :quarter] + four_sum[channels:, quarter:]
        ).astype(narrow_type)
    smooth_back(1)
    pieces = []
    for tap in range(4):
        a, b = tap // 2, tap % 2
        for i in range(strip_rows):
            at = (2 * i + a) * levels.cols[1] + b
            pieces.append(get_strided(spread, at, width, 2))
    low = reduced_back(1, jnp.concatenate(pieces, axis=0), levels.at[1])
    eight_sum[...] = dot_tn(low, source_one[...])
    eight_lows = dot_nn(low, lat_eight[...]).astype(narrow_type)
    for tap in range(4):
        cols = slice(tap * mid, (tap + 1) * mid)
        eight_low = eight_lows[tap * tokens : (tap + 1) * tokens]
        sums[4:5, :mid] += column_sum(eight_low.astype(wide_type))
        keep_tap(eight_grad, tap, eight_parts, dot_nn(turned_y, eight_low))
        total_grad[...] += dot_nt(eight_low, eight[:, cols])
    done(eight_grad)
    if rest_grad is None:
        lat_eight_grad[...] = eight_sum[...].astype(narrow_type)
    smooth_back(2)
    low = reduced_back(2, join_parts(spread, 0, tokens), levels.at[2])
    sixteen = dot_tn(low, y[...])
    if rest_grad is None:
        lat_sixteen_grad[...] = sixteen.astype(narrow_type)
    total_grad[...] += dot_nn(low, lat_sixteen[...])
    smooth_back(3)
    low = reduced_back(3, join_parts(spread, 0, tokens // 4), levels.at[3])
    thirty = dot_tn(low, pooled[...])
    if rest_grad is None:
        lat_thirty_grad[...] = thirty.astype(narrow_type)
    else:
        count = rest_grad.shape[0]
        turned = pltpu.roll(four_sum[channels:, :], quarter, 1)
        both = four_sum[:channels, :] + turned
        four = jnp.where(lane_ids(both.shape) < quarter, both, 0.0)
        for part in range(mid // lanes):
            here = slice(part * lanes, (part + 1) * lanes)
            pieces = [second_sum[:, here]]
            for value in (sixteen, thirty):
                for half in range(2):
                    at = half * mid + part * lanes
                    pieces.append(value[:, at : at + lanes])
            pieces += [eight_sum[:, here], four[:, here]]
            pieces = [piece.reshape(count, piece.shape[0] // count, lanes) for piece in pieces]
            used = sum(piece.shape[1] for piece in pieces)
            pieces.append(jnp.zeros((count, rest_grad.shape[1] - used, lanes), wide_type))
            rest_grad[:, :, here] = jnp.concatenate(pieces, axis=1).astype(narrow_type)
    for target in rest:
        done(target)
    pooled_grad = dot_nn(low, lat_thirty[...]) * 0.25
    count = width // 2
    for i in range(strip_rows // 2):
        piece = pooled_grad[i * count : (i + 1) * count]
        for a in range(2):
            for b in range(2):
                at = (2 * i + a) * width + b
                put_strided(pool_grad, at, count, 2, piece)
    y_grad[...] = (total_grad[...] + join_parts(pool_grad, 0, tokens)).astype(narrow_type)
    if plan is not None:
        for number in range(1, plan.waves()):
            reducer.wave(number)


def region_weights(levels, strip_rows, width, roi, anchors, weight):
    scale = lax.axis_index("scale")
    channels = weight.shape[1]
    ones = jnp.ones((1, channels), narrow_type)

    def own(rows, count):
        shape = (count, rows.shape[0])
        wanted = lax.broadcasted_iota(jnp.int32, shape, 0) + scale * count
        pick = (lax.broadcasted_iota(jnp.int32, shape, 1) == wanted).astype(wide_type)
        rows = rows.astype(wide_type).astype(narrow_type)
        return dot_nn(pick.astype(narrow_type), rows)

    region = own(roi[0], strip_rows).astype(narrow_type)
    for level in range(4):
        rows, cols = levels.rows[level], levels.cols[level]
        shape = (width, cols)
        patch = lax.broadcasted_iota(jnp.int32, shape, 0)
        cell = lax.broadcasted_iota(jnp.int32, shape, 1)
        cell = lax.div(cell, cols // width) if level < 3 else 2 * cell
        spread = (patch == cell).astype(wide_type).astype(narrow_type)
        regions = dot_nn(region, spread)
        positives = own(anchors[level][0], rows)
        for row in range(rows):
            patch_row = row * strip_rows // rows
            factor = positives[row : row + 1] + regions[patch_row : patch_row + 1]
            wide = dot_tn(factor.astype(narrow_type), ones)
            at = levels.at[level] + row * cols
            here = slice(at, at + cols)
            weight[here, :] = (weight[here, :].astype(wide_type) * wide).astype(narrow_type)


def pyramid_kernel(levels, strip_rows, width, base, plan, count, refs):
    y, vec, roi, *anchors = refs[:7]
    far, cotans, refs = refs[7:15], refs[15:19], refs[19:]
    y_grad, sums, gain_sums = refs[:3]
    far_outs, left, scratch = refs[3 : 3 + count], [], refs[3 + count :]
    if plan is not None:
        left, scratch = scratch[: len(plan.pieces)], scratch[len(plan.pieces) :]
    near, scratch = scratch[:9], scratch[9:]
    near_outs, scratch = scratch[:count], scratch[count:]
    sems, smooth_grad = scratch[:2]
    lateral, first_map, active, source_zero, source_one, pooled, reduced = scratch[2:9]
    grads, slabs, spread_one = scratch[9:12]
    edge_refs, scratch = scratch[12:24], scratch[24:]
    work, scratch = scratch[:11], scratch[11:]
    copies = [
        pltpu.make_async_copy(source, target, sems.at[i])
        for i, (source, target) in enumerate(zip(far, near))
    ]
    weight = near[8]
    given = []
    for level, source in enumerate(cotans):
        rows, cols = levels.rows[level], levels.cols[level]
        for row in range(rows):
            at = levels.at[level] + row * cols
            view = source.at[0, lax.axis_index("scale") * rows + row]
            semaphore = sems.at[9 + count + len(given)]
            given.append(pltpu.make_async_copy(view, weight.at[at : at + cols], semaphore))
    for copy in copies + given:
        copy.start()
    first, second, lat_four, eight, lat_eight, lat_sixteen, lat_thirty, smooth, weight = near
    edges, edges_back = [
        EdgeExchange(levels, *edge_refs[6 * i : 6 * i + 6]) for i in range(2)
    ]
    barrier = pltpu.get_barrier_semaphore()
    greeted = edges.greet(barrier)
    reducer = None
    if plan is not None:
        reducer = Reducer(plan, [smooth_grad], [dict(enumerate(left))], scratch)
        greeted = greeted + reducer.greet(barrier)
    for copy in copies[:7]:
        copy.wait()
    padded, _, spread, _, _, _, _, pool_grad = work[:8]
    top, bottom = edge_refs[:2]

    def first_ready():
        pl.semaphore_wait(barrier, greeted)
        edges.clear()
        edges_back.clear()
        edges.send(0)

    level_source_kernel(
        levels,
        strip_rows,
        width,
        base,
        y,
        vec,
        first,
        second,
        eight,
        lat_four,
        lat_eight,
        lat_sixteen,
        lat_thirty,
        lateral,
        top,
        bottom,
        first_map,
        active,
        source_zero,
        source_one,
        pooled,
        reduced,
        spread,
        spread_one,
        pool_grad,
        first_ready,
    )
    edges.send(1)
    for copy in copies[7:] + given:
        copy.wait()
    region_weights(levels, strip_rows, width, roi, anchors, weight)
    top, bottom = edge_refs[6:8]
    smooth_kernel(
        levels,
        base,
        lateral,
        edges,
        weight,
        smooth,
        vec,
        grads,
        top,
        bottom,
        slabs,
        gain_sums,
        padded,
        lambda: edges_back.send(0),
    )
    edges_back.send(1)
    backs = []

    def done(target):
        for i, near_out in enumerate(near_outs):
            if near_out is target:
                backs.append(pltpu.make_async_copy(target, far_outs[i], sems.at[9 + i]))
                backs[-1].start()

    given = (grads, slabs, reduced, first_map, active, source_zero, source_one, pooled, y, vec)
    weights = (smooth, first, second, eight, lat_four, lat_eight, lat_sixteen, lat_thirty)
    outs = (y_grad, sums, smooth_grad, *near_outs)
    if plan is None:
        outs = (y_grad, sums, near_outs[-1], *near_outs[:-1])
    level_back_kernel(
        levels, strip_rows, width, base, reducer, edges_back, given + weights, outs, work, done
    )
    if plan is None:
        done(near_outs[-1])
    for copy in backs:
        copy.wait()
    if plan is not None:
        reducer.finish()


def pyramid(levels, strip_rows, width, base, y, vec, maps, weights, cotans, devices, plan, call_id):
    first, second, four_pair, eight, lat_eight, lat_sixteen, lat_thirty, smooth = weights
    tokens, model = y.shape
    channels = smooth.shape[2]
    mid = first.shape[1] // 4

    def shape(rows, cols, kind=narrow_type):
        return jax.ShapeDtypeStruct((rows, cols), kind)

    outs = [shape(tokens, model), shape(16, model, wide_type), shape(8, channels, wide_type)]
    total = smooth.shape[0] * smooth.shape[1]
    if devices:
        folded = (devices, first.shape[0] // devices * 4, mid)
        rows = second.shape[0] // devices + channels // devices * 6
        rest = (devices, -(-rows // 16) * 16, mid)
        far = [jax.ShapeDtypeStruct(dims, narrow_type) for dims in (folded, folded, rest)]
        smooth_dims = (2,) * plan.stages + (total // devices, channels)
        left = [jax.ShapeDtypeStruct(plan.left(t), narrow_type) for t in range(len(plan.pieces))]
    else:
        far = [
            shape(*first.shape),
            shape(*eight.shape),
            shape(*second.shape),
            shape(channels, four_pair.shape[1] // 2),
            shape(*lat_eight.shape),
            shape(*lat_sixteen.shape),
            shape(*lat_thirty.shape),
            shape(total, channels),
        ]
        smooth_dims = (16, lanes)
        left = []
    count = len(far)

    def body(*refs):
        pyramid_kernel(levels, strip_rows, width, base, plan, count, refs)

    def vmem(rows, cols, kind=narrow_type):
        return pltpu.VMEM((rows, cols), kind)

    size = levels.rows[0] * levels.cols[0]
    edge = [vmem(levels.edge, channels)] * 4 + [pltpu.SemaphoreType.DMA((2, 2))] * 2
    scratch = [pltpu.VMEM(weight_in.shape, narrow_type) for weight_in in weights]
    scratch.append(vmem(levels.total, channels))
    scratch += [pltpu.VMEM(out.shape, narrow_type) for out in far]
    scratch += [
        pltpu.SemaphoreType.DMA((9 + count + sum(levels.rows),)),
        pltpu.VMEM(smooth_dims, narrow_type),
        vmem(levels.total, channels),
        vmem(tokens, 4 * mid, wide_type),
        vmem(4 * tokens, mid),
        vmem(4 * tokens, second.shape[0]),
        vmem(4 * tokens, mid),
        vmem(tokens // 4, model),
        vmem(levels.total, channels, wide_type),
        vmem(levels.total, channels),
        vmem(levels.wide, 3 * channels),
        pltpu.VMEM((channels // lanes, levels.at[2] - levels.at[1], lanes), wide_type),
    ]
    scratch += edge + edge
    scratch += [
        vmem(size + 16, channels, wide_type),
        vmem(size + 2 * levels.cols[0], 3 * channels),
        pltpu.VMEM((channels // lanes, size, lanes), wide_type),
        pltpu.VMEM(second.shape, wide_type),
        pltpu.VMEM(four_pair.shape, wide_type),
        pltpu.VMEM(lat_eight.shape, wide_type),
        vmem(tokens, model, wide_type),
        pltpu.VMEM((model // lanes, tokens, lanes), wide_type),
        vmem(4 * tokens, 2 * channels),
        vmem(4 * tokens, second.shape[0]),
        vmem(4 * tokens, mid, wide_type),
    ]
    if plan is not None:
        scratch += plan.scratch()
    return pl.pallas_call(
        body,
        out_shape=outs + far + left,
        in_specs=vmem_specs(2 + len(maps)) + any_specs(len(weights) + len(cotans)),
        out_specs=vmem_specs(3) + any_specs(count) + vmem_specs(len(left)),
        scratch_shapes=scratch,
        compiler_params=pltpu.CompilerParams(
            collective_id=call_id, has_side_effects=True, vmem_limit_bytes=62 << 20
        ),
        name="pyramid",
    )(y, vec, *maps, *weights, *cotans)


def on_device(
    block_input,
    pre_gain,
    pre_shift,
    qkv_weight,
    qv_bias,
    rel_rows,
    rel_cols,
    proj_weight,
    proj_bias,
    mid_gain,
    mid_shift,
    fc1_weight,
    fc1_bias,
    fc2_weight,
    fc2_bias,
    deconv_first,
    first_bias,
    upnorm_gain,
    upnorm_shift,
    deconv_second,
    second_bias,
    deconv_eight,
    eight_bias,
    lateral_four,
    lateral_eight,
    lateral_sixteen,
    lateral_thirty,
    lateral_gain,
    lateral_shift,
    smooth_weight,
    output_gain,
    grad_four,
    grad_eight,
    grad_sixteen,
    grad_thirty,
    anchor_four,
    anchor_eight,
    anchor_sixteen,
    anchor_thirty,
    roi_mask,
):
    _, strip_rows, width, model = block_input.shape
    head_size = rel_rows.shape[1]
    tokens = strip_rows * width
    height = strip_rows * lax.axis_size(("rows", "scale"))
    channels = smooth_weight.shape[2]
    ff = fc1_weight.shape[1]
    mid = first_bias.shape[0]
    quarter = second_bias.shape[0]
    levels = Levels(strip_rows, width)
    devices = lax.axis_size(("img", "rows", "scale"))
    fused = devices if (model // devices) % 8 == 0 and height <= 16 else 0
    x_own = block_input.reshape(tokens, model)

    base = 8 + ff // model
    (
        vec,
        tables,
        rel_all,
        hot,
        hot_turned,
        lat_four_pair,
        q_all,
        k_all,
        v_all,
        attended,
        attended_wide,
        log_norm,
        middle,
        normed_mid,
        hidden_pre,
        hidden,
        result,
    ) = block_forward(
        height,
        width,
        x_own,
        (
            pre_gain,
            pre_shift,
            qv_bias,
            proj_bias,
            mid_gain,
            mid_shift,
            fc2_bias,
            fc1_bias,
            first_bias,
            upnorm_gain,
            upnorm_shift,
            second_bias,
            eight_bias,
            lateral_gain,
            lateral_shift,
            output_gain,
        ),
        (rel_rows, rel_cols.T, lateral_four.T),
        (qkv_weight, proj_weight, fc1_weight, fc2_weight),
        2,
    )
    smooth_plan = None
    if fused:
        rows = smooth_weight.shape[0] * smooth_weight.shape[1] // devices
        smooth_shape = (devices, rows, channels)
        stages = len(halving_dims())
        cut = -(-rows // 32) * 16
        smooth_cuts = [(0, 0, cut, "x"), (0, cut, rows - cut, "y")]
        smooth_plan = ReducePlan(
            [smooth_shape], [piece + (0, 0, (0, 1)) for piece in smooth_cuts], near=(0,)
        )
    result_grad, level_sums, gain_sums, first_grad, eight_grad, *rest_grads = pyramid(
        levels,
        strip_rows,
        width,
        base,
        result,
        vec,
        (roi_mask, anchor_four, anchor_eight, anchor_sixteen, anchor_thirty),
        (
            deconv_first,
            deconv_second,
            lat_four_pair,
            deconv_eight,
            lateral_eight,
            lateral_sixteen,
            lateral_thirty,
            smooth_weight,
        ),
        (grad_four, grad_eight, grad_sixteen, grad_thirty),
        fused,
        smooth_plan,
        1,
    )
    if fused:
        smooth_rows = smooth_weight.shape[0] * smooth_weight.shape[1] // devices
    else:
        *rest_grads, smooth_grad = rest_grads
    names, final = [], []

    def share(shares, shapes, name, source, weight_in, begin=0):
        rows, columns = weight_in
        own, width_in = rows // devices, shapes[source][-1]
        names.append(name)
        if columns % lanes:
            flat = jax.ShapeDtypeStruct((own, width_in), wide_type)
            places = [(begin, own, 0, 0)]
            final.append((own * columns // lanes, lanes))
        else:
            tiles = columns // lanes
            flat = jax.ShapeDtypeStruct((own * tiles, lanes), wide_type)
            places = [
                (begin + f * own, own, f * width_in // lanes, tiles)
                for f in range(max(columns // width_in, 1))
            ]
            final.append((own * tiles, lanes))
        shares.append((flat, (source, places)))
        return begin + own * max(columns // width_in, 1)

    if fused:
        rest_grad, *smooth_left = rest_grads
    (
        middle_grad,
        attended_grad,
        stats,
        stat_rows,
        block_sums,
        fc1_sum,
        pre_grad,
        branch_grad,
        *block_grads,
    ) = block_backward(
        result_grad,
        (hidden_pre, hidden, normed_mid, middle, attended, attended_wide),
        log_norm,
        vec,
        proj_weight,
        fc1_weight,
        fc2_weight,
        fused,
    )
    operands = (
        x_own,
        q_all,
        k_all,
        v_all,
        attended_grad,
        stats,
        stat_rows,
        middle_grad,
        vec,
        tables,
        rel_all,
        hot,
        hot_turned,
        qkv_weight,
    )
    small_operands = (
        block_sums,
        fc1_sum,
        level_sums,
        gain_sums,
        normed_mid,
        pre_grad,
        hidden,
        result_grad,
        attended,
        branch_grad,
    )
    if fused:
        arrays = (first_grad, eight_grad, rest_grad, *smooth_left)
        own = model // devices
        shapes = [
            (devices, own * (ff // model), model),
            (devices, ff // devices, model),
            (devices, own * (model // mid), mid),
            *(array.shape for array in arrays),
        ]
        query, keys = len(shapes), len(shapes) + 1
        shapes.append((devices, own * (model // mid), mid))
        shapes.append((devices, own * (2 * model // mid), mid))

        def half(source, part):
            size = shapes[source][1]
            first = -(-size // 32) * 16
            return (source, 0, first) if part == 0 else (source, first, size - first)

        def whole(source):
            return (source, 0, shapes[source][-2])

        pieces = [
            (6, *smooth_cuts[0][1:], 0, 2, (2, 4, 6)),
            (7, *smooth_cuts[1][1:], 6, 2, (9, 12, 18)),
            (*whole(3), "z", 0, 0, (5, 8, 11, 13, 22)),
            (*whole(4), "z", 0, 0, (7, 11, 15, 29, 37)),
            (*half(1, 1), "y", 0, 0, (1, 5, 7, 9, 12)),
            (*whole(5), "x", 0, 0, (8, 12, 19, 23, 30)),
            (*whole(query), "z", 0, 0, (11, 14, 28, 34, 39)),
            (*whole(2), "x", 0, 0, (11, 17, 31, 36, 41)),
            (*half(0, 1), "y", 0, 0, (3, 7, 10, 12, 16)),
            (*half(1, 0), "y", 0, 0, (6, 10, 12, 20, 26)),
            (*half(0, 0), "y", 0, 0, (9, 12, 21, 27, 33)),
            (*half(keys, 0), "x", 0, 0, (13, 25, 35, 40, 43)),
            (*half(keys, 1), "y", 0, 0, (13, 24, 32, 38, 42)),
        ]
        plan = ReducePlan(shapes, pieces, near=(0, 1, 2, query, keys))
        plan.riders = (12, 4, 6)
        shares = []
        tiles = channels // lanes
        names.append("smooth")
        final.append((rows * tiles, lanes))
        flat = jax.ShapeDtypeStruct((rows * tiles, lanes), wide_type)
        places = [(0, rows, 0, tiles)]
        shares.append((flat, [(6, places), (7, places)]))
        share(shares, shapes, "first", 3, deconv_first.shape)
        share(shares, shapes, "eight", 4, deconv_eight.shape)
        share(shares, shapes, "fc1", 0, fc1_weight.shape)
        share(shares, shapes, "fc2", 1, fc2_weight.shape)
        share(shares, shapes, "proj", 2, proj_weight.shape)
        at = 0
        for name, weight_in in (
            ("second", deconv_second),
            ("lat_sixteen", lateral_sixteen),
            ("lat_thirty", lateral_thirty),
            ("lat_eight", lateral_eight),
            ("lat_four", lateral_four),
        ):
            at = share(shares, shapes, name, 5, weight_in.shape, at)
        tiles = 3 * model // lanes
        names.append("qkv")
        final.append((own * tiles, lanes))
        flat = jax.ShapeDtypeStruct((own * tiles, lanes), wide_type)
        folds = [(own, f * mid // lanes, tiles) for f in range(3 * model // mid)]
        count = model // mid
        of_query = [(f * own, *fold) for f, fold in enumerate(folds[:count])]
        of_keys = [(f * own, *fold) for f, fold in enumerate(folds[count:])]
        shares.append((flat, [(query, of_query), (keys, of_keys)]))
        got = attention_backward(
            height, width, operands, small_operands, arrays, plan, shares, 0
        )
        vectors = (
            ((3,), 0, model, model),
            ((4,), 0, model, model),
            ((0, 2), 0, model, 2 * model),
            ((8,), 0, model, model),
            ((9,), 0, model, model),
            ((10,), 0, model, model),
            ((12, 13, 14, 15), 0, model, ff),
            ((11,), 0, model, model),
            ((16,), 0, mid, mid),
            ((16,), mid, mid, mid),
            ((17,), 0, mid, mid),
            ((18,), 0, model, quarter),
            ((17,), mid, mid, mid),
        )
        tables_out = (rel_rows.shape, rel_cols.shape[::-1]) + (lateral_gain.shape,) * 3
        result, input_grad, *got = finish(
            result, got[0], got[1:4], got[4:], final, vectors, tables_out
        )
        weight_sums = {name: value.reshape(-1) for name, value in zip(names, got)}
        small = got[len(names) :]
        small = (
            *small[:3],
            small[-5],
            small[-4].T,
            *small[3:13],
            *small[-3:],
        )
    else:
        input_grad, mix_sums, rel_sum, qkv_grad = attention_backward(
            height, width, operands, (), (), None, (), 0
        )
        proj_grad, fc1_grad, fc2_grad = block_grads
        second_grad, four_grad, lat_eight_grad, lat_sixteen_grad, lat_thirty_grad = rest_grads
        packed, folds = [], []
        for grads_in, columns, called in (
            ((smooth_grad,), channels, ("smooth",)),
            ((first_grad, eight_grad), model, ("first", "eight")),
            ((fc1_grad,), model, ("fc1",)),
            ((fc2_grad,), model, ("fc2",)),
            ((qkv_grad,), mid, ("qkv",)),
            (
                (
                    proj_grad,
                    second_grad,
                    lat_sixteen_grad,
                    lat_thirty_grad,
                    lat_eight_grad,
                    four_grad,
                ),
                mid,
                ("proj", "second", "lat_sixteen", "lat_thirty", "lat_eight", "lat_four"),
            ),
        ):
            stacked, fold = fold_chunks(grads_in, columns)
            packed.append(stacked)
            folds.append(fold)
            names += called
        gain_rows = jnp.pad(gain_sums, ((0, 0), (0, model - channels)))
        small_in = (
            jnp.concatenate(
                [mix_sums, block_sums, fc1_sum.reshape(-1, model), level_sums, gain_rows]
            ),
            rel_sum,
        )
        got, small = last_reduce(packed, pack_small(small_in), 3)
        sums, rel_sum = unpack_small(small, small_in)
        flat = []
        for summed, fold in zip(got, folds):
            flat += unfold_chunks(summed, fold)
        weight_sums = dict(zip(names, flat))
        small = (
            sums[3],
            sums[4],
            jnp.concatenate([sums[0], sums[2]]),
            rel_sum[: rel_rows.shape[0], head_size : 2 * head_size],
            rel_sum[: rel_cols.shape[0], :head_size],
            sums[8],
            sums[9],
            sums[10],
            sums[16:20].reshape(-1),
            sums[11],
            sums[20, :mid],
            sums[21, :mid],
            sums[22, :mid],
            jnp.sum(sums[23].reshape(4, quarter), axis=0),
            sums[24, :mid],
            sums[25:29, :channels],
            sums[29:33, :channels],
            sums[36:40, :channels],
        )
    return (
        result.reshape(block_input.shape),
        input_grad.reshape(block_input.shape),
        small[0],
        small[1],
        weight_sums["qkv"],
        small[2],
        small[3],
        small[4],
        weight_sums["proj"],
        small[5],
        small[6],
        small[7],
        weight_sums["fc1"],
        small[8],
        weight_sums["fc2"],
        small[9],
        weight_sums["first"],
        small[10],
        small[11],
        small[12],
        weight_sums["second"],
        small[13],
        weight_sums["eight"],
        small[14],
        weight_sums["lat_four"],
        weight_sums["lat_eight"],
        weight_sums["lat_sixteen"],
        weight_sums["lat_thirty"],
        small[15],
        small[16],
        weight_sums["smooth"],
        small[17],
    )


def solution(mesh):
    in_specs = (
        P("img", ("rows", "scale"), None, None),
        P(),
        P(),
        P(),
        P(),
        P(),
        P(),
        P(),
        P(),
        P(),
        P(),
        P(),
        P(),
        P(),
        P(),
        P(),
        P(),
        P(),
        P(),
        P(),
        P(),
        P(),
        P(),
        P(),
        P(),
        P(),
        P(),
        P(),
        P(),
        P(),
        P(),
        P("img", "rows", None, None),
        P("img", "rows", None, None),
        P("img", "rows", None, None),
        P("img", "rows", None, None),
        P("img", "rows", None),
        P("img", "rows", None),
        P("img", "rows", None),
        P("img", "rows", None),
        P("img", "rows", None),
    )
    out_specs = (
        P("img", ("rows", "scale"), None, None),
        P("img", ("rows", "scale"), None, None),
        P(),
        P(),
        P(("img", "rows", "scale")),
        P(),
        P(),
        P(),
        P(("img", "rows", "scale")),
        P(),
        P(),
        P(),
        P(("img", "rows", "scale")),
        P(),
        P(("img", "rows", "scale")),
        P(),
        P(("img", "rows", "scale")),
        P(),
        P(),
        P(),
        P(("img", "rows", "scale")),
        P(),
        P(("img", "rows", "scale")),
        P(),
        P(("img", "rows", "scale")),
        P(("img", "rows", "scale")),
        P(("img", "rows", "scale")),
        P(("img", "rows", "scale")),
        P(),
        P(),
        P(("img", "rows", "scale")),
        P(),
    )
    return jax.shard_map(
        on_device, mesh=mesh, in_specs=in_specs, out_specs=out_specs, check_vma=False
    )
```
